32 devices in a mesh: band: 8 (over z, y), lev: 4 (over x, core).
Axes of the slice: x: 2, y: 2, z: 4, core: 2. Of those that a mesh axis runs over, the one named last changes fastest.
Arguments:
- spectra: bfloat16 [1280, 2, 120, 1280], P('band', None, 'lev'), may hold values from -6 to 6
- legendre: bfloat16 [1280, 1280, 16], P('band'), may hold values from -0.15625 to 0.15625
- slot_wave: int32 [1280], replicated, may hold values from -1 to 1279, as said below
- row_points: int32 [16], replicated, may hold values from 20 to 5136, as said below
- gauss_weight: float32 [16], replicated, may hold values from 0.5 to 2
- layer_depth: float32 [24], replicated, may hold values from 0.1 to 1
- mode_speed: float32 [120], P('lev'), may hold values from 0.5 to 8
Outputs:
- advanced: float32 [1280, 2, 120, 1280], P('band', None, 'lev')
The draws below stay inside these ranges and needn't reach their ends.
Inputs may be any that keep to these rules, and one draw needn't show every extreme that they name: `slot_wave`: every wavenumber 0 to 1279 stands in exactly one slot. Slots 2k and 2k + 1 of one index of band hold a pair m and 1279 - m, or are both empty. `row_points`: rows 2k and 2k + 1 have 20 + 4 i and 20 + 4 (1279 - i) points for some i in 0 to 1279, in either order, so that together they have 4 * 1279 + 40 points.
All inputs are finite; a program needn't handle non-finite values.
Results may differ from the reference program's by a relative error of at most 0.0043.
Values may be sent and summed in bfloat16 or wider, within the bound.
No kernel may reach another device: no remote copies, remote signals or barrier semaphores. Data moves between devices by JAX's collectives and lax.ppermute only.
A program may use at most 192 MiB of HBM per device.

```python
import math
import jax
import jax.numpy as jnp
from jax import lax

TRUNC = 1279
FIELDS = 5
LEVELS = 24
NDEG = 1280
FLD = 120
SLOTS = 1280
NLAT = 16
NLON_MAX = 5136
N_BAND = 8


def draw_slot_wave(key, part):
    pair_count = (TRUNC + 1) // 2
    slot_count = 2 * ((pair_count + N_BAND - 1) // N_BAND)
    shuffled = jax.random.permutation(key, pair_count).astype(jnp.int32)
    swapped = jax.random.randint(jax.random.fold_in(key, 7), (pair_count,), 0, 2)
    high_wave = TRUNC - shuffled
    first_wave = jnp.where(swapped == 1, high_wave, shuffled)
    second = jnp.where(swapped == 1, shuffled, high_wave)
    position = jnp.arange(pair_count, dtype=jnp.int32)
    device = position % N_BAND
    slot_at = device * slot_count + 2 * (position // N_BAND)
    wave_table = jnp.full((slot_count * N_BAND,), -1, jnp.int32)
    wave_table = wave_table.at[slot_at].set(first_wave).at[slot_at + 1].set(second)
    return wave_table


def draw_row_points(key, part):
    chosen = jax.random.randint(key, (N_BAND,), 0, TRUNC + 1).astype(jnp.int32)
    chosen = chosen.at[0].set(TRUNC)
    swapped = jax.random.randint(jax.random.fold_in(key, 3), (N_BAND,), 0, 2)
    north_pts = 20 + 4 * chosen
    south_pts = 20 + 4 * (TRUNC - chosen)
    first_row = jnp.where(swapped == 1, south_pts, north_pts)
    second = jnp.where(swapped == 1, north_pts, south_pts)
    return jnp.stack([first_row, second], axis=1).reshape(2 * N_BAND).astype(jnp.int32)


def steps_of(stream_key, dims, split, smallest, top_value):
    def one(dim, blocks):
        heights = jax.random.uniform(jax.random.fold_in(jax.random.fold_in(stream_key, 6), dim), (blocks,), jnp.float32, smallest / len(split), top_value / len(split))
        return jnp.repeat(jnp.exp(heights), dims[dim] // blocks).reshape((-1,) + (1,) * (len(dims) - dim - 1))

    loudness = one(*split[0])
    for cut in split[1:]:
        loudness = loudness * one(*cut)
    return loudness


def centred(stream_key, dims, spread, limit, shards=(), kind=jnp.bfloat16):
    loudness = steps_of(stream_key, dims, shards, -0.22, 0.18) if shards else 1.0
    result = jax.random.normal(stream_key, dims, jnp.float32) * spread * loudness
    return jnp.minimum(jnp.maximum(result, -limit), limit).astype(kind)


def setup_inputs(seed: int = 0) -> dict:
    keys = jax.random.split(jax.random.key(seed), 8)
    spectra = centred(keys[0], (SLOTS, 2, FLD, NDEG), 1.0, 6.0, ((0, 8), (2, 4)))
    legendre = centred(keys[1], (SLOTS, NDEG, NLAT), NDEG ** -0.5, 0.15625, ((0, 8),))
    slot_wave = draw_slot_wave(jax.random.fold_in(keys[7], 71), 0)
    row_points = draw_row_points(jax.random.fold_in(keys[7], 71), 0)
    gauss_weight = jnp.clip(jnp.exp(jax.random.uniform(keys[4], (NLAT,), jnp.float32, math.log(0.5), math.log(2.0))), 0.5, 2.0)
    layer_depth = jnp.clip(jnp.exp(jax.random.uniform(keys[5], (LEVELS,), jnp.float32, math.log(0.1), math.log(1.0))), 0.1, 1.0)
    mode_speed = jnp.clip(jnp.exp(math.log(8.0) - 2.7725887 * jax.random.uniform(keys[6], (FLD,), jnp.float32) ** steps_of(keys[6], (FLD,), ((0, 4),), -0.2, 0.2)), 0.5, 8.0)
    return dict(spectra=spectra, legendre=legendre, slot_wave=slot_wave, row_points=row_points, gauss_weight=gauss_weight, layer_depth=layer_depth, mode_speed=mode_speed)


precise = lax.Precision.HIGHEST
time_step = 1.0

def make_basis(wave_table, row_len, column, inside):
    wave_num = jnp.maximum(wave_table, 0)[:, None]
    residue = wave_num * column[None, :] % row_len[None, :]
    row_float = row_len.astype(jnp.float32)[None, :]
    phase_angle = residue.astype(jnp.float32) * (2.0 * math.pi / row_float)
    active = (wave_table[:, None] >= 0) & (2 * wave_table[:, None] <= row_len[None, :] - 1) & inside[None, :]
    norm_scale = jnp.where(active, 1.0 / jnp.sqrt(row_float), jnp.zeros((), jnp.float32))
    return jnp.stack([jnp.cos(phase_angle) * norm_scale, -jnp.sin(phase_angle) * norm_scale]).astype(jnp.bfloat16)

def grid_terms(grid_vals, layer_depth):
    width = grid_vals.shape[1]
    stacked = grid_vals.reshape(FIELDS, LEVELS, width)
    wind_u = stacked[0]
    wind_v = stacked[1]
    temper = stacked[2]
    humid = stacked[3]
    ozone_mix = stacked[4]
    level_ids = jnp.arange(LEVELS, dtype=jnp.int32)
    tri_ones = (level_ids[None, :] >= level_ids[:, None]).astype(jnp.float32) * layer_depth[None, :]
    geopotential = jnp.dot(tri_ones, temper, precision=precise)
    energy = 0.5 * (wind_u * wind_u + wind_v * wind_v) + geopotential
    outputs = jnp.stack([wind_u * temper, wind_v * temper, wind_u * humid, wind_v * ozone_mix, energy])
    return outputs.reshape(FIELDS * LEVELS, width).astype(jnp.bfloat16)

def reference(spectra, legendre, slot_wave, row_points, gauss_weight, layer_depth, mode_speed):
    degree = jnp.arange(NDEG, dtype=jnp.int32)
    live_mask = (slot_wave[:, None] >= 0) & (degree[None, :] >= slot_wave[:, None])
    masked = jnp.where(live_mask[:, None, None, :], spectra, jnp.zeros((), spectra.dtype))

    def inverse_slot(operands):
        coeffs, table = operands
        product = jnp.einsum('cfn,nr->rcf', coeffs.astype(jnp.float32), table.astype(jnp.float32), precision=precise)
        return product.astype(jnp.bfloat16)
    fourier = jnp.transpose(lax.map(inverse_slot, (masked, legendre)), (1, 0, 2, 3))
    weight_mult = (jnp.where(slot_wave == 0, 1.0, 2.0) * (slot_wave >= 0)).astype(jnp.float32)
    column = jnp.arange(NLON_MAX, dtype=jnp.int32)

    def one_row(operands):
        coeffs, row_count, row_weight = operands
        row_len = jnp.full((NLON_MAX,), row_count, jnp.int32)
        basis_table = make_basis(slot_wave, row_len, column, column < row_count).astype(jnp.float32)
        scaled = coeffs.astype(jnp.float32) * weight_mult[:, None, None]
        grid_vals = jnp.einsum('scf,csp->fp', scaled, basis_table, precision=precise)
        tendency = grid_terms(grid_vals, layer_depth).astype(jnp.float32)
        analysed = jnp.einsum('fp,csp->scf', tendency, basis_table, precision=precise)
        return (analysed * row_weight).astype(jnp.bfloat16)
    returned = lax.map(one_row, (fourier, row_points, gauss_weight))

    def forward_slot(operands):
        coeffs, table = operands
        return jnp.einsum('rcf,nr->cfn', coeffs.astype(jnp.float32), table.astype(jnp.float32), precision=precise)
    tendency_spec = lax.map(forward_slot, (jnp.transpose(returned, (1, 0, 2, 3)), legendre))
    helm_factor = (degree * (degree + 1)).astype(jnp.float32) / float(TRUNC * (TRUNC + 1))
    denominator = 1.0 + time_step * time_step * helm_factor[None, None, None, :] * mode_speed[None, None, :, None]
    advanced = (masked.astype(jnp.float32) + time_step * tendency_spec) / denominator
    return jnp.where(live_mask[:, None, None, :], advanced, jnp.zeros((), advanced.dtype))
```

```python
import functools
import math

import jax
import jax.numpy as jnp
from jax import lax
from jax.experimental import pallas as pl
from jax.experimental.layout import Layout, with_layout_constraint
from jax.experimental.pallas import tpu as pltpu
from jax.sharding import PartitionSpec as P

FIELDS = 5
LEVELS = 24
TEMPER = 2
ENERGY = 4
LVL_ROWS = 8
SLAB = 128
MIB = 1024 * 1024

time_step = 1.0

COS_POLY = (
    0.9999999890590235, -19.739204499453994, 64.93911745989843, -85.45013953092186,
    60.167630951185615, -25.967599249120923, 6.528658161956132,
)
SIN_POLY = (
    6.283185302511506, -41.3417004053176, 81.60513138579954, -76.70301535389986,
    42.02592698629647, -14.89984666973851, 3.2381375126489513,
)


def up_to(value, unit):
    return -(-value // unit) * unit


class Sizes:
    def __init__(self, bands, groups, slots, fields, degrees, rows):
        self.bands, self.groups = bands, groups
        self.slots, self.fields, self.degrees, self.rows = slots, fields, degrees, rows
        self.tiles = degrees // SLAB
        self.slot_rows = fields * self.tiles * 2
        self.field_pad = up_to(fields, 8)
        self.share = -(-fields // groups)
        self.lanes = 4 * self.share
        self.quarters = 2
        if 4 * self.lanes <= SLAB and slots % 4 == 0:
            self.quarters = 4
        self.halves = self.quarters // 2
        self.chunk_live = slots // self.quarters
        self.chunk = up_to(self.chunk_live, 8)
        self.spots = self.quarters * self.chunk
        self.block = slots
        for size in (8, 4):
            if slots % size == 0 and (size * self.slot_rows) % 16 == 0:
                self.block = size
                break
        self.steps = slots // self.block
        self.pairs = self.halves * bands * self.chunk
        self.trunc = degrees - 1
        self.orbits = up_to((4 * self.trunc + 40) // 4 + 2, SLAB)
        self.levels = LEVELS // groups
        self.row_fields = FIELDS * LVL_ROWS


def owners(sizes, field):
    first, last = field * LEVELS, (field + 1) * LEVELS
    return [
        g for g in range(sizes.groups)
        if g * sizes.fields < last and (g + 1) * sizes.fields > first
    ]


def geo_rounds(sizes):
    sources, targets = owners(sizes, TEMPER), owners(sizes, ENERGY)
    wide = max(len(sources), len(targets))
    rounds = []
    for turn in range(wide):
        pairs = []
        for k in range(wide):
            s, t = k, (k + turn) % wide
            if s < len(sources) and t < len(targets):
                pairs.append((sources[s], targets[t]))
        if pairs:
            rounds.append(pairs)
    return rounds


def iota(shape, dim):
    return lax.broadcasted_iota(jnp.int32, shape, dim)


def one_hot(cond):
    return jnp.where(cond, 1.0, 0.0).astype(jnp.bfloat16)


def dot(a, b, dims=((1,), (0,))):
    return lax.dot_general(a, b, (dims, ((), ())), preferred_element_type=jnp.float32)


def chunk_position(sizes, lane):
    quarter = lane // sizes.lanes
    rest = lane % sizes.lanes
    row = rest // (2 * sizes.share)
    comp = rest // sizes.share % 2
    item = rest % sizes.share
    return quarter, row, comp, item


def spread_matrix(sizes, lev, transposed):
    tall = sizes.quarters * 4 * sizes.field_pad
    wide = sizes.groups * SLAB
    shape = (wide, tall) if transposed else (tall, wide)
    src = iota(shape, 1 if transposed else 0)
    dst = iota(shape, 0 if transposed else 1)
    group = dst // SLAB
    quarter, row, comp, item = chunk_position(sizes, dst % SLAB)
    start = lev * sizes.fields
    field = lax.rem(group - start % sizes.groups + sizes.groups, sizes.groups) + sizes.groups * item
    want = ((quarter * 2 + row) * 2 + comp) * sizes.field_pad + field
    return one_hot((src == want) & (field < sizes.fields) & (quarter < sizes.quarters))


def inverse_kernel(
    sizes, wave, lev_ref, geo_at, x_ref, leg_ref, depth_ref, active_ref,
    send_ref, geo_ref, wide, spots,
):
    step = pl.program_id(0)
    sz = sizes
    height = 2 * sz.slot_rows

    @pl.when(step == 0)
    def _():
        spots[...] = jnp.zeros_like(spots)
        wide[:, pl.ds(height, wide.shape[1] - height), :] = jnp.zeros(
            (wide.shape[0], wide.shape[1] - height, SLAB), jnp.float32
        )

    degree = iota((1, sz.degrees), 1)
    for pair in range(sz.block // 2):
        buf = wide.at[pair % wide.shape[0]]
        buf[pl.ds(0, height), :] = x_ref[pl.ds(pair * height, height), :].astype(jnp.float32)
        place = step * (sz.block // 2) + pair
        first_odd = wave[2 * place] & 1
        for side in range(2):
            number = wave[2 * place + side]
            table = jnp.where(degree >= number, leg_ref[2 * pair + side].astype(jnp.float32), 0.0)
            table = table.astype(jnp.bfloat16)
            total = jnp.zeros((sz.rows, 2 * sz.field_pad), jnp.float32)
            for t in range(0, sz.tiles, 2):
                parts = []
                for tt in range(t, min(t + 2, sz.tiles)):
                    parts.append(jnp.concatenate([
                        buf[pl.ds(side * sz.slot_rows + 2 * tt + c, sz.field_pad, stride=2 * sz.tiles), :]
                        for c in range(2)
                    ], axis=0).astype(jnp.bfloat16))
                values = jnp.concatenate(parts, axis=1)
                piece = table[:, t * SLAB:t * SLAB + values.shape[1]]
                total += dot(piece, values, ((1,), (1,)))
            odd = first_odd if side == 0 else 1 - first_odd
            half = place // sz.chunk_live
            spot = (odd * sz.halves + half) * sz.chunk + (place - half * sz.chunk_live)
            at = pl.multiple_of(spot * sz.rows, sz.rows)
            spots[pl.ds(at, sz.rows), 0:2 * sz.field_pad] = total

    @pl.when(step == sz.steps - 1)
    def _():
        lev = lev_ref[0]
        spread = spread_matrix(sz, lev, False)
        pad = 2 * sz.field_pad
        shape = (2 * pad, SLAB)
        src, dst = iota(shape, 0), iota(shape, 1)
        weights = []
        for turn in range(geo_ref.shape[0]):
            field = lev * sz.fields + src % sz.field_pad
            under = field - TEMPER * LEVELS
            above = geo_at[turn] + dst % sz.field_pad
            hit = (
                (src // sz.field_pad == dst // sz.field_pad) & (src % sz.field_pad < sz.fields)
                & (under >= 0) & (under < LEVELS) & (above >= 0) & (above <= under)
                & (dst % sz.field_pad < sz.fields)
            )
            weight = jnp.where(hit, depth_ref[...], 0.0)
            high = weight.astype(jnp.bfloat16)
            low = (weight - high.astype(jnp.float32)).astype(jnp.bfloat16)
            weights.append(jnp.concatenate([high, low], axis=0))
        number = active_ref[:, 0:1]
        mult = jnp.where(number > 0, 2.0, jnp.where(number == 0, 1.0, 0.0))
        geo_lane = iota((sz.spots, SLAB), 1)
        for rp in range(sz.rows // 2):
            both = jnp.concatenate([
                spots[pl.ds(2 * rp + r, sz.spots, stride=sz.rows), :][:, 0:pad] for r in range(2)
            ], axis=1)
            exact = both.astype(jnp.bfloat16)
            scaled = (exact.astype(jnp.float32) * mult)
            cut = jnp.concatenate([
                scaled[q * sz.chunk:(q + 1) * sz.chunk] for q in range(sz.quarters)
            ], axis=1).astype(jnp.bfloat16)
            chunk = dot(cut, spread).astype(jnp.bfloat16)
            for g in range(sz.groups):
                send_ref[rp, g] = chunk[:, g * SLAB:(g + 1) * SLAB]
            points = jnp.where(
                geo_lane // pad == 0, active_ref[:, 1 + 2 * rp:2 + 2 * rp],
                active_ref[:, 2 + 2 * rp:3 + 2 * rp],
            )
            sine_zero = (number == 0) & (geo_lane // sz.field_pad % 2 == 1)
            points = jnp.where(sine_zero, 0.0, points)
            double = jnp.concatenate([exact, exact], axis=1)
            for turn in range(geo_ref.shape[0]):
                geo_ref[turn, rp] = (dot(double, weights[turn]) * points).astype(jnp.bfloat16)


def basis_kernel(sizes, points_ref, even_ref, out_ref, rows):
    sz = sizes
    width = sz.orbits

    def turn_of(mj, length, inverse):
        whole = jnp.floor(mj * inverse + 0.5)
        return (mj - whole * length) * inverse

    def cos_sin(z):
        y = z * z
        c = jnp.full_like(y, COS_POLY[-1])
        for a in COS_POLY[-2::-1]:
            c = c * y + a
        s = jnp.full_like(y, SIN_POLY[-1])
        for a in SIN_POLY[-2::-1]:
            s = s * y + a
        return c, s * z

    @pl.when(pl.program_id(0) == 0)
    def _():
        length_a = points_ref[0].astype(jnp.float32)
        length_b = points_ref[1].astype(jnp.float32)
        count_a = points_ref[0] // 4 + 1
        at = iota((8, width), 1)
        second = at >= count_a
        column = (at - jnp.where(second, count_a, 0)).astype(jnp.float32)
        length = jnp.where(second, length_b, length_a)
        inverse = 1.0 / length
        c, s = cos_sin(turn_of(sz.trunc * column, length, inverse))
        rows[0] = column
        rows[1] = length
        rows[2] = inverse
        rows[3] = 1.0 / jnp.sqrt(length)
        rows[4] = c
        rows[5] = s

    high = out_ref.shape[1]
    tall = 32
    for at in range(0, width, SLAB):
        cols = pl.ds(at, SLAB)
        column, length, inverse, scale, top_c, top_s = (
            jnp.concatenate([rows[k, :, cols]] * (tall // 8), axis=0) for k in range(6)
        )
        bound = 0.5 * (length - 1.0)

        def body(i, carry):
            start = pl.multiple_of(i * tall, tall)
            even = even_ref[pl.ds(start, tall), :]
            c, s = cos_sin(turn_of(even * column, length, inverse))
            c = c * scale
            s = s * scale
            oc = top_c * c + top_s * s
            os = top_s * c - top_c * s
            live = even <= bound
            odd_live = (sz.trunc - even) <= bound
            dest = pl.ds(start, tall)
            out_ref[0, dest, cols] = jnp.where(live, c, 0.0).astype(jnp.bfloat16)
            out_ref[1, dest, cols] = jnp.where(live, -s, 0.0).astype(jnp.bfloat16)
            out_ref[2, dest, cols] = jnp.where(odd_live, oc, 0.0).astype(jnp.bfloat16)
            out_ref[3, dest, cols] = jnp.where(odd_live, -os, 0.0).astype(jnp.bfloat16)
            return carry

        lax.fori_loop(0, high // tall, body, 0)


def take_matrix(sizes, lev, transposed):
    sz = sizes
    tall = sz.groups * SLAB
    wide = sz.quarters * 2 * SLAB
    shape = (wide, tall) if transposed else (tall, wide)
    src = iota(shape, 1 if transposed else 0)
    dst = iota(shape, 0 if transposed else 1)
    piece = dst // SLAB
    lane = dst % SLAB
    row = lane // sz.row_fields
    field = lane % sz.row_fields // LVL_ROWS
    level = lane % LVL_ROWS
    whole = field * LEVELS + level * sz.groups + lev
    owner = whole // sz.fields
    start = owner * sz.fields
    first = lax.rem(lev - start % sz.groups + sz.groups, sz.groups)
    item = (whole - start - first) // sz.groups
    want = owner * SLAB + (piece // 2) * sz.lanes + (row * 2 + piece % 2) * sz.share + item
    return one_hot((src == want) & (row < 2) & (level < sz.levels))


def grid_kernel(sizes, points_ref, gauss_ref, lev_ref, recv_ref, basis_ref, send_ref, terms):
    sz = sizes
    lev = lev_ref[0]
    width = sz.bands * sz.chunk
    joined = jnp.concatenate([
        recv_ref[:, g].astype(jnp.float32).reshape(width, SLAB) for g in range(sz.groups)
    ], axis=1).astype(jnp.bfloat16)
    taken = dot(joined, take_matrix(sz, lev, False))
    coeffs = []
    for parity in range(2):
        for comp in range(2):
            parts = []
            for half in range(sz.halves):
                piece = (parity * sz.halves + half) * 2 + comp
                parts.append(taken[:, piece * SLAB:(piece + 1) * SLAB])
            coeffs.append(jnp.concatenate(parts, axis=0).T.astype(jnp.bfloat16)[0:2 * sz.row_fields])
    count_a = points_ref[0] // 4 + 1
    count_b = points_ref[1] // 4 + 1
    high = sz.row_fields
    for at in range(0, sz.orbits, SLAB):
        cols = pl.ds(at, SLAB)
        place = iota((1, SLAB), 1) + at
        second = place >= count_a
        grids = []
        for k in range(4):
            both = dot(coeffs[k], basis_ref[k, :, cols])
            grids.append(jnp.where(second, both[high:], both[:high]))
        ce, se, co, so = grids
        plus, minus = ce + co, ce - co
        splus, sminus = se + so, se - so
        values = (plus + splus, minus - sminus, minus + sminus, plus - splus)
        outs = []
        for v in values:
            u, w, tem, hum, ozo = (v[i * LVL_ROWS:(i + 1) * LVL_ROWS] for i in range(FIELDS))
            outs.append(jnp.concatenate(
                [u * tem, w * tem, u * hum, w * ozo, 0.5 * (u * u + w * w)], axis=0
            ))
        offset = place - jnp.where(second, count_a, 0)
        count = jnp.where(second, count_b, count_a)
        weight = jnp.where((offset == 0) | (offset == count - 1), 0.5, 1.0)
        weight = jnp.where(offset < count, weight, 0.0)
        t0, t1, t2, t3 = (o * weight for o in outs)
        a, b, c, d = t0 + t3, t1 + t2, t0 - t3, t2 - t1
        folds = (a + b, c + d, a - b, c - d)
        for k in range(4):
            first = jnp.where(second, 0.0, folds[k])
            last = jnp.where(second, folds[k], 0.0)
            empty = jnp.zeros((SLAB - 2 * high, SLAB), jnp.float32)
            terms[k, :, cols] = jnp.concatenate([first, last, empty], axis=0).astype(jnp.bfloat16)
    gauss = jnp.where(iota((1, SLAB), 1) < high, gauss_ref[0], gauss_ref[1])
    back = []
    for k in range(4):
        back.append((dot(basis_ref[k], terms[k], ((1,), (1,))) * gauss).astype(jnp.bfloat16))
    columns = []
    for parity in range(2):
        for half in range(sz.halves):
            for comp in range(2):
                columns.append(back[parity * 2 + comp][half * width:(half + 1) * width])
    sent = dot(jnp.concatenate(columns, axis=1), take_matrix(sz, lev, True))
    for g in range(sz.groups):
        part = sent[:, g * SLAB:(g + 1) * SLAB].reshape(sz.bands, sz.chunk, SLAB)
        send_ref[:, g] = part.astype(jnp.bfloat16)


def forward_kernel(
    sizes, wave, lev_ref, back_ref, geo_ref, x_ref, leg_ref, speed_ref, out_ref,
    wide, spots, inverse,
):
    sz = sizes
    step = pl.program_id(0)
    pad = 2 * sz.field_pad
    height = 2 * sz.slot_rows

    @pl.when(step == 0)
    def _():
        wide[:, pl.ds(height, wide.shape[1] - height), :] = jnp.zeros(
            (wide.shape[0], wide.shape[1] - height, SLAB), jnp.float32
        )
        gather = spread_matrix(sz, lev_ref[0], True)
        for rp in range(sz.rows // 2):
            cut = jnp.concatenate([back_ref[rp, g] for g in range(sz.groups)], axis=1)
            whole = dot(cut, gather)
            rows = jnp.concatenate([
                whole[:, q * 2 * pad:(q + 1) * 2 * pad] for q in range(sz.quarters)
            ], axis=0)
            for turn in range(geo_ref.shape[0]):
                rows = rows + geo_ref[turn, rp].astype(jnp.float32)[:, 0:2 * pad]
            for r in range(2):
                part = rows[:, r * pad:(r + 1) * pad]
                part = jnp.concatenate([part, jnp.zeros((sz.spots, SLAB - pad), jnp.float32)], axis=1)
                spots[pl.ds(2 * rp + r, sz.spots, stride=sz.rows), :] = part
        for t in range(sz.tiles):
            degree = iota((sz.field_pad, SLAB), 1) + t * SLAB
            helm = (degree * (degree + 1)).astype(jnp.float32) / float(sz.trunc * (sz.trunc + 1))
            inverse[t] = 1.0 / (1.0 + time_step * time_step * helm * speed_ref[...])

    for pair in range(sz.block // 2):
        buf = wide.at[pair % wide.shape[0]]
        buf[pl.ds(0, height), :] = x_ref[pl.ds(pair * height, height), :].astype(jnp.float32)
        place = step * (sz.block // 2) + pair
        first_odd = wave[2 * place] & 1
        for side in range(2):
            number = wave[2 * place + side]
            floor = jnp.where(number < 0, sz.degrees, number)
            odd = first_odd if side == 0 else 1 - first_odd
            half = place // sz.chunk_live
            spot = (odd * sz.halves + half) * sz.chunk + (place - half * sz.chunk_live)
            at = pl.multiple_of(spot * sz.rows, sz.rows)
            left = spots[pl.ds(at, sz.rows), :].T.astype(jnp.bfloat16)[0:pad]
            base = (2 * pair + side) * sz.slot_rows
            for t in range(sz.tiles):
                tend = dot(left, leg_ref[2 * pair + side, :, t * SLAB:(t + 1) * SLAB])
                live = iota((1, SLAB), 1) + t * SLAB >= floor
                for c in range(2):
                    old = buf[pl.ds(side * sz.slot_rows + 2 * t + c, sz.field_pad, stride=2 * sz.tiles), :]
                    new = (old + time_step * tend[c * sz.field_pad:(c + 1) * sz.field_pad]) * inverse[t]
                    new = jnp.where(live, new, 0.0)
                    out_ref[pl.ds(base + 2 * t + c, sz.fields, stride=2 * sz.tiles), :] = new[0:sz.fields]


def params(mib):
    return pltpu.CompilerParams(vmem_limit_bytes=mib * MIB)


def smem():
    return pl.BlockSpec(memory_space=pltpu.SMEM)


def whole_block(shape):
    return pl.BlockSpec(shape, lambda *_: (0,) * len(shape))


def shards(spectra, legendre, slot_wave, row_points, gauss_weight, layer_depth, mode_speed):
    slots, _, fields, degrees = spectra.shape
    rows = legendre.shape[2]
    sz = Sizes(lax.axis_size("band"), lax.axis_size("lev"), slots, fields, degrees, rows)
    band_index = lax.axis_index("band")
    lev_index = lax.axis_index("lev")
    lev = lev_index.astype(jnp.int32).reshape(1)
    wave = lax.dynamic_slice_in_dim(slot_wave, band_index * slots, slots)
    own_points = lax.dynamic_slice_in_dim(row_points, band_index * 2, 2)
    own_weight = lax.dynamic_slice_in_dim(gauss_weight, band_index * 2, 2)

    lines = spectra.reshape(slots, 2, fields, sz.tiles, SLAB)
    lines = with_layout_constraint(lines, Layout((0, 2, 3, 1, 4)))
    lines = lines.transpose(0, 2, 3, 1, 4).reshape(slots * sz.slot_rows, SLAB)
    tables = legendre.transpose(0, 2, 1)

    pair_wave = slot_wave.reshape(-1, 2)
    even_wave = jnp.where(pair_wave[:, 0] % 2 == 0, pair_wave[:, 0], pair_wave[:, 1])
    even_wave = even_wave.reshape(sz.bands, sz.halves, sz.chunk_live)
    even_wave = jnp.pad(even_wave, ((0, 0), (0, 0), (0, sz.chunk - sz.chunk_live)), constant_values=0)
    even_wave = even_wave.transpose(1, 0, 2).reshape(sz.pairs, 1).astype(jnp.float32)

    own_pair = wave.reshape(-1, 2)
    swap = own_pair[:, :1] % 2 != 0
    own_pair = jnp.where(swap, own_pair[:, ::-1], own_pair)
    spot_wave = own_pair.reshape(sz.halves, sz.chunk_live, 2).transpose(2, 0, 1)
    spot_wave = jnp.pad(
        spot_wave, ((0, 0), (0, 0), (0, sz.chunk - sz.chunk_live)), constant_values=-1
    ).reshape(sz.spots, 1)
    reach = (spot_wave >= 0) & (2 * spot_wave <= row_points[None, :] - 1)
    active = jnp.concatenate(
        [spot_wave.astype(jnp.float32), jnp.where(reach, gauss_weight[None, :], 0.0)], axis=1
    )

    rounds = geo_rounds(sz)
    places = []
    for pairs in rounds:
        table = [2 * LEVELS + sz.fields] * sz.groups
        for source, target in pairs:
            table[source] = target * sz.fields - ENERGY * LEVELS
        places.append(table)
    geo_at = jnp.array(places, jnp.int32)[:, lev_index]
    held = lev_index * sz.fields + jnp.arange(sz.field_pad, dtype=jnp.int32) - TEMPER * LEVELS
    depth = layer_depth[jnp.clip(held, 0, LEVELS - 1)]
    depth = jnp.tile(depth, 4).reshape(4 * sz.field_pad, 1)

    tail = up_to((sz.field_pad - sz.fields) * 2 * sz.tiles, 16)
    wide_shape = pltpu.VMEM((2, 2 * sz.slot_rows + tail, SLAB), jnp.float32)
    spots_shape = pltpu.VMEM((sz.spots * sz.rows, SLAB), jnp.float32)
    lines_block = (sz.block * sz.slot_rows, SLAB)
    table_block = (sz.block, sz.rows, degrees)
    send_shape = (sz.bands, sz.groups, sz.chunk, SLAB)
    geo_shape = (len(rounds), sz.rows // 2, sz.spots, SLAB)

    sent, geo = pl.pallas_call(
        functools.partial(inverse_kernel, sz),
        grid=(sz.steps,),
        in_specs=[
            smem(), smem(), smem(),
            pl.BlockSpec(lines_block, lambda i: (i, 0)),
            pl.BlockSpec(table_block, lambda i: (i, 0, 0)),
            whole_block(depth.shape),
            whole_block(active.shape),
        ],
        out_specs=[whole_block(send_shape), whole_block(geo_shape)],
        out_shape=[
            jax.ShapeDtypeStruct(send_shape, jnp.bfloat16),
            jax.ShapeDtypeStruct(geo_shape, jnp.bfloat16),
        ],
        scratch_shapes=[wide_shape, spots_shape],
        compiler_params=params(32),
        name="inverse_legendre",
    )(wave, lev, geo_at, lines, tables, depth, active)

    both = ("band", "lev")
    total = sz.bands * sz.groups
    flat = (total * sz.chunk, SLAB)
    arrived = lax.all_to_all(sent.reshape(flat), both, split_axis=0, concat_axis=0, tiled=True)
    geo_here = jnp.stack([
        lax.ppermute(geo[turn], "lev", pairs) for turn, pairs in enumerate(rounds)
    ])

    basis_shape = (4, sz.pairs, sz.orbits)
    high = SLAB if sz.pairs % SLAB == 0 else sz.pairs
    basis = pl.pallas_call(
        functools.partial(basis_kernel, sz),
        grid=(sz.pairs // high,),
        in_specs=[smem(), pl.BlockSpec((high, 1), lambda i: (i, 0))],
        out_specs=pl.BlockSpec((4, high, sz.orbits), lambda i: (0, i, 0)),
        out_shape=jax.ShapeDtypeStruct(basis_shape, jnp.bfloat16),
        scratch_shapes=[pltpu.VMEM((6, 8, sz.orbits), jnp.float32)],
        compiler_params=params(32),
        cost_estimate=pl.CostEstimate(flops=60 * sz.pairs * sz.orbits, bytes_accessed=8 * sz.pairs * sz.orbits, transcendentals=0),
        name="basis",
    )(own_points, even_wave)

    returned = pl.pallas_call(
        functools.partial(grid_kernel, sz),
        in_specs=[smem(), smem(), smem()] + [pl.BlockSpec(memory_space=pltpu.VMEM)] * 2,
        out_specs=pl.BlockSpec(memory_space=pltpu.VMEM),
        out_shape=jax.ShapeDtypeStruct(send_shape, jnp.bfloat16),
        scratch_shapes=[pltpu.VMEM((4, SLAB, sz.orbits), jnp.bfloat16)],
        compiler_params=params(40),
        name="grid_products",
    )(own_points, own_weight, lev, arrived.reshape(send_shape), basis)

    back = lax.all_to_all(returned.reshape(flat), both, split_axis=0, concat_axis=0, tiled=True)

    speed = jnp.pad(mode_speed, (0, sz.field_pad - fields)).reshape(sz.field_pad, 1)
    out = pl.pallas_call(
        functools.partial(forward_kernel, sz),
        grid=(sz.steps,),
        in_specs=[
            smem(), smem(),
            whole_block(send_shape), whole_block(geo_shape),
            pl.BlockSpec(lines_block, lambda i: (i, 0)),
            pl.BlockSpec(table_block, lambda i: (i, 0, 0)),
            whole_block(speed.shape),
        ],
        out_specs=pl.BlockSpec(lines_block, lambda i: (i, 0)),
        out_shape=jax.ShapeDtypeStruct((slots * sz.slot_rows, SLAB), jnp.float32),
        scratch_shapes=[wide_shape, spots_shape, pltpu.VMEM((sz.tiles, sz.field_pad, SLAB), jnp.float32)],
        compiler_params=params(40),
        name="forward_legendre",
    )(wave, lev, back.reshape(send_shape), geo_here, lines, tables, speed)

    out = out.reshape(slots, fields, sz.tiles, 2, SLAB).transpose(0, 1, 3, 2, 4)
    return out.reshape(slots, fields, 2, degrees).transpose(0, 2, 1, 3)


def solution(mesh):
    return jax.shard_map(
        shards,
        mesh=mesh,
        in_specs=(
            P("band", None, "lev", None),
            P("band", None, None),
            P(),
            P(),
            P(),
            P(),
            P("lev"),
        ),
        out_specs=P("band", None, "lev", None),
        check_vma=False,
    )
```

```python
import functools
import math

import jax
import jax.numpy as jnp
from jax import lax
from jax.experimental import pallas as pl
from jax.experimental.layout import Layout, with_layout_constraint
from jax.experimental.pallas import tpu as pltpu
from jax.sharding import PartitionSpec as P

FIELDS = 5
LEVELS = 24
TEMPER = 2
ENERGY = 4
LVL_ROWS = 8
SLAB = 128
MIB = 1024 * 1024

time_step = 1.0

COS_POLY = (
    0.9999999890590235, -19.739204499453994, 64.93911745989843, -85.45013953092186,
    60.167630951185615, -25.967599249120923, 6.528658161956132,
)
SIN_POLY = (
    6.283185302511506, -41.3417004053176, 81.60513138579954, -76.70301535389986,
    42.02592698629647, -14.89984666973851, 3.2381375126489513,
)


def up_to(value, unit):
    return -(-value // unit) * unit


class Sizes:
    def __init__(self, bands, groups, slots, fields, degrees, rows):
        self.bands, self.groups = bands, groups
        self.slots, self.fields, self.degrees, self.rows = slots, fields, degrees, rows
        self.tiles = degrees // SLAB
        self.slot_rows = fields * self.tiles * 2
        self.field_pad = up_to(fields, 8)
        self.share = -(-fields // groups)
        self.lanes = 4 * self.share
        self.quarters = 2
        if 4 * self.lanes <= SLAB and slots % 4 == 0:
            self.quarters = 4
        self.halves = self.quarters // 2
        self.chunk_live = slots // self.quarters
        self.chunk = up_to(self.chunk_live, 8)
        self.spots = self.quarters * self.chunk
        self.block = slots
        for size in (8, 4):
            if slots % size == 0 and (size * self.slot_rows) % 16 == 0:
                self.block = size
                break
        self.steps = slots // self.block
        self.pairs = self.halves * bands * self.chunk
        self.trunc = degrees - 1
        self.sorted = degrees // 2
        self.orbits = up_to((4 * self.trunc + 40) // 4 + 2, SLAB)
        self.levels = LEVELS // groups


def owners(sizes, field):
    first, last = field * LEVELS, (field + 1) * LEVELS
    return [
        g for g in range(sizes.groups)
        if g * sizes.fields < last and (g + 1) * sizes.fields > first
    ]


def geo_rounds(sizes):
    sources, targets = owners(sizes, TEMPER), owners(sizes, ENERGY)
    wide = max(len(sources), len(targets))
    rounds = []
    for turn in range(wide):
        pairs = []
        for k in range(wide):
            s, t = k, (k + turn) % wide
            if s < len(sources) and t < len(targets):
                pairs.append((sources[s], targets[t]))
        if pairs:
            rounds.append(pairs)
    return rounds


def iota(shape, dim):
    return lax.broadcasted_iota(jnp.int32, shape, dim)


def one_hot(cond):
    return jnp.where(cond, 1.0, 0.0).astype(jnp.bfloat16)


def dot(a, b, dims=((1,), (0,))):
    return lax.dot_general(a, b, (dims, ((), ())), preferred_element_type=jnp.float32)


def halving(value):
    return value.bit_length() - 1 if value & (value - 1) == 0 else None


def quotient(x, by):
    bits = halving(by)
    return x >> bits if bits is not None else lax.div(x, jnp.int32(by))


def remainder(x, by):
    return x & (by - 1) if halving(by) is not None else lax.rem(x, jnp.int32(by))


def spread_matrix(sizes, lev):
    sz = sizes
    tall = sz.quarters * 4 * sz.field_pad
    wide = sz.groups * SLAB
    dst = iota((1, wide), 1)
    group = quotient(dst, SLAB)
    lane = remainder(dst, SLAB)
    quarter = quotient(lane, sz.lanes)
    rest = remainder(lane, sz.lanes)
    row = quotient(rest, 2 * sz.share)
    rest = remainder(rest, 2 * sz.share)
    comp = quotient(rest, sz.share)
    item = remainder(rest, sz.share)
    start = remainder(lev * sz.fields, sz.groups)
    field = remainder(group - start + sz.groups, sz.groups) + sz.groups * item
    want = ((quarter * 2 + row) * sz.field_pad + field) * 2 + comp
    want = jnp.where((field < sz.fields) & (quarter < sz.quarters), want, -1)
    return one_hot(iota((tall, wide), 0) == want)


def inverse_kernel(sizes, rounds, wave, points, gauss, layer_depth, *refs):
    sz = sizes
    x_refs = refs[:sz.tiles]
    leg_ref, send_ref, geo_ref, spots, numbers = refs[sz.tiles:]
    step = pl.program_id(0)
    band = lax.axis_index("band")
    lev = lax.axis_index("lev")
    pad = 2 * sz.field_pad
    live_rows = 2 * sz.fields

    @pl.when(step == 0)
    def _():
        spots[...] = jnp.zeros_like(spots)
        numbers[...] = jnp.full_like(numbers, -1)

    views = [ref.reshape(sz.block, live_rows, SLAB) for ref in x_refs]
    degree = iota((1, sz.degrees), 1)
    for pair in range(sz.block // 2):
        place = step * (sz.block // 2) + pair
        slot = band * sz.slots + 2 * place
        first_odd = wave[slot] & 1
        for side in range(2):
            number = wave[slot + side]
            table = jnp.where(degree >= number, leg_ref[2 * pair + side].astype(jnp.float32), 0.0)
            table = table.astype(jnp.bfloat16)
            total = jnp.zeros((sz.rows, live_rows), jnp.float32)
            for t in range(0, sz.tiles, 2):
                values = jnp.concatenate(
                    [views[tt][2 * pair + side] for tt in range(t, min(t + 2, sz.tiles))], axis=1
                )
                piece = table[:, t * SLAB:t * SLAB + values.shape[1]]
                total += dot(piece, values, ((1,), (1,)))
            odd = first_odd if side == 0 else 1 - first_odd
            half = place // sz.chunk_live
            spot = (odd * sz.halves + half) * sz.chunk + (place - half * sz.chunk_live)
            at = pl.multiple_of(spot * sz.rows, sz.rows)
            spots[pl.ds(at, sz.rows), 0:live_rows] = total
            numbers[pl.ds(spot, 1), :] = jnp.full((1, SLAB), number, jnp.int32)

    @pl.when(step == sz.steps - 1)
    def _():
        spread = spread_matrix(sz, lev)
        shape = (2 * pad, SLAB)
        src, dst = iota(shape, 0), iota(shape, 1)
        from_row, from_field, from_comp = src // pad, (src % pad) >> 1, src & 1
        to_row, to_field, to_comp = dst // pad, (dst % pad) >> 1, dst & 1
        weights = []
        for pairs in rounds:
            first = jnp.int32(2 * LEVELS + sz.fields)
            for source, target in pairs:
                first = jnp.where(lev == source, target * sz.fields - ENERGY * LEVELS, first)
            under = lev * sz.fields + from_field - TEMPER * LEVELS
            above = first + to_field
            hit = (
                (from_row == to_row) & (from_comp == to_comp)
                & (from_field < sz.fields) & (to_field < sz.fields)
                & (above >= 0) & (above <= under)
            )
            weight = jnp.zeros(shape, jnp.float32)
            for level in range(LEVELS):
                weight = jnp.where(hit & (under == level), layer_depth[level], weight)
            high = weight.astype(jnp.bfloat16)
            low = (weight - high.astype(jnp.float32)).astype(jnp.bfloat16)
            weights.append(jnp.concatenate([high, low], axis=0))
        number = numbers[...]
        lane = iota((sz.spots, SLAB), 1)
        known = (number >= 0) & ~((number == 0) & (lane & 1 == 1))
        for rp in range(sz.rows // 2):
            exact = jnp.concatenate([
                spots[pl.ds(2 * rp + r, sz.spots, stride=sz.rows), :][:, 0:pad] for r in range(2)
            ], axis=1)
            cut = jnp.concatenate([
                exact[q * sz.chunk:(q + 1) * sz.chunk] for q in range(sz.quarters)
            ], axis=1).astype(jnp.bfloat16)
            chunk = dot(cut, spread).astype(jnp.bfloat16)
            for g in range(sz.groups):
                send_ref[rp, g] = chunk[:, g * SLAB:(g + 1) * SLAB]
            count = jnp.where(lane < pad, points[2 * rp], points[2 * rp + 1])
            scale = jnp.where(lane < pad, gauss[2 * rp], gauss[2 * rp + 1])
            scale = jnp.where(known & (2 * number <= count - 1), scale, 0.0)
            exact = exact.astype(jnp.bfloat16)
            double = jnp.concatenate([exact, exact], axis=1)
            for turn in range(len(rounds)):
                geo_ref[turn, rp] = (dot(double, weights[turn]) * scale).astype(jnp.bfloat16)


def cos_sin(z):
    y = z * z
    c = jnp.full_like(y, COS_POLY[-1])
    for a in COS_POLY[-2::-1]:
        c = c * y + a
    s = jnp.full_like(y, SIN_POLY[-1])
    for a in SIN_POLY[-2::-1]:
        s = s * y + a
    return c, s * z


def basis_kernel(sizes, points, out_ref, cosines, sines):
    sz = sizes
    step = pl.program_id(0)
    turns = sz.sorted // 16
    bands_row = 16 + up_to(turns, 8)

    @pl.when(step == 0)
    def _():
        first = lax.axis_index("band") * 2
        length_a, length_b = points[first], points[first + 1]
        count_a = length_a // 4 + 1
        high = cosines.shape[0]
        row = iota((high, SLAB), 0)
        number = jnp.where(row < 16, 2 * row, jnp.where(row < bands_row, 32 * (row - 16), sz.trunc))
        number = number.astype(jnp.float32)
        for at in range(0, sz.orbits, SLAB):
            place = iota((1, SLAB), 1) + at
            second = place >= count_a
            column = (place - jnp.where(second, count_a, 0)).astype(jnp.float32)
            length = jnp.where(second, length_b, length_a).astype(jnp.float32)
            inverse = 1.0 / length
            scale = jnp.where(row < 16, 1.0 / jnp.sqrt(length), 1.0)
            product = number * column
            whole = jnp.floor(product * inverse + 0.5)
            c, s = cos_sin((product - whole * length) * inverse)
            cosines[:, pl.ds(at, SLAB)] = c * scale
            sines[:, pl.ds(at, SLAB)] = s * scale

    groups = out_ref.shape[1] // 16
    for at in range(0, sz.orbits, SLAB):
        cols = pl.ds(at, SLAB)
        base_c, base_n = cosines[0:16, cols], -sines[0:16, cols]
        top_c, top_n = cosines[pl.ds(bands_row, 1), cols], -sines[pl.ds(bands_row, 1), cols]
        turn_rows = pl.ds(pl.multiple_of(16 + step * groups, 8), groups)
        all_c, all_s = cosines[turn_rows, cols], sines[turn_rows, cols]
        for k in range(groups):
            turn_c, turn_s = all_c[k:k + 1], all_s[k:k + 1]
            c = turn_c * base_c + turn_s * base_n
            n = turn_c * base_n - turn_s * base_c
            rows = pl.ds(16 * k, 16)
            out_ref[0, rows, cols] = c.astype(jnp.bfloat16)
            out_ref[1, rows, cols] = n.astype(jnp.bfloat16)
            out_ref[2, rows, cols] = (top_c * c + top_n * n).astype(jnp.bfloat16)
            out_ref[3, rows, cols] = (top_n * c - top_c * n).astype(jnp.bfloat16)


def take_matrix(sizes, lev):
    sz = sizes
    tall = sz.groups * SLAB
    wide = sz.quarters * 2 * SLAB
    dst = iota((1, wide), 1)
    piece = quotient(dst, SLAB)
    lane = remainder(dst, SLAB)
    row = quotient(lane, SLAB // 2)
    field = quotient(remainder(lane, SLAB // 2), LVL_ROWS)
    level = remainder(lane, LVL_ROWS)
    whole = field * LEVELS + level * sz.groups + lev
    owner = quotient(whole, sz.fields)
    start = owner * sz.fields
    first = remainder(lev - remainder(start, sz.groups) + sz.groups, sz.groups)
    item = quotient(whole - start - first, sz.groups)
    want = owner * SLAB + (piece >> 1) * sz.lanes + (row * 2 + (piece & 1)) * sz.share + item
    want = jnp.where((field < FIELDS) & (level < sz.levels), want, -1)
    return one_hot(iota((tall, wide), 0) == want)


def grid_kernel(
    sizes, points, gauss, recv_ref, even_row, even_col, basis_hbm, send_ref, basis, terms, arrivals,
):
    sz = sizes
    parts = sz.orbits // SLAB
    copies = []
    for part in range(parts):
        cols = pl.ds(part * SLAB, SLAB)
        copies.append(pltpu.make_async_copy(basis_hbm.at[:, :, cols], basis.at[:, :, cols], arrivals.at[part]))
        copies[-1].start()
    lev = lax.axis_index("lev")
    first_row = lax.axis_index("band") * 2
    length_a, length_b = points[first_row], points[first_row + 1]
    count_a, count_b = length_a // 4 + 1, length_b // 4 + 1
    high = FIELDS * LVL_ROWS
    half_slab = SLAB // 2
    width = sz.bands * sz.chunk
    take = take_matrix(sz, lev)
    order = one_hot(iota((sz.sorted, sz.pairs), 0) * 2 == even_row[...])
    joined = jnp.concatenate([
        recv_ref[:, g].astype(jnp.float32).reshape(width, SLAB) for g in range(sz.groups)
    ], axis=1).astype(jnp.bfloat16)
    taken = dot(joined, take)
    coeffs = []
    number = iota((2 * SLAB, sz.sorted), 1) * 2
    bound = jnp.where(iota((2 * SLAB, sz.sorted), 0) & half_slab == 0, length_a, length_b) - 1
    for parity in range(2):
        rows = []
        for half in range(sz.halves):
            piece = (parity * sz.halves + half) * 2
            rows.append(taken[:, piece * SLAB:(piece + 2) * SLAB])
        values = jnp.concatenate(rows, axis=0).T.astype(jnp.bfloat16)
        placed = dot(values, order, ((1,), (1,)))
        mine = number if parity == 0 else sz.trunc - number
        mult = jnp.where(mine == 0, 1.0, 2.0)
        placed = jnp.where(2 * mine <= bound, placed * mult, 0.0).astype(jnp.bfloat16)
        coeffs += [placed[:SLAB], placed[SLAB:]]
    for part in range(parts):
        copies[part].wait()
        at = part * SLAB
        cols = pl.ds(at, SLAB)
        place = iota((1, SLAB), 1) + at
        second = place >= count_a
        grids = []
        for k in range(4):
            both = dot(coeffs[k], basis[k, :, cols])
            grids.append(jnp.where(second, both[half_slab:half_slab + high], both[:high]))
        ce, se, co, so = grids
        plus, minus = ce + co, ce - co
        splus, sminus = se + so, se - so
        values = (plus + splus, minus - sminus, minus + sminus, plus - splus)
        outs = []
        for v in values:
            u, w, tem, hum, ozo = (v[i * LVL_ROWS:(i + 1) * LVL_ROWS] for i in range(FIELDS))
            outs.append(jnp.concatenate(
                [u * tem, w * tem, u * hum, w * ozo, 0.5 * (u * u + w * w)], axis=0
            ))
        offset = place - jnp.where(second, count_a, 0)
        count = jnp.where(second, count_b, count_a)
        weight = jnp.where((offset == 0) | (offset == count - 1), 0.5, 1.0)
        weight = jnp.where(offset < count, weight, 0.0)
        t0, t1, t2, t3 = (o * weight for o in outs)
        a, b, c, d = t0 + t3, t1 + t2, t0 - t3, t2 - t1
        folds = (a + b, c + d, a - b, c - d)
        empty = jnp.zeros((half_slab - high, SLAB), jnp.float32)
        for k in range(4):
            first = jnp.where(second, 0.0, folds[k])
            last = jnp.where(second, folds[k], 0.0)
            terms[k, :, cols] = jnp.concatenate([first, empty, last, empty], axis=0).astype(jnp.bfloat16)
    lane = iota((1, SLAB), 1)
    scale = jnp.where(lane < half_slab, gauss[first_row], gauss[first_row + 1])
    bound = jnp.where(lane < half_slab, length_a, length_b) - 1
    number = iota((sz.sorted, SLAB), 0) * 2
    back_order = one_hot(iota((sz.pairs, sz.sorted), 1) * 2 == even_col[...])
    pieces = []
    for parity in range(2):
        mine = number if parity == 0 else sz.trunc - number
        sums = jnp.concatenate([
            jnp.where(
                2 * mine <= bound,
                dot(basis[parity * 2 + comp], terms[parity * 2 + comp], ((1,), (1,))) * scale, 0.0,
            ).astype(jnp.bfloat16)
            for comp in range(2)
        ], axis=1)
        slots = dot(back_order, sums).astype(jnp.bfloat16)
        pieces += [slots[half * width:(half + 1) * width] for half in range(sz.halves)]
    sent = dot(jnp.concatenate(pieces, axis=1), take, ((1,), (1,)))
    for g in range(sz.groups):
        part = sent[:, g * SLAB:(g + 1) * SLAB].reshape(sz.bands, sz.chunk, SLAB)
        send_ref[:, g] = part.astype(jnp.bfloat16)


def forward_kernel(
    sizes, wave, speed, back_ref, geo_ref, x_ref, leg_ref, out_ref, wide, spots, inverse, speeds,
):
    sz = sizes
    step = pl.program_id(0)
    band = lax.axis_index("band")
    pad = 2 * sz.field_pad
    height = 2 * sz.slot_rows

    @pl.when(step == 0)
    def _():
        wide[:, pl.ds(height, wide.shape[1] - height), :] = jnp.zeros(
            (wide.shape[0], wide.shape[1] - height, SLAB), jnp.float32
        )
        gather = spread_matrix(sz, lax.axis_index("lev"))
        src, dst = iota((2 * pad, 1), 0), iota((1, 2 * pad), 1)
        place = src & (2 * pad - pad) | ((src & 1) * sz.field_pad) | ((src & (pad - 1)) >> 1)
        sort = one_hot(place == dst)
        for rp in range(sz.rows // 2):
            cut = jnp.concatenate([back_ref[rp, g] for g in range(sz.groups)], axis=1)
            whole = dot(cut, gather, ((1,), (1,)))
            rows = jnp.concatenate([
                whole[:, q * 2 * pad:(q + 1) * 2 * pad] for q in range(sz.quarters)
            ], axis=0)
            for turn in range(geo_ref.shape[0]):
                rows = rows + geo_ref[turn, rp].astype(jnp.float32)[:, 0:2 * pad]
            rows = dot(rows.astype(jnp.bfloat16), sort)
            for r in range(2):
                part = rows[:, r * pad:(r + 1) * pad]
                part = jnp.concatenate([part, jnp.zeros((sz.spots, SLAB - pad), jnp.float32)], axis=1)
                spots[pl.ds(2 * rp + r, sz.spots, stride=sz.rows), :] = part
        speeds[...] = jnp.ones_like(speeds)
        for f in range(sz.fields):
            speeds[pl.ds(f, 1), :] = jnp.full((1, SLAB), speed[f], jnp.float32)
        for t in range(sz.tiles):
            degree = iota((1, SLAB), 1) + t * SLAB
            helm = (degree * (degree + 1)).astype(jnp.float32) / float(sz.trunc * (sz.trunc + 1))
            inverse[t] = 1.0 / (1.0 + time_step * time_step * helm * speeds[...])

    for pair in range(sz.block // 2):
        buf = wide.at[pair % wide.shape[0]]
        buf[pl.ds(0, height), :] = x_ref[pl.ds(pair * height, height), :].astype(jnp.float32)
        place = step * (sz.block // 2) + pair
        slot = band * sz.slots + 2 * place
        first_odd = wave[slot] & 1
        for side in range(2):
            number = wave[slot + side]
            floor = jnp.where(number < 0, sz.degrees, number)
            odd = first_odd if side == 0 else 1 - first_odd
            half = place // sz.chunk_live
            spot = (odd * sz.halves + half) * sz.chunk + (place - half * sz.chunk_live)
            at = pl.multiple_of(spot * sz.rows, sz.rows)
            left = spots[pl.ds(at, sz.rows), :].T.astype(jnp.bfloat16)[0:pad]
            base = (2 * pair + side) * sz.slot_rows
            for t in range(sz.tiles):
                tend = dot(left, leg_ref[2 * pair + side, :, t * SLAB:(t + 1) * SLAB])
                live = iota((1, SLAB), 1) + t * SLAB >= floor
                for c in range(2):
                    old = buf[pl.ds(side * sz.slot_rows + 2 * t + c, sz.field_pad, stride=2 * sz.tiles), :]
                    new = (old + time_step * tend[c * sz.field_pad:(c + 1) * sz.field_pad]) * inverse[t]
                    new = jnp.where(live, new, 0.0)
                    out_ref[pl.ds(base + 2 * t + c, sz.fields, stride=2 * sz.tiles), :] = new[0:sz.fields]


def params(mib):
    return pltpu.CompilerParams(vmem_limit_bytes=mib * MIB)


def smem():
    return pl.BlockSpec(memory_space=pltpu.SMEM)


def whole_block(shape):
    return pl.BlockSpec(shape, lambda *_: (0,) * len(shape))


def shards(spectra, legendre, slot_wave, row_points, gauss_weight, layer_depth, mode_speed):
    slots, _, fields, degrees = spectra.shape
    rows = legendre.shape[2]
    sz = Sizes(lax.axis_size("band"), lax.axis_size("lev"), slots, fields, degrees, rows)

    tiled = spectra.reshape(slots, 2, fields, sz.tiles, SLAB)
    tiled = with_layout_constraint(tiled, Layout((0, 2, 3, 1, 4)))
    tiled = tiled.transpose(0, 2, 3, 1, 4)
    lines = tiled.reshape(slots * sz.slot_rows, SLAB)
    tables = legendre.transpose(0, 2, 1)

    rounds = geo_rounds(sz)
    tail = up_to((sz.field_pad - sz.fields) * 2 * sz.tiles, 16)
    wide_shape = pltpu.VMEM((2, 2 * sz.slot_rows + tail, SLAB), jnp.float32)
    spots_shape = pltpu.VMEM((sz.spots * sz.rows, SLAB), jnp.float32)
    lines_block = (sz.block * sz.slot_rows, SLAB)
    table_block = (sz.block, sz.rows, degrees)
    send_shape = (sz.bands, sz.groups, sz.chunk, SLAB)
    geo_shape = (len(rounds), sz.rows // 2, sz.spots, SLAB)

    def tile_spec(t):
        return pl.BlockSpec((sz.block, fields, 1, 2, SLAB), lambda i: (i, 0, t, 0, 0))

    sent, geo = pl.pallas_call(
        functools.partial(inverse_kernel, sz, rounds),
        grid=(sz.steps,),
        in_specs=[smem(), smem(), smem(), smem()]
        + [tile_spec(t) for t in range(sz.tiles)]
        + [pl.BlockSpec(table_block, lambda i: (i, 0, 0))],
        out_specs=[whole_block(send_shape), whole_block(geo_shape)],
        out_shape=[
            jax.ShapeDtypeStruct(send_shape, jnp.bfloat16),
            jax.ShapeDtypeStruct(geo_shape, jnp.bfloat16),
        ],
        scratch_shapes=[spots_shape, pltpu.VMEM((sz.spots, SLAB), jnp.int32)],
        compiler_params=params(56),
        name="inverse_legendre",
    )(slot_wave, row_points, gauss_weight, layer_depth, *([tiled] * sz.tiles), tables)

    both = ("band", "lev")
    total = sz.bands * sz.groups
    flat = (total * sz.chunk, SLAB)
    arrived = lax.all_to_all(sent.reshape(flat), both, split_axis=0, concat_axis=0, tiled=True)

    pair_wave = slot_wave.reshape(-1, 2)
    even_wave = jnp.where(pair_wave[:, 0] % 2 == 0, pair_wave[:, 0], pair_wave[:, 1])
    even_wave = even_wave.reshape(sz.bands, sz.halves, sz.chunk_live)
    even_wave = jnp.pad(even_wave, ((0, 0), (0, 0), (0, sz.chunk - sz.chunk_live)), constant_values=-1)
    even_wave = even_wave.transpose(1, 0, 2).reshape(sz.pairs)

    high = SLAB if sz.sorted % SLAB == 0 else sz.sorted
    table_rows = 16 + up_to(sz.sorted // 16, 8) + 8
    basis = pl.pallas_call(
        functools.partial(basis_kernel, sz),
        grid=(sz.sorted // high,),
        in_specs=[smem()],
        out_specs=pl.BlockSpec((4, high, sz.orbits), lambda i: (0, i, 0)),
        out_shape=jax.ShapeDtypeStruct((4, sz.sorted, sz.orbits), jnp.bfloat16),
        scratch_shapes=[pltpu.VMEM((table_rows, sz.orbits), jnp.float32)] * 2,
        compiler_params=params(56),
        cost_estimate=pl.CostEstimate(
            flops=20 * sz.sorted * sz.orbits, bytes_accessed=8 * sz.sorted * sz.orbits, transcendentals=0,
        ),
        name="basis",
    )(row_points)

    geo, arrived = lax.optimization_barrier((geo, arrived))
    moved = [lax.ppermute(geo[turn], "lev", pairs) for turn, pairs in enumerate(rounds)]
    vmem = pl.BlockSpec(memory_space=pltpu.VMEM)
    returned = pl.pallas_call(
        functools.partial(grid_kernel, sz),
        in_specs=[smem(), smem(), vmem, vmem, vmem, pl.BlockSpec(memory_space=pl.ANY)],
        out_specs=vmem,
        out_shape=jax.ShapeDtypeStruct(send_shape, jnp.bfloat16),
        scratch_shapes=[
            pltpu.VMEM((4, sz.sorted, sz.orbits), jnp.bfloat16),
            pltpu.VMEM((4, SLAB, sz.orbits), jnp.bfloat16),
            pltpu.SemaphoreType.DMA((sz.orbits // SLAB,)),
        ],
        compiler_params=params(56),
        cost_estimate=pl.CostEstimate(
            flops=4 * 4 * SLAB * sz.sorted * sz.orbits, bytes_accessed=8 * sz.sorted * sz.orbits, transcendentals=0,
        ),
        name="grid_products",
    )(
        row_points, gauss_weight, arrived.reshape(send_shape),
        even_wave.reshape(1, sz.pairs), even_wave.reshape(sz.pairs, 1), basis,
    )
    *moved, returned = lax.optimization_barrier((*moved, returned))

    back = lax.all_to_all(returned.reshape(flat), both, split_axis=0, concat_axis=0, tiled=True)

    out = pl.pallas_call(
        functools.partial(forward_kernel, sz),
        grid=(sz.steps,),
        in_specs=[
            smem(), smem(),
            whole_block(send_shape), whole_block(geo_shape),
            pl.BlockSpec(lines_block, lambda i: (i, 0)),
            pl.BlockSpec(table_block, lambda i: (i, 0, 0)),
        ],
        out_specs=pl.BlockSpec(lines_block, lambda i: (i, 0)),
        out_shape=jax.ShapeDtypeStruct((slots * sz.slot_rows, SLAB), jnp.float32),
        scratch_shapes=[
            wide_shape, spots_shape,
            pltpu.VMEM((sz.tiles, sz.field_pad, SLAB), jnp.float32),
            pltpu.VMEM((sz.field_pad, SLAB), jnp.float32),
        ],
        compiler_params=params(56),
        name="forward_legendre",
    )(slot_wave, mode_speed, back.reshape(send_shape), jnp.stack(moved), lines, tables)

    out = out.reshape(slots, fields, sz.tiles, 2, SLAB).transpose(0, 1, 3, 2, 4)
    return out.reshape(slots, fields, 2, degrees).transpose(0, 2, 1, 3)


def solution(mesh):
    return jax.shard_map(
        shards,
        mesh=mesh,
        in_specs=(
            P("band", None, "lev", None),
            P("band", None, None),
            P(),
            P(),
            P(),
            P(),
            P("lev"),
        ),
        out_specs=P("band", None, "lev", None),
        check_vma=False,
    )
```

```python
import functools
import math

import jax
import jax.numpy as jnp
from jax import lax
from jax.experimental import pallas as pl
from jax.experimental.layout import Layout, with_layout_constraint
from jax.experimental.pallas import tpu as pltpu
from jax.sharding import PartitionSpec as P

FIELDS = 5
LEVELS = 24
TEMPER = 2
ENERGY = 4
LVL_ROWS = 8
SLAB = 128
MIB = 1024 * 1024

time_step = 1.0

COS_POLY = (
    0.9999999890590235, -19.739204499453994, 64.93911745989843, -85.45013953092186,
    60.167630951185615, -25.967599249120923, 6.528658161956132,
)
SIN_POLY = (
    6.283185302511506, -41.3417004053176, 81.60513138579954, -76.70301535389986,
    42.02592698629647, -14.89984666973851, 3.2381375126489513,
)


def up_to(value, unit):
    return -(-value // unit) * unit


class Sizes:
    def __init__(self, bands, groups, slots, fields, degrees, rows):
        self.bands, self.groups = bands, groups
        self.slots, self.fields, self.degrees, self.rows = slots, fields, degrees, rows
        self.tiles = degrees // SLAB
        self.slot_rows = fields * self.tiles * 2
        self.field_pad = up_to(fields, 8)
        self.share = -(-fields // groups)
        self.lanes = 4 * self.share
        self.quarters = 2
        if 4 * self.lanes <= SLAB and slots % 4 == 0:
            self.quarters = 4
        self.halves = self.quarters // 2
        self.chunk_live = slots // self.quarters
        self.chunk = up_to(self.chunk_live, 8)
        self.spots = self.quarters * self.chunk
        self.block = slots
        for size in (8, 4):
            if slots % size == 0 and (size * self.slot_rows) % 16 == 0:
                self.block = size
                break
        self.steps = slots // self.block
        self.pairs = self.halves * bands * self.chunk
        self.trunc = degrees - 1
        self.sorted = degrees // 2
        self.orbits = up_to((4 * self.trunc + 40) // 4 + 2, SLAB)
        self.levels = LEVELS // groups


def owners(sizes, field):
    first, last = field * LEVELS, (field + 1) * LEVELS
    return [
        g for g in range(sizes.groups)
        if g * sizes.fields < last and (g + 1) * sizes.fields > first
    ]


def geo_rounds(sizes):
    sources, targets = owners(sizes, TEMPER), owners(sizes, ENERGY)
    wide = max(len(sources), len(targets))
    rounds = []
    for turn in range(wide):
        pairs = []
        for k in range(wide):
            s, t = k, (k + turn) % wide
            if s < len(sources) and t < len(targets):
                pairs.append((sources[s], targets[t]))
        if pairs:
            rounds.append(pairs)
    return rounds


def iota(shape, dim):
    return lax.broadcasted_iota(jnp.int32, shape, dim)


def one_hot(cond):
    return jnp.where(cond, 1.0, 0.0).astype(jnp.bfloat16)


def dot(a, b, dims=((1,), (0,))):
    return lax.dot_general(a, b, (dims, ((), ())), preferred_element_type=jnp.float32)


def halving(value):
    return value.bit_length() - 1 if value & (value - 1) == 0 else None


def quotient(x, by):
    bits = halving(by)
    return x >> bits if bits is not None else lax.div(x, jnp.int32(by))


def remainder(x, by):
    return x & (by - 1) if halving(by) is not None else lax.rem(x, jnp.int32(by))


def spread_matrix(sizes, lev):
    sz = sizes
    tall = sz.quarters * 4 * sz.field_pad
    wide = sz.groups * SLAB
    dst = iota((1, wide), 1)
    group = quotient(dst, SLAB)
    lane = remainder(dst, SLAB)
    quarter = quotient(lane, sz.lanes)
    rest = remainder(lane, sz.lanes)
    row = quotient(rest, 2 * sz.share)
    rest = remainder(rest, 2 * sz.share)
    comp = quotient(rest, sz.share)
    item = remainder(rest, sz.share)
    start = remainder(lev * sz.fields, sz.groups)
    field = remainder(group - start + sz.groups, sz.groups) + sz.groups * item
    want = ((quarter * 2 + row) * 2 + comp) * sz.field_pad + field
    want = jnp.where((field < sz.fields) & (quarter < sz.quarters), want, -1)
    return one_hot(iota((tall, wide), 0) == want)


def spot_of(sizes, place, odd):
    half = place // sizes.chunk_live
    return (odd * sizes.halves + half) * sizes.chunk + (place - half * sizes.chunk_live)


def inverse_kernel(sizes, rounds, wave, points, gauss, layer_depth, x_ref, leg_ref, send_ref, *refs):
    sz = sizes
    geo_refs = refs[:len(rounds)]
    wide, spots, numbers = refs[len(rounds):]
    step = pl.program_id(0)
    band = lax.axis_index("band")
    lev = lax.axis_index("lev")
    pad = 2 * sz.field_pad
    height = 2 * sz.slot_rows

    @pl.when(step == 0)
    def _():
        spots[...] = jnp.zeros_like(spots)
        numbers[...] = jnp.full_like(numbers, -1)
        wide[:, pl.ds(height, wide.shape[1] - height), :] = jnp.zeros(
            (wide.shape[0], wide.shape[1] - height, SLAB), jnp.float32
        )

    degree = iota((1, sz.degrees), 1)
    found = []
    for pair in range(sz.block // 2):
        buf = wide.at[pair % wide.shape[0]]
        buf[pl.ds(0, height), :] = x_ref[pl.ds(pair * height, height), :].astype(jnp.float32)
        place = step * (sz.block // 2) + pair
        slot = band * sz.slots + 2 * place
        first_odd = wave[slot] & 1
        for side in range(2):
            number = wave[slot + side]
            table = jnp.where(degree >= number, leg_ref[2 * pair + side].astype(jnp.float32), 0.0)
            table = table.astype(jnp.bfloat16)
            total = jnp.zeros((sz.rows, pad), jnp.float32)
            for t in range(0, sz.tiles, 2):
                parts = []
                for tt in range(t, min(t + 2, sz.tiles)):
                    first = side * sz.slot_rows + 2 * tt
                    parts.append(jnp.concatenate([
                        buf[pl.ds(first + c, sz.field_pad, stride=2 * sz.tiles), :] for c in range(2)
                    ], axis=0).astype(jnp.bfloat16))
                values = jnp.concatenate(parts, axis=1)
                piece = table[:, t * SLAB:t * SLAB + values.shape[1]]
                total += dot(piece, values, ((1,), (1,)))
            odd = first_odd if side == 0 else 1 - first_odd
            found.append((spot_of(sz, place, odd), number, total))
    for spot, number, total in found:
        at = pl.multiple_of(spot * sz.rows, sz.rows)
        spots[pl.ds(at, sz.rows), 0:pad] = total
        numbers[pl.ds(spot, 1), :] = jnp.full((1, SLAB), number, jnp.int32)

    @pl.when(step == sz.steps - 1)
    def _():
        spread = spread_matrix(sz, lev)
        shape = (2 * pad, SLAB)
        src, dst = iota(shape, 0), iota(shape, 1)
        bits = sz.field_pad.bit_length() - 1
        from_field, from_side = src & (sz.field_pad - 1), src >> bits
        to_field, to_side = dst & (sz.field_pad - 1), dst >> bits
        weights = []
        for pairs in rounds:
            first = jnp.int32(2 * LEVELS + sz.fields)
            for source, target in pairs:
                first = jnp.where(lev == source, target * sz.fields - ENERGY * LEVELS, first)
            under = lev * sz.fields + from_field - TEMPER * LEVELS
            above = first + to_field
            hit = (
                (from_side == to_side)
                & (from_field < sz.fields) & (to_field < sz.fields)
                & (above >= 0) & (above <= under)
            )
            weight = jnp.zeros(shape, jnp.float32)
            for level in range(LEVELS):
                weight = jnp.where(hit & (under == level), layer_depth[level], weight)
            high = weight.astype(jnp.bfloat16)
            low = (weight - high.astype(jnp.float32)).astype(jnp.bfloat16)
            weights.append(jnp.concatenate([high, low], axis=0))
        number = numbers[...]
        lane = iota((sz.spots, SLAB), 1)
        known = (number >= 0) & ~((number == 0) & (lane & sz.field_pad != 0))
        for rp in range(sz.rows // 2):
            exact = jnp.concatenate([
                spots[pl.ds(2 * rp + r, sz.spots, stride=sz.rows), :][:, 0:pad] for r in range(2)
            ], axis=1)
            cut = jnp.concatenate([
                exact[q * sz.chunk:(q + 1) * sz.chunk] for q in range(sz.quarters)
            ], axis=1).astype(jnp.bfloat16)
            chunk = dot(cut, spread).astype(jnp.bfloat16)
            for g in range(sz.groups):
                send_ref[rp, g] = chunk[:, g * SLAB:(g + 1) * SLAB]
            count = jnp.where(lane < pad, points[2 * rp], points[2 * rp + 1])
            scale = jnp.where(lane < pad, gauss[2 * rp], gauss[2 * rp + 1])
            scale = jnp.where(known & (2 * number <= count - 1), scale, 0.0)
            exact = exact.astype(jnp.bfloat16)
            double = jnp.concatenate([exact, exact], axis=1)
            for turn in range(len(rounds)):
                geo_refs[turn][rp] = (dot(double, weights[turn]) * scale).astype(jnp.bfloat16)


def cos_sin(z):
    y = z * z
    c = jnp.full_like(y, COS_POLY[-1])
    for a in COS_POLY[-2::-1]:
        c = c * y + a
    s = jnp.full_like(y, SIN_POLY[-1])
    for a in SIN_POLY[-2::-1]:
        s = s * y + a
    return c, s * z


def basis_kernel(sizes, points, out_ref, cosines, sines):
    sz = sizes
    step = pl.program_id(0)
    turns = sz.sorted // 16
    bands_row = 16 + up_to(turns, 8)

    @pl.when(step == 0)
    def _():
        first = lax.axis_index("band") * 2
        length_a, length_b = points[first], points[first + 1]
        count_a = length_a // 4 + 1
        high = cosines.shape[0]
        row = iota((high, SLAB), 0)
        number = jnp.where(row < 16, 2 * row, jnp.where(row < bands_row, 32 * (row - 16), sz.trunc))
        number = number.astype(jnp.float32)
        for at in range(0, sz.orbits, SLAB):
            place = iota((1, SLAB), 1) + at
            second = place >= count_a
            column = (place - jnp.where(second, count_a, 0)).astype(jnp.float32)
            length = jnp.where(second, length_b, length_a).astype(jnp.float32)
            inverse = 1.0 / length
            scale = jnp.where(row < 16, 1.0 / jnp.sqrt(length), 1.0)
            product = number * column
            whole = jnp.floor(product * inverse + 0.5)
            c, s = cos_sin((product - whole * length) * inverse)
            cosines[:, pl.ds(at, SLAB)] = c * scale
            sines[:, pl.ds(at, SLAB)] = s * scale

    groups = out_ref.shape[1] // 16
    for at in range(0, sz.orbits, SLAB):
        cols = pl.ds(at, SLAB)
        base_c, base_n = cosines[0:16, cols], -sines[0:16, cols]
        top_c, top_n = cosines[pl.ds(bands_row, 1), cols], -sines[pl.ds(bands_row, 1), cols]
        turn_rows = pl.ds(pl.multiple_of(16 + step * groups, 8), groups)
        all_c, all_s = cosines[turn_rows, cols], sines[turn_rows, cols]
        for k in range(groups):
            turn_c, turn_s = all_c[k:k + 1], all_s[k:k + 1]
            c = turn_c * base_c + turn_s * base_n
            n = turn_c * base_n - turn_s * base_c
            rows = pl.ds(16 * k, 16)
            out_ref[0, rows, cols] = c.astype(jnp.bfloat16)
            out_ref[1, rows, cols] = n.astype(jnp.bfloat16)
            out_ref[2, rows, cols] = (top_c * c + top_n * n).astype(jnp.bfloat16)
            out_ref[3, rows, cols] = (top_n * c - top_c * n).astype(jnp.bfloat16)


def take_matrix(sizes, lev):
    sz = sizes
    tall = sz.groups * SLAB
    wide = sz.quarters * 2 * SLAB
    dst = iota((1, wide), 1)
    piece = quotient(dst, SLAB)
    lane = remainder(dst, SLAB)
    row = quotient(lane, SLAB // 2)
    field = quotient(remainder(lane, SLAB // 2), LVL_ROWS)
    level = remainder(lane, LVL_ROWS)
    whole = field * LEVELS + level * sz.groups + lev
    owner = quotient(whole, sz.fields)
    start = owner * sz.fields
    first = remainder(lev - remainder(start, sz.groups) + sz.groups, sz.groups)
    item = quotient(whole - start - first, sz.groups)
    want = owner * SLAB + (piece >> 1) * sz.lanes + (row * 2 + (piece & 1)) * sz.share + item
    want = jnp.where((field < FIELDS) & (level < sz.levels), want, -1)
    return one_hot(iota((tall, wide), 0) == want)


def grid_kernel(
    sizes, points, gauss, recv_ref, even_row, even_col, basis_hbm, send_ref, basis, terms, arrivals,
):
    sz = sizes
    step = 2 * SLAB
    parts = -(-sz.orbits // step)
    copies = []
    for part in range(parts):
        cols = pl.ds(part * step, min(step, sz.orbits - part * step))
        copies.append(pltpu.make_async_copy(basis_hbm.at[:, :, cols], basis.at[:, :, cols], arrivals.at[part]))
        copies[-1].start()
    lev = lax.axis_index("lev")
    first_row = lax.axis_index("band") * 2
    length_a, length_b = points[first_row], points[first_row + 1]
    count_a, count_b = length_a // 4 + 1, length_b // 4 + 1
    high = FIELDS * LVL_ROWS
    half_slab = SLAB // 2
    width = sz.bands * sz.chunk
    take = take_matrix(sz, lev)
    order = one_hot(iota((sz.sorted, sz.pairs), 0) * 2 == even_row[...])
    joined = jnp.concatenate([
        recv_ref[:, g].astype(jnp.float32).reshape(width, SLAB) for g in range(sz.groups)
    ], axis=1).astype(jnp.bfloat16)
    taken = dot(joined, take)
    coeffs = []
    number = iota((2 * SLAB, sz.sorted), 1) * 2
    bound = jnp.where(iota((2 * SLAB, sz.sorted), 0) & half_slab == 0, length_a, length_b) - 1
    kept = (0, half_slab, SLAB, SLAB + half_slab)
    for parity in range(2):
        rows = []
        for half in range(sz.halves):
            piece = (parity * sz.halves + half) * 2
            rows.append(taken[:, piece * SLAB:(piece + 2) * SLAB])
        values = jnp.concatenate(rows, axis=0).T.astype(jnp.bfloat16)
        placed = dot(values, order, ((1,), (1,)))
        mine = number if parity == 0 else sz.trunc - number
        mult = jnp.where(mine == 0, 1.0, 2.0)
        placed = jnp.where(2 * mine <= bound, placed * mult, 0.0)
        placed = jnp.concatenate([placed[k:k + high] for k in kept], axis=0).astype(jnp.bfloat16)
        coeffs += [placed[:2 * high], placed[2 * high:]]
    for part in range(parts):
        copies[part].wait()
        at = part * step
        many = min(step, sz.orbits - at)
        cols = pl.ds(at, many)
        place = iota((1, many), 1) + at
        second = place >= count_a
        grids = []
        for k in range(4):
            both = dot(coeffs[k], basis[k, :, cols])
            grids.append(jnp.where(second, both[high:], both[:high]))
        ce, se, co, so = grids
        plus, minus = ce + co, ce - co
        splus, sminus = se + so, se - so
        values = (plus + splus, minus - sminus, minus + sminus, plus - splus)
        outs = []
        for v in values:
            u, w, tem, hum, ozo = (v[i * LVL_ROWS:(i + 1) * LVL_ROWS] for i in range(FIELDS))
            outs.append(jnp.concatenate(
                [u * tem, w * tem, u * hum, w * ozo, 0.5 * (u * u + w * w)], axis=0
            ))
        offset = place - jnp.where(second, count_a, 0)
        count = jnp.where(second, count_b, count_a)
        weight = jnp.where((offset == 0) | (offset == count - 1), 0.5, 1.0)
        weight = jnp.where(offset < count, weight, 0.0)
        t0, t1, t2, t3 = (o * weight for o in outs)
        a, b, c, d = t0 + t3, t1 + t2, t0 - t3, t2 - t1
        folds = (a + b, c + d, a - b, c - d)
        empty = jnp.zeros((half_slab - high, many), jnp.float32)
        for k in range(4):
            first = jnp.where(second, 0.0, folds[k])
            last = jnp.where(second, folds[k], 0.0)
            terms[k, :, cols] = jnp.concatenate([first, empty, last, empty], axis=0).astype(jnp.bfloat16)
    lane = iota((1, SLAB), 1)
    scale = jnp.where(lane < half_slab, gauss[first_row], gauss[first_row + 1])
    bound = jnp.where(lane < half_slab, length_a, length_b) - 1
    number = iota((sz.sorted, SLAB), 0) * 2
    back_order = one_hot(iota((sz.pairs, sz.sorted), 1) * 2 == even_col[...])
    pieces = []
    for parity in range(2):
        mine = number if parity == 0 else sz.trunc - number
        sums = jnp.concatenate([
            jnp.where(
                2 * mine <= bound,
                dot(basis[parity * 2 + comp], terms[parity * 2 + comp], ((1,), (1,))) * scale, 0.0,
            ).astype(jnp.bfloat16)
            for comp in range(2)
        ], axis=1)
        slots = dot(back_order, sums).astype(jnp.bfloat16)
        pieces += [slots[half * width:(half + 1) * width] for half in range(sz.halves)]
    sent = dot(jnp.concatenate(pieces, axis=1), take, ((1,), (1,)))
    for g in range(sz.groups):
        part = sent[:, g * SLAB:(g + 1) * SLAB].reshape(sz.bands, sz.chunk, SLAB)
        send_ref[:, g] = part.astype(jnp.bfloat16)


def forward_kernel(
    sizes, wave, speed, back_ref, *refs,
):
    sz = sizes
    *geo_refs, x_ref, leg_ref, out_ref, wide, spots, inverse, speeds = refs
    step = pl.program_id(0)
    band = lax.axis_index("band")
    pad = 2 * sz.field_pad
    height = 2 * sz.slot_rows

    @pl.when(step == 0)
    def _():
        wide[:, pl.ds(height, wide.shape[1] - height), :] = jnp.zeros(
            (wide.shape[0], wide.shape[1] - height, SLAB), jnp.float32
        )
        gather = spread_matrix(sz, lax.axis_index("lev"))
        for rp in range(sz.rows // 2):
            cut = jnp.concatenate([back_ref[rp, g] for g in range(sz.groups)], axis=1)
            whole = dot(cut, gather, ((1,), (1,)))
            rows = jnp.concatenate([
                whole[:, q * 2 * pad:(q + 1) * 2 * pad] for q in range(sz.quarters)
            ], axis=0)
            for geo_ref in geo_refs:
                rows = rows + geo_ref[rp].astype(jnp.float32)[:, 0:2 * pad]
            for r in range(2):
                part = rows[:, r * pad:(r + 1) * pad]
                part = jnp.concatenate([part, jnp.zeros((sz.spots, SLAB - pad), jnp.float32)], axis=1)
                spots[pl.ds(2 * rp + r, sz.spots, stride=sz.rows), :] = part
        speeds[...] = jnp.ones_like(speeds)
        for f in range(sz.fields):
            speeds[pl.ds(f, 1), :] = jnp.full((1, SLAB), speed[f], jnp.float32)
        for t in range(sz.tiles):
            degree = iota((1, SLAB), 1) + t * SLAB
            helm = (degree * (degree + 1)).astype(jnp.float32) / float(sz.trunc * (sz.trunc + 1))
            inverse[t] = 1.0 / (1.0 + time_step * time_step * helm * speeds[...])

    work = []
    for pair in range(sz.block // 2):
        place = step * (sz.block // 2) + pair
        slot = band * sz.slots + 2 * place
        first_odd = wave[slot] & 1
        for side in range(2):
            number = wave[slot + side]
            floor = jnp.where(number < 0, sz.degrees, number)
            odd = first_odd if side == 0 else 1 - first_odd
            at = pl.multiple_of(spot_of(sz, place, odd) * sz.rows, sz.rows)
            work.append((floor, spots[pl.ds(at, sz.rows), :].T.astype(jnp.bfloat16)[0:pad]))

    for pair in range(sz.block // 2):
        buf = wide.at[pair % wide.shape[0]]
        buf[pl.ds(0, height), :] = x_ref[pl.ds(pair * height, height), :].astype(jnp.float32)
        for side in range(2):
            floor, left = work[2 * pair + side]
            base = (2 * pair + side) * sz.slot_rows
            for first in range(0, sz.tiles, 2):
                count = min(2, sz.tiles - first)
                tends = dot(left, leg_ref[2 * pair + side, :, first * SLAB:(first + count) * SLAB])
                for t in range(first, first + count):
                    tend = tends[:, (t - first) * SLAB:(t - first + 1) * SLAB]
                    live = iota((1, SLAB), 1) + t * SLAB >= floor
                    for c in range(2):
                        rows = pl.ds(side * sz.slot_rows + 2 * t + c, sz.field_pad, stride=2 * sz.tiles)
                        new = buf[rows, :] + time_step * tend[c * sz.field_pad:(c + 1) * sz.field_pad]
                        new = jnp.where(live, new * inverse[t], 0.0)
                        rows = pl.ds(base + 2 * t + c, sz.fields, stride=2 * sz.tiles)
                        out_ref[rows, :] = new[0:sz.fields]


def params(mib):
    return pltpu.CompilerParams(vmem_limit_bytes=mib * MIB)


def smem():
    return pl.BlockSpec(memory_space=pltpu.SMEM)


def whole_block(shape):
    return pl.BlockSpec(shape, lambda *_: (0,) * len(shape))


def shards(spectra, legendre, slot_wave, row_points, gauss_weight, layer_depth, mode_speed):
    slots, _, fields, degrees = spectra.shape
    rows = legendre.shape[2]
    sz = Sizes(lax.axis_size("band"), lax.axis_size("lev"), slots, fields, degrees, rows)

    tiled = spectra.reshape(slots, 2, fields, sz.tiles, SLAB)
    tiled = with_layout_constraint(tiled, Layout((0, 2, 3, 1, 4)))
    lines = tiled.transpose(0, 2, 3, 1, 4).reshape(slots * sz.slot_rows, SLAB)
    tables = legendre.transpose(0, 2, 1)

    rounds = geo_rounds(sz)
    tail = up_to((sz.field_pad - sz.fields) * 2 * sz.tiles, 16)
    wide_shape = pltpu.VMEM((4, 2 * sz.slot_rows + tail, SLAB), jnp.float32)
    spots_shape = pltpu.VMEM((sz.spots * sz.rows, SLAB), jnp.float32)
    lines_block = (sz.block * sz.slot_rows, SLAB)
    table_block = (sz.block, sz.rows, degrees)
    send_shape = (sz.bands, sz.groups, sz.chunk, SLAB)
    geo_shape = (sz.rows // 2, sz.spots, SLAB)

    sent, *geo = pl.pallas_call(
        functools.partial(inverse_kernel, sz, rounds),
        grid=(sz.steps,),
        in_specs=[
            smem(), smem(), smem(), smem(),
            pl.BlockSpec(lines_block, lambda i: (i, 0)),
            pl.BlockSpec(table_block, lambda i: (i, 0, 0)),
        ],
        out_specs=[whole_block(send_shape)] + [whole_block(geo_shape)] * len(rounds),
        out_shape=[jax.ShapeDtypeStruct(send_shape, jnp.bfloat16)]
        + [jax.ShapeDtypeStruct(geo_shape, jnp.bfloat16)] * len(rounds),
        scratch_shapes=[wide_shape, spots_shape, pltpu.VMEM((sz.spots, SLAB), jnp.int32)],
        compiler_params=params(56),
        name="inverse_legendre",
    )(slot_wave, row_points, gauss_weight, layer_depth, lines, tables)

    sent, points_later, wave_later = lax.optimization_barrier((sent, row_points, slot_wave))
    both = ("band", "lev")
    total = sz.bands * sz.groups
    flat = (total * sz.chunk, SLAB)
    arrived = lax.all_to_all(sent.reshape(flat), both, split_axis=0, concat_axis=0, tiled=True)

    pair_wave = wave_later.reshape(-1, 2)
    even_wave = jnp.where(pair_wave[:, 0] % 2 == 0, pair_wave[:, 0], pair_wave[:, 1])
    even_wave = even_wave.reshape(sz.bands, sz.halves, sz.chunk_live)
    even_wave = jnp.pad(even_wave, ((0, 0), (0, 0), (0, sz.chunk - sz.chunk_live)), constant_values=-1)
    even_wave = even_wave.transpose(1, 0, 2).reshape(sz.pairs)

    high = SLAB if sz.sorted % SLAB == 0 else sz.sorted
    table_rows = 16 + up_to(sz.sorted // 16, 8) + 8
    basis = pl.pallas_call(
        functools.partial(basis_kernel, sz),
        grid=(sz.sorted // high,),
        in_specs=[smem()],
        out_specs=pl.BlockSpec((4, high, sz.orbits), lambda i: (0, i, 0)),
        out_shape=jax.ShapeDtypeStruct((4, sz.sorted, sz.orbits), jnp.bfloat16),
        scratch_shapes=[pltpu.VMEM((table_rows, sz.orbits), jnp.float32)] * 2,
        compiler_params=params(56),
        cost_estimate=pl.CostEstimate(
            flops=20 * sz.sorted * sz.orbits, bytes_accessed=8 * sz.sorted * sz.orbits, transcendentals=0,
        ),
        name="basis",
    )(points_later)

    even_row, even_col = even_wave.reshape(1, sz.pairs), even_wave.reshape(sz.pairs, 1)
    *geo, arrived, basis, even_row, even_col = lax.optimization_barrier(
        (*geo, arrived, basis, even_row, even_col)
    )
    moved = [lax.ppermute(geo[turn], "lev", pairs) for turn, pairs in enumerate(rounds)]
    vmem = pl.BlockSpec(memory_space=pltpu.VMEM)
    returned = pl.pallas_call(
        functools.partial(grid_kernel, sz),
        in_specs=[smem(), smem(), vmem, vmem, vmem, pl.BlockSpec(memory_space=pl.ANY)],
        out_specs=vmem,
        out_shape=jax.ShapeDtypeStruct(send_shape, jnp.bfloat16),
        scratch_shapes=[
            pltpu.VMEM((4, sz.sorted, sz.orbits), jnp.bfloat16),
            pltpu.VMEM((4, SLAB, sz.orbits), jnp.bfloat16),
            pltpu.SemaphoreType.DMA((-(-sz.orbits // (2 * SLAB)),)),
        ],
        compiler_params=params(56),
        cost_estimate=pl.CostEstimate(
            flops=4 * 4 * SLAB * sz.sorted * sz.orbits, bytes_accessed=8 * sz.sorted * sz.orbits, transcendentals=0,
        ),
        name="grid_products",
    )(
        row_points, gauss_weight, arrived.reshape(send_shape), even_row, even_col, basis,
    )
    *moved, returned = lax.optimization_barrier((*moved, returned))

    back = lax.all_to_all(returned.reshape(flat), both, split_axis=0, concat_axis=0, tiled=True)

    out = pl.pallas_call(
        functools.partial(forward_kernel, sz),
        grid=(sz.steps,),
        in_specs=[
            smem(), smem(),
            whole_block(send_shape), *([whole_block(geo_shape)] * len(rounds)),
            pl.BlockSpec(lines_block, lambda i: (i, 0)),
            pl.BlockSpec(table_block, lambda i: (i, 0, 0)),
        ],
        out_specs=pl.BlockSpec(lines_block, lambda i: (i, 0)),
        out_shape=jax.ShapeDtypeStruct((slots * sz.slot_rows, SLAB), jnp.float32),
        scratch_shapes=[
            wide_shape, spots_shape,
            pltpu.VMEM((sz.tiles, sz.field_pad, SLAB), jnp.float32),
            pltpu.VMEM((sz.field_pad, SLAB), jnp.float32),
        ],
        compiler_params=params(56),
        name="forward_legendre",
    )(slot_wave, mode_speed, back.reshape(send_shape), *moved, lines, tables)

    out = out.reshape(slots, fields, sz.tiles, 2, SLAB).transpose(0, 1, 3, 2, 4)
    return out.reshape(slots, fields, 2, degrees).transpose(0, 2, 1, 3)


def solution(mesh):
    return jax.shard_map(
        shards,
        mesh=mesh,
        in_specs=(
            P("band", None, "lev", None),
            P("band", None, None),
            P(),
            P(),
            P(),
            P(),
            P("lev"),
        ),
        out_specs=P("band", None, "lev", None),
        check_vma=False,
    )
```

```python
import functools
import math

import jax
import jax.numpy as jnp
from jax import lax
from jax.experimental import pallas as pl
from jax.experimental.layout import Layout, with_layout_constraint
from jax.experimental.pallas import tpu as pltpu
from jax.sharding import PartitionSpec as P

FIELDS = 5
LEVELS = 24
TEMPER = 2
ENERGY = 4
LVL_ROWS = 8
SLAB = 128
MIB = 1024 * 1024

time_step = 1.0

COS_POLY = (
    0.9999999890590235, -19.739204499453994, 64.93911745989843, -85.45013953092186,
    60.167630951185615, -25.967599249120923, 6.528658161956132,
)
SIN_POLY = (
    6.283185302511506, -41.3417004053176, 81.60513138579954, -76.70301535389986,
    42.02592698629647, -14.89984666973851, 3.2381375126489513,
)


def up_to(value, unit):
    return -(-value // unit) * unit


class Sizes:
    def __init__(self, bands, groups, slots, fields, degrees, rows):
        self.bands, self.groups = bands, groups
        self.slots, self.fields, self.degrees, self.rows = slots, fields, degrees, rows
        self.tiles = degrees // SLAB
        self.slot_rows = fields * self.tiles * 2
        self.field_pad = up_to(fields, 8)
        self.share = -(-fields // groups)
        self.lanes = 4 * self.share
        self.quarters = 2
        if 4 * self.lanes <= SLAB and slots % 4 == 0:
            self.quarters = 4
        self.halves = self.quarters // 2
        self.chunk_live = slots // self.quarters
        self.chunk = up_to(self.chunk_live, 8)
        self.spots = self.quarters * self.chunk
        self.block = slots
        for size in (8, 4):
            if slots % size == 0 and (size * self.slot_rows) % 16 == 0:
                self.block = size
                break
        self.steps = slots // self.block
        self.pairs = self.halves * bands * self.chunk
        self.trunc = degrees - 1
        self.sorted = degrees // 2
        self.orbits = up_to((4 * self.trunc + 40) // 4 + 2, SLAB)
        self.levels = LEVELS // groups


def owners(sizes, field):
    first, last = field * LEVELS, (field + 1) * LEVELS
    return [
        g for g in range(sizes.groups)
        if g * sizes.fields < last and (g + 1) * sizes.fields > first
    ]


def geo_rounds(sizes):
    sources, targets = owners(sizes, TEMPER), owners(sizes, ENERGY)
    wide = max(len(sources), len(targets))
    rounds = []
    for turn in range(wide):
        pairs = []
        for k in range(wide):
            s, t = k, (k + turn) % wide
            if s < len(sources) and t < len(targets):
                pairs.append((sources[s], targets[t]))
        if pairs:
            rounds.append(pairs)
    return rounds


def iota(shape, dim):
    return lax.broadcasted_iota(jnp.int32, shape, dim)


def one_hot(cond):
    return jnp.where(cond, 1.0, 0.0).astype(jnp.bfloat16)


def dot(a, b, dims=((1,), (0,))):
    return lax.dot_general(a, b, (dims, ((), ())), preferred_element_type=jnp.float32)


def halving(value):
    return value.bit_length() - 1 if value & (value - 1) == 0 else None


def quotient(x, by):
    bits = halving(by)
    return x >> bits if bits is not None else lax.div(x, jnp.int32(by))


def remainder(x, by):
    return x & (by - 1) if halving(by) is not None else lax.rem(x, jnp.int32(by))


def spread_matrix(sizes, lev):
    sz = sizes
    tall = sz.quarters * 4 * sz.field_pad
    wide = sz.groups * SLAB
    dst = iota((1, wide), 1)
    group = quotient(dst, SLAB)
    lane = remainder(dst, SLAB)
    quarter = quotient(lane, sz.lanes)
    rest = remainder(lane, sz.lanes)
    row = quotient(rest, 2 * sz.share)
    rest = remainder(rest, 2 * sz.share)
    comp = quotient(rest, sz.share)
    item = remainder(rest, sz.share)
    start = remainder(lev * sz.fields, sz.groups)
    field = remainder(group - start + sz.groups, sz.groups) + sz.groups * item
    want = ((quarter * 2 + row) * 2 + comp) * sz.field_pad + field
    want = jnp.where((field < sz.fields) & (quarter < sz.quarters), want, -1)
    return one_hot(iota((tall, wide), 0) == want)


def spot_of(sizes, place, odd):
    half = place // sizes.chunk_live
    return (odd * sizes.halves + half) * sizes.chunk + (place - half * sizes.chunk_live)


def pair_state(sizes, wave, band, place):
    slot = band * sizes.slots + 2 * place
    first, second = wave[slot], wave[slot + 1]
    odd = first & 1
    start = quotient(jnp.maximum(first, 0), SLAB)
    live = sizes.tiles - start
    tiles = []
    for k in range(sizes.tiles + 1):
        side = jnp.where(k < live, 0, 1)
        tiles.append((side, jnp.where(k < live, start + k, k - 1)))
    return (first, second), (odd, 1 - odd), tiles


def inverse_kernel(sizes, rounds, wave, points, gauss, layer_depth, x_ref, leg_ref, send_ref, *refs):
    sz = sizes
    geo_refs = refs[:len(rounds)]
    wide, spots, numbers = refs[len(rounds):]
    step = pl.program_id(0)
    band = lax.axis_index("band")
    lev = lax.axis_index("lev")
    pad = 2 * sz.field_pad
    height = 2 * sz.slot_rows

    @pl.when(step == 0)
    def _():
        spots[...] = jnp.zeros_like(spots)
        numbers[...] = jnp.full_like(numbers, -1)
        wide[:, pl.ds(height, wide.shape[1] - height), :] = jnp.zeros(
            (wide.shape[0], wide.shape[1] - height, SLAB), jnp.float32
        )

    for pair in range(sz.block // 2):
        rows = x_ref[pl.ds(pair * height, height), :]
        wide[pair, pl.ds(0, height), :] = rows.astype(jnp.float32)
    found = []
    for pair in range(sz.block // 2):
        place = step * (sz.block // 2) + pair
        numbers_here, odds, tiles = pair_state(sz, wave, band, place)
        values, tables = [], []
        for side, tile in tiles:
            start = side * sz.slot_rows + 2 * tile
            values.append(jnp.concatenate([
                wide[pair, pl.ds(start + c, sz.field_pad, stride=2 * sz.tiles), :] for c in range(2)
            ], axis=0).astype(jnp.bfloat16))
            cols = pl.ds(pl.multiple_of(tile * SLAB, SLAB), SLAB)
            table = leg_ref[2 * pair + side, :, cols].astype(jnp.float32)
            number = jnp.where(side == 0, numbers_here[0], numbers_here[1])
            table = jnp.where(iota((1, SLAB), 1) + tile * SLAB >= number, table, 0.0)
            tables.append(jnp.concatenate([
                jnp.where(side == 0, table, 0.0), jnp.where(side == 1, table, 0.0),
            ], axis=0).astype(jnp.bfloat16))
        total = dot(
            jnp.concatenate(tables, axis=1), jnp.concatenate(values, axis=1), ((1,), (1,))
        )
        for side in range(2):
            found.append((
                spot_of(sz, place, odds[side]), numbers_here[side],
                total[side * sz.rows:(side + 1) * sz.rows],
            ))
    for spot, number, total in found:
        at = pl.multiple_of(spot * sz.rows, sz.rows)
        spots[pl.ds(at, sz.rows), 0:pad] = total
        numbers[pl.ds(spot, 1), :] = jnp.full((1, SLAB), number, jnp.int32)

    @pl.when(step == sz.steps - 1)
    def _():
        spread = spread_matrix(sz, lev)
        shape = (2 * pad, SLAB)
        src, dst = iota(shape, 0), iota(shape, 1)
        bits = sz.field_pad.bit_length() - 1
        from_field, from_side = src & (sz.field_pad - 1), src >> bits
        to_field, to_side = dst & (sz.field_pad - 1), dst >> bits
        weights = []
        for pairs in rounds:
            first = jnp.int32(2 * LEVELS + sz.fields)
            for source, target in pairs:
                first = jnp.where(lev == source, target * sz.fields - ENERGY * LEVELS, first)
            under = lev * sz.fields + from_field - TEMPER * LEVELS
            above = first + to_field
            hit = (
                (from_side == to_side)
                & (from_field < sz.fields) & (to_field < sz.fields)
                & (above >= 0) & (above <= under)
            )
            weight = jnp.zeros(shape, jnp.float32)
            for level in range(LEVELS):
                weight = jnp.where(hit & (under == level), layer_depth[level], weight)
            high = weight.astype(jnp.bfloat16)
            low = (weight - high.astype(jnp.float32)).astype(jnp.bfloat16)
            weights.append(jnp.concatenate([high, low], axis=0))
        number = numbers[...]
        lane = iota((sz.spots, SLAB), 1)
        known = (number >= 0) & ~((number == 0) & (lane & sz.field_pad != 0))
        for rp in range(sz.rows // 2):
            exact = jnp.concatenate([
                spots[pl.ds(2 * rp + r, sz.spots, stride=sz.rows), :][:, 0:pad] for r in range(2)
            ], axis=1)
            cut = jnp.concatenate([
                exact[q * sz.chunk:(q + 1) * sz.chunk] for q in range(sz.quarters)
            ], axis=1).astype(jnp.bfloat16)
            chunk = dot(cut, spread).astype(jnp.bfloat16)
            for g in range(sz.groups):
                send_ref[rp, g] = chunk[:, g * SLAB:(g + 1) * SLAB]
            count = jnp.where(lane < pad, points[2 * rp], points[2 * rp + 1])
            scale = jnp.where(lane < pad, gauss[2 * rp], gauss[2 * rp + 1])
            scale = jnp.where(known & (2 * number <= count - 1), scale, 0.0)
            exact = exact.astype(jnp.bfloat16)
            double = jnp.concatenate([exact, exact], axis=1)
            for turn in range(len(rounds)):
                geo_refs[turn][rp] = (dot(double, weights[turn]) * scale).astype(jnp.bfloat16)


def cos_sin(z):
    y = z * z
    c = jnp.full_like(y, COS_POLY[-1])
    for a in COS_POLY[-2::-1]:
        c = c * y + a
    s = jnp.full_like(y, SIN_POLY[-1])
    for a in SIN_POLY[-2::-1]:
        s = s * y + a
    return c, s * z


def basis_kernel(sizes, points, out_ref, cosines, sines):
    sz = sizes
    step = pl.program_id(0)
    turns = sz.sorted // 16
    bands_row = 16 + up_to(turns, 8)

    @pl.when(step == 0)
    def _():
        first = lax.axis_index("band") * 2
        length_a, length_b = points[first], points[first + 1]
        count_a = length_a // 4 + 1
        high = cosines.shape[0]
        row = iota((high, SLAB), 0)
        number = jnp.where(row < 16, 2 * row, jnp.where(row < bands_row, 32 * (row - 16), sz.trunc))
        number = number.astype(jnp.float32)
        for at in range(0, sz.orbits, SLAB):
            place = iota((1, SLAB), 1) + at
            second = place >= count_a
            column = (place - jnp.where(second, count_a, 0)).astype(jnp.float32)
            length = jnp.where(second, length_b, length_a).astype(jnp.float32)
            inverse = 1.0 / length
            scale = jnp.where(row < 16, 1.0 / jnp.sqrt(length), 1.0)
            product = number * column
            whole = jnp.floor(product * inverse + 0.5)
            c, s = cos_sin((product - whole * length) * inverse)
            cosines[:, pl.ds(at, SLAB)] = c * scale
            sines[:, pl.ds(at, SLAB)] = s * scale

    groups = out_ref.shape[1] // 16
    for at in range(0, sz.orbits, SLAB):
        cols = pl.ds(at, SLAB)
        base_c, base_n = cosines[0:16, cols], -sines[0:16, cols]
        top_c, top_n = cosines[pl.ds(bands_row, 1), cols], -sines[pl.ds(bands_row, 1), cols]
        turn_rows = pl.ds(pl.multiple_of(16 + step * groups, 8), groups)
        all_c, all_s = cosines[turn_rows, cols], sines[turn_rows, cols]
        for k in range(groups):
            turn_c, turn_s = all_c[k:k + 1], all_s[k:k + 1]
            c = turn_c * base_c + turn_s * base_n
            n = turn_c * base_n - turn_s * base_c
            rows = pl.ds(16 * k, 16)
            out_ref[0, rows, cols] = c.astype(jnp.bfloat16)
            out_ref[1, rows, cols] = n.astype(jnp.bfloat16)
            out_ref[2, rows, cols] = (top_c * c + top_n * n).astype(jnp.bfloat16)
            out_ref[3, rows, cols] = (top_n * c - top_c * n).astype(jnp.bfloat16)


def take_matrix(sizes, lev):
    sz = sizes
    tall = sz.groups * SLAB
    wide = sz.quarters * 2 * SLAB
    dst = iota((1, wide), 1)
    piece = quotient(dst, SLAB)
    lane = remainder(dst, SLAB)
    row = quotient(lane, SLAB // 2)
    field = quotient(remainder(lane, SLAB // 2), LVL_ROWS)
    level = remainder(lane, LVL_ROWS)
    whole = field * LEVELS + level * sz.groups + lev
    owner = quotient(whole, sz.fields)
    start = owner * sz.fields
    first = remainder(lev - remainder(start, sz.groups) + sz.groups, sz.groups)
    item = quotient(whole - start - first, sz.groups)
    want = owner * SLAB + (piece >> 1) * sz.lanes + (row * 2 + (piece & 1)) * sz.share + item
    want = jnp.where((field < FIELDS) & (level < sz.levels), want, -1)
    return one_hot(iota((tall, wide), 0) == want)


def grid_kernel(
    sizes, points, gauss, recv_ref, even_row, even_col, basis_hbm, send_ref, basis, terms, arrivals,
):
    sz = sizes
    step = 2 * SLAB
    parts = -(-sz.orbits // step)
    copies = []
    for part in range(parts):
        cols = pl.ds(part * step, min(step, sz.orbits - part * step))
        copies.append(pltpu.make_async_copy(basis_hbm.at[:, :, cols], basis.at[:, :, cols], arrivals.at[part]))
        copies[-1].start()
    lev = lax.axis_index("lev")
    first_row = lax.axis_index("band") * 2
    length_a, length_b = points[first_row], points[first_row + 1]
    count_a, count_b = length_a // 4 + 1, length_b // 4 + 1
    high = FIELDS * LVL_ROWS
    half_slab = SLAB // 2
    width = sz.bands * sz.chunk
    take = take_matrix(sz, lev)
    order = one_hot(iota((sz.sorted, sz.pairs), 0) * 2 == even_row[...])
    joined = jnp.concatenate([
        recv_ref[:, g].astype(jnp.float32).reshape(width, SLAB) for g in range(sz.groups)
    ], axis=1).astype(jnp.bfloat16)
    taken = dot(joined, take)
    coeffs = []
    number = iota((2 * SLAB, sz.sorted), 1) * 2
    bound = jnp.where(iota((2 * SLAB, sz.sorted), 0) & half_slab == 0, length_a, length_b) - 1
    kept = (0, half_slab, SLAB, SLAB + half_slab)
    for parity in range(2):
        rows = []
        for half in range(sz.halves):
            piece = (parity * sz.halves + half) * 2
            rows.append(taken[:, piece * SLAB:(piece + 2) * SLAB])
        values = jnp.concatenate(rows, axis=0).T.astype(jnp.bfloat16)
        placed = dot(values, order, ((1,), (1,)))
        mine = number if parity == 0 else sz.trunc - number
        mult = jnp.where(mine == 0, 1.0, 2.0)
        placed = jnp.where(2 * mine <= bound, placed * mult, 0.0)
        placed = jnp.concatenate([placed[k:k + high] for k in kept], axis=0).astype(jnp.bfloat16)
        coeffs += [placed[:2 * high], placed[2 * high:]]
    for part in range(parts):
        copies[part].wait()
        at = part * step
        many = min(step, sz.orbits - at)
        cols = pl.ds(at, many)
        place = iota((1, many), 1) + at
        second = place >= count_a
        grids = []
        for k in range(4):
            both = dot(coeffs[k], basis[k, :, cols])
            grids.append(jnp.where(second, both[high:], both[:high]))
        ce, se, co, so = grids
        plus, minus = ce + co, ce - co
        splus, sminus = se + so, se - so
        values = (plus + splus, minus - sminus, minus + sminus, plus - splus)
        outs = []
        for v in values:
            u, w, tem, hum, ozo = (v[i * LVL_ROWS:(i + 1) * LVL_ROWS] for i in range(FIELDS))
            outs.append(jnp.concatenate(
                [u * tem, w * tem, u * hum, w * ozo, 0.5 * (u * u + w * w)], axis=0
            ))
        offset = place - jnp.where(second, count_a, 0)
        count = jnp.where(second, count_b, count_a)
        weight = jnp.where((offset == 0) | (offset == count - 1), 0.5, 1.0)
        weight = jnp.where(offset < count, weight, 0.0)
        t0, t1, t2, t3 = (o * weight for o in outs)
        a, b, c, d = t0 + t3, t1 + t2, t0 - t3, t2 - t1
        folds = (a + b, c + d, a - b, c - d)
        empty = jnp.zeros((half_slab - high, many), jnp.float32)
        for k in range(4):
            first = jnp.where(second, 0.0, folds[k])
            last = jnp.where(second, folds[k], 0.0)
            terms[k, :, cols] = jnp.concatenate([first, empty, last, empty], axis=0).astype(jnp.bfloat16)
    lane = iota((1, SLAB), 1)
    scale = jnp.where(lane < half_slab, gauss[first_row], gauss[first_row + 1])
    bound = jnp.where(lane < half_slab, length_a, length_b) - 1
    number = iota((sz.sorted, SLAB), 0) * 2
    back_order = one_hot(iota((sz.pairs, sz.sorted), 1) * 2 == even_col[...])
    pieces = []
    for parity in range(2):
        mine = number if parity == 0 else sz.trunc - number
        sums = jnp.concatenate([
            jnp.where(
                2 * mine <= bound,
                dot(basis[parity * 2 + comp], terms[parity * 2 + comp], ((1,), (1,))) * scale, 0.0,
            ).astype(jnp.bfloat16)
            for comp in range(2)
        ], axis=1)
        slots = dot(back_order, sums).astype(jnp.bfloat16)
        pieces += [slots[half * width:(half + 1) * width] for half in range(sz.halves)]
    sent = dot(jnp.concatenate(pieces, axis=1), take, ((1,), (1,)))
    for g in range(sz.groups):
        part = sent[:, g * SLAB:(g + 1) * SLAB].reshape(sz.bands, sz.chunk, SLAB)
        send_ref[:, g] = part.astype(jnp.bfloat16)


def forward_kernel(
    sizes, wave, speed, back_ref, *refs,
):
    sz = sizes
    *geo_refs, x_ref, leg_ref, out_ref, wide, spots, inverse = refs
    step = pl.program_id(0)
    band = lax.axis_index("band")
    pad = 2 * sz.field_pad
    height = 2 * sz.slot_rows

    @pl.when(step == 0)
    def _():
        gather = spread_matrix(sz, lax.axis_index("lev"))
        for rp in range(sz.rows // 2):
            cut = jnp.concatenate([back_ref[rp, g] for g in range(sz.groups)], axis=1)
            whole = dot(cut, gather, ((1,), (1,)))
            rows = jnp.concatenate([
                whole[:, q * 2 * pad:(q + 1) * 2 * pad] for q in range(sz.quarters)
            ], axis=0)
            for geo_ref in geo_refs:
                rows = rows + geo_ref[rp].astype(jnp.float32)[:, 0:2 * pad]
            for r in range(2):
                part = rows[:, r * pad:(r + 1) * pad]
                part = jnp.concatenate([part, jnp.zeros((sz.spots, SLAB - pad), jnp.float32)], axis=1)
                spots[pl.ds(2 * rp + r, sz.spots, stride=sz.rows), :] = part
        for f in range(sz.fields):
            rows = 2 * sz.tiles
            degree = quotient(iota((rows, SLAB), 0), 2) * SLAB + iota((rows, SLAB), 1)
            helm = (degree * (degree + 1)).astype(jnp.float32) / float(sz.trunc * (sz.trunc + 1))
            inverse[pl.ds(f * rows, rows), :] = 1.0 / (1.0 + time_step * time_step * helm * speed[f])

    pitch = sz.field_pad * 2 * sz.tiles
    work = []
    for pair in range(sz.block // 2):
        place = step * (sz.block // 2) + pair
        numbers, odds, tiles = pair_state(sz, wave, band, place)
        lefts = []
        for side in range(2):
            at = pl.multiple_of(spot_of(sz, place, odds[side]) * sz.rows, sz.rows)
            lefts.append(spots[pl.ds(at, sz.rows), :])
        left = jnp.concatenate(lefts, axis=0).T.astype(jnp.bfloat16)[0:pad]
        tables = []
        for side, tile in tiles:
            cols = pl.ds(pl.multiple_of(tile * SLAB, SLAB), SLAB)
            table = leg_ref[2 * pair + side, :, cols].astype(jnp.float32)
            tables.append(jnp.concatenate([
                jnp.where(side == 0, table, 0.0), jnp.where(side == 1, table, 0.0),
            ], axis=0).astype(jnp.bfloat16))
        work.append((numbers, tiles, left, tables))
    for pair in range(sz.block // 2):
        _, tiles, left, tables = work[pair]
        for k in range(0, len(tiles), 2):
            count = min(2, len(tiles) - k)
            tends = dot(left, jnp.concatenate(tables[k:k + count], axis=1))
            for kk in range(count):
                side, tile = tiles[k + kk]
                for c in range(2):
                    rows = pl.ds(side * pitch + 2 * tile + c, sz.field_pad, stride=2 * sz.tiles)
                    wide[pair, rows, :] = tends[
                        c * sz.field_pad:(c + 1) * sz.field_pad, kk * SLAB:(kk + 1) * SLAB
                    ]
    run = 4 * sz.tiles if sz.fields % 2 == 0 else 2 * sz.tiles
    row = remainder(iota((run, SLAB), 0), 2 * sz.tiles)
    degree = quotient(row, 2) * SLAB + iota((run, SLAB), 1)
    for pair in range(sz.block // 2):
        numbers = work[pair][0]
        old = x_ref[pl.ds(pair * height, height), :].astype(jnp.float32)
        for side in range(2):
            live = degree >= jnp.where(numbers[side] < 0, sz.degrees, numbers[side])
            for at in range(0, sz.slot_rows, run):
                tend = wide[pair, pl.ds(side * pitch + at, run), :]
                new = old[side * sz.slot_rows + at:side * sz.slot_rows + at + run] + time_step * tend
                new = jnp.where(live, new * inverse[pl.ds(at, run), :], 0.0)
                out_ref[pl.ds(pair * height + side * sz.slot_rows + at, run), :] = new


def params(mib):
    return pltpu.CompilerParams(vmem_limit_bytes=mib * MIB)


def smem():
    return pl.BlockSpec(memory_space=pltpu.SMEM)


def whole_block(shape):
    return pl.BlockSpec(shape, lambda *_: (0,) * len(shape))


def shards(spectra, legendre, slot_wave, row_points, gauss_weight, layer_depth, mode_speed):
    slots, _, fields, degrees = spectra.shape
    rows = legendre.shape[2]
    sz = Sizes(lax.axis_size("band"), lax.axis_size("lev"), slots, fields, degrees, rows)

    tiled = spectra.reshape(slots, 2, fields, sz.tiles, SLAB)
    tiled = with_layout_constraint(tiled, Layout((0, 2, 3, 1, 4)))
    lines = tiled.transpose(0, 2, 3, 1, 4).reshape(slots * sz.slot_rows, SLAB)
    tables = legendre.transpose(0, 2, 1)

    rounds = geo_rounds(sz)
    tail = up_to((sz.field_pad - sz.fields) * 2 * sz.tiles, 16)
    wide_shape = pltpu.VMEM((sz.block // 2, 2 * sz.slot_rows + tail, SLAB), jnp.float32)
    spots_shape = pltpu.VMEM((sz.spots * sz.rows, SLAB), jnp.float32)
    lines_block = (sz.block * sz.slot_rows, SLAB)
    table_block = (sz.block, sz.rows, degrees)
    send_shape = (sz.bands, sz.groups, sz.chunk, SLAB)
    geo_shape = (sz.rows // 2, sz.spots, SLAB)

    sent, *geo = pl.pallas_call(
        functools.partial(inverse_kernel, sz, rounds),
        grid=(sz.steps,),
        in_specs=[
            smem(), smem(), smem(), smem(),
            pl.BlockSpec(lines_block, lambda i: (i, 0)),
            pl.BlockSpec(table_block, lambda i: (i, 0, 0)),
        ],
        out_specs=[whole_block(send_shape)] + [whole_block(geo_shape)] * len(rounds),
        out_shape=[jax.ShapeDtypeStruct(send_shape, jnp.bfloat16)]
        + [jax.ShapeDtypeStruct(geo_shape, jnp.bfloat16)] * len(rounds),
        scratch_shapes=[wide_shape, spots_shape, pltpu.VMEM((sz.spots, SLAB), jnp.int32)],
        compiler_params=params(56),
        name="inverse_legendre",
    )(slot_wave, row_points, gauss_weight, layer_depth, lines, tables)

    sent, points_later, wave_later = lax.optimization_barrier((sent, row_points, slot_wave))
    both = ("band", "lev")
    total = sz.bands * sz.groups
    flat = (total * sz.chunk, SLAB)
    arrived = lax.all_to_all(sent.reshape(flat), both, split_axis=0, concat_axis=0, tiled=True)

    pair_wave = wave_later.reshape(-1, 2)
    even_wave = jnp.where(pair_wave[:, 0] % 2 == 0, pair_wave[:, 0], pair_wave[:, 1])
    even_wave = even_wave.reshape(sz.bands, sz.halves, sz.chunk_live)
    even_wave = jnp.pad(even_wave, ((0, 0), (0, 0), (0, sz.chunk - sz.chunk_live)), constant_values=-1)
    even_wave = even_wave.transpose(1, 0, 2).reshape(sz.pairs)

    high = SLAB if sz.sorted % SLAB == 0 else sz.sorted
    table_rows = 16 + up_to(sz.sorted // 16, 8) + 8
    basis = pl.pallas_call(
        functools.partial(basis_kernel, sz),
        grid=(sz.sorted // high,),
        in_specs=[smem()],
        out_specs=pl.BlockSpec((4, high, sz.orbits), lambda i: (0, i, 0)),
        out_shape=jax.ShapeDtypeStruct((4, sz.sorted, sz.orbits), jnp.bfloat16),
        scratch_shapes=[pltpu.VMEM((table_rows, sz.orbits), jnp.float32)] * 2,
        compiler_params=params(56),
        cost_estimate=pl.CostEstimate(
            flops=20 * sz.sorted * sz.orbits, bytes_accessed=8 * sz.sorted * sz.orbits, transcendentals=0,
        ),
        name="basis",
    )(points_later)

    even_row, even_col = even_wave.reshape(1, sz.pairs), even_wave.reshape(sz.pairs, 1)
    *geo, arrived, basis, even_row, even_col = lax.optimization_barrier(
        (*geo, arrived, basis, even_row, even_col)
    )
    moved = [lax.ppermute(geo[turn], "lev", pairs) for turn, pairs in enumerate(rounds)]
    vmem = pl.BlockSpec(memory_space=pltpu.VMEM)
    returned = pl.pallas_call(
        functools.partial(grid_kernel, sz),
        in_specs=[smem(), smem(), vmem, vmem, vmem, pl.BlockSpec(memory_space=pl.ANY)],
        out_specs=vmem,
        out_shape=jax.ShapeDtypeStruct(send_shape, jnp.bfloat16),
        scratch_shapes=[
            pltpu.VMEM((4, sz.sorted, sz.orbits), jnp.bfloat16),
            pltpu.VMEM((4, SLAB, sz.orbits), jnp.bfloat16),
            pltpu.SemaphoreType.DMA((-(-sz.orbits // (2 * SLAB)),)),
        ],
        compiler_params=params(56),
        cost_estimate=pl.CostEstimate(
            flops=4 * 4 * SLAB * sz.sorted * sz.orbits, bytes_accessed=8 * sz.sorted * sz.orbits, transcendentals=0,
        ),
        name="grid_products",
    )(
        row_points, gauss_weight, arrived.reshape(send_shape), even_row, even_col, basis,
    )
    *moved, returned = lax.optimization_barrier((*moved, returned))

    back = lax.all_to_all(returned.reshape(flat), both, split_axis=0, concat_axis=0, tiled=True)

    out = pl.pallas_call(
        functools.partial(forward_kernel, sz),
        grid=(sz.steps,),
        in_specs=[
            smem(), smem(),
            whole_block(send_shape), *([whole_block(geo_shape)] * len(rounds)),
            pl.BlockSpec(lines_block, lambda i: (i, 0)),
            pl.BlockSpec(table_block, lambda i: (i, 0, 0)),
        ],
        out_specs=pl.BlockSpec(lines_block, lambda i: (i, 0)),
        out_shape=jax.ShapeDtypeStruct((slots * sz.slot_rows, SLAB), jnp.float32),
        scratch_shapes=[
            pltpu.VMEM((sz.block // 2, 4 * sz.field_pad * sz.tiles, SLAB), jnp.float32), spots_shape,
            pltpu.VMEM((sz.slot_rows, SLAB), jnp.float32),
        ],
        compiler_params=params(56),
        name="forward_legendre",
    )(slot_wave, mode_speed, back.reshape(send_shape), *moved, lines, tables)

    out = out.reshape(slots, fields, sz.tiles, 2, SLAB).transpose(0, 1, 3, 2, 4)
    return out.reshape(slots, fields, 2, degrees).transpose(0, 2, 1, 3)


def solution(mesh):
    return jax.shard_map(
        shards,
        mesh=mesh,
        in_specs=(
            P("band", None, "lev", None),
            P("band", None, None),
            P(),
            P(),
            P(),
            P(),
            P("lev"),
        ),
        out_specs=P("band", None, "lev", None),
        check_vma=False,
    )
```

```python
import functools
import math

import jax
import jax.numpy as jnp
from jax import lax
from jax.experimental import pallas as pl
from jax.experimental.layout import Layout, with_layout_constraint
from jax.experimental.pallas import tpu as pltpu
from jax.sharding import PartitionSpec as P

FIELDS = 5
LEVELS = 24
TEMPER = 2
ENERGY = 4
LVL_ROWS = 8
SLAB = 128
MIB = 1024 * 1024

time_step = 1.0

COS_POLY = (
    0.9999999890590235, -19.739204499453994, 64.93911745989843, -85.45013953092186,
    60.167630951185615, -25.967599249120923, 6.528658161956132,
)
SIN_POLY = (
    6.283185302511506, -41.3417004053176, 81.60513138579954, -76.70301535389986,
    42.02592698629647, -14.89984666973851, 3.2381375126489513,
)


def up_to(value, unit):
    return -(-value // unit) * unit


class Sizes:
    def __init__(self, bands, groups, slots, fields, degrees, rows):
        self.bands, self.groups = bands, groups
        self.slots, self.fields, self.degrees, self.rows = slots, fields, degrees, rows
        self.tiles = degrees // SLAB
        self.slot_rows = fields * self.tiles * 2
        self.field_pad = up_to(fields, 8)
        self.share = -(-fields // groups)
        self.lanes = 4 * self.share
        self.quarters = 2
        if 4 * self.lanes <= SLAB and slots % 4 == 0:
            self.quarters = 4
        self.halves = self.quarters // 2
        self.chunk_live = slots // self.quarters
        self.chunk = up_to(self.chunk_live, 8)
        self.spots = self.quarters * self.chunk
        self.block = slots
        for size in (8, 4):
            if slots % size == 0 and (size * self.slot_rows) % 16 == 0:
                self.block = size
                break
        self.steps = slots // self.block
        self.pairs = self.halves * bands * self.chunk
        self.trunc = degrees - 1
        self.sorted = degrees // 2
        self.orbits = up_to((4 * self.trunc + 40) // 4 + 2, SLAB)
        self.levels = LEVELS // groups


def owners(sizes, field):
    first, last = field * LEVELS, (field + 1) * LEVELS
    return [
        g for g in range(sizes.groups)
        if g * sizes.fields < last and (g + 1) * sizes.fields > first
    ]


def geo_rounds(sizes):
    sources, targets = owners(sizes, TEMPER), owners(sizes, ENERGY)
    wide = max(len(sources), len(targets))
    rounds = []
    for turn in range(wide):
        pairs = []
        for k in range(wide):
            s, t = k, (k + turn) % wide
            if s < len(sources) and t < len(targets):
                pairs.append((sources[s], targets[t]))
        if pairs:
            rounds.append(pairs)
    return rounds


def iota(shape, dim):
    return lax.broadcasted_iota(jnp.int32, shape, dim)


def one_hot(cond):
    return jnp.where(cond, 1.0, 0.0).astype(jnp.bfloat16)


def dot(a, b, dims=((1,), (0,))):
    return lax.dot_general(a, b, (dims, ((), ())), preferred_element_type=jnp.float32)


def halving(value):
    return value.bit_length() - 1 if value & (value - 1) == 0 else None


def quotient(x, by):
    bits = halving(by)
    return x >> bits if bits is not None else lax.div(x, jnp.int32(by))


def remainder(x, by):
    return x & (by - 1) if halving(by) is not None else lax.rem(x, jnp.int32(by))


def spread_matrix(sizes, lev):
    sz = sizes
    tall = sz.quarters * 4 * sz.field_pad
    wide = sz.groups * SLAB
    dst = iota((1, wide), 1)
    group = quotient(dst, SLAB)
    lane = remainder(dst, SLAB)
    quarter = quotient(lane, sz.lanes)
    rest = remainder(lane, sz.lanes)
    row = quotient(rest, 2 * sz.share)
    rest = remainder(rest, 2 * sz.share)
    comp = quotient(rest, sz.share)
    item = remainder(rest, sz.share)
    start = remainder(lev * sz.fields, sz.groups)
    field = remainder(group - start + sz.groups, sz.groups) + sz.groups * item
    want = ((quarter * 2 + row) * 2 + comp) * sz.field_pad + field
    want = jnp.where((field < sz.fields) & (quarter < sz.quarters), want, -1)
    return one_hot(iota((tall, wide), 0) == want)


def spot_of(sizes, place, odd):
    half = place // sizes.chunk_live
    return (odd * sizes.halves + half) * sizes.chunk + (place - half * sizes.chunk_live)


def pair_state(sizes, wave, band, place):
    slot = band * sizes.slots + 2 * place
    first, second = wave[slot], wave[slot + 1]
    odd = first & 1
    start = quotient(jnp.maximum(first, 0), SLAB)
    live = sizes.tiles - start
    tiles = []
    for k in range(sizes.tiles + 1):
        side = jnp.where(k < live, 0, 1)
        tiles.append((side, jnp.where(k < live, start + k, k - 1)))
    return (first, second), (odd, 1 - odd), tiles


AHEAD = 6
BEHIND = 4


class Stream:
    def __init__(self, sizes, x_hbm, leg_hbm, x_all, leg_all, x_sems, leg_sems):
        self.sizes = sizes
        self.pairs = ((x_hbm, x_all, x_sems), (leg_hbm, leg_all, leg_sems))

    def copies(self, step):
        return [
            pltpu.make_async_copy(hbm.at[step], here.at[step], sems.at[step])
            for hbm, here, sems in self.pairs
        ]

    def start(self, step):
        for copy in self.copies(step):
            copy.start()

    def begin(self):
        for step in range(min(AHEAD, self.sizes.steps)):
            self.start(step)

    def take(self, step):
        @pl.when(step + AHEAD < self.sizes.steps)
        def _():
            self.start(step + AHEAD)

        for copy in self.copies(step):
            copy.wait()
        return tuple(here.at[step] for _, here, _ in self.pairs)


def inverse_kernel(sizes, rounds, wave, points, gauss, layer_depth, x_hbm, leg_hbm, send_ref, *refs):
    sz = sizes
    geo_refs = refs[:len(rounds)]
    wide, spots, numbers, *stream = refs[len(rounds):]
    stream = Stream(sz, x_hbm, leg_hbm, *stream)
    stream.begin()
    band = lax.axis_index("band")
    lev = lax.axis_index("lev")
    pad = 2 * sz.field_pad
    height = 2 * sz.slot_rows
    spots[...] = jnp.zeros_like(spots)
    numbers[...] = jnp.full_like(numbers, -1)
    wide[:, pl.ds(height, wide.shape[1] - height), :] = jnp.zeros(
        (wide.shape[0], wide.shape[1] - height, SLAB), jnp.float32
    )

    def block(step, carry):
        x_ref, leg_ref = stream.take(step)
        for pair in range(sz.block // 2):
            rows = x_ref[pl.ds(pair * height, height), :]
            wide[pair, pl.ds(0, height), :] = rows.astype(jnp.float32)
        found = []
        for pair in range(sz.block // 2):
            place = step * (sz.block // 2) + pair
            numbers_here, odds, tiles = pair_state(sz, wave, band, place)
            values, tables = [], []
            for side, tile in tiles:
                start = side * sz.slot_rows + 2 * tile
                values.append(jnp.concatenate([
                    wide[pair, pl.ds(start + c, sz.field_pad, stride=2 * sz.tiles), :] for c in range(2)
                ], axis=0).astype(jnp.bfloat16))
                cols = pl.ds(pl.multiple_of(tile * SLAB, SLAB), SLAB)
                table = leg_ref[2 * pair + side, :, cols].astype(jnp.float32)
                number = jnp.where(side == 0, numbers_here[0], numbers_here[1])
                table = jnp.where(iota((1, SLAB), 1) + tile * SLAB >= number, table, 0.0)
                tables.append(jnp.concatenate([
                    jnp.where(side == 0, table, 0.0), jnp.where(side == 1, table, 0.0),
                ], axis=0).astype(jnp.bfloat16))
            total = dot(
                jnp.concatenate(tables, axis=1), jnp.concatenate(values, axis=1), ((1,), (1,))
            )
            for side in range(2):
                found.append((
                    spot_of(sz, place, odds[side]), numbers_here[side],
                    total[side * sz.rows:(side + 1) * sz.rows],
                ))
        for spot, number, total in found:
            at = pl.multiple_of(spot * sz.rows, sz.rows)
            spots[pl.ds(at, sz.rows), 0:pad] = total
            numbers[pl.ds(spot, 1), :] = jnp.full((1, SLAB), number, jnp.int32)
        return carry

    lax.fori_loop(0, sz.steps, block, 0)
    spread = spread_matrix(sz, lev)
    shape = (2 * pad, SLAB)
    src, dst = iota(shape, 0), iota(shape, 1)
    bits = sz.field_pad.bit_length() - 1
    from_field, from_side = src & (sz.field_pad - 1), src >> bits
    to_field, to_side = dst & (sz.field_pad - 1), dst >> bits
    weights = []
    for pairs in rounds:
        first = jnp.int32(2 * LEVELS + sz.fields)
        for source, target in pairs:
            first = jnp.where(lev == source, target * sz.fields - ENERGY * LEVELS, first)
        under = lev * sz.fields + from_field - TEMPER * LEVELS
        above = first + to_field
        hit = (
            (from_side == to_side)
            & (from_field < sz.fields) & (to_field < sz.fields)
            & (above >= 0) & (above <= under)
        )
        weight = jnp.zeros(shape, jnp.float32)
        for level in range(LEVELS):
            weight = jnp.where(hit & (under == level), layer_depth[level], weight)
        high = weight.astype(jnp.bfloat16)
        low = (weight - high.astype(jnp.float32)).astype(jnp.bfloat16)
        weights.append(jnp.concatenate([high, low], axis=0))
    number = numbers[...]
    lane = iota((sz.spots, SLAB), 1)
    known = (number >= 0) & ~((number == 0) & (lane & sz.field_pad != 0))
    for rp in range(sz.rows // 2):
        exact = jnp.concatenate([
            spots[pl.ds(2 * rp + r, sz.spots, stride=sz.rows), :][:, 0:pad] for r in range(2)
        ], axis=1)
        cut = jnp.concatenate([
            exact[q * sz.chunk:(q + 1) * sz.chunk] for q in range(sz.quarters)
        ], axis=1).astype(jnp.bfloat16)
        chunk = dot(cut, spread).astype(jnp.bfloat16)
        for g in range(sz.groups):
            send_ref[rp, g] = chunk[:, g * SLAB:(g + 1) * SLAB]
        count = jnp.where(lane < pad, points[2 * rp], points[2 * rp + 1])
        scale = jnp.where(lane < pad, gauss[2 * rp], gauss[2 * rp + 1])
        scale = jnp.where(known & (2 * number <= count - 1), scale, 0.0)
        exact = exact.astype(jnp.bfloat16)
        double = jnp.concatenate([exact, exact], axis=1)
        for turn in range(len(rounds)):
            geo_refs[turn][rp] = (dot(double, weights[turn]) * scale).astype(jnp.bfloat16)


def cos_sin(z):
    y = z * z
    c = jnp.full_like(y, COS_POLY[-1])
    for a in COS_POLY[-2::-1]:
        c = c * y + a
    s = jnp.full_like(y, SIN_POLY[-1])
    for a in SIN_POLY[-2::-1]:
        s = s * y + a
    return c, s * z


def basis_kernel(sizes, points, out_ref, cosines, sines):
    sz = sizes
    step = pl.program_id(0)
    turns = sz.sorted // 16
    bands_row = 16 + up_to(turns, 8)

    @pl.when(step == 0)
    def _():
        first = lax.axis_index("band") * 2
        length_a, length_b = points[first], points[first + 1]
        count_a = length_a // 4 + 1
        high = cosines.shape[0]
        row = iota((high, SLAB), 0)
        number = jnp.where(row < 16, 2 * row, jnp.where(row < bands_row, 32 * (row - 16), sz.trunc))
        number = number.astype(jnp.float32)
        for at in range(0, sz.orbits, SLAB):
            place = iota((1, SLAB), 1) + at
            second = place >= count_a
            column = (place - jnp.where(second, count_a, 0)).astype(jnp.float32)
            length = jnp.where(second, length_b, length_a).astype(jnp.float32)
            inverse = 1.0 / length
            scale = jnp.where(row < 16, 1.0 / jnp.sqrt(length), 1.0)
            product = number * column
            whole = jnp.floor(product * inverse + 0.5)
            c, s = cos_sin((product - whole * length) * inverse)
            cosines[:, pl.ds(at, SLAB)] = c * scale
            sines[:, pl.ds(at, SLAB)] = s * scale

    groups = out_ref.shape[1] // 16
    for at in range(0, sz.orbits, SLAB):
        cols = pl.ds(at, SLAB)
        base_c, base_n = cosines[0:16, cols], -sines[0:16, cols]
        top_c, top_n = cosines[pl.ds(bands_row, 1), cols], -sines[pl.ds(bands_row, 1), cols]
        turn_rows = pl.ds(pl.multiple_of(16 + step * groups, 8), groups)
        all_c, all_s = cosines[turn_rows, cols], sines[turn_rows, cols]
        for k in range(groups):
            turn_c, turn_s = all_c[k:k + 1], all_s[k:k + 1]
            c = turn_c * base_c + turn_s * base_n
            n = turn_c * base_n - turn_s * base_c
            rows = pl.ds(16 * k, 16)
            out_ref[0, rows, cols] = c.astype(jnp.bfloat16)
            out_ref[1, rows, cols] = n.astype(jnp.bfloat16)
            out_ref[2, rows, cols] = (top_c * c + top_n * n).astype(jnp.bfloat16)
            out_ref[3, rows, cols] = (top_n * c - top_c * n).astype(jnp.bfloat16)


def take_matrix(sizes, lev):
    sz = sizes
    tall = sz.groups * SLAB
    wide = sz.quarters * 2 * SLAB
    dst = iota((1, wide), 1)
    piece = quotient(dst, SLAB)
    lane = remainder(dst, SLAB)
    row = quotient(lane, SLAB // 2)
    field = quotient(remainder(lane, SLAB // 2), LVL_ROWS)
    level = remainder(lane, LVL_ROWS)
    whole = field * LEVELS + level * sz.groups + lev
    owner = quotient(whole, sz.fields)
    start = owner * sz.fields
    first = remainder(lev - remainder(start, sz.groups) + sz.groups, sz.groups)
    item = quotient(whole - start - first, sz.groups)
    want = owner * SLAB + (piece >> 1) * sz.lanes + (row * 2 + (piece & 1)) * sz.share + item
    want = jnp.where((field < FIELDS) & (level < sz.levels), want, -1)
    return one_hot(iota((tall, wide), 0) == want)


def grid_kernel(
    sizes, points, gauss, recv_ref, even_row, even_col, basis_hbm, send_ref, basis, terms, arrivals,
):
    sz = sizes
    step = 2 * SLAB
    parts = -(-sz.orbits // step)
    copies = []
    for part in range(parts):
        cols = pl.ds(part * step, min(step, sz.orbits - part * step))
        copies.append(pltpu.make_async_copy(basis_hbm.at[:, :, cols], basis.at[:, :, cols], arrivals.at[part]))
        copies[-1].start()
    lev = lax.axis_index("lev")
    first_row = lax.axis_index("band") * 2
    length_a, length_b = points[first_row], points[first_row + 1]
    count_a, count_b = length_a // 4 + 1, length_b // 4 + 1
    high = FIELDS * LVL_ROWS
    half_slab = SLAB // 2
    width = sz.bands * sz.chunk
    take = take_matrix(sz, lev)
    order = one_hot(iota((sz.sorted, sz.pairs), 0) * 2 == even_row[...])
    joined = jnp.concatenate([
        recv_ref[:, g].astype(jnp.float32).reshape(width, SLAB) for g in range(sz.groups)
    ], axis=1).astype(jnp.bfloat16)
    taken = dot(joined, take)
    coeffs = []
    number = iota((2 * SLAB, sz.sorted), 1) * 2
    bound = jnp.where(iota((2 * SLAB, sz.sorted), 0) & half_slab == 0, length_a, length_b) - 1
    kept = (0, half_slab, SLAB, SLAB + half_slab)
    for parity in range(2):
        rows = []
        for half in range(sz.halves):
            piece = (parity * sz.halves + half) * 2
            rows.append(taken[:, piece * SLAB:(piece + 2) * SLAB])
        values = jnp.concatenate(rows, axis=0).T.astype(jnp.bfloat16)
        placed = dot(values, order, ((1,), (1,)))
        mine = number if parity == 0 else sz.trunc - number
        mult = jnp.where(mine == 0, 1.0, 2.0)
        placed = jnp.where(2 * mine <= bound, placed * mult, 0.0)
        placed = jnp.concatenate([placed[k:k + high] for k in kept], axis=0).astype(jnp.bfloat16)
        coeffs += [placed[:2 * high], placed[2 * high:]]
    for part in range(parts):
        copies[part].wait()
        at = part * step
        many = min(step, sz.orbits - at)
        cols = pl.ds(at, many)
        place = iota((1, many), 1) + at
        second = place >= count_a
        grids = []
        for k in range(4):
            both = dot(coeffs[k], basis[k, :, cols])
            grids.append(jnp.where(second, both[high:], both[:high]))
        ce, se, co, so = grids
        plus, minus = ce + co, ce - co
        splus, sminus = se + so, se - so
        values = (plus + splus, minus - sminus, minus + sminus, plus - splus)
        outs = []
        for v in values:
            u, w, tem, hum, ozo = (v[i * LVL_ROWS:(i + 1) * LVL_ROWS] for i in range(FIELDS))
            outs.append(jnp.concatenate(
                [u * tem, w * tem, u * hum, w * ozo, 0.5 * (u * u + w * w)], axis=0
            ))
        offset = place - jnp.where(second, count_a, 0)
        count = jnp.where(second, count_b, count_a)
        weight = jnp.where((offset == 0) | (offset == count - 1), 0.5, 1.0)
        weight = jnp.where(offset < count, weight, 0.0)
        t0, t1, t2, t3 = (o * weight for o in outs)
        a, b, c, d = t0 + t3, t1 + t2, t0 - t3, t2 - t1
        folds = (a + b, c + d, a - b, c - d)
        empty = jnp.zeros((half_slab - high, many), jnp.float32)
        for k in range(4):
            first = jnp.where(second, 0.0, folds[k])
            last = jnp.where(second, folds[k], 0.0)
            terms[k, :, cols] = jnp.concatenate([first, empty, last, empty], axis=0).astype(jnp.bfloat16)
    lane = iota((1, SLAB), 1)
    scale = jnp.where(lane < half_slab, gauss[first_row], gauss[first_row + 1])
    bound = jnp.where(lane < half_slab, length_a, length_b) - 1
    number = iota((sz.sorted, SLAB), 0) * 2
    back_order = one_hot(iota((sz.pairs, sz.sorted), 1) * 2 == even_col[...])
    pieces = []
    for parity in range(2):
        mine = number if parity == 0 else sz.trunc - number
        sums = jnp.concatenate([
            jnp.where(
                2 * mine <= bound,
                dot(basis[parity * 2 + comp], terms[parity * 2 + comp], ((1,), (1,))) * scale, 0.0,
            ).astype(jnp.bfloat16)
            for comp in range(2)
        ], axis=1)
        slots = dot(back_order, sums).astype(jnp.bfloat16)
        pieces += [slots[half * width:(half + 1) * width] for half in range(sz.halves)]
    sent = dot(jnp.concatenate(pieces, axis=1), take, ((1,), (1,)))
    for g in range(sz.groups):
        part = sent[:, g * SLAB:(g + 1) * SLAB].reshape(sz.bands, sz.chunk, SLAB)
        send_ref[:, g] = part.astype(jnp.bfloat16)


def forward_kernel(
    sizes, wave, speed, back_ref, *refs,
):
    sz = sizes
    geo_refs = refs[:-12]
    x_hbm, leg_hbm, out_hbm, wide, spots, inverse, out_all, out_sems, *stream = refs[-12:]
    stream = Stream(sz, x_hbm, leg_hbm, *stream)
    stream.begin()
    band = lax.axis_index("band")
    pad = 2 * sz.field_pad
    height = 2 * sz.slot_rows

    gather = spread_matrix(sz, lax.axis_index("lev"))
    for rp in range(sz.rows // 2):
        cut = jnp.concatenate([back_ref[rp, g] for g in range(sz.groups)], axis=1)
        whole = dot(cut, gather, ((1,), (1,)))
        rows = jnp.concatenate([
            whole[:, q * 2 * pad:(q + 1) * 2 * pad] for q in range(sz.quarters)
        ], axis=0)
        for geo_ref in geo_refs:
            rows = rows + geo_ref[rp].astype(jnp.float32)[:, 0:2 * pad]
        for r in range(2):
            part = rows[:, r * pad:(r + 1) * pad]
            part = jnp.concatenate([part, jnp.zeros((sz.spots, SLAB - pad), jnp.float32)], axis=1)
            spots[pl.ds(2 * rp + r, sz.spots, stride=sz.rows), :] = part
    for f in range(sz.fields):
        rows = 2 * sz.tiles
        degree = quotient(iota((rows, SLAB), 0), 2) * SLAB + iota((rows, SLAB), 1)
        helm = (degree * (degree + 1)).astype(jnp.float32) / float(sz.trunc * (sz.trunc + 1))
        inverse[pl.ds(f * rows, rows), :] = 1.0 / (1.0 + time_step * time_step * helm * speed[f])

    pitch = sz.field_pad * 2 * sz.tiles

    def leave(step):
        at = lax.rem(step, BEHIND)
        return pltpu.make_async_copy(out_all.at[at], out_hbm.at[step], out_sems.at[at])

    def block(step, carry):
        x_ref, leg_ref = stream.take(step)
        place_out = lax.rem(step, BEHIND)
        out_ref = out_all.at[place_out]
        work = []
        for pair in range(sz.block // 2):
            place = step * (sz.block // 2) + pair
            numbers, odds, tiles = pair_state(sz, wave, band, place)
            lefts = []
            for side in range(2):
                at = pl.multiple_of(spot_of(sz, place, odds[side]) * sz.rows, sz.rows)
                lefts.append(spots[pl.ds(at, sz.rows), :])
            left = jnp.concatenate(lefts, axis=0).T.astype(jnp.bfloat16)[0:pad]
            tables = []
            for side, tile in tiles:
                cols = pl.ds(pl.multiple_of(tile * SLAB, SLAB), SLAB)
                table = leg_ref[2 * pair + side, :, cols].astype(jnp.float32)
                tables.append(jnp.concatenate([
                    jnp.where(side == 0, table, 0.0), jnp.where(side == 1, table, 0.0),
                ], axis=0).astype(jnp.bfloat16))
            work.append((numbers, tiles, left, tables))
        for pair in range(sz.block // 2):
            _, tiles, left, tables = work[pair]
            for k in range(0, len(tiles), 2):
                count = min(2, len(tiles) - k)
                tends = dot(left, jnp.concatenate(tables[k:k + count], axis=1))
                for kk in range(count):
                    side, tile = tiles[k + kk]
                    for c in range(2):
                        rows = pl.ds(side * pitch + 2 * tile + c, sz.field_pad, stride=2 * sz.tiles)
                        wide[pair, rows, :] = tends[
                            c * sz.field_pad:(c + 1) * sz.field_pad, kk * SLAB:(kk + 1) * SLAB
                        ]
        @pl.when(step >= BEHIND)
        def _():
            leave(step - BEHIND).wait()

        run = 4 * sz.tiles if sz.fields % 2 == 0 else 2 * sz.tiles
        row = remainder(iota((run, SLAB), 0), 2 * sz.tiles)
        degree = quotient(row, 2) * SLAB + iota((run, SLAB), 1)
        for pair in range(sz.block // 2):
            numbers = work[pair][0]
            old = x_ref[pl.ds(pair * height, height), :].astype(jnp.float32)
            for side in range(2):
                live = degree >= jnp.where(numbers[side] < 0, sz.degrees, numbers[side])
                for at in range(0, sz.slot_rows, run):
                    tend = wide[pair, pl.ds(side * pitch + at, run), :]
                    new = old[side * sz.slot_rows + at:side * sz.slot_rows + at + run] + time_step * tend
                    new = jnp.where(live, new * inverse[pl.ds(at, run), :], 0.0)
                    out_ref[pl.ds(pair * height + side * sz.slot_rows + at, run), :] = new
        leave(step).start()
        return carry

    lax.fori_loop(0, sz.steps, block, 0)
    for step in range(max(0, sz.steps - BEHIND), sz.steps):
        leave(jnp.int32(step)).wait()


def params(mib):
    return pltpu.CompilerParams(vmem_limit_bytes=mib * MIB)


def smem():
    return pl.BlockSpec(memory_space=pltpu.SMEM)


def shards(spectra, legendre, slot_wave, row_points, gauss_weight, layer_depth, mode_speed):
    slots, _, fields, degrees = spectra.shape
    rows = legendre.shape[2]
    sz = Sizes(lax.axis_size("band"), lax.axis_size("lev"), slots, fields, degrees, rows)

    tiled = spectra.reshape(slots, 2, fields, sz.tiles, SLAB)
    tiled = with_layout_constraint(tiled, Layout((0, 2, 3, 1, 4)))
    lines = tiled.transpose(0, 2, 3, 1, 4).reshape(sz.steps, sz.block * sz.slot_rows, SLAB)
    tables = legendre.transpose(0, 2, 1).reshape(sz.steps, sz.block, sz.rows, degrees)

    rounds = geo_rounds(sz)
    tail = up_to((sz.field_pad - sz.fields) * 2 * sz.tiles, 16)
    wide_shape = pltpu.VMEM((sz.block // 2, 2 * sz.slot_rows + tail, SLAB), jnp.float32)
    spots_shape = pltpu.VMEM((sz.spots * sz.rows, SLAB), jnp.float32)
    stream_scratch = [
        pltpu.VMEM(lines.shape, jnp.bfloat16),
        pltpu.VMEM(tables.shape, jnp.bfloat16),
        pltpu.SemaphoreType.DMA((sz.steps,)),
        pltpu.SemaphoreType.DMA((sz.steps,)),
    ]
    anywhere = pl.BlockSpec(memory_space=pl.ANY)
    vmem = pl.BlockSpec(memory_space=pltpu.VMEM)
    send_shape = (sz.bands, sz.groups, sz.chunk, SLAB)
    geo_shape = (sz.rows // 2, sz.spots, SLAB)

    sent, *geo = pl.pallas_call(
        functools.partial(inverse_kernel, sz, rounds),
        in_specs=[smem(), smem(), smem(), smem(), anywhere, anywhere],
        out_specs=[vmem] * (1 + len(rounds)),
        out_shape=[jax.ShapeDtypeStruct(send_shape, jnp.bfloat16)]
        + [jax.ShapeDtypeStruct(geo_shape, jnp.bfloat16)] * len(rounds),
        scratch_shapes=[wide_shape, spots_shape, pltpu.VMEM((sz.spots, SLAB), jnp.int32), *stream_scratch],
        compiler_params=params(56),
        name="inverse_legendre",
    )(slot_wave, row_points, gauss_weight, layer_depth, lines, tables)

    sent, points_later, wave_later = lax.optimization_barrier((sent, row_points, slot_wave))
    both = ("band", "lev")
    total = sz.bands * sz.groups
    flat = (total * sz.chunk, SLAB)
    arrived = lax.all_to_all(sent.reshape(flat), both, split_axis=0, concat_axis=0, tiled=True)

    pair_wave = wave_later.reshape(-1, 2)
    even_wave = jnp.where(pair_wave[:, 0] % 2 == 0, pair_wave[:, 0], pair_wave[:, 1])
    even_wave = even_wave.reshape(sz.bands, sz.halves, sz.chunk_live)
    even_wave = jnp.pad(even_wave, ((0, 0), (0, 0), (0, sz.chunk - sz.chunk_live)), constant_values=-1)
    even_wave = even_wave.transpose(1, 0, 2).reshape(sz.pairs)

    high = SLAB if sz.sorted % SLAB == 0 else sz.sorted
    table_rows = 16 + up_to(sz.sorted // 16, 8) + 8
    basis = pl.pallas_call(
        functools.partial(basis_kernel, sz),
        grid=(sz.sorted // high,),
        in_specs=[smem()],
        out_specs=pl.BlockSpec((4, high, sz.orbits), lambda i: (0, i, 0)),
        out_shape=jax.ShapeDtypeStruct((4, sz.sorted, sz.orbits), jnp.bfloat16),
        scratch_shapes=[pltpu.VMEM((table_rows, sz.orbits), jnp.float32)] * 2,
        compiler_params=params(56),
        cost_estimate=pl.CostEstimate(
            flops=20 * sz.sorted * sz.orbits, bytes_accessed=8 * sz.sorted * sz.orbits, transcendentals=0,
        ),
        name="basis",
    )(points_later)

    even_row, even_col = even_wave.reshape(1, sz.pairs), even_wave.reshape(sz.pairs, 1)
    *geo, arrived, basis, even_row, even_col = lax.optimization_barrier(
        (*geo, arrived, basis, even_row, even_col)
    )
    moved = [lax.ppermute(geo[turn], "lev", pairs) for turn, pairs in enumerate(rounds)]
    returned = pl.pallas_call(
        functools.partial(grid_kernel, sz),
        in_specs=[smem(), smem(), vmem, vmem, vmem, anywhere],
        out_specs=vmem,
        out_shape=jax.ShapeDtypeStruct(send_shape, jnp.bfloat16),
        scratch_shapes=[
            pltpu.VMEM((4, sz.sorted, sz.orbits), jnp.bfloat16),
            pltpu.VMEM((4, SLAB, sz.orbits), jnp.bfloat16),
            pltpu.SemaphoreType.DMA((-(-sz.orbits // (2 * SLAB)),)),
        ],
        compiler_params=params(56),
        cost_estimate=pl.CostEstimate(
            flops=4 * 4 * SLAB * sz.sorted * sz.orbits, bytes_accessed=8 * sz.sorted * sz.orbits, transcendentals=0,
        ),
        name="grid_products",
    )(
        row_points, gauss_weight, arrived.reshape(send_shape), even_row, even_col, basis,
    )
    *moved, returned = lax.optimization_barrier((*moved, returned))

    back = lax.all_to_all(returned.reshape(flat), both, split_axis=0, concat_axis=0, tiled=True)

    out = pl.pallas_call(
        functools.partial(forward_kernel, sz),
        in_specs=[smem(), smem()] + [vmem] * (1 + len(rounds)) + [anywhere, anywhere],
        out_specs=anywhere,
        out_shape=jax.ShapeDtypeStruct(lines.shape, jnp.float32),
        scratch_shapes=[
            pltpu.VMEM((sz.block // 2, 4 * sz.field_pad * sz.tiles, SLAB), jnp.float32), spots_shape,
            pltpu.VMEM((sz.slot_rows, SLAB), jnp.float32),
            pltpu.VMEM((BEHIND, *lines.shape[1:]), jnp.float32),
            pltpu.SemaphoreType.DMA((BEHIND,)),
            *stream_scratch,
        ],
        compiler_params=params(56),
        name="forward_legendre",
    )(slot_wave, mode_speed, back.reshape(send_shape), *moved, lines, tables)

    out = out.reshape(slots, fields, sz.tiles, 2, SLAB).transpose(0, 1, 3, 2, 4)
    return out.reshape(slots, fields, 2, degrees).transpose(0, 2, 1, 3)


def solution(mesh):
    return jax.shard_map(
        shards,
        mesh=mesh,
        in_specs=(
            P("band", None, "lev", None),
            P("band", None, None),
            P(),
            P(),
            P(),
            P(),
            P("lev"),
        ),
        out_specs=P("band", None, "lev", None),
        check_vma=False,
    )
```

```python
import functools
import math

import jax
import jax.numpy as jnp
from jax import lax
from jax.experimental import pallas as pl
from jax.experimental.layout import Layout, with_layout_constraint
from jax.experimental.pallas import tpu as pltpu
from jax.sharding import PartitionSpec as P

FIELDS = 5
LEVELS = 24
TEMPER = 2
ENERGY = 4
LVL_ROWS = 8
SLAB = 128
MIB = 1024 * 1024

time_step = 1.0

COS_POLY = (
    0.9999999890590235, -19.739204499453994, 64.93911745989843, -85.45013953092186,
    60.167630951185615, -25.967599249120923, 6.528658161956132,
)
SIN_POLY = (
    6.283185302511506, -41.3417004053176, 81.60513138579954, -76.70301535389986,
    42.02592698629647, -14.89984666973851, 3.2381375126489513,
)


def up_to(value, unit):
    return -(-value // unit) * unit


class Sizes:
    def __init__(self, bands, groups, slots, fields, degrees, rows):
        self.bands, self.groups = bands, groups
        self.slots, self.fields, self.degrees, self.rows = slots, fields, degrees, rows
        self.tiles = degrees // SLAB
        self.packed = self.tiles + 1
        self.slot_rows = fields * self.tiles * 2
        self.field_pad = up_to(fields, 8)
        self.share = -(-fields // groups)
        self.lanes = 4 * self.share
        self.quarters = 2
        if 4 * self.lanes <= SLAB and slots % 4 == 0:
            self.quarters = 4
        self.halves = self.quarters // 2
        self.chunk_live = slots // self.quarters
        self.chunk = up_to(self.chunk_live, 8)
        self.spots = self.quarters * self.chunk
        self.block = slots
        for size in (8, 4):
            if slots % size == 0 and (size * self.slot_rows) % 16 == 0:
                self.block = size
                break
        self.steps = slots // self.block
        self.pairs = self.halves * bands * self.chunk
        self.trunc = degrees - 1
        self.sorted = degrees // 2
        self.orbits = up_to((4 * self.trunc + 40) // 4 + 2, SLAB)
        self.levels = LEVELS // groups


def owners(sizes, field):
    first, last = field * LEVELS, (field + 1) * LEVELS
    return [
        g for g in range(sizes.groups)
        if g * sizes.fields < last and (g + 1) * sizes.fields > first
    ]


def geo_rounds(sizes):
    sources, targets = owners(sizes, TEMPER), owners(sizes, ENERGY)
    wide = max(len(sources), len(targets))
    rounds = []
    for turn in range(wide):
        pairs = []
        for k in range(wide):
            s, t = k, (k + turn) % wide
            if s < len(sources) and t < len(targets):
                pairs.append((sources[s], targets[t]))
        if pairs:
            rounds.append(pairs)
    return rounds


def iota(shape, dim):
    return lax.broadcasted_iota(jnp.int32, shape, dim)


def one_hot(cond):
    return jnp.where(cond, 1.0, 0.0).astype(jnp.bfloat16)


def dot(a, b, dims=((1,), (0,))):
    return lax.dot_general(a, b, (dims, ((), ())), preferred_element_type=jnp.float32)


def halving(value):
    return value.bit_length() - 1 if value & (value - 1) == 0 else None


def quotient(x, by):
    bits = halving(by)
    return x >> bits if bits is not None else lax.div(x, jnp.int32(by))


def remainder(x, by):
    return x & (by - 1) if halving(by) is not None else lax.rem(x, jnp.int32(by))


def spread_matrix(sizes, lev):
    sz = sizes
    tall = sz.quarters * 4 * sz.field_pad
    wide = sz.groups * SLAB
    dst = iota((1, wide), 1)
    group = quotient(dst, SLAB)
    lane = remainder(dst, SLAB)
    quarter = quotient(lane, sz.lanes)
    rest = remainder(lane, sz.lanes)
    row = quotient(rest, 2 * sz.share)
    rest = remainder(rest, 2 * sz.share)
    comp = quotient(rest, sz.share)
    item = remainder(rest, sz.share)
    start = remainder(lev * sz.fields, sz.groups)
    field = remainder(group - start + sz.groups, sz.groups) + sz.groups * item
    want = ((quarter * 2 + row) * sz.field_pad + field) * 2 + comp
    want = jnp.where((field < sz.fields) & (quarter < sz.quarters), want, -1)
    return one_hot(iota((tall, wide), 0) == want)


def spot_of(sizes, place, odd):
    half = place // sizes.chunk_live
    return (odd * sizes.halves + half) * sizes.chunk + (place - half * sizes.chunk_live)


class Pair:
    def __init__(self, sizes, wave, band, place):
        self.sizes, self.place = sizes, place
        slot = band * sizes.slots + 2 * place
        self.numbers = wave[slot], wave[slot + 1]
        odd = self.numbers[0] & 1
        self.odds = odd, 1 - odd
        self.start = quotient(jnp.maximum(self.numbers[0], 0), SLAB)
        self.split = sizes.tiles - self.start

    def spot(self, side):
        sz = self.sizes
        half = self.place // sz.chunk_live
        first = (self.odds[side] * sz.halves + half) * sz.chunk
        return first + (self.place - half * sz.chunk_live)

    def rows(self, side):
        return pl.ds(pl.multiple_of(self.spot(side) * self.sizes.rows, self.sizes.rows), self.sizes.rows)

    def tile(self, k):
        return jnp.where(k < self.split, self.start + k, k - 1)

    def columns(self):
        place = iota((1, self.sizes.packed * SLAB), 1)
        first = place < self.split * SLAB
        degree = jnp.where(first, place + self.start * SLAB, place - SLAB)
        floors = [jnp.where(n < 0, self.sizes.degrees, n) for n in self.numbers]
        return first, degree >= jnp.where(first, floors[0], floors[1])

    def by_start(self, emit):
        def branch(low, high):
            if high - low == 1:
                emit(low)
                return
            middle = (low + high) // 2
            pl.when(self.start < middle)(lambda: branch(low, middle))
            pl.when(self.start >= middle)(lambda: branch(middle, high))

        branch(0, self.sizes.tiles)

    def tables(self, leg):
        first, live = self.columns()
        leg = leg.astype(jnp.float32)
        own = jnp.where(first & live, leg, 0.0)
        other = jnp.where(first, 0.0, jnp.where(live, leg, 0.0))
        return jnp.concatenate([own, other], axis=0).astype(jnp.bfloat16)


AHEAD = 6
BEHIND = 4


class Stream:
    def __init__(self, sizes, pair_at, x_hbm, leg_hbm, x_all, leg_all, x_sems, leg_sems):
        self.sizes, self.pair_at = sizes, pair_at
        self.x_hbm, self.leg_hbm, self.x_all, self.leg_all = x_hbm, leg_hbm, x_all, leg_all
        self.x_sems, self.leg_sems = x_sems, leg_sems

    def start(self, place):
        pair = self.pair_at(place)
        tiles = self.sizes.tiles

        def emit(start):
            split = tiles - start
            for side, first, here in ((0, start, (0, split)), (1, split - 1, (split, tiles + 1))):
                slot = 2 * place + side
                pltpu.make_async_copy(
                    self.x_hbm.at[slot, :, pl.ds(first, tiles - first)],
                    self.x_all.at[place, :, pl.ds(here[0], here[1] - here[0])],
                    self.x_sems.at[place],
                ).start()
                pltpu.make_async_copy(
                    self.leg_hbm.at[slot, :, pl.ds(first * SLAB, (tiles - first) * SLAB)],
                    self.leg_all.at[place, :, pl.ds(here[0] * SLAB, (here[1] - here[0]) * SLAB)],
                    self.leg_sems.at[place],
                ).start()

        pair.by_start(emit)

    def begin(self):
        def one(place, carry):
            self.start(place)
            return carry

        lax.fori_loop(0, min(AHEAD * self.sizes.block // 2, self.sizes.slots // 2), one, 0)

    def take(self, step):
        each = self.sizes.block // 2

        @pl.when(step + AHEAD < self.sizes.steps)
        def _():
            for k in range(each):
                self.start((step + AHEAD) * each + k)

        for k in range(each):
            place = step * each + k
            for here, sems in ((self.x_all, self.x_sems), (self.leg_all, self.leg_sems)):
                pltpu.make_async_copy(here.at[place], here.at[place], sems.at[place]).wait()


def inverse_kernel(sizes, rounds, wave, points, gauss, layer_depth, x_hbm, leg_hbm, send_ref, *refs):
    sz = sizes
    geo_refs = refs[:len(rounds)]
    spots, numbers, x_all, leg_all, *sems = refs[len(rounds):]
    band = lax.axis_index("band")
    lev = lax.axis_index("lev")
    pair_at = functools.partial(Pair, sz, wave, band)
    stream = Stream(sz, pair_at, x_hbm, leg_hbm, x_all, leg_all, *sems)
    stream.begin()
    pad = 2 * sz.field_pad
    spots[...] = jnp.zeros_like(spots)
    numbers[...] = jnp.full_like(numbers, -1)

    def block(step, carry):
        stream.take(step)
        found = []
        for k in range(sz.block // 2):
            place = step * (sz.block // 2) + k
            pair = pair_at(place)
            values = jnp.concatenate([
                x_all[place, :, t].reshape(2 * sz.fields, SLAB) for t in range(sz.packed)
            ], axis=1)
            total = dot(pair.tables(leg_all[place]), values, ((1,), (1,)))
            for side in range(2):
                found.append((pair, side, total[side * sz.rows:(side + 1) * sz.rows]))
        for pair, side, total in found:
            spots[pair.rows(side), 0:2 * sz.fields] = total
            number = jnp.full((1, SLAB), pair.numbers[side], jnp.int32)
            numbers[pl.ds(pair.spot(side), 1), :] = number
        return carry

    lax.fori_loop(0, sz.steps, block, 0)
    spread = spread_matrix(sz, lev)
    shape = (2 * pad, SLAB)
    src, dst = iota(shape, 0), iota(shape, 1)
    from_row, from_field, from_comp = src // pad, (src & (pad - 1)) >> 1, src & 1
    to_row, to_field, to_comp = dst // pad, (dst & (pad - 1)) >> 1, dst & 1
    weights = []
    for pairs in rounds:
        first = jnp.int32(2 * LEVELS + sz.fields)
        for source, target in pairs:
            first = jnp.where(lev == source, target * sz.fields - ENERGY * LEVELS, first)
        under = lev * sz.fields + from_field - TEMPER * LEVELS
        above = first + to_field
        hit = (
            (from_row == to_row) & (from_comp == to_comp)
            & (from_field < sz.fields) & (to_field < sz.fields)
            & (above >= 0) & (above <= under)
        )
        weight = jnp.zeros(shape, jnp.float32)
        for level in range(LEVELS):
            weight = jnp.where(hit & (under == level), layer_depth[level], weight)
        high = weight.astype(jnp.bfloat16)
        low = (weight - high.astype(jnp.float32)).astype(jnp.bfloat16)
        weights.append(jnp.concatenate([high, low], axis=0))
    number = numbers[...]
    lane = iota((sz.spots, SLAB), 1)
    known = (number >= 0) & ~((number == 0) & (lane & 1 == 1))
    for rp in range(sz.rows // 2):
        exact = jnp.concatenate([
            spots[pl.ds(2 * rp + r, sz.spots, stride=sz.rows), :][:, 0:pad] for r in range(2)
        ], axis=1)
        cut = jnp.concatenate([
            exact[q * sz.chunk:(q + 1) * sz.chunk] for q in range(sz.quarters)
        ], axis=1).astype(jnp.bfloat16)
        chunk = dot(cut, spread).astype(jnp.bfloat16)
        for g in range(sz.groups):
            send_ref[rp, g] = chunk[:, g * SLAB:(g + 1) * SLAB]
        count = jnp.where(lane < pad, points[2 * rp], points[2 * rp + 1])
        scale = jnp.where(lane < pad, gauss[2 * rp], gauss[2 * rp + 1])
        scale = jnp.where(known & (2 * number <= count - 1), scale, 0.0)
        exact = exact.astype(jnp.bfloat16)
        double = jnp.concatenate([exact, exact], axis=1)
        for turn in range(len(rounds)):
            geo_refs[turn][rp] = (dot(double, weights[turn]) * scale).astype(jnp.bfloat16)


def cos_sin(z):
    y = z * z
    c = jnp.full_like(y, COS_POLY[-1])
    for a in COS_POLY[-2::-1]:
        c = c * y + a
    s = jnp.full_like(y, SIN_POLY[-1])
    for a in SIN_POLY[-2::-1]:
        s = s * y + a
    return c, s * z


def basis_kernel(sizes, points, out_ref, cosines, sines):
    sz = sizes
    step = pl.program_id(0)
    turns = sz.sorted // 16
    bands_row = 16 + up_to(turns, 8)

    @pl.when(step == 0)
    def _():
        first = lax.axis_index("band") * 2
        length_a, length_b = points[first], points[first + 1]
        count_a = length_a // 4 + 1
        high = cosines.shape[0]
        row = iota((high, SLAB), 0)
        number = jnp.where(row < 16, 2 * row, jnp.where(row < bands_row, 32 * (row - 16), sz.trunc))
        number = number.astype(jnp.float32)
        for at in range(0, sz.orbits, SLAB):
            place = iota((1, SLAB), 1) + at
            second = place >= count_a
            column = (place - jnp.where(second, count_a, 0)).astype(jnp.float32)
            length = jnp.where(second, length_b, length_a).astype(jnp.float32)
            inverse = 1.0 / length
            scale = jnp.where(row < 16, 1.0 / jnp.sqrt(length), 1.0)
            product = number * column
            whole = jnp.floor(product * inverse + 0.5)
            c, s = cos_sin((product - whole * length) * inverse)
            cosines[:, pl.ds(at, SLAB)] = c * scale
            sines[:, pl.ds(at, SLAB)] = s * scale

    groups = out_ref.shape[1] // 16
    for at in range(0, sz.orbits, SLAB):
        cols = pl.ds(at, SLAB)
        base_c, base_n = cosines[0:16, cols], -sines[0:16, cols]
        top_c, top_n = cosines[pl.ds(bands_row, 1), cols], -sines[pl.ds(bands_row, 1), cols]
        turn_rows = pl.ds(pl.multiple_of(16 + step * groups, 8), groups)
        all_c, all_s = cosines[turn_rows, cols], sines[turn_rows, cols]
        for k in range(groups):
            turn_c, turn_s = all_c[k:k + 1], all_s[k:k + 1]
            c = turn_c * base_c + turn_s * base_n
            n = turn_c * base_n - turn_s * base_c
            rows = pl.ds(16 * k, 16)
            out_ref[0, rows, cols] = c.astype(jnp.bfloat16)
            out_ref[1, rows, cols] = n.astype(jnp.bfloat16)
            out_ref[2, rows, cols] = (top_c * c + top_n * n).astype(jnp.bfloat16)
            out_ref[3, rows, cols] = (top_n * c - top_c * n).astype(jnp.bfloat16)


def take_matrix(sizes, lev):
    sz = sizes
    tall = sz.groups * SLAB
    wide = sz.quarters * 2 * SLAB
    dst = iota((1, wide), 1)
    piece = quotient(dst, SLAB)
    lane = remainder(dst, SLAB)
    row = quotient(lane, SLAB // 2)
    field = quotient(remainder(lane, SLAB // 2), LVL_ROWS)
    level = remainder(lane, LVL_ROWS)
    whole = field * LEVELS + level * sz.groups + lev
    owner = quotient(whole, sz.fields)
    start = owner * sz.fields
    first = remainder(lev - remainder(start, sz.groups) + sz.groups, sz.groups)
    item = quotient(whole - start - first, sz.groups)
    want = owner * SLAB + (piece >> 1) * sz.lanes + (row * 2 + (piece & 1)) * sz.share + item
    want = jnp.where((field < FIELDS) & (level < sz.levels), want, -1)
    return one_hot(iota((tall, wide), 0) == want)


def grid_kernel(
    sizes, points, gauss, recv_ref, even_row, even_col, basis_hbm, send_ref, basis, terms, arrivals,
):
    sz = sizes
    step = 2 * SLAB
    parts = -(-sz.orbits // step)
    copies = []
    for part in range(parts):
        cols = pl.ds(part * step, min(step, sz.orbits - part * step))
        copies.append(pltpu.make_async_copy(basis_hbm.at[:, :, cols], basis.at[:, :, cols], arrivals.at[part]))
        copies[-1].start()
    lev = lax.axis_index("lev")
    first_row = lax.axis_index("band") * 2
    length_a, length_b = points[first_row], points[first_row + 1]
    count_a, count_b = length_a // 4 + 1, length_b // 4 + 1
    high = FIELDS * LVL_ROWS
    half_slab = SLAB // 2
    width = sz.bands * sz.chunk
    take = take_matrix(sz, lev)
    order = one_hot(iota((sz.sorted, sz.pairs), 0) * 2 == even_row[...])
    joined = jnp.concatenate([
        recv_ref[:, g].astype(jnp.float32).reshape(width, SLAB) for g in range(sz.groups)
    ], axis=1).astype(jnp.bfloat16)
    taken = dot(joined, take)
    coeffs = []
    number = iota((2 * SLAB, sz.sorted), 1) * 2
    bound = jnp.where(iota((2 * SLAB, sz.sorted), 0) & half_slab == 0, length_a, length_b) - 1
    kept = (0, half_slab, SLAB, SLAB + half_slab)
    for parity in range(2):
        rows = []
        for half in range(sz.halves):
            piece = (parity * sz.halves + half) * 2
            rows.append(taken[:, piece * SLAB:(piece + 2) * SLAB])
        values = jnp.concatenate(rows, axis=0).T.astype(jnp.bfloat16)
        placed = dot(values, order, ((1,), (1,)))
        mine = number if parity == 0 else sz.trunc - number
        mult = jnp.where(mine == 0, 1.0, 2.0)
        placed = jnp.where(2 * mine <= bound, placed * mult, 0.0)
        placed = jnp.concatenate([placed[k:k + high] for k in kept], axis=0).astype(jnp.bfloat16)
        coeffs += [placed[:2 * high], placed[2 * high:]]
    for part in range(parts):
        copies[part].wait()
        at = part * step
        many = min(step, sz.orbits - at)
        cols = pl.ds(at, many)
        place = iota((1, many), 1) + at
        second = place >= count_a
        grids = []
        for k in range(4):
            both = dot(coeffs[k], basis[k, :, cols])
            grids.append(jnp.where(second, both[high:], both[:high]))
        ce, se, co, so = grids
        plus, minus = ce + co, ce - co
        splus, sminus = se + so, se - so
        values = (plus + splus, minus - sminus, minus + sminus, plus - splus)
        outs = []
        for v in values:
            u, w, tem, hum, ozo = (v[i * LVL_ROWS:(i + 1) * LVL_ROWS] for i in range(FIELDS))
            outs.append(jnp.concatenate(
                [u * tem, w * tem, u * hum, w * ozo, 0.5 * (u * u + w * w)], axis=0
            ))
        offset = place - jnp.where(second, count_a, 0)
        count = jnp.where(second, count_b, count_a)
        weight = jnp.where((offset == 0) | (offset == count - 1), 0.5, 1.0)
        weight = jnp.where(offset < count, weight, 0.0)
        t0, t1, t2, t3 = (o * weight for o in outs)
        a, b, c, d = t0 + t3, t1 + t2, t0 - t3, t2 - t1
        folds = (a + b, c + d, a - b, c - d)
        empty = jnp.zeros((half_slab - high, many), jnp.float32)
        for k in range(4):
            first = jnp.where(second, 0.0, folds[k])
            last = jnp.where(second, folds[k], 0.0)
            terms[k, :, cols] = jnp.concatenate([first, empty, last, empty], axis=0).astype(jnp.bfloat16)
    lane = iota((1, SLAB), 1)
    scale = jnp.where(lane < half_slab, gauss[first_row], gauss[first_row + 1])
    bound = jnp.where(lane < half_slab, length_a, length_b) - 1
    number = iota((sz.sorted, SLAB), 0) * 2
    back_order = one_hot(iota((sz.pairs, sz.sorted), 1) * 2 == even_col[...])
    pieces = []
    for parity in range(2):
        mine = number if parity == 0 else sz.trunc - number
        sums = jnp.concatenate([
            jnp.where(
                2 * mine <= bound,
                dot(basis[parity * 2 + comp], terms[parity * 2 + comp], ((1,), (1,))) * scale, 0.0,
            ).astype(jnp.bfloat16)
            for comp in range(2)
        ], axis=1)
        slots = dot(back_order, sums).astype(jnp.bfloat16)
        pieces += [slots[half * width:(half + 1) * width] for half in range(sz.halves)]
    sent = dot(jnp.concatenate(pieces, axis=1), take, ((1,), (1,)))
    for g in range(sz.groups):
        part = sent[:, g * SLAB:(g + 1) * SLAB].reshape(sz.bands, sz.chunk, SLAB)
        send_ref[:, g] = part.astype(jnp.bfloat16)


def zeros_kernel(sizes, wave, out_hbm, zeros, sems):
    sz = sizes
    band = lax.axis_index("band")
    zeros[...] = jnp.zeros_like(zeros)

    def one(place, carry):
        def emit(start):
            for side, count in ((0, start), (1, sz.tiles - 1 - start)):
                if count:
                    pltpu.make_async_copy(
                        zeros.at[:, pl.ds(0, count)],
                        out_hbm.at[2 * place + side, :, pl.ds(0, count)],
                        sems.at[place],
                    ).start()

        Pair(sz, wave, band, place).by_start(emit)
        return carry

    def done(place, carry):
        pltpu.make_async_copy(zeros, zeros, sems.at[place]).wait()
        return carry

    lax.fori_loop(0, sz.slots // 2, one, 0)
    lax.fori_loop(0, sz.slots // 2, done, 0)


def forward_kernel(sizes, wave, speed, back_ref, *refs):
    sz = sizes
    geo_refs = refs[:-12]
    x_hbm, leg_hbm, _, out_hbm, spots, inverse, out_all, out_sems, x_all, leg_all, *sems = refs[-12:]
    band = lax.axis_index("band")
    pair_at = functools.partial(Pair, sz, wave, band)
    stream = Stream(sz, pair_at, x_hbm, leg_hbm, x_all, leg_all, *sems)
    stream.begin()
    pad = 2 * sz.field_pad
    each = sz.block // 2

    gather = spread_matrix(sz, lax.axis_index("lev"))
    for rp in range(sz.rows // 2):
        cut = jnp.concatenate([back_ref[rp, g] for g in range(sz.groups)], axis=1)
        whole = dot(cut, gather, ((1,), (1,)))
        rows = jnp.concatenate([
            whole[:, q * 2 * pad:(q + 1) * 2 * pad] for q in range(sz.quarters)
        ], axis=0)
        for geo_ref in geo_refs:
            rows = rows + geo_ref[rp].astype(jnp.float32)[:, 0:2 * pad]
        for r in range(2):
            part = rows[:, r * pad:(r + 1) * pad]
            part = jnp.concatenate([part, jnp.zeros((sz.spots, SLAB - pad), jnp.float32)], axis=1)
            spots[pl.ds(2 * rp + r, sz.spots, stride=sz.rows), :] = part
    row = iota((pad, SLAB), 0)
    speeds = jnp.ones((pad, SLAB), jnp.float32)
    for f in range(sz.fields):
        speeds = jnp.where(row >> 1 == f, speed[f], speeds)
    for t in range(sz.tiles):
        degree = iota((1, SLAB), 1) + t * SLAB
        helm = (degree * (degree + 1)).astype(jnp.float32) / float(sz.trunc * (sz.trunc + 1))
        inverse[t] = 1.0 / (1.0 + time_step * time_step * helm * speeds)

    def leave(place, k):
        at = lax.rem(place // each, BEHIND)

        def emit(start):
            split = sz.tiles - start
            for side, first, here in ((0, start, (0, split)), (1, split - 1, (split, sz.packed))):
                pltpu.make_async_copy(
                    out_all.at[at, k, :, pl.ds(here[0], here[1] - here[0])],
                    out_hbm.at[2 * place + side, :, pl.ds(first, sz.tiles - first)],
                    out_sems.at[at, k],
                ).start()

        pair_at(place).by_start(emit)

    def left(step):
        at = lax.rem(step, BEHIND)
        for k in range(each):
            pltpu.make_async_copy(out_all.at[at, k], out_all.at[at, k], out_sems.at[at, k]).wait()

    def block(step, carry):
        stream.take(step)
        work = []
        for k in range(each):
            place = step * each + k
            pair = pair_at(place)
            values = jnp.concatenate([spots[pair.rows(side), :] for side in range(2)], axis=0)
            values = values.T.astype(jnp.bfloat16)[0:pad]
            work.append((place, pair, values, pair.tables(leg_all[place])))

        @pl.when(step >= BEHIND)
        def _():
            left(step)

        at = lax.rem(step, BEHIND)
        for k in range(each):
            place, pair, values, tables = work[k]
            _, live = pair.columns()
            for first in range(0, sz.packed, 2):
                count = min(2, sz.packed - first)
                tends = dot(values, tables[:, first * SLAB:(first + count) * SLAB])
                for t in range(first, first + count):
                    old = x_all[place, :, t].reshape(2 * sz.fields, SLAB).astype(jnp.float32)
                    tend = tends[0:2 * sz.fields, (t - first) * SLAB:(t - first + 1) * SLAB]
                    new = (old + time_step * tend) * inverse[pair.tile(t), 0:2 * sz.fields]
                    new = jnp.where(live[:, t * SLAB:(t + 1) * SLAB], new, 0.0)
                    out_all[at, k, :, t] = new.reshape(sz.fields, 2, SLAB)
        for k in range(each):
            leave(step * each + k, k)
        return carry

    lax.fori_loop(0, sz.steps, block, 0)
    for step in range(max(0, sz.steps - BEHIND), sz.steps):
        left(jnp.int32(step))


def params(mib):
    return pltpu.CompilerParams(vmem_limit_bytes=mib * MIB)


def smem():
    return pl.BlockSpec(memory_space=pltpu.SMEM)


def shards(spectra, legendre, slot_wave, row_points, gauss_weight, layer_depth, mode_speed):
    slots, _, fields, degrees = spectra.shape
    rows = legendre.shape[2]
    sz = Sizes(lax.axis_size("band"), lax.axis_size("lev"), slots, fields, degrees, rows)

    tiled = spectra.reshape(slots, 2, fields, sz.tiles, SLAB)
    tiled = with_layout_constraint(tiled, Layout((0, 2, 3, 1, 4)))
    tiled = tiled.transpose(0, 2, 3, 1, 4)
    tables = legendre.transpose(0, 2, 1)

    rounds = geo_rounds(sz)
    spots_shape = pltpu.VMEM((sz.spots * sz.rows, SLAB), jnp.float32)
    pairs = slots // 2
    stream_scratch = [
        pltpu.VMEM((pairs, fields, sz.packed, 2, SLAB), jnp.bfloat16),
        pltpu.VMEM((pairs, rows, sz.packed * SLAB), jnp.bfloat16),
        pltpu.SemaphoreType.DMA((pairs,)),
        pltpu.SemaphoreType.DMA((pairs,)),
    ]
    anywhere = pl.BlockSpec(memory_space=pl.ANY)
    vmem = pl.BlockSpec(memory_space=pltpu.VMEM)
    send_shape = (sz.bands, sz.groups, sz.chunk, SLAB)
    geo_shape = (sz.rows // 2, sz.spots, SLAB)

    sent, *geo = pl.pallas_call(
        functools.partial(inverse_kernel, sz, rounds),
        in_specs=[smem(), smem(), smem(), smem(), anywhere, anywhere],
        out_specs=[vmem] * (1 + len(rounds)),
        out_shape=[jax.ShapeDtypeStruct(send_shape, jnp.bfloat16)]
        + [jax.ShapeDtypeStruct(geo_shape, jnp.bfloat16)] * len(rounds),
        scratch_shapes=[spots_shape, pltpu.VMEM((sz.spots, SLAB), jnp.int32), *stream_scratch],
        compiler_params=params(56),
        name="inverse_legendre",
    )(slot_wave, row_points, gauss_weight, layer_depth, tiled, tables)

    sent, points_later, wave_later = lax.optimization_barrier((sent, row_points, slot_wave))
    both = ("band", "lev")
    total = sz.bands * sz.groups
    flat = (total * sz.chunk, SLAB)
    arrived = lax.all_to_all(sent.reshape(flat), both, split_axis=0, concat_axis=0, tiled=True)

    pair_wave = wave_later.reshape(-1, 2)
    even_wave = jnp.where(pair_wave[:, 0] % 2 == 0, pair_wave[:, 0], pair_wave[:, 1])
    even_wave = even_wave.reshape(sz.bands, sz.halves, sz.chunk_live)
    even_wave = jnp.pad(even_wave, ((0, 0), (0, 0), (0, sz.chunk - sz.chunk_live)), constant_values=-1)
    even_wave = even_wave.transpose(1, 0, 2).reshape(sz.pairs)

    high = SLAB if sz.sorted % SLAB == 0 else sz.sorted
    table_rows = 16 + up_to(sz.sorted // 16, 8) + 8
    basis = pl.pallas_call(
        functools.partial(basis_kernel, sz),
        grid=(sz.sorted // high,),
        in_specs=[smem()],
        out_specs=pl.BlockSpec((4, high, sz.orbits), lambda i: (0, i, 0)),
        out_shape=jax.ShapeDtypeStruct((4, sz.sorted, sz.orbits), jnp.bfloat16),
        scratch_shapes=[pltpu.VMEM((table_rows, sz.orbits), jnp.float32)] * 2,
        compiler_params=params(56),
        cost_estimate=pl.CostEstimate(
            flops=20 * sz.sorted * sz.orbits, bytes_accessed=8 * sz.sorted * sz.orbits, transcendentals=0,
        ),
        name="basis",
    )(points_later)

    even_row, even_col = even_wave.reshape(1, sz.pairs), even_wave.reshape(sz.pairs, 1)
    *geo, arrived, basis, even_row, even_col = lax.optimization_barrier(
        (*geo, arrived, basis, even_row, even_col)
    )
    moved = [lax.ppermute(geo[turn], "lev", pairs) for turn, pairs in enumerate(rounds)]
    returned = pl.pallas_call(
        functools.partial(grid_kernel, sz),
        in_specs=[smem(), smem(), vmem, vmem, vmem, anywhere],
        out_specs=vmem,
        out_shape=jax.ShapeDtypeStruct(send_shape, jnp.bfloat16),
        scratch_shapes=[
            pltpu.VMEM((4, sz.sorted, sz.orbits), jnp.bfloat16),
            pltpu.VMEM((4, SLAB, sz.orbits), jnp.bfloat16),
            pltpu.SemaphoreType.DMA((-(-sz.orbits // (2 * SLAB)),)),
        ],
        compiler_params=params(56),
        cost_estimate=pl.CostEstimate(
            flops=4 * 4 * SLAB * sz.sorted * sz.orbits, bytes_accessed=8 * sz.sorted * sz.orbits, transcendentals=0,
        ),
        name="grid_products",
    )(
        row_points, gauss_weight, arrived.reshape(send_shape), even_row, even_col, basis,
    )
    *moved, returned, wave_last = lax.optimization_barrier((*moved, returned, slot_wave))

    back = lax.all_to_all(returned.reshape(flat), both, split_axis=0, concat_axis=0, tiled=True)

    out_shape = jax.ShapeDtypeStruct(tiled.shape, jnp.float32)
    zeroed = pl.pallas_call(
        functools.partial(zeros_kernel, sz),
        in_specs=[smem()],
        out_specs=anywhere,
        out_shape=out_shape,
        scratch_shapes=[
            pltpu.VMEM((fields, sz.tiles - 1, 2, SLAB), jnp.float32),
            pltpu.SemaphoreType.DMA((pairs,)),
        ],
        compiler_params=params(56),
        cost_estimate=pl.CostEstimate(
            flops=0, bytes_accessed=2 * slots * fields * degrees * 2, transcendentals=0,
        ),
        name="dead_zeros",
    )(wave_last)
    out = pl.pallas_call(
        functools.partial(forward_kernel, sz),
        in_specs=[smem(), smem()] + [vmem] * (1 + len(rounds)) + [anywhere] * 3,
        out_specs=anywhere,
        out_shape=out_shape,
        input_output_aliases={5 + len(rounds): 0},
        scratch_shapes=[
            spots_shape,
            pltpu.VMEM((sz.tiles, 2 * sz.field_pad, SLAB), jnp.float32),
            pltpu.VMEM((BEHIND, sz.block // 2, fields, sz.packed, 2, SLAB), jnp.float32),
            pltpu.SemaphoreType.DMA((BEHIND, sz.block // 2)),
            *stream_scratch,
        ],
        compiler_params=params(56),
        name="forward_legendre",
    )(slot_wave, mode_speed, back.reshape(send_shape), *moved, tiled, tables, zeroed)

    out = out.transpose(0, 1, 3, 2, 4)
    return out.reshape(slots, fields, 2, degrees).transpose(0, 2, 1, 3)


def solution(mesh):
    return jax.shard_map(
        shards,
        mesh=mesh,
        in_specs=(
            P("band", None, "lev", None),
            P("band", None, None),
            P(),
            P(),
            P(),
            P(),
            P("lev"),
        ),
        out_specs=P("band", None, "lev", None),
        check_vma=False,
    )
```

```python
import functools
import math

import jax
import jax.numpy as jnp
from jax import lax
from jax.experimental import pallas as pl
from jax.experimental.layout import Layout, with_layout_constraint
from jax.experimental.pallas import tpu as pltpu
from jax.sharding import PartitionSpec as P

FIELDS = 5
LEVELS = 24
TEMPER = 2
ENERGY = 4
LVL_ROWS = 8
SLAB = 128
MIB = 1024 * 1024

time_step = 1.0

COS_POLY = (
    0.9999999890590235, -19.739204499453994, 64.93911745989843, -85.45013953092186,
    60.167630951185615, -25.967599249120923, 6.528658161956132,
)
SIN_POLY = (
    6.283185302511506, -41.3417004053176, 81.60513138579954, -76.70301535389986,
    42.02592698629647, -14.89984666973851, 3.2381375126489513,
)


def up_to(value, unit):
    return -(-value // unit) * unit


class Sizes:
    def __init__(self, bands, groups, slots, fields, degrees, rows):
        self.bands, self.groups = bands, groups
        self.slots, self.fields, self.degrees, self.rows = slots, fields, degrees, rows
        self.tiles = degrees // SLAB
        self.packed = self.tiles + 1
        self.pitch = up_to(2 * self.packed, 8)
        self.pitch_bf16 = up_to(2 * self.packed, 16)
        self.slot_rows = fields * self.tiles * 2
        self.field_pad = up_to(fields, 8)
        self.share = -(-fields // groups)
        self.lanes = 4 * self.share
        self.quarters = 2
        if 4 * self.lanes <= SLAB and slots % 4 == 0:
            self.quarters = 4
        self.halves = self.quarters // 2
        self.chunk_live = slots // self.quarters
        self.chunk = up_to(self.chunk_live, 8)
        self.spots = self.quarters * self.chunk
        self.block = slots
        for size in (8, 4):
            if slots % size == 0 and (size * self.slot_rows) % 16 == 0:
                self.block = size
                break
        self.steps = slots // self.block
        self.pairs = self.halves * bands * self.chunk
        self.trunc = degrees - 1
        self.sorted = degrees // 2
        self.orbits = up_to((4 * self.trunc + 40) // 4 + 2, SLAB)
        self.levels = LEVELS // groups


def owners(sizes, field):
    first, last = field * LEVELS, (field + 1) * LEVELS
    return [
        g for g in range(sizes.groups)
        if g * sizes.fields < last and (g + 1) * sizes.fields > first
    ]


def geo_rounds(sizes):
    sources, targets = owners(sizes, TEMPER), owners(sizes, ENERGY)
    wide = max(len(sources), len(targets))
    rounds = []
    for turn in range(wide):
        pairs = []
        for k in range(wide):
            s, t = k, (k + turn) % wide
            if s < len(sources) and t < len(targets):
                pairs.append((sources[s], targets[t]))
        if pairs:
            rounds.append(pairs)
    return rounds


def iota(shape, dim):
    return lax.broadcasted_iota(jnp.int32, shape, dim)


def one_hot(cond):
    return jnp.where(cond, 1.0, 0.0).astype(jnp.bfloat16)


def dot(a, b, dims=((1,), (0,))):
    return lax.dot_general(a, b, (dims, ((), ())), preferred_element_type=jnp.float32)


def halving(value):
    return value.bit_length() - 1 if value & (value - 1) == 0 else None


def quotient(x, by):
    bits = halving(by)
    return x >> bits if bits is not None else lax.div(x, jnp.int32(by))


def remainder(x, by):
    return x & (by - 1) if halving(by) is not None else lax.rem(x, jnp.int32(by))


def spread_matrix(sizes, lev):
    sz = sizes
    tall = sz.quarters * 4 * sz.field_pad
    wide = sz.groups * SLAB
    dst = iota((1, wide), 1)
    group = quotient(dst, SLAB)
    lane = remainder(dst, SLAB)
    quarter = quotient(lane, sz.lanes)
    rest = remainder(lane, sz.lanes)
    row = quotient(rest, 2 * sz.share)
    rest = remainder(rest, 2 * sz.share)
    comp = quotient(rest, sz.share)
    item = remainder(rest, sz.share)
    start = remainder(lev * sz.fields, sz.groups)
    field = remainder(group - start + sz.groups, sz.groups) + sz.groups * item
    want = ((quarter * 2 + row) * 2 + comp) * sz.field_pad + field
    want = jnp.where((field < sz.fields) & (quarter < sz.quarters), want, -1)
    return one_hot(iota((tall, wide), 0) == want)


def spot_of(sizes, place, odd):
    half = place // sizes.chunk_live
    return (odd * sizes.halves + half) * sizes.chunk + (place - half * sizes.chunk_live)


class Pair:
    def __init__(self, sizes, wave, band, place):
        self.sizes, self.place = sizes, place
        slot = band * sizes.slots + 2 * place
        self.numbers = wave[slot], wave[slot + 1]
        odd = self.numbers[0] & 1
        self.odds = odd, 1 - odd
        self.start = quotient(jnp.maximum(self.numbers[0], 0), SLAB)
        self.split = sizes.tiles - self.start

    def spot(self, side):
        sz = self.sizes
        half = self.place // sz.chunk_live
        first = (self.odds[side] * sz.halves + half) * sz.chunk
        return first + (self.place - half * sz.chunk_live)

    def rows(self, side):
        return pl.ds(pl.multiple_of(self.spot(side) * self.sizes.rows, self.sizes.rows), self.sizes.rows)

    def tile(self, k):
        return jnp.where(k < self.split, self.start + k, k - 1)

    def columns(self):
        place = iota((1, self.sizes.packed * SLAB), 1)
        first = place < self.split * SLAB
        degree = jnp.where(first, place + self.start * SLAB, place - SLAB)
        floors = [jnp.where(n < 0, self.sizes.degrees, n) for n in self.numbers]
        return first, degree >= jnp.where(first, floors[0], floors[1])

    def by_start(self, emit):
        def branch(low, high):
            if high - low == 1:
                emit(low)
                return
            middle = (low + high) // 2
            pl.when(self.start < middle)(lambda: branch(low, middle))
            pl.when(self.start >= middle)(lambda: branch(middle, high))

        branch(0, self.sizes.tiles)

    def tables(self, leg):
        first, live = self.columns()
        leg = leg.astype(jnp.float32)
        own = jnp.where(first & live, leg, 0.0)
        other = jnp.where(first, 0.0, jnp.where(live, leg, 0.0))
        return jnp.concatenate([own, other], axis=0).astype(jnp.bfloat16)


AHEAD = 6
BEHIND = 4


def await_tiles(hbm, sem):
    for some in (hbm.at[0], hbm.at[0, :, pl.ds(0, 1)]):
        pltpu.make_async_copy(some, some, sem).wait()


class Stream:
    def __init__(self, sizes, pair_at, x_hbm, leg_hbm, x_all, leg_all, x_sems, leg_sems):
        self.sizes, self.pair_at = sizes, pair_at
        self.x_hbm, self.leg_hbm, self.x_all, self.leg_all = x_hbm, leg_hbm, x_all, leg_all
        self.x_sems, self.leg_sems = x_sems, leg_sems

    def start(self, place):
        pair = self.pair_at(place)
        sz = self.sizes
        tiles = sz.tiles
        x_rows = self.x_hbm.reshape(sz.slots, sz.fields, 2 * tiles, SLAB)

        def emit(start):
            split = tiles - start
            for side, first, here in ((0, start, (0, split)), (1, split - 1, (split, tiles + 1))):
                slot = 2 * place + side
                pltpu.make_async_copy(
                    x_rows.at[slot, :, pl.ds(2 * first, 2 * (tiles - first))],
                    self.x_all.at[place, :, pl.ds(2 * here[0], 2 * (here[1] - here[0]))],
                    self.x_sems.at[place],
                ).start()
                pltpu.make_async_copy(
                    self.leg_hbm.at[slot, :, pl.ds(first * SLAB, (tiles - first) * SLAB)],
                    self.leg_all.at[place, :, pl.ds(here[0] * SLAB, (here[1] - here[0]) * SLAB)],
                    self.leg_sems.at[place],
                ).start()

        pair.by_start(emit)

    def begin(self):
        def one(place, carry):
            self.start(place)
            return carry

        lax.fori_loop(0, min(AHEAD * self.sizes.block // 2, self.sizes.slots // 2), one, 0)

    def take(self, step):
        each = self.sizes.block // 2

        @pl.when(step + AHEAD < self.sizes.steps)
        def _():
            for k in range(each):
                self.start((step + AHEAD) * each + k)

        for k in range(each):
            place = step * each + k
            await_tiles(self.x_hbm, self.x_sems.at[place])
            here = self.leg_all.at[place]
            pltpu.make_async_copy(here, here, self.leg_sems.at[place]).wait()


def inverse_kernel(sizes, rounds, wave, points, gauss, layer_depth, x_hbm, leg_hbm, send_ref, *refs):
    sz = sizes
    geo_refs = refs[:len(rounds)]
    wide, spots, numbers, x_all, leg_all, *sems = refs[len(rounds):]
    band = lax.axis_index("band")
    lev = lax.axis_index("lev")
    pair_at = functools.partial(Pair, sz, wave, band)
    stream = Stream(sz, pair_at, x_hbm, leg_hbm, x_all, leg_all, *sems)
    stream.begin()
    pad = 2 * sz.field_pad
    spots[...] = jnp.zeros_like(spots)
    numbers[...] = jnp.full_like(numbers, -1)
    wide[...] = jnp.zeros_like(wide)

    def block(step, carry):
        stream.take(step)
        found = []
        for k in range(sz.block // 2):
            place = step * (sz.block // 2) + k
            for f in range(sz.fields):
                rows = x_all[place, f].astype(jnp.float32)
                wide[k, pl.ds(f * sz.pitch, sz.pitch), :] = rows[0:sz.pitch]
        for k in range(sz.block // 2):
            place = step * (sz.block // 2) + k
            pair = pair_at(place)
            values = jnp.concatenate([
                jnp.concatenate([
                    wide[k, pl.ds(2 * t + c, sz.field_pad, stride=sz.pitch), :] for c in range(2)
                ], axis=0).astype(jnp.bfloat16)
                for t in range(sz.packed)
            ], axis=1)
            total = dot(pair.tables(leg_all[place]), values, ((1,), (1,)))
            for side in range(2):
                found.append((pair, side, total[side * sz.rows:(side + 1) * sz.rows]))
        for pair, side, total in found:
            spots[pair.rows(side), 0:pad] = total
            number = jnp.full((1, SLAB), pair.numbers[side], jnp.int32)
            numbers[pl.ds(pair.spot(side), 1), :] = number
        return carry

    lax.fori_loop(0, sz.steps, block, 0)
    spread = spread_matrix(sz, lev)
    shape = (2 * pad, SLAB)
    src, dst = iota(shape, 0), iota(shape, 1)
    bits = sz.field_pad.bit_length() - 1
    from_field, from_side = src & (sz.field_pad - 1), src >> bits
    to_field, to_side = dst & (sz.field_pad - 1), dst >> bits
    weights = []
    for pairs in rounds:
        first = jnp.int32(2 * LEVELS + sz.fields)
        for source, target in pairs:
            first = jnp.where(lev == source, target * sz.fields - ENERGY * LEVELS, first)
        under = lev * sz.fields + from_field - TEMPER * LEVELS
        above = first + to_field
        hit = (
            (from_side == to_side)
            & (from_field < sz.fields) & (to_field < sz.fields)
            & (above >= 0) & (above <= under)
        )
        weight = jnp.zeros(shape, jnp.float32)
        for level in range(LEVELS):
            weight = jnp.where(hit & (under == level), layer_depth[level], weight)
        high = weight.astype(jnp.bfloat16)
        low = (weight - high.astype(jnp.float32)).astype(jnp.bfloat16)
        weights.append(jnp.concatenate([high, low], axis=0))
    number = numbers[...]
    lane = iota((sz.spots, SLAB), 1)
    known = (number >= 0) & ~((number == 0) & (lane & sz.field_pad != 0))
    for rp in range(sz.rows // 2):
        exact = jnp.concatenate([
            spots[pl.ds(2 * rp + r, sz.spots, stride=sz.rows), :][:, 0:pad] for r in range(2)
        ], axis=1)
        cut = jnp.concatenate([
            exact[q * sz.chunk:(q + 1) * sz.chunk] for q in range(sz.quarters)
        ], axis=1).astype(jnp.bfloat16)
        chunk = dot(cut, spread).astype(jnp.bfloat16)
        for g in range(sz.groups):
            send_ref[rp, g] = chunk[:, g * SLAB:(g + 1) * SLAB]
        count = jnp.where(lane < pad, points[2 * rp], points[2 * rp + 1])
        scale = jnp.where(lane < pad, gauss[2 * rp], gauss[2 * rp + 1])
        scale = jnp.where(known & (2 * number <= count - 1), scale, 0.0)
        exact = exact.astype(jnp.bfloat16)
        double = jnp.concatenate([exact, exact], axis=1)
        for turn in range(len(rounds)):
            geo_refs[turn][rp] = (dot(double, weights[turn]) * scale).astype(jnp.bfloat16)


def cos_sin(z):
    y = z * z
    c = jnp.full_like(y, COS_POLY[-1])
    for a in COS_POLY[-2::-1]:
        c = c * y + a
    s = jnp.full_like(y, SIN_POLY[-1])
    for a in SIN_POLY[-2::-1]:
        s = s * y + a
    return c, s * z


def basis_kernel(sizes, points, out_ref, cosines, sines):
    sz = sizes
    step = pl.program_id(0)
    turns = sz.sorted // 16
    bands_row = 16 + up_to(turns, 8)

    @pl.when(step == 0)
    def _():
        first = lax.axis_index("band") * 2
        length_a, length_b = points[first], points[first + 1]
        count_a = length_a // 4 + 1
        high = cosines.shape[0]
        row = iota((high, SLAB), 0)
        number = jnp.where(row < 16, 2 * row, jnp.where(row < bands_row, 32 * (row - 16), sz.trunc))
        number = number.astype(jnp.float32)
        for at in range(0, sz.orbits, SLAB):
            place = iota((1, SLAB), 1) + at
            second = place >= count_a
            column = (place - jnp.where(second, count_a, 0)).astype(jnp.float32)
            length = jnp.where(second, length_b, length_a).astype(jnp.float32)
            inverse = 1.0 / length
            scale = jnp.where(row < 16, 1.0 / jnp.sqrt(length), 1.0)
            product = number * column
            whole = jnp.floor(product * inverse + 0.5)
            c, s = cos_sin((product - whole * length) * inverse)
            cosines[:, pl.ds(at, SLAB)] = c * scale
            sines[:, pl.ds(at, SLAB)] = s * scale

    groups = out_ref.shape[1] // 16
    for at in range(0, sz.orbits, SLAB):
        cols = pl.ds(at, SLAB)
        base_c, base_n = cosines[0:16, cols], -sines[0:16, cols]
        top_c, top_n = cosines[pl.ds(bands_row, 1), cols], -sines[pl.ds(bands_row, 1), cols]
        turn_rows = pl.ds(pl.multiple_of(16 + step * groups, 8), groups)
        all_c, all_s = cosines[turn_rows, cols], sines[turn_rows, cols]
        for k in range(groups):
            turn_c, turn_s = all_c[k:k + 1], all_s[k:k + 1]
            c = turn_c * base_c + turn_s * base_n
            n = turn_c * base_n - turn_s * base_c
            rows = pl.ds(16 * k, 16)
            out_ref[0, rows, cols] = c.astype(jnp.bfloat16)
            out_ref[1, rows, cols] = n.astype(jnp.bfloat16)
            out_ref[2, rows, cols] = (top_c * c + top_n * n).astype(jnp.bfloat16)
            out_ref[3, rows, cols] = (top_n * c - top_c * n).astype(jnp.bfloat16)


def take_matrix(sizes, lev):
    sz = sizes
    tall = sz.groups * SLAB
    wide = sz.quarters * 2 * SLAB
    dst = iota((1, wide), 1)
    piece = quotient(dst, SLAB)
    lane = remainder(dst, SLAB)
    row = quotient(lane, SLAB // 2)
    field = quotient(remainder(lane, SLAB // 2), LVL_ROWS)
    level = remainder(lane, LVL_ROWS)
    whole = field * LEVELS + level * sz.groups + lev
    owner = quotient(whole, sz.fields)
    start = owner * sz.fields
    first = remainder(lev - remainder(start, sz.groups) + sz.groups, sz.groups)
    item = quotient(whole - start - first, sz.groups)
    want = owner * SLAB + (piece >> 1) * sz.lanes + (row * 2 + (piece & 1)) * sz.share + item
    want = jnp.where((field < FIELDS) & (level < sz.levels), want, -1)
    return one_hot(iota((tall, wide), 0) == want)


def grid_kernel(
    sizes, points, gauss, recv_ref, even_row, even_col, basis_hbm, send_ref, basis, terms, arrivals,
):
    sz = sizes
    step = 2 * SLAB
    parts = -(-sz.orbits // step)
    copies = []
    for part in range(parts):
        cols = pl.ds(part * step, min(step, sz.orbits - part * step))
        copies.append(pltpu.make_async_copy(basis_hbm.at[:, :, cols], basis.at[:, :, cols], arrivals.at[part]))
        copies[-1].start()
    lev = lax.axis_index("lev")
    first_row = lax.axis_index("band") * 2
    length_a, length_b = points[first_row], points[first_row + 1]
    count_a, count_b = length_a // 4 + 1, length_b // 4 + 1
    high = FIELDS * LVL_ROWS
    half_slab = SLAB // 2
    width = sz.bands * sz.chunk
    take = take_matrix(sz, lev)
    order = one_hot(iota((sz.sorted, sz.pairs), 0) * 2 == even_row[...])
    joined = jnp.concatenate([
        recv_ref[:, g].astype(jnp.float32).reshape(width, SLAB) for g in range(sz.groups)
    ], axis=1).astype(jnp.bfloat16)
    taken = dot(joined, take)
    coeffs = []
    number = iota((2 * SLAB, sz.sorted), 1) * 2
    bound = jnp.where(iota((2 * SLAB, sz.sorted), 0) & half_slab == 0, length_a, length_b) - 1
    kept = (0, half_slab, SLAB, SLAB + half_slab)
    for parity in range(2):
        rows = []
        for half in range(sz.halves):
            piece = (parity * sz.halves + half) * 2
            rows.append(taken[:, piece * SLAB:(piece + 2) * SLAB])
        values = jnp.concatenate(rows, axis=0).T.astype(jnp.bfloat16)
        placed = dot(values, order, ((1,), (1,)))
        mine = number if parity == 0 else sz.trunc - number
        mult = jnp.where(mine == 0, 1.0, 2.0)
        placed = jnp.where(2 * mine <= bound, placed * mult, 0.0)
        placed = jnp.concatenate([placed[k:k + high] for k in kept], axis=0).astype(jnp.bfloat16)
        coeffs += [placed[:2 * high], placed[2 * high:]]
    for part in range(parts):
        copies[part].wait()
        at = part * step
        many = min(step, sz.orbits - at)
        cols = pl.ds(at, many)
        place = iota((1, many), 1) + at
        second = place >= count_a
        grids = []
        for k in range(4):
            both = dot(coeffs[k], basis[k, :, cols])
            grids.append(jnp.where(second, both[high:], both[:high]))
        ce, se, co, so = grids
        plus, minus = ce + co, ce - co
        splus, sminus = se + so, se - so
        values = (plus + splus, minus - sminus, minus + sminus, plus - splus)
        outs = []
        for v in values:
            u, w, tem, hum, ozo = (v[i * LVL_ROWS:(i + 1) * LVL_ROWS] for i in range(FIELDS))
            outs.append(jnp.concatenate(
                [u * tem, w * tem, u * hum, w * ozo, 0.5 * (u * u + w * w)], axis=0
            ))
        offset = place - jnp.where(second, count_a, 0)
        count = jnp.where(second, count_b, count_a)
        weight = jnp.where((offset == 0) | (offset == count - 1), 0.5, 1.0)
        weight = jnp.where(offset < count, weight, 0.0)
        t0, t1, t2, t3 = (o * weight for o in outs)
        a, b, c, d = t0 + t3, t1 + t2, t0 - t3, t2 - t1
        folds = (a + b, c + d, a - b, c - d)
        empty = jnp.zeros((half_slab - high, many), jnp.float32)
        for k in range(4):
            first = jnp.where(second, 0.0, folds[k])
            last = jnp.where(second, folds[k], 0.0)
            terms[k, :, cols] = jnp.concatenate([first, empty, last, empty], axis=0).astype(jnp.bfloat16)
    lane = iota((1, SLAB), 1)
    scale = jnp.where(lane < half_slab, gauss[first_row], gauss[first_row + 1])
    bound = jnp.where(lane < half_slab, length_a, length_b) - 1
    number = iota((sz.sorted, SLAB), 0) * 2
    back_order = one_hot(iota((sz.pairs, sz.sorted), 1) * 2 == even_col[...])
    pieces = []
    for parity in range(2):
        mine = number if parity == 0 else sz.trunc - number
        sums = jnp.concatenate([
            jnp.where(
                2 * mine <= bound,
                dot(basis[parity * 2 + comp], terms[parity * 2 + comp], ((1,), (1,))) * scale, 0.0,
            ).astype(jnp.bfloat16)
            for comp in range(2)
        ], axis=1)
        slots = dot(back_order, sums).astype(jnp.bfloat16)
        pieces += [slots[half * width:(half + 1) * width] for half in range(sz.halves)]
    sent = dot(jnp.concatenate(pieces, axis=1), take, ((1,), (1,)))
    for g in range(sz.groups):
        part = sent[:, g * SLAB:(g + 1) * SLAB].reshape(sz.bands, sz.chunk, SLAB)
        send_ref[:, g] = part.astype(jnp.bfloat16)


def zeros_kernel(sizes, wave, out_hbm, zeros, sems):
    sz = sizes
    band = lax.axis_index("band")
    zeros[...] = jnp.zeros_like(zeros)

    def one(place, carry):
        def emit(start):
            for side, count in ((0, start), (1, sz.tiles - 1 - start)):
                if count:
                    pltpu.make_async_copy(
                        zeros.at[:, pl.ds(0, count)],
                        out_hbm.at[2 * place + side, :, pl.ds(0, count)],
                        sems.at[place],
                    ).start()

        Pair(sz, wave, band, place).by_start(emit)
        return carry

    def done(place, carry):
        pltpu.make_async_copy(zeros, zeros, sems.at[place]).wait()
        return carry

    lax.fori_loop(0, sz.slots // 2, one, 0)
    lax.fori_loop(0, sz.slots // 2, done, 0)


def forward_kernel(sizes, wave, speed, back_ref, *refs):
    sz = sizes
    geo_refs = refs[:-13]
    x_hbm, leg_hbm, _, out_hbm, wide, spots, inverse, out_all, out_sems, x_all, leg_all, *sems = refs[-13:]
    band = lax.axis_index("band")
    pair_at = functools.partial(Pair, sz, wave, band)
    stream = Stream(sz, pair_at, x_hbm, leg_hbm, x_all, leg_all, *sems)
    stream.begin()
    pad = 2 * sz.field_pad
    each = sz.block // 2

    gather = spread_matrix(sz, lax.axis_index("lev"))
    for rp in range(sz.rows // 2):
        cut = jnp.concatenate([back_ref[rp, g] for g in range(sz.groups)], axis=1)
        whole = dot(cut, gather, ((1,), (1,)))
        rows = jnp.concatenate([
            whole[:, q * 2 * pad:(q + 1) * 2 * pad] for q in range(sz.quarters)
        ], axis=0)
        for geo_ref in geo_refs:
            rows = rows + geo_ref[rp].astype(jnp.float32)[:, 0:2 * pad]
        for r in range(2):
            part = rows[:, r * pad:(r + 1) * pad]
            part = jnp.concatenate([part, jnp.zeros((sz.spots, SLAB - pad), jnp.float32)], axis=1)
            spots[pl.ds(2 * rp + r, sz.spots, stride=sz.rows), :] = part
    row = quotient(iota((sz.pitch, SLAB), 0), 2)
    lane = iota((sz.pitch, SLAB), 1)
    for start in range(sz.tiles):
        degree = jnp.where(row < sz.tiles - start, row + start, row - 1) * SLAB + lane
        helm = (degree * (degree + 1)).astype(jnp.float32) / float(sz.trunc * (sz.trunc + 1))
        for f in range(sz.fields):
            denominator = 1.0 + time_step * time_step * helm * speed[f]
            inverse[start, pl.ds(f * sz.pitch, sz.pitch), :] = 1.0 / denominator
    out_tiles = out_all.reshape(BEHIND, each, sz.fields, sz.pitch // 2, 2, SLAB)

    def leave(place, k):
        at = lax.rem(place // each, BEHIND)

        def emit(start):
            split = sz.tiles - start
            for side, first, here in ((0, start, (0, split)), (1, split - 1, (split, sz.packed))):
                pltpu.make_async_copy(
                    out_tiles.at[at, k, :, pl.ds(here[0], here[1] - here[0])],
                    out_hbm.at[2 * place + side, :, pl.ds(first, sz.tiles - first)],
                    out_sems.at[at, k],
                ).start()

        pair_at(place).by_start(emit)

    def left(step):
        at = lax.rem(step, BEHIND)
        for k in range(each):
            await_tiles(out_hbm, out_sems.at[at, k])

    def block(step, carry):
        stream.take(step)
        work = []
        for k in range(each):
            place = step * each + k
            pair = pair_at(place)
            values = jnp.concatenate([spots[pair.rows(side), :] for side in range(2)], axis=0)
            values = values.T.astype(jnp.bfloat16)[0:pad]
            work.append((place, pair, values, pair.tables(leg_all[place])))

        for k in range(each):
            _, _, values, tables = work[k]
            for first in range(0, sz.packed, 2):
                count = min(2, sz.packed - first)
                tends = dot(values, tables[:, first * SLAB:(first + count) * SLAB])
                for t in range(first, first + count):
                    for c in range(2):
                        rows = pl.ds(2 * t + c, sz.field_pad, stride=sz.pitch)
                        wide[k, rows, :] = tends[
                            c * sz.field_pad:(c + 1) * sz.field_pad, (t - first) * SLAB:(t - first + 1) * SLAB
                        ]

        @pl.when(step >= BEHIND)
        def _():
            left(step)

        at = lax.rem(step, BEHIND)
        for k in range(each):
            place, pair, _, _ = work[k]
            mine = row < pair.split
            degree = jnp.where(mine, row + pair.start, row - 1) * SLAB + lane
            floors = [jnp.where(n < 0, sz.degrees, n) for n in pair.numbers]
            live = degree >= jnp.where(mine, floors[0], floors[1])
            for f in range(sz.fields):
                rows = pl.ds(f * sz.pitch, sz.pitch)
                old = x_all[place, f].astype(jnp.float32)[0:sz.pitch]
                new = (old + time_step * wide[k, rows, :]) * inverse[pair.start, rows, :]
                out_all[at, k, rows, :] = jnp.where(live, new, 0.0)
        for k in range(each):
            leave(step * each + k, k)
        return carry

    lax.fori_loop(0, sz.steps, block, 0)
    for step in range(max(0, sz.steps - BEHIND), sz.steps):
        left(jnp.int32(step))


def params(mib):
    return pltpu.CompilerParams(vmem_limit_bytes=mib * MIB)


def smem():
    return pl.BlockSpec(memory_space=pltpu.SMEM)


def shards(spectra, legendre, slot_wave, row_points, gauss_weight, layer_depth, mode_speed):
    slots, _, fields, degrees = spectra.shape
    rows = legendre.shape[2]
    sz = Sizes(lax.axis_size("band"), lax.axis_size("lev"), slots, fields, degrees, rows)

    tiled = spectra.reshape(slots, 2, fields, sz.tiles, SLAB)
    tiled = with_layout_constraint(tiled, Layout((0, 2, 3, 1, 4)))
    tiled = tiled.transpose(0, 2, 3, 1, 4)
    tables = legendre.transpose(0, 2, 1)

    rounds = geo_rounds(sz)
    spots_shape = pltpu.VMEM((sz.spots * sz.rows, SLAB), jnp.float32)
    pairs = slots // 2
    stream_scratch = [
        pltpu.VMEM((pairs, fields, sz.pitch_bf16, SLAB), jnp.bfloat16),
        pltpu.VMEM((pairs, rows, sz.packed * SLAB), jnp.bfloat16),
        pltpu.SemaphoreType.DMA((pairs,)),
        pltpu.SemaphoreType.DMA((pairs,)),
    ]
    wide_shape = pltpu.VMEM((sz.block // 2, sz.field_pad * sz.pitch, SLAB), jnp.float32)
    anywhere = pl.BlockSpec(memory_space=pl.ANY)
    vmem = pl.BlockSpec(memory_space=pltpu.VMEM)
    send_shape = (sz.bands, sz.groups, sz.chunk, SLAB)
    geo_shape = (sz.rows // 2, sz.spots, SLAB)

    sent, *geo = pl.pallas_call(
        functools.partial(inverse_kernel, sz, rounds),
        in_specs=[smem(), smem(), smem(), smem(), anywhere, anywhere],
        out_specs=[vmem] * (1 + len(rounds)),
        out_shape=[jax.ShapeDtypeStruct(send_shape, jnp.bfloat16)]
        + [jax.ShapeDtypeStruct(geo_shape, jnp.bfloat16)] * len(rounds),
        scratch_shapes=[wide_shape, spots_shape, pltpu.VMEM((sz.spots, SLAB), jnp.int32), *stream_scratch],
        compiler_params=params(56),
        name="inverse_legendre",
    )(slot_wave, row_points, gauss_weight, layer_depth, tiled, tables)

    sent, points_later, wave_later = lax.optimization_barrier((sent, row_points, slot_wave))
    both = ("band", "lev")
    total = sz.bands * sz.groups
    flat = (total * sz.chunk, SLAB)
    arrived = lax.all_to_all(sent.reshape(flat), both, split_axis=0, concat_axis=0, tiled=True)

    pair_wave = wave_later.reshape(-1, 2)
    even_wave = jnp.where(pair_wave[:, 0] % 2 == 0, pair_wave[:, 0], pair_wave[:, 1])
    even_wave = even_wave.reshape(sz.bands, sz.halves, sz.chunk_live)
    even_wave = jnp.pad(even_wave, ((0, 0), (0, 0), (0, sz.chunk - sz.chunk_live)), constant_values=-1)
    even_wave = even_wave.transpose(1, 0, 2).reshape(sz.pairs)

    high = SLAB if sz.sorted % SLAB == 0 else sz.sorted
    table_rows = 16 + up_to(sz.sorted // 16, 8) + 8
    basis = pl.pallas_call(
        functools.partial(basis_kernel, sz),
        grid=(sz.sorted // high,),
        in_specs=[smem()],
        out_specs=pl.BlockSpec((4, high, sz.orbits), lambda i: (0, i, 0)),
        out_shape=jax.ShapeDtypeStruct((4, sz.sorted, sz.orbits), jnp.bfloat16),
        scratch_shapes=[pltpu.VMEM((table_rows, sz.orbits), jnp.float32)] * 2,
        compiler_params=params(56),
        cost_estimate=pl.CostEstimate(
            flops=20 * sz.sorted * sz.orbits, bytes_accessed=8 * sz.sorted * sz.orbits, transcendentals=0,
        ),
        name="basis",
    )(points_later)

    even_row, even_col = even_wave.reshape(1, sz.pairs), even_wave.reshape(sz.pairs, 1)
    *geo, arrived, basis, even_row, even_col = lax.optimization_barrier(
        (*geo, arrived, basis, even_row, even_col)
    )
    moved = [lax.ppermute(geo[turn], "lev", pairs) for turn, pairs in enumerate(rounds)]
    returned = pl.pallas_call(
        functools.partial(grid_kernel, sz),
        in_specs=[smem(), smem(), vmem, vmem, vmem, anywhere],
        out_specs=vmem,
        out_shape=jax.ShapeDtypeStruct(send_shape, jnp.bfloat16),
        scratch_shapes=[
            pltpu.VMEM((4, sz.sorted, sz.orbits), jnp.bfloat16),
            pltpu.VMEM((4, SLAB, sz.orbits), jnp.bfloat16),
            pltpu.SemaphoreType.DMA((-(-sz.orbits // (2 * SLAB)),)),
        ],
        compiler_params=params(56),
        cost_estimate=pl.CostEstimate(
            flops=4 * 4 * SLAB * sz.sorted * sz.orbits, bytes_accessed=8 * sz.sorted * sz.orbits, transcendentals=0,
        ),
        name="grid_products",
    )(
        row_points, gauss_weight, arrived.reshape(send_shape), even_row, even_col, basis,
    )
    *moved, returned, wave_last = lax.optimization_barrier((*moved, returned, slot_wave))

    back = lax.all_to_all(returned.reshape(flat), both, split_axis=0, concat_axis=0, tiled=True)

    out_shape = jax.ShapeDtypeStruct(tiled.shape, jnp.float32)
    zeroed = pl.pallas_call(
        functools.partial(zeros_kernel, sz),
        in_specs=[smem()],
        out_specs=anywhere,
        out_shape=out_shape,
        scratch_shapes=[
            pltpu.VMEM((fields, sz.tiles - 1, 2, SLAB), jnp.float32),
            pltpu.SemaphoreType.DMA((pairs,)),
        ],
        compiler_params=params(56),
        cost_estimate=pl.CostEstimate(
            flops=0, bytes_accessed=2 * slots * fields * degrees * 2, transcendentals=0,
        ),
        name="dead_zeros",
    )(wave_last)
    out = pl.pallas_call(
        functools.partial(forward_kernel, sz),
        in_specs=[smem(), smem()] + [vmem] * (1 + len(rounds)) + [anywhere] * 3,
        out_specs=anywhere,
        out_shape=out_shape,
        input_output_aliases={5 + len(rounds): 0},
        scratch_shapes=[
            wide_shape, spots_shape,
            pltpu.VMEM((sz.tiles, fields * sz.pitch, SLAB), jnp.float32),
            pltpu.VMEM((BEHIND, sz.block // 2, fields * sz.pitch, SLAB), jnp.float32),
            pltpu.SemaphoreType.DMA((BEHIND, sz.block // 2)),
            *stream_scratch,
        ],
        compiler_params=params(56),
        name="forward_legendre",
    )(slot_wave, mode_speed, back.reshape(send_shape), *moved, tiled, tables, zeroed)

    out = out.transpose(0, 1, 3, 2, 4)
    return out.reshape(slots, fields, 2, degrees).transpose(0, 2, 1, 3)


def solution(mesh):
    return jax.shard_map(
        shards,
        mesh=mesh,
        in_specs=(
            P("band", None, "lev", None),
            P("band", None, None),
            P(),
            P(),
            P(),
            P(),
            P("lev"),
        ),
        out_specs=P("band", None, "lev", None),
        check_vma=False,
    )
```

```python
import functools
import math

import jax
import jax.numpy as jnp
from jax import lax
from jax.experimental import pallas as pl
from jax.experimental.layout import Layout, with_layout_constraint
from jax.experimental.pallas import tpu as pltpu
from jax.sharding import PartitionSpec as P

FIELDS = 5
LEVELS = 24
TEMPER = 2
ENERGY = 4
LVL_ROWS = 8
SLAB = 128
MIB = 1024 * 1024

time_step = 1.0

COS_POLY = (
    0.9999999890590235, -19.739204499453994, 64.93911745989843, -85.45013953092186,
    60.167630951185615, -25.967599249120923, 6.528658161956132,
)
SIN_POLY = (
    6.283185302511506, -41.3417004053176, 81.60513138579954, -76.70301535389986,
    42.02592698629647, -14.89984666973851, 3.2381375126489513,
)


def up_to(value, unit):
    return -(-value // unit) * unit


class Sizes:
    def __init__(self, bands, groups, slots, fields, degrees, rows):
        self.bands, self.groups = bands, groups
        self.slots, self.fields, self.degrees, self.rows = slots, fields, degrees, rows
        self.tiles = degrees // SLAB
        self.packed = self.tiles + 1
        self.pitch = up_to(2 * self.packed, 8)
        self.pitch_bf16 = up_to(2 * self.packed, 16)
        self.slot_rows = fields * self.tiles * 2
        self.field_pad = up_to(fields, 8)
        self.share = -(-fields // groups)
        self.lanes = 4 * self.share
        self.quarters = 2
        if 4 * self.lanes <= SLAB and slots % 4 == 0:
            self.quarters = 4
        self.halves = self.quarters // 2
        self.chunk_live = slots // self.quarters
        self.chunk = up_to(self.chunk_live, 8)
        self.spots = self.quarters * self.chunk
        self.block = slots
        for size in (8, 4):
            if slots % size == 0 and (size * self.slot_rows) % 16 == 0:
                self.block = size
                break
        self.steps = slots // self.block
        self.pairs = self.halves * bands * self.chunk
        self.trunc = degrees - 1
        self.sorted = degrees // 2
        self.orbits = up_to((4 * self.trunc + 40) // 4 + 2, SLAB)
        self.levels = LEVELS // groups


def owners(sizes, field):
    first, last = field * LEVELS, (field + 1) * LEVELS
    return [
        g for g in range(sizes.groups)
        if g * sizes.fields < last and (g + 1) * sizes.fields > first
    ]


def geo_rounds(sizes):
    sources, targets = owners(sizes, TEMPER), owners(sizes, ENERGY)
    wide = max(len(sources), len(targets))
    rounds = []
    for turn in range(wide):
        pairs = []
        for k in range(wide):
            s, t = k, (k + turn) % wide
            if s < len(sources) and t < len(targets):
                pairs.append((sources[s], targets[t]))
        if pairs:
            rounds.append(pairs)
    return rounds


def iota(shape, dim):
    return lax.broadcasted_iota(jnp.int32, shape, dim)


def one_hot(cond):
    return jnp.where(cond, 1.0, 0.0).astype(jnp.bfloat16)


def dot(a, b, dims=((1,), (0,))):
    return lax.dot_general(a, b, (dims, ((), ())), preferred_element_type=jnp.float32)


def halving(value):
    return value.bit_length() - 1 if value & (value - 1) == 0 else None


def quotient(x, by):
    bits = halving(by)
    return x >> bits if bits is not None else lax.div(x, jnp.int32(by))


def remainder(x, by):
    return x & (by - 1) if halving(by) is not None else lax.rem(x, jnp.int32(by))


def spread_matrix(sizes, lev):
    sz = sizes
    tall = sz.quarters * 4 * sz.field_pad
    wide = sz.groups * SLAB
    dst = iota((1, wide), 1)
    group = quotient(dst, SLAB)
    lane = remainder(dst, SLAB)
    quarter = quotient(lane, sz.lanes)
    rest = remainder(lane, sz.lanes)
    row = quotient(rest, 2 * sz.share)
    rest = remainder(rest, 2 * sz.share)
    comp = quotient(rest, sz.share)
    item = remainder(rest, sz.share)
    start = remainder(lev * sz.fields, sz.groups)
    field = remainder(group - start + sz.groups, sz.groups) + sz.groups * item
    want = ((quarter * 2 + row) * 2 + comp) * sz.field_pad + field
    want = jnp.where((field < sz.fields) & (quarter < sz.quarters), want, -1)
    return one_hot(iota((tall, wide), 0) == want)


def spot_of(sizes, place, odd):
    half = place // sizes.chunk_live
    return (odd * sizes.halves + half) * sizes.chunk + (place - half * sizes.chunk_live)


class Pair:
    def __init__(self, sizes, wave, band, place):
        self.sizes, self.place = sizes, place
        slot = band * sizes.slots + 2 * place
        self.numbers = wave[slot], wave[slot + 1]
        odd = self.numbers[0] & 1
        self.odds = odd, 1 - odd
        self.start = quotient(jnp.maximum(self.numbers[0], 0), SLAB)
        self.split = sizes.tiles - self.start

    def spot(self, side):
        sz = self.sizes
        half = self.place // sz.chunk_live
        first = (self.odds[side] * sz.halves + half) * sz.chunk
        return first + (self.place - half * sz.chunk_live)

    def rows(self, side):
        return pl.ds(pl.multiple_of(self.spot(side) * self.sizes.rows, self.sizes.rows), self.sizes.rows)

    def tile(self, k):
        return jnp.where(k < self.split, self.start + k, k - 1)

    def columns(self):
        place = iota((1, self.sizes.packed * SLAB), 1)
        first = place < self.split * SLAB
        degree = jnp.where(first, place + self.start * SLAB, place - SLAB)
        floors = [jnp.where(n < 0, self.sizes.degrees, n) for n in self.numbers]
        return first, degree >= jnp.where(first, floors[0], floors[1])

    def parts(self):
        tiles = self.sizes.tiles
        first = 2 * self.place
        return (
            (first, self.start, self.split, 0),
            (first + 1, self.split - 1, tiles + 1 - self.split, self.split),
        )

    def tables(self, leg):
        first, live = self.columns()
        leg = leg.astype(jnp.float32)
        own = jnp.where(first & live, leg, 0.0)
        other = jnp.where(first, 0.0, jnp.where(live, leg, 0.0))
        return jnp.concatenate([own, other], axis=0).astype(jnp.bfloat16)


AHEAD = 6
BEHIND = 4


def span(first, count, unit):
    return pl.ds(pl.multiple_of(first * unit, unit), pl.multiple_of(count * unit, unit))


def await_tiles(hbm, sem):
    for some in (hbm.at[0], hbm.at[0, :, pl.ds(0, 1)]):
        pltpu.make_async_copy(some, some, sem).wait()


class Stream:
    def __init__(self, sizes, pair_at, x_hbm, leg_hbm, x_all, leg_all, x_sems, leg_sems):
        self.sizes, self.pair_at = sizes, pair_at
        self.x_hbm, self.leg_hbm, self.x_all, self.leg_all = x_hbm, leg_hbm, x_all, leg_all
        self.x_sems, self.leg_sems = x_sems, leg_sems

    def start(self, place):
        sz = self.sizes
        x_rows = self.x_hbm.reshape(sz.slots, sz.fields, 2 * sz.tiles, SLAB)
        for slot, first, count, here in self.pair_at(place).parts():
            pltpu.make_async_copy(
                x_rows.at[slot, :, span(first, count, 2)],
                self.x_all.at[place, :, span(here, count, 2)],
                self.x_sems.at[place],
            ).start()
            pltpu.make_async_copy(
                self.leg_hbm.at[slot, :, span(first, count, SLAB)],
                self.leg_all.at[place, :, span(here, count, SLAB)],
                self.leg_sems.at[place],
            ).start()

    def begin(self):
        def one(place, carry):
            self.start(place)
            return carry

        lax.fori_loop(0, min(AHEAD * self.sizes.block // 2, self.sizes.slots // 2), one, 0)

    def take(self, step):
        each = self.sizes.block // 2

        @pl.when(step + AHEAD < self.sizes.steps)
        def _():
            for k in range(each):
                self.start((step + AHEAD) * each + k)

        for k in range(each):
            place = step * each + k
            await_tiles(self.x_hbm, self.x_sems.at[place])
            here = self.leg_all.at[place]
            pltpu.make_async_copy(here, here, self.leg_sems.at[place]).wait()


def inverse_kernel(sizes, rounds, wave, points, gauss, layer_depth, x_hbm, leg_hbm, send_ref, *refs):
    sz = sizes
    geo_refs = refs[:len(rounds)]
    wide, spots, numbers, x_all, leg_all, *sems = refs[len(rounds):]
    band = lax.axis_index("band")
    lev = lax.axis_index("lev")
    pair_at = functools.partial(Pair, sz, wave, band)
    stream = Stream(sz, pair_at, x_hbm, leg_hbm, x_all, leg_all, *sems)
    stream.begin()
    pad = 2 * sz.field_pad
    spots[...] = jnp.zeros_like(spots)
    numbers[...] = jnp.full_like(numbers, -1)
    wide[...] = jnp.zeros_like(wide)

    def block(step, carry):
        stream.take(step)
        found = []
        for k in range(sz.block // 2):
            place = step * (sz.block // 2) + k
            for f in range(sz.fields):
                rows = x_all[place, f].astype(jnp.float32)
                wide[k, pl.ds(f * sz.pitch, sz.pitch), :] = rows[0:sz.pitch]
        for k in range(sz.block // 2):
            place = step * (sz.block // 2) + k
            pair = pair_at(place)
            values = jnp.concatenate([
                jnp.concatenate([
                    wide[k, pl.ds(2 * t + c, sz.field_pad, stride=sz.pitch), :] for c in range(2)
                ], axis=0).astype(jnp.bfloat16)
                for t in range(sz.packed)
            ], axis=1)
            total = dot(pair.tables(leg_all[place]), values, ((1,), (1,)))
            for side in range(2):
                found.append((pair, side, total[side * sz.rows:(side + 1) * sz.rows]))
        for pair, side, total in found:
            spots[pair.rows(side), 0:pad] = total
            number = jnp.full((1, SLAB), pair.numbers[side], jnp.int32)
            numbers[pl.ds(pair.spot(side), 1), :] = number
        return carry

    lax.fori_loop(0, sz.steps, block, 0)
    spread = spread_matrix(sz, lev)
    shape = (2 * pad, SLAB)
    src, dst = iota(shape, 0), iota(shape, 1)
    bits = sz.field_pad.bit_length() - 1
    from_field, from_side = src & (sz.field_pad - 1), src >> bits
    to_field, to_side = dst & (sz.field_pad - 1), dst >> bits
    weights = []
    for pairs in rounds:
        first = jnp.int32(2 * LEVELS + sz.fields)
        for source, target in pairs:
            first = jnp.where(lev == source, target * sz.fields - ENERGY * LEVELS, first)
        under = lev * sz.fields + from_field - TEMPER * LEVELS
        above = first + to_field
        hit = (
            (from_side == to_side)
            & (from_field < sz.fields) & (to_field < sz.fields)
            & (above >= 0) & (above <= under)
        )
        weight = jnp.zeros(shape, jnp.float32)
        for level in range(LEVELS):
            weight = jnp.where(hit & (under == level), layer_depth[level], weight)
        high = weight.astype(jnp.bfloat16)
        low = (weight - high.astype(jnp.float32)).astype(jnp.bfloat16)
        weights.append(jnp.concatenate([high, low], axis=0))
    number = numbers[...]
    lane = iota((sz.spots, SLAB), 1)
    known = (number >= 0) & ~((number == 0) & (lane & sz.field_pad != 0))
    for rp in range(sz.rows // 2):
        exact = jnp.concatenate([
            spots[pl.ds(2 * rp + r, sz.spots, stride=sz.rows), :][:, 0:pad] for r in range(2)
        ], axis=1)
        cut = jnp.concatenate([
            exact[q * sz.chunk:(q + 1) * sz.chunk] for q in range(sz.quarters)
        ], axis=1).astype(jnp.bfloat16)
        chunk = dot(cut, spread).astype(jnp.bfloat16)
        for g in range(sz.groups):
            send_ref[rp, g] = chunk[:, g * SLAB:(g + 1) * SLAB]
        count = jnp.where(lane < pad, points[2 * rp], points[2 * rp + 1])
        scale = jnp.where(lane < pad, gauss[2 * rp], gauss[2 * rp + 1])
        scale = jnp.where(known & (2 * number <= count - 1), scale, 0.0)
        exact = exact.astype(jnp.bfloat16)
        double = jnp.concatenate([exact, exact], axis=1)
        for turn in range(len(rounds)):
            geo_refs[turn][rp] = (dot(double, weights[turn]) * scale).astype(jnp.bfloat16)


def cos_sin(z):
    y = z * z
    c = jnp.full_like(y, COS_POLY[-1])
    for a in COS_POLY[-2::-1]:
        c = c * y + a
    s = jnp.full_like(y, SIN_POLY[-1])
    for a in SIN_POLY[-2::-1]:
        s = s * y + a
    return c, s * z


def basis_kernel(sizes, points, out_ref, cosines, sines):
    sz = sizes
    step = pl.program_id(0)
    turns = sz.sorted // 16
    bands_row = 16 + up_to(turns, 8)

    @pl.when(step == 0)
    def _():
        first = lax.axis_index("band") * 2
        length_a, length_b = points[first], points[first + 1]
        count_a = length_a // 4 + 1
        high = cosines.shape[0]
        row = iota((high, SLAB), 0)
        number = jnp.where(row < 16, 2 * row, jnp.where(row < bands_row, 32 * (row - 16), sz.trunc))
        number = number.astype(jnp.float32)
        for at in range(0, sz.orbits, SLAB):
            place = iota((1, SLAB), 1) + at
            second = place >= count_a
            column = (place - jnp.where(second, count_a, 0)).astype(jnp.float32)
            length = jnp.where(second, length_b, length_a).astype(jnp.float32)
            inverse = 1.0 / length
            scale = jnp.where(row < 16, 1.0 / jnp.sqrt(length), 1.0)
            product = number * column
            whole = jnp.floor(product * inverse + 0.5)
            c, s = cos_sin((product - whole * length) * inverse)
            cosines[:, pl.ds(at, SLAB)] = c * scale
            sines[:, pl.ds(at, SLAB)] = s * scale

    groups = out_ref.shape[1] // 16
    for at in range(0, sz.orbits, SLAB):
        cols = pl.ds(at, SLAB)
        base_c, base_n = cosines[0:16, cols], -sines[0:16, cols]
        top_c, top_n = cosines[pl.ds(bands_row, 1), cols], -sines[pl.ds(bands_row, 1), cols]
        turn_rows = pl.ds(pl.multiple_of(16 + step * groups, 8), groups)
        all_c, all_s = cosines[turn_rows, cols], sines[turn_rows, cols]
        for k in range(groups):
            turn_c, turn_s = all_c[k:k + 1], all_s[k:k + 1]
            c = turn_c * base_c + turn_s * base_n
            n = turn_c * base_n - turn_s * base_c
            rows = pl.ds(16 * k, 16)
            out_ref[0, rows, cols] = c.astype(jnp.bfloat16)
            out_ref[1, rows, cols] = n.astype(jnp.bfloat16)
            out_ref[2, rows, cols] = (top_c * c + top_n * n).astype(jnp.bfloat16)
            out_ref[3, rows, cols] = (top_n * c - top_c * n).astype(jnp.bfloat16)


def take_matrix(sizes, lev):
    sz = sizes
    tall = sz.groups * SLAB
    wide = sz.quarters * 2 * SLAB
    dst = iota((1, wide), 1)
    piece = quotient(dst, SLAB)
    lane = remainder(dst, SLAB)
    row = quotient(lane, SLAB // 2)
    field = quotient(remainder(lane, SLAB // 2), LVL_ROWS)
    level = remainder(lane, LVL_ROWS)
    whole = field * LEVELS + level * sz.groups + lev
    owner = quotient(whole, sz.fields)
    start = owner * sz.fields
    first = remainder(lev - remainder(start, sz.groups) + sz.groups, sz.groups)
    item = quotient(whole - start - first, sz.groups)
    want = owner * SLAB + (piece >> 1) * sz.lanes + (row * 2 + (piece & 1)) * sz.share + item
    want = jnp.where((field < FIELDS) & (level < sz.levels), want, -1)
    return one_hot(iota((tall, wide), 0) == want)


def grid_kernel(
    sizes, points, gauss, recv_ref, even_row, basis_hbm, send_ref, basis, terms, arrivals,
):
    sz = sizes
    step = 2 * SLAB
    parts = -(-sz.orbits // step)
    copies = []
    for part in range(parts):
        cols = pl.ds(part * step, min(step, sz.orbits - part * step))
        copies.append(pltpu.make_async_copy(basis_hbm.at[:, :, cols], basis.at[:, :, cols], arrivals.at[part]))
        copies[-1].start()
    lev = lax.axis_index("lev")
    first_row = lax.axis_index("band") * 2
    length_a, length_b = points[first_row], points[first_row + 1]
    count_a, count_b = length_a // 4 + 1, length_b // 4 + 1
    high = FIELDS * LVL_ROWS
    half_slab = SLAB // 2
    width = sz.bands * sz.chunk
    take = take_matrix(sz, lev)
    order = one_hot(iota((sz.sorted, sz.pairs), 0) * 2 == even_row[...])
    joined = jnp.concatenate([
        recv_ref[:, g].astype(jnp.float32).reshape(width, SLAB) for g in range(sz.groups)
    ], axis=1).astype(jnp.bfloat16)
    taken = dot(joined, take)
    coeffs = []
    number = iota((2 * SLAB, sz.sorted), 1) * 2
    bound = jnp.where(iota((2 * SLAB, sz.sorted), 0) & half_slab == 0, length_a, length_b) - 1
    kept = (0, half_slab, SLAB, SLAB + half_slab)
    for parity in range(2):
        rows = []
        for half in range(sz.halves):
            piece = (parity * sz.halves + half) * 2
            rows.append(taken[:, piece * SLAB:(piece + 2) * SLAB])
        values = jnp.concatenate(rows, axis=0).T.astype(jnp.bfloat16)
        placed = dot(values, order, ((1,), (1,)))
        mine = number if parity == 0 else sz.trunc - number
        mult = jnp.where(mine == 0, 1.0, 2.0)
        placed = jnp.where(2 * mine <= bound, placed * mult, 0.0)
        placed = jnp.concatenate([placed[k:k + high] for k in kept], axis=0).astype(jnp.bfloat16)
        coeffs += [placed[:2 * high], placed[2 * high:]]
    for part in range(parts):
        copies[part].wait()
        at = part * step
        many = min(step, sz.orbits - at)
        cols = pl.ds(at, many)
        place = iota((1, many), 1) + at
        second = place >= count_a
        grids = []
        for k in range(4):
            both = dot(coeffs[k], basis[k, :, cols])
            grids.append(jnp.where(second, both[high:], both[:high]))
        ce, se, co, so = grids
        plus, minus = ce + co, ce - co
        splus, sminus = se + so, se - so
        values = (plus + splus, minus - sminus, minus + sminus, plus - splus)
        outs = []
        for v in values:
            u, w, tem, hum, ozo = (v[i * LVL_ROWS:(i + 1) * LVL_ROWS] for i in range(FIELDS))
            outs.append(jnp.concatenate(
                [u * tem, w * tem, u * hum, w * ozo, 0.5 * (u * u + w * w)], axis=0
            ))
        offset = place - jnp.where(second, count_a, 0)
        count = jnp.where(second, count_b, count_a)
        weight = jnp.where((offset == 0) | (offset == count - 1), 0.5, 1.0)
        weight = jnp.where(offset < count, weight, 0.0)
        t0, t1, t2, t3 = (o * weight for o in outs)
        a, b, c, d = t0 + t3, t1 + t2, t0 - t3, t2 - t1
        folds = (a + b, c + d, a - b, c - d)
        empty = jnp.zeros((half_slab - high, many), jnp.float32)
        for k in range(4):
            first = jnp.where(second, 0.0, folds[k])
            last = jnp.where(second, folds[k], 0.0)
            terms[k, :, cols] = jnp.concatenate([first, empty, last, empty], axis=0).astype(jnp.bfloat16)
    lane = iota((1, SLAB), 1)
    scale = jnp.where(lane < half_slab, gauss[first_row], gauss[first_row + 1])
    bound = jnp.where(lane < half_slab, length_a, length_b) - 1
    number = iota((sz.sorted, SLAB), 0) * 2
    even_col = jnp.broadcast_to(even_row[...].astype(jnp.float32), (8, sz.pairs)).T[:, 0:1]
    back_order = one_hot(iota((sz.pairs, sz.sorted), 1) * 2 == even_col.astype(jnp.int32))
    pieces = []
    for parity in range(2):
        mine = number if parity == 0 else sz.trunc - number
        sums = jnp.concatenate([
            jnp.where(
                2 * mine <= bound,
                dot(basis[parity * 2 + comp], terms[parity * 2 + comp], ((1,), (1,))) * scale, 0.0,
            ).astype(jnp.bfloat16)
            for comp in range(2)
        ], axis=1)
        slots = dot(back_order, sums).astype(jnp.bfloat16)
        pieces += [slots[half * width:(half + 1) * width] for half in range(sz.halves)]
    sent = dot(jnp.concatenate(pieces, axis=1), take, ((1,), (1,)))
    for g in range(sz.groups):
        part = sent[:, g * SLAB:(g + 1) * SLAB].reshape(sz.bands, sz.chunk, SLAB)
        send_ref[:, g] = part.astype(jnp.bfloat16)


def zeros_kernel(sizes, wave, out_hbm, zeros, sems):
    sz = sizes
    band = lax.axis_index("band")
    zeros[...] = jnp.zeros_like(zeros)

    def one(place, carry):
        pair = Pair(sz, wave, band, place)
        for side, count in ((0, pair.start), (1, pair.split - 1)):

            @pl.when(count > 0)
            def _():
                pltpu.make_async_copy(
                    zeros.at[:, pl.ds(0, count)],
                    out_hbm.at[2 * place + side, :, pl.ds(0, count)],
                    sems.at[place],
                ).start()

        return carry

    def done(place, carry):
        pltpu.make_async_copy(zeros, zeros, sems.at[place]).wait()
        return carry

    lax.fori_loop(0, sz.slots // 2, one, 0)
    lax.fori_loop(0, sz.slots // 2, done, 0)


def forward_kernel(sizes, wave, speed, back_ref, *refs):
    sz = sizes
    geo_refs = refs[:-13]
    x_hbm, leg_hbm, _, out_hbm, wide, spots, inverse, out_all, out_sems, x_all, leg_all, *sems = refs[-13:]
    band = lax.axis_index("band")
    pair_at = functools.partial(Pair, sz, wave, band)
    stream = Stream(sz, pair_at, x_hbm, leg_hbm, x_all, leg_all, *sems)
    stream.begin()
    pad = 2 * sz.field_pad
    each = sz.block // 2

    gather = spread_matrix(sz, lax.axis_index("lev"))
    for rp in range(sz.rows // 2):
        cut = jnp.concatenate([back_ref[rp, g] for g in range(sz.groups)], axis=1)
        whole = dot(cut, gather, ((1,), (1,)))
        rows = jnp.concatenate([
            whole[:, q * 2 * pad:(q + 1) * 2 * pad] for q in range(sz.quarters)
        ], axis=0)
        for geo_ref in geo_refs:
            rows = rows + geo_ref[rp].astype(jnp.float32)[:, 0:2 * pad]
        for r in range(2):
            part = rows[:, r * pad:(r + 1) * pad]
            part = jnp.concatenate([part, jnp.zeros((sz.spots, SLAB - pad), jnp.float32)], axis=1)
            spots[pl.ds(2 * rp + r, sz.spots, stride=sz.rows), :] = part
    row = quotient(iota((sz.pitch, SLAB), 0), 2)
    lane = iota((sz.pitch, SLAB), 1)
    for start in range(sz.tiles):
        degree = jnp.where(row < sz.tiles - start, row + start, row - 1) * SLAB + lane
        helm = (degree * (degree + 1)).astype(jnp.float32) / float(sz.trunc * (sz.trunc + 1))
        for f in range(sz.fields):
            denominator = 1.0 + time_step * time_step * helm * speed[f]
            inverse[start, pl.ds(f * sz.pitch, sz.pitch), :] = 1.0 / denominator
    out_tiles = out_all.reshape(BEHIND, each, sz.fields, sz.pitch // 2, 2, SLAB)

    def leave(place, k):
        at = lax.rem(place // each, BEHIND)

        for slot, first, count, here in pair_at(place).parts():
            pltpu.make_async_copy(
                out_tiles.at[at, k, :, pl.ds(here, count)],
                out_hbm.at[slot, :, pl.ds(first, count)],
                out_sems.at[at, k],
            ).start()

    def left(step):
        at = lax.rem(step, BEHIND)
        for k in range(each):
            await_tiles(out_hbm, out_sems.at[at, k])

    def block(step, carry):
        stream.take(step)
        work = []
        for k in range(each):
            place = step * each + k
            pair = pair_at(place)
            values = jnp.concatenate([spots[pair.rows(side), :] for side in range(2)], axis=0)
            values = values.T.astype(jnp.bfloat16)[0:pad]
            work.append((place, pair, values, pair.tables(leg_all[place])))

        for k in range(each):
            _, _, values, tables = work[k]
            for first in range(0, sz.packed, 2):
                count = min(2, sz.packed - first)
                tends = dot(values, tables[:, first * SLAB:(first + count) * SLAB])
                for t in range(first, first + count):
                    for c in range(2):
                        rows = pl.ds(2 * t + c, sz.field_pad, stride=sz.pitch)
                        wide[k, rows, :] = tends[
                            c * sz.field_pad:(c + 1) * sz.field_pad, (t - first) * SLAB:(t - first + 1) * SLAB
                        ]

        @pl.when(step >= BEHIND)
        def _():
            left(step)

        at = lax.rem(step, BEHIND)
        for k in range(each):
            place, pair, _, _ = work[k]
            mine = row < pair.split
            degree = jnp.where(mine, row + pair.start, row - 1) * SLAB + lane
            floors = [jnp.where(n < 0, sz.degrees, n) for n in pair.numbers]
            live = degree >= jnp.where(mine, floors[0], floors[1])
            for f in range(sz.fields):
                rows = pl.ds(f * sz.pitch, sz.pitch)
                old = x_all[place, f].astype(jnp.float32)[0:sz.pitch]
                new = (old + time_step * wide[k, rows, :]) * inverse[pair.start, rows, :]
                out_all[at, k, rows, :] = jnp.where(live, new, 0.0)
        for k in range(each):
            leave(step * each + k, k)
        return carry

    lax.fori_loop(0, sz.steps, block, 0)
    for step in range(max(0, sz.steps - BEHIND), sz.steps):
        left(jnp.int32(step))


def params(mib):
    return pltpu.CompilerParams(vmem_limit_bytes=mib * MIB)


def smem():
    return pl.BlockSpec(memory_space=pltpu.SMEM)


def shards(spectra, legendre, slot_wave, row_points, gauss_weight, layer_depth, mode_speed):
    slots, _, fields, degrees = spectra.shape
    rows = legendre.shape[2]
    sz = Sizes(lax.axis_size("band"), lax.axis_size("lev"), slots, fields, degrees, rows)

    tiled = spectra.reshape(slots, 2, fields, sz.tiles, SLAB)
    tiled = with_layout_constraint(tiled, Layout((0, 2, 3, 1, 4)))
    tiled = tiled.transpose(0, 2, 3, 1, 4)
    tables = legendre.transpose(0, 2, 1)

    rounds = geo_rounds(sz)
    spots_shape = pltpu.VMEM((sz.spots * sz.rows, SLAB), jnp.float32)
    pairs = slots // 2
    stream_scratch = [
        pltpu.VMEM((pairs, fields, sz.pitch_bf16, SLAB), jnp.bfloat16),
        pltpu.VMEM((pairs, rows, sz.packed * SLAB), jnp.bfloat16),
        pltpu.SemaphoreType.DMA((pairs,)),
        pltpu.SemaphoreType.DMA((pairs,)),
    ]
    wide_shape = pltpu.VMEM((sz.block // 2, sz.field_pad * sz.pitch, SLAB), jnp.float32)
    anywhere = pl.BlockSpec(memory_space=pl.ANY)
    vmem = pl.BlockSpec(memory_space=pltpu.VMEM)
    send_shape = (sz.bands, sz.groups, sz.chunk, SLAB)
    geo_shape = (sz.rows // 2, sz.spots, SLAB)

    sent, *geo = pl.pallas_call(
        functools.partial(inverse_kernel, sz, rounds),
        in_specs=[smem(), smem(), smem(), smem(), anywhere, anywhere],
        out_specs=[vmem] * (1 + len(rounds)),
        out_shape=[jax.ShapeDtypeStruct(send_shape, jnp.bfloat16)]
        + [jax.ShapeDtypeStruct(geo_shape, jnp.bfloat16)] * len(rounds),
        scratch_shapes=[wide_shape, spots_shape, pltpu.VMEM((sz.spots, SLAB), jnp.int32), *stream_scratch],
        compiler_params=params(56),
        name="inverse_legendre",
    )(slot_wave, row_points, gauss_weight, layer_depth, tiled, tables)

    sent, points_later, wave_later = lax.optimization_barrier((sent, row_points, slot_wave))
    both = ("band", "lev")
    total = sz.bands * sz.groups
    flat = (total * sz.chunk, SLAB)
    arrived = lax.all_to_all(sent.reshape(flat), both, split_axis=0, concat_axis=0, tiled=True)

    pair_wave = wave_later.reshape(-1, 2)
    even_wave = jnp.where(pair_wave[:, 0] % 2 == 0, pair_wave[:, 0], pair_wave[:, 1])
    even_wave = even_wave.reshape(sz.bands, sz.halves, sz.chunk_live)
    even_wave = jnp.pad(even_wave, ((0, 0), (0, 0), (0, sz.chunk - sz.chunk_live)), constant_values=-1)
    even_wave = even_wave.transpose(1, 0, 2).reshape(sz.pairs)

    high = SLAB if sz.sorted % SLAB == 0 else sz.sorted
    table_rows = 16 + up_to(sz.sorted // 16, 8) + 8
    basis = pl.pallas_call(
        functools.partial(basis_kernel, sz),
        grid=(sz.sorted // high,),
        in_specs=[smem()],
        out_specs=pl.BlockSpec((4, high, sz.orbits), lambda i: (0, i, 0)),
        out_shape=jax.ShapeDtypeStruct((4, sz.sorted, sz.orbits), jnp.bfloat16),
        scratch_shapes=[pltpu.VMEM((table_rows, sz.orbits), jnp.float32)] * 2,
        compiler_params=params(56),
        cost_estimate=pl.CostEstimate(
            flops=20 * sz.sorted * sz.orbits, bytes_accessed=8 * sz.sorted * sz.orbits, transcendentals=0,
        ),
        name="basis",
    )(points_later)

    even_row = even_wave.reshape(1, sz.pairs)
    *geo, arrived, basis, even_row = lax.optimization_barrier((*geo, arrived, basis, even_row))
    moved = [lax.ppermute(geo[turn], "lev", pairs) for turn, pairs in enumerate(rounds)]
    returned = pl.pallas_call(
        functools.partial(grid_kernel, sz),
        in_specs=[smem(), smem(), vmem, vmem, anywhere],
        out_specs=vmem,
        out_shape=jax.ShapeDtypeStruct(send_shape, jnp.bfloat16),
        scratch_shapes=[
            pltpu.VMEM((4, sz.sorted, sz.orbits), jnp.bfloat16),
            pltpu.VMEM((4, SLAB, sz.orbits), jnp.bfloat16),
            pltpu.SemaphoreType.DMA((-(-sz.orbits // (2 * SLAB)),)),
        ],
        compiler_params=params(56),
        cost_estimate=pl.CostEstimate(
            flops=4 * 4 * SLAB * sz.sorted * sz.orbits, bytes_accessed=8 * sz.sorted * sz.orbits, transcendentals=0,
        ),
        name="grid_products",
    )(
        row_points, gauss_weight, arrived.reshape(send_shape), even_row, basis,
    )
    *moved, returned, wave_last = lax.optimization_barrier((*moved, returned, slot_wave))

    back = lax.all_to_all(returned.reshape(flat), both, split_axis=0, concat_axis=0, tiled=True)

    out_shape = jax.ShapeDtypeStruct(tiled.shape, jnp.float32)
    zeroed = pl.pallas_call(
        functools.partial(zeros_kernel, sz),
        in_specs=[smem()],
        out_specs=anywhere,
        out_shape=out_shape,
        scratch_shapes=[
            pltpu.VMEM((fields, sz.tiles - 1, 2, SLAB), jnp.float32),
            pltpu.SemaphoreType.DMA((pairs,)),
        ],
        compiler_params=params(56),
        cost_estimate=pl.CostEstimate(
            flops=0, bytes_accessed=2 * slots * fields * degrees * 2, transcendentals=0,
        ),
        name="dead_zeros",
    )(wave_last)
    out = pl.pallas_call(
        functools.partial(forward_kernel, sz),
        in_specs=[smem(), smem()] + [vmem] * (1 + len(rounds)) + [anywhere] * 3,
        out_specs=anywhere,
        out_shape=out_shape,
        input_output_aliases={5 + len(rounds): 0},
        scratch_shapes=[
            wide_shape, spots_shape,
            pltpu.VMEM((sz.tiles, fields * sz.pitch, SLAB), jnp.float32),
            pltpu.VMEM((BEHIND, sz.block // 2, fields * sz.pitch, SLAB), jnp.float32),
            pltpu.SemaphoreType.DMA((BEHIND, sz.block // 2)),
            *stream_scratch,
        ],
        compiler_params=params(56),
        name="forward_legendre",
    )(slot_wave, mode_speed, back.reshape(send_shape), *moved, tiled, tables, zeroed)

    out = out.transpose(0, 1, 3, 2, 4)
    return out.reshape(slots, fields, 2, degrees).transpose(0, 2, 1, 3)


def solution(mesh):
    return jax.shard_map(
        shards,
        mesh=mesh,
        in_specs=(
            P("band", None, "lev", None),
            P("band", None, None),
            P(),
            P(),
            P(),
            P(),
            P("lev"),
        ),
        out_specs=P("band", None, "lev", None),
        check_vma=False,
    )
```

```python
import functools
import math

import jax
import jax.numpy as jnp
from jax import lax
from jax.experimental import pallas as pl
from jax.experimental.layout import Layout, with_layout_constraint
from jax.experimental.pallas import tpu as pltpu
from jax.sharding import PartitionSpec as P

FIELDS = 5
LEVELS = 24
TEMPER = 2
ENERGY = 4
LVL_ROWS = 8
SLAB = 128
MIB = 1024 * 1024

time_step = 1.0

COS_POLY = (
    0.9999999890590235, -19.739204499453994, 64.93911745989843, -85.45013953092186,
    60.167630951185615, -25.967599249120923, 6.528658161956132,
)
SIN_POLY = (
    6.283185302511506, -41.3417004053176, 81.60513138579954, -76.70301535389986,
    42.02592698629647, -14.89984666973851, 3.2381375126489513,
)


def up_to(value, unit):
    return -(-value // unit) * unit


class Sizes:
    def __init__(self, bands, groups, slots, fields, degrees, rows):
        self.bands, self.groups = bands, groups
        self.slots, self.fields, self.degrees, self.rows = slots, fields, degrees, rows
        self.tiles = degrees // SLAB
        self.packed = self.tiles + 1
        self.pitch = up_to(2 * self.packed, 8)
        self.stride = self.pitch + 1
        self.pitch_bf16 = up_to(2 * self.packed, 16)
        self.slot_rows = fields * self.tiles * 2
        self.field_pad = up_to(fields, 8)
        self.share = -(-fields // groups)
        self.lanes = 4 * self.share
        self.quarters = 2
        if 4 * self.lanes <= SLAB and slots % 4 == 0:
            self.quarters = 4
        self.halves = self.quarters // 2
        self.chunk_live = slots // self.quarters
        self.chunk = up_to(self.chunk_live, 8)
        self.spots = self.quarters * self.chunk
        self.block = slots
        for size in (8, 4):
            if slots % size == 0 and (size * self.slot_rows) % 16 == 0:
                self.block = size
                break
        self.steps = slots // self.block
        self.pairs = self.halves * bands * self.chunk
        self.trunc = degrees - 1
        self.sorted = degrees // 2
        self.orbits = up_to((4 * self.trunc + 40) // 4 + 2, SLAB)
        self.levels = LEVELS // groups


def owners(sizes, field):
    first, last = field * LEVELS, (field + 1) * LEVELS
    return [
        g for g in range(sizes.groups)
        if g * sizes.fields < last and (g + 1) * sizes.fields > first
    ]


def geo_rounds(sizes):
    sources, targets = owners(sizes, TEMPER), owners(sizes, ENERGY)
    wide = max(len(sources), len(targets))
    rounds = []
    for turn in range(wide):
        pairs = []
        for k in range(wide):
            s, t = k, (k + turn) % wide
            if s < len(sources) and t < len(targets):
                pairs.append((sources[s], targets[t]))
        if pairs:
            rounds.append(pairs)
    return rounds


def iota(shape, dim):
    return lax.broadcasted_iota(jnp.int32, shape, dim)


def one_hot(cond):
    return jnp.where(cond, 1.0, 0.0).astype(jnp.bfloat16)


def dot(a, b, dims=((1,), (0,))):
    return lax.dot_general(a, b, (dims, ((), ())), preferred_element_type=jnp.float32)


def halving(value):
    return value.bit_length() - 1 if value & (value - 1) == 0 else None


def quotient(x, by):
    bits = halving(by)
    return x >> bits if bits is not None else lax.div(x, jnp.int32(by))


def remainder(x, by):
    return x & (by - 1) if halving(by) is not None else lax.rem(x, jnp.int32(by))


def spread_matrix(sizes, lev):
    sz = sizes
    tall = sz.quarters * 4 * sz.field_pad
    wide = sz.groups * SLAB
    dst = iota((1, wide), 1)
    group = quotient(dst, SLAB)
    lane = remainder(dst, SLAB)
    quarter = quotient(lane, sz.lanes)
    rest = remainder(lane, sz.lanes)
    row = quotient(rest, 2 * sz.share)
    rest = remainder(rest, 2 * sz.share)
    comp = quotient(rest, sz.share)
    item = remainder(rest, sz.share)
    start = remainder(lev * sz.fields, sz.groups)
    field = remainder(group - start + sz.groups, sz.groups) + sz.groups * item
    want = ((quarter * 2 + row) * 2 + comp) * sz.field_pad + field
    want = jnp.where((field < sz.fields) & (quarter < sz.quarters), want, -1)
    return one_hot(iota((tall, wide), 0) == want)


def spot_of(sizes, place, odd):
    half = place // sizes.chunk_live
    return (odd * sizes.halves + half) * sizes.chunk + (place - half * sizes.chunk_live)


class Pair:
    def __init__(self, sizes, wave, band, place):
        self.sizes, self.place = sizes, place
        slot = band * sizes.slots + 2 * place
        self.numbers = wave[slot], wave[slot + 1]
        odd = self.numbers[0] & 1
        self.odds = odd, 1 - odd
        self.start = quotient(jnp.maximum(self.numbers[0], 0), SLAB)
        self.split = sizes.tiles - self.start

    def spot(self, side):
        sz = self.sizes
        half = self.place // sz.chunk_live
        first = (self.odds[side] * sz.halves + half) * sz.chunk
        return first + (self.place - half * sz.chunk_live)

    def rows(self, side):
        return pl.ds(pl.multiple_of(self.spot(side) * self.sizes.rows, self.sizes.rows), self.sizes.rows)

    def tile(self, k):
        return jnp.where(k < self.split, self.start + k, k - 1)

    def columns(self):
        place = iota((1, self.sizes.packed * SLAB), 1)
        first = place < self.split * SLAB
        degree = jnp.where(first, place + self.start * SLAB, place - SLAB)
        floors = [jnp.where(n < 0, self.sizes.degrees, n) for n in self.numbers]
        return first, degree >= jnp.where(first, floors[0], floors[1])

    def parts(self):
        tiles = self.sizes.tiles
        first = 2 * self.place
        return (
            (first, self.start, self.split, 0),
            (first + 1, self.split - 1, tiles + 1 - self.split, self.split),
        )

    def tables(self, leg):
        first, live = self.columns()
        leg = leg.astype(jnp.float32)
        own = jnp.where(first & live, leg, 0.0)
        other = jnp.where(first, 0.0, jnp.where(live, leg, 0.0))
        return jnp.concatenate([own, other], axis=0).astype(jnp.bfloat16)


AHEAD = 4
BEHIND = 4


def span(first, count, unit):
    return pl.ds(pl.multiple_of(first * unit, unit), pl.multiple_of(count * unit, unit))


def await_tiles(hbm, sem):
    for some in (hbm.at[0], hbm.at[0, :, pl.ds(0, 1)]):
        pltpu.make_async_copy(some, some, sem).wait()


class Stream:
    def __init__(self, sizes, pair_at, x_hbm, leg_hbm, x_all, leg_all, x_sems, leg_sems):
        self.sizes, self.pair_at = sizes, pair_at
        self.x_hbm, self.leg_hbm, self.x_all, self.leg_all = x_hbm, leg_hbm, x_all, leg_all
        self.x_sems, self.leg_sems = x_sems, leg_sems

    def start(self, place):
        sz = self.sizes
        x_rows = self.x_hbm.reshape(sz.slots, sz.fields, 2 * sz.tiles, SLAB)
        for slot, first, count, here in self.pair_at(place).parts():
            pltpu.make_async_copy(
                x_rows.at[slot, :, span(first, count, 2)],
                self.x_all.at[place, :, span(here, count, 2)],
                self.x_sems.at[place],
            ).start()
            pltpu.make_async_copy(
                self.leg_hbm.at[slot, :, span(first, count, SLAB)],
                self.leg_all.at[place, :, span(here, count, SLAB)],
                self.leg_sems.at[place],
            ).start()

    def begin(self):
        def one(place, carry):
            self.start(place)
            return carry

        lax.fori_loop(0, min(AHEAD * self.sizes.block // 2, self.sizes.slots // 2), one, 0)

    def take(self, step):
        each = self.sizes.block // 2

        @pl.when(step + AHEAD < self.sizes.steps)
        def _():
            for k in range(each):
                self.start((step + AHEAD) * each + k)

        for k in range(each):
            place = step * each + k
            await_tiles(self.x_hbm, self.x_sems.at[place])
            here = self.leg_all.at[place]
            pltpu.make_async_copy(here, here, self.leg_sems.at[place]).wait()


def inverse_kernel(sizes, rounds, wave, points, gauss, layer_depth, x_hbm, leg_hbm, send_ref, *refs):
    sz = sizes
    geo_refs = refs[:len(rounds)]
    wide, spots, numbers, x_all, leg_all, *sems = refs[len(rounds):]
    band = lax.axis_index("band")
    lev = lax.axis_index("lev")
    pair_at = functools.partial(Pair, sz, wave, band)
    stream = Stream(sz, pair_at, x_hbm, leg_hbm, x_all, leg_all, *sems)
    stream.begin()
    pad = 2 * sz.field_pad
    spots[...] = jnp.zeros_like(spots)
    numbers[...] = jnp.full_like(numbers, -1)
    wide[...] = jnp.zeros_like(wide)

    def block(step, carry):
        stream.take(step)
        found = []
        for k in range(sz.block // 2):
            place = step * (sz.block // 2) + k
            for f in range(sz.fields):
                rows = x_all[place, f].astype(jnp.float32)
                wide[k, pl.ds(f * sz.stride, sz.pitch), :] = rows[0:sz.pitch]
        for k in range(sz.block // 2):
            place = step * (sz.block // 2) + k
            pair = pair_at(place)
            values = jnp.concatenate([
                jnp.concatenate([
                    wide[k, pl.ds(2 * t + c, sz.field_pad, stride=sz.stride), :] for c in range(2)
                ], axis=0).astype(jnp.bfloat16)
                for t in range(sz.packed)
            ], axis=1)
            total = dot(pair.tables(leg_all[place]), values, ((1,), (1,)))
            for side in range(2):
                found.append((pair, side, total[side * sz.rows:(side + 1) * sz.rows]))
        for pair, side, total in found:
            spots[pair.rows(side), 0:pad] = total
            number = jnp.full((1, SLAB), pair.numbers[side], jnp.int32)
            numbers[pl.ds(pair.spot(side), 1), :] = number
        return carry

    lax.fori_loop(0, sz.steps, block, 0)
    spread = spread_matrix(sz, lev)
    shape = (2 * pad, SLAB)
    src, dst = iota(shape, 0), iota(shape, 1)
    bits = sz.field_pad.bit_length() - 1
    from_field, from_side = src & (sz.field_pad - 1), src >> bits
    to_field, to_side = dst & (sz.field_pad - 1), dst >> bits
    weights = []
    for pairs in rounds:
        first = jnp.int32(2 * LEVELS + sz.fields)
        for source, target in pairs:
            first = jnp.where(lev == source, target * sz.fields - ENERGY * LEVELS, first)
        under = lev * sz.fields + from_field - TEMPER * LEVELS
        above = first + to_field
        hit = (
            (from_side == to_side)
            & (from_field < sz.fields) & (to_field < sz.fields)
            & (above >= 0) & (above <= under)
        )
        weight = jnp.zeros(shape, jnp.float32)
        for level in range(LEVELS):
            weight = jnp.where(hit & (under == level), layer_depth[level], weight)
        high = weight.astype(jnp.bfloat16)
        low = (weight - high.astype(jnp.float32)).astype(jnp.bfloat16)
        weights.append(jnp.concatenate([high, low], axis=0))
    number = numbers[...]
    lane = iota((sz.spots, SLAB), 1)
    known = (number >= 0) & ~((number == 0) & (lane & sz.field_pad != 0))
    for rp in range(sz.rows // 2):
        exact = jnp.concatenate([
            spots[pl.ds(2 * rp + r, sz.spots, stride=sz.rows), :][:, 0:pad] for r in range(2)
        ], axis=1)
        cut = jnp.concatenate([
            exact[q * sz.chunk:(q + 1) * sz.chunk] for q in range(sz.quarters)
        ], axis=1).astype(jnp.bfloat16)
        chunk = dot(cut, spread).astype(jnp.bfloat16)
        for g in range(sz.groups):
            send_ref[rp, g] = chunk[:, g * SLAB:(g + 1) * SLAB]
        count = jnp.where(lane < pad, points[2 * rp], points[2 * rp + 1])
        scale = jnp.where(lane < pad, gauss[2 * rp], gauss[2 * rp + 1])
        scale = jnp.where(known & (2 * number <= count - 1), scale, 0.0)
        exact = exact.astype(jnp.bfloat16)
        double = jnp.concatenate([exact, exact], axis=1)
        for turn in range(len(rounds)):
            geo_refs[turn][rp] = (dot(double, weights[turn]) * scale).astype(jnp.bfloat16)


def cos_sin(z):
    y = z * z
    c = jnp.full_like(y, COS_POLY[-1])
    for a in COS_POLY[-2::-1]:
        c = c * y + a
    s = jnp.full_like(y, SIN_POLY[-1])
    for a in SIN_POLY[-2::-1]:
        s = s * y + a
    return c, s * z


def basis_kernel(sizes, points, out_ref, cosines, sines):
    sz = sizes
    step = pl.program_id(0)
    turns = sz.sorted // 16
    bands_row = 16 + up_to(turns, 8)

    @pl.when(step == 0)
    def _():
        first = lax.axis_index("band") * 2
        length_a, length_b = points[first], points[first + 1]
        count_a = length_a // 4 + 1
        high = cosines.shape[0]
        row = iota((high, SLAB), 0)
        number = jnp.where(row < 16, 2 * row, jnp.where(row < bands_row, 32 * (row - 16), sz.trunc))
        number = number.astype(jnp.float32)
        for at in range(0, sz.orbits, SLAB):
            place = iota((1, SLAB), 1) + at
            second = place >= count_a
            column = (place - jnp.where(second, count_a, 0)).astype(jnp.float32)
            length = jnp.where(second, length_b, length_a).astype(jnp.float32)
            inverse = 1.0 / length
            scale = jnp.where(row < 16, 1.0 / jnp.sqrt(length), 1.0)
            product = number * column
            whole = jnp.floor(product * inverse + 0.5)
            c, s = cos_sin((product - whole * length) * inverse)
            cosines[:, pl.ds(at, SLAB)] = c * scale
            sines[:, pl.ds(at, SLAB)] = s * scale

    groups = out_ref.shape[1] // 16
    for at in range(0, sz.orbits, SLAB):
        cols = pl.ds(at, SLAB)
        base_c, base_n = cosines[0:16, cols], -sines[0:16, cols]
        top_c, top_n = cosines[pl.ds(bands_row, 1), cols], -sines[pl.ds(bands_row, 1), cols]
        turn_rows = pl.ds(pl.multiple_of(16 + step * groups, 8), groups)
        all_c, all_s = cosines[turn_rows, cols], sines[turn_rows, cols]
        for k in range(groups):
            turn_c, turn_s = all_c[k:k + 1], all_s[k:k + 1]
            c = turn_c * base_c + turn_s * base_n
            n = turn_c * base_n - turn_s * base_c
            rows = pl.ds(16 * k, 16)
            out_ref[0, rows, cols] = c.astype(jnp.bfloat16)
            out_ref[1, rows, cols] = n.astype(jnp.bfloat16)
            out_ref[2, rows, cols] = (top_c * c + top_n * n).astype(jnp.bfloat16)
            out_ref[3, rows, cols] = (top_n * c - top_c * n).astype(jnp.bfloat16)


def take_matrix(sizes, lev):
    sz = sizes
    tall = sz.groups * SLAB
    wide = sz.quarters * 2 * SLAB
    dst = iota((1, wide), 1)
    piece = quotient(dst, SLAB)
    lane = remainder(dst, SLAB)
    row = quotient(lane, SLAB // 2)
    field = quotient(remainder(lane, SLAB // 2), LVL_ROWS)
    level = remainder(lane, LVL_ROWS)
    whole = field * LEVELS + level * sz.groups + lev
    owner = quotient(whole, sz.fields)
    start = owner * sz.fields
    first = remainder(lev - remainder(start, sz.groups) + sz.groups, sz.groups)
    item = quotient(whole - start - first, sz.groups)
    want = owner * SLAB + (piece >> 1) * sz.lanes + (row * 2 + (piece & 1)) * sz.share + item
    want = jnp.where((field < FIELDS) & (level < sz.levels), want, -1)
    return one_hot(iota((tall, wide), 0) == want)


def grid_kernel(
    sizes, points, gauss, recv_ref, even_row, basis_hbm, send_ref, basis, terms, arrivals,
):
    sz = sizes
    step = 2 * SLAB
    parts = -(-sz.orbits // step)
    copies = []
    for part in range(parts):
        cols = pl.ds(part * step, min(step, sz.orbits - part * step))
        copies.append(pltpu.make_async_copy(basis_hbm.at[:, :, cols], basis.at[:, :, cols], arrivals.at[part]))
        copies[-1].start()
    lev = lax.axis_index("lev")
    first_row = lax.axis_index("band") * 2
    length_a, length_b = points[first_row], points[first_row + 1]
    count_a, count_b = length_a // 4 + 1, length_b // 4 + 1
    high = FIELDS * LVL_ROWS
    half_slab = SLAB // 2
    width = sz.bands * sz.chunk
    take = take_matrix(sz, lev)
    order = one_hot(iota((sz.sorted, sz.pairs), 0) * 2 == even_row[...])
    joined = jnp.concatenate([
        recv_ref[:, g].astype(jnp.float32).reshape(width, SLAB) for g in range(sz.groups)
    ], axis=1).astype(jnp.bfloat16)
    taken = dot(joined, take)
    coeffs = []
    number = iota((2 * SLAB, sz.sorted), 1) * 2
    bound = jnp.where(iota((2 * SLAB, sz.sorted), 0) & half_slab == 0, length_a, length_b) - 1
    kept = (0, half_slab, SLAB, SLAB + half_slab)
    for parity in range(2):
        rows = []
        for half in range(sz.halves):
            piece = (parity * sz.halves + half) * 2
            rows.append(taken[:, piece * SLAB:(piece + 2) * SLAB])
        values = jnp.concatenate(rows, axis=0).T.astype(jnp.bfloat16)
        placed = dot(values, order, ((1,), (1,)))
        mine = number if parity == 0 else sz.trunc - number
        mult = jnp.where(mine == 0, 1.0, 2.0)
        placed = jnp.where(2 * mine <= bound, placed * mult, 0.0)
        placed = jnp.concatenate([placed[k:k + high] for k in kept], axis=0).astype(jnp.bfloat16)
        coeffs += [placed[:2 * high], placed[2 * high:]]
    for part in range(parts):
        copies[part].wait()
        at = part * step
        many = min(step, sz.orbits - at)
        cols = pl.ds(at, many)
        place = iota((1, many), 1) + at
        second = place >= count_a
        grids = []
        for k in range(4):
            both = dot(coeffs[k], basis[k, :, cols])
            grids.append(jnp.where(second, both[high:], both[:high]))
        ce, se, co, so = grids
        plus, minus = ce + co, ce - co
        splus, sminus = se + so, se - so
        values = (plus + splus, minus - sminus, minus + sminus, plus - splus)
        outs = []
        for v in values:
            u, w, tem, hum, ozo = (v[i * LVL_ROWS:(i + 1) * LVL_ROWS] for i in range(FIELDS))
            outs.append(jnp.concatenate(
                [u * tem, w * tem, u * hum, w * ozo, 0.5 * (u * u + w * w)], axis=0
            ))
        offset = place - jnp.where(second, count_a, 0)
        count = jnp.where(second, count_b, count_a)
        weight = jnp.where((offset == 0) | (offset == count - 1), 0.5, 1.0)
        weight = jnp.where(offset < count, weight, 0.0)
        t0, t1, t2, t3 = (o * weight for o in outs)
        a, b, c, d = t0 + t3, t1 + t2, t0 - t3, t2 - t1
        folds = (a + b, c + d, a - b, c - d)
        empty = jnp.zeros((half_slab - high, many), jnp.float32)
        for k in range(4):
            first = jnp.where(second, 0.0, folds[k])
            last = jnp.where(second, folds[k], 0.0)
            terms[k, :, cols] = jnp.concatenate([first, empty, last, empty], axis=0).astype(jnp.bfloat16)
    lane = iota((1, SLAB), 1)
    scale = jnp.where(lane < half_slab, gauss[first_row], gauss[first_row + 1])
    bound = jnp.where(lane < half_slab, length_a, length_b) - 1
    number = iota((sz.sorted, SLAB), 0) * 2
    even_col = jnp.broadcast_to(even_row[...].astype(jnp.float32), (8, sz.pairs)).T[:, 0:1]
    back_order = one_hot(iota((sz.pairs, sz.sorted), 1) * 2 == even_col.astype(jnp.int32))
    pieces = []
    for parity in range(2):
        mine = number if parity == 0 else sz.trunc - number
        sums = jnp.concatenate([
            jnp.where(
                2 * mine <= bound,
                dot(basis[parity * 2 + comp], terms[parity * 2 + comp], ((1,), (1,))) * scale, 0.0,
            ).astype(jnp.bfloat16)
            for comp in range(2)
        ], axis=1)
        slots = dot(back_order, sums).astype(jnp.bfloat16)
        pieces += [slots[half * width:(half + 1) * width] for half in range(sz.halves)]
    sent = dot(jnp.concatenate(pieces, axis=1), take, ((1,), (1,)))
    for g in range(sz.groups):
        part = sent[:, g * SLAB:(g + 1) * SLAB].reshape(sz.bands, sz.chunk, SLAB)
        send_ref[:, g] = part.astype(jnp.bfloat16)


def zeros_kernel(sizes, wave, out_hbm, zeros, sems):
    sz = sizes
    band = lax.axis_index("band")
    zeros[...] = jnp.zeros_like(zeros)

    def one(place, carry):
        pair = Pair(sz, wave, band, place)
        for side, count in ((0, pair.start), (1, pair.split - 1)):

            @pl.when(count > 0)
            def _():
                pltpu.make_async_copy(
                    zeros.at[:, pl.ds(0, count)],
                    out_hbm.at[2 * place + side, :, pl.ds(0, count)],
                    sems.at[place],
                ).start()

        return carry

    def done(place, carry):
        pltpu.make_async_copy(zeros, zeros, sems.at[place]).wait()
        return carry

    lax.fori_loop(0, sz.slots // 2, one, 0)
    lax.fori_loop(0, sz.slots // 2, done, 0)


def forward_kernel(sizes, wave, speed, back_ref, *refs):
    sz = sizes
    geo_refs = refs[:-13]
    x_hbm, leg_hbm, _, out_hbm, wide, spots, inverse, out_all, out_sems, x_all, leg_all, *sems = refs[-13:]
    band = lax.axis_index("band")
    pair_at = functools.partial(Pair, sz, wave, band)
    stream = Stream(sz, pair_at, x_hbm, leg_hbm, x_all, leg_all, *sems)
    stream.begin()
    pad = 2 * sz.field_pad
    each = sz.block // 2

    gather = spread_matrix(sz, lax.axis_index("lev"))
    for rp in range(sz.rows // 2):
        cut = jnp.concatenate([back_ref[rp, g] for g in range(sz.groups)], axis=1)
        whole = dot(cut, gather, ((1,), (1,)))
        rows = jnp.concatenate([
            whole[:, q * 2 * pad:(q + 1) * 2 * pad] for q in range(sz.quarters)
        ], axis=0)
        for geo_ref in geo_refs:
            rows = rows + geo_ref[rp].astype(jnp.float32)[:, 0:2 * pad]
        for r in range(2):
            part = rows[:, r * pad:(r + 1) * pad]
            part = jnp.concatenate([part, jnp.zeros((sz.spots, SLAB - pad), jnp.float32)], axis=1)
            spots[pl.ds(2 * rp + r, sz.spots, stride=sz.rows), :] = part
    row = quotient(iota((sz.pitch, SLAB), 0), 2)
    lane = iota((sz.pitch, SLAB), 1)
    for start in range(sz.tiles):
        degree = jnp.where(row < sz.tiles - start, row + start, row - 1) * SLAB + lane
        helm = (degree * (degree + 1)).astype(jnp.float32) / float(sz.trunc * (sz.trunc + 1))
        for f in range(sz.fields):
            denominator = 1.0 + time_step * time_step * helm * speed[f]
            inverse[start, pl.ds(f * sz.pitch, sz.pitch), :] = 1.0 / denominator
    out_tiles = out_all.reshape(BEHIND, each, sz.fields, sz.pitch // 2, 2, SLAB)

    def leave(place, k):
        at = lax.rem(place // each, BEHIND)

        for slot, first, count, here in pair_at(place).parts():
            pltpu.make_async_copy(
                out_tiles.at[at, k, :, pl.ds(here, count)],
                out_hbm.at[slot, :, pl.ds(first, count)],
                out_sems.at[at, k],
            ).start()

    def left(step):
        at = lax.rem(step, BEHIND)
        for k in range(each):
            await_tiles(out_hbm, out_sems.at[at, k])

    def block(step, carry):
        stream.take(step)
        work = []
        for k in range(each):
            place = step * each + k
            pair = pair_at(place)
            values = jnp.concatenate([spots[pair.rows(side), :] for side in range(2)], axis=0)
            values = values.T.astype(jnp.bfloat16)[0:pad]
            work.append((place, pair, values, pair.tables(leg_all[place])))

        for k in range(each):
            _, _, values, tables = work[k]
            for first in range(0, sz.packed, 2):
                count = min(2, sz.packed - first)
                tends = dot(values, tables[:, first * SLAB:(first + count) * SLAB])
                for t in range(first, first + count):
                    for c in range(2):
                        rows = pl.ds(2 * t + c, sz.field_pad, stride=sz.stride)
                        wide[k, rows, :] = tends[
                            c * sz.field_pad:(c + 1) * sz.field_pad, (t - first) * SLAB:(t - first + 1) * SLAB
                        ]

        @pl.when(step >= BEHIND)
        def _():
            left(step)

        at = lax.rem(step, BEHIND)
        for k in range(each):
            place, pair, _, _ = work[k]
            mine = row < pair.split
            degree = jnp.where(mine, row + pair.start, row - 1) * SLAB + lane
            floors = [jnp.where(n < 0, sz.degrees, n) for n in pair.numbers]
            live = degree >= jnp.where(mine, floors[0], floors[1])
            for f in range(sz.fields):
                rows = pl.ds(f * sz.pitch, sz.pitch)
                old = x_all[place, f].astype(jnp.float32)[0:sz.pitch]
                tend = wide[k, pl.ds(f * sz.stride, sz.pitch), :]
                new = (old + time_step * tend) * inverse[pair.start, rows, :]
                out_all[at, k, rows, :] = jnp.where(live, new, 0.0)
        for k in range(each):
            leave(step * each + k, k)
        return carry

    lax.fori_loop(0, sz.steps, block, 0)
    for step in range(max(0, sz.steps - BEHIND), sz.steps):
        left(jnp.int32(step))


def params(mib):
    return pltpu.CompilerParams(vmem_limit_bytes=mib * MIB)


def smem():
    return pl.BlockSpec(memory_space=pltpu.SMEM)


def shards(spectra, legendre, slot_wave, row_points, gauss_weight, layer_depth, mode_speed):
    slots, _, fields, degrees = spectra.shape
    rows = legendre.shape[2]
    sz = Sizes(lax.axis_size("band"), lax.axis_size("lev"), slots, fields, degrees, rows)

    tiled = spectra.reshape(slots, 2, fields, sz.tiles, SLAB)
    tiled = with_layout_constraint(tiled, Layout((0, 2, 3, 1, 4)))
    tiled = tiled.transpose(0, 2, 3, 1, 4)
    tables = legendre.transpose(0, 2, 1)

    rounds = geo_rounds(sz)
    senders = [source for pairs in rounds for source, _ in pairs]
    sums = [sum(rounds, [])] if len(set(senders)) == len(senders) else rounds
    spots_shape = pltpu.VMEM((sz.spots * sz.rows, SLAB), jnp.float32)
    pairs = slots // 2
    stream_scratch = [
        pltpu.VMEM((pairs, fields, sz.pitch_bf16, SLAB), jnp.bfloat16),
        pltpu.VMEM((pairs, rows, sz.packed * SLAB), jnp.bfloat16),
        pltpu.SemaphoreType.DMA((pairs,)),
        pltpu.SemaphoreType.DMA((pairs,)),
    ]
    wide_shape = pltpu.VMEM((sz.block // 2, up_to(sz.field_pad * sz.stride, 8), SLAB), jnp.float32)
    anywhere = pl.BlockSpec(memory_space=pl.ANY)
    vmem = pl.BlockSpec(memory_space=pltpu.VMEM)
    send_shape = (sz.bands, sz.groups, sz.chunk, SLAB)
    geo_shape = (sz.rows // 2, sz.spots, SLAB)

    sent, *geo = pl.pallas_call(
        functools.partial(inverse_kernel, sz, sums),
        in_specs=[smem(), smem(), smem(), smem(), anywhere, anywhere],
        out_specs=[vmem] * (1 + len(sums)),
        out_shape=[jax.ShapeDtypeStruct(send_shape, jnp.bfloat16)]
        + [jax.ShapeDtypeStruct(geo_shape, jnp.bfloat16)] * len(sums),
        scratch_shapes=[wide_shape, spots_shape, pltpu.VMEM((sz.spots, SLAB), jnp.int32), *stream_scratch],
        compiler_params=params(56),
        name="inverse_legendre",
    )(slot_wave, row_points, gauss_weight, layer_depth, tiled, tables)

    sent, points_later, wave_later = lax.optimization_barrier((sent, row_points, slot_wave))
    both = ("band", "lev")
    total = sz.bands * sz.groups
    flat = (total * sz.chunk, SLAB)
    arrived = lax.all_to_all(sent.reshape(flat), both, split_axis=0, concat_axis=0, tiled=True)

    pair_wave = wave_later.reshape(-1, 2)
    even_wave = jnp.where(pair_wave[:, 0] % 2 == 0, pair_wave[:, 0], pair_wave[:, 1])
    even_wave = even_wave.reshape(sz.bands, sz.halves, sz.chunk_live)
    even_wave = jnp.pad(even_wave, ((0, 0), (0, 0), (0, sz.chunk - sz.chunk_live)), constant_values=-1)
    even_wave = even_wave.transpose(1, 0, 2).reshape(sz.pairs)

    high = SLAB if sz.sorted % SLAB == 0 else sz.sorted
    table_rows = 16 + up_to(sz.sorted // 16, 8) + 8
    basis = pl.pallas_call(
        functools.partial(basis_kernel, sz),
        grid=(sz.sorted // high,),
        in_specs=[smem()],
        out_specs=pl.BlockSpec((4, high, sz.orbits), lambda i: (0, i, 0)),
        out_shape=jax.ShapeDtypeStruct((4, sz.sorted, sz.orbits), jnp.bfloat16),
        scratch_shapes=[pltpu.VMEM((table_rows, sz.orbits), jnp.float32)] * 2,
        compiler_params=params(56),
        cost_estimate=pl.CostEstimate(
            flops=20 * sz.sorted * sz.orbits, bytes_accessed=8 * sz.sorted * sz.orbits, transcendentals=0,
        ),
        name="basis",
    )(points_later)

    even_row = even_wave.reshape(1, sz.pairs)
    *geo, arrived, basis, even_row = lax.optimization_barrier((*geo, arrived, basis, even_row))
    moved = [lax.ppermute(geo[turn % len(sums)], "lev", pairs) for turn, pairs in enumerate(rounds)]
    returned = pl.pallas_call(
        functools.partial(grid_kernel, sz),
        in_specs=[smem(), smem(), vmem, vmem, anywhere],
        out_specs=vmem,
        out_shape=jax.ShapeDtypeStruct(send_shape, jnp.bfloat16),
        scratch_shapes=[
            pltpu.VMEM((4, sz.sorted, sz.orbits), jnp.bfloat16),
            pltpu.VMEM((4, SLAB, sz.orbits), jnp.bfloat16),
            pltpu.SemaphoreType.DMA((-(-sz.orbits // (2 * SLAB)),)),
        ],
        compiler_params=params(56),
        cost_estimate=pl.CostEstimate(
            flops=4 * 4 * SLAB * sz.sorted * sz.orbits, bytes_accessed=8 * sz.sorted * sz.orbits, transcendentals=0,
        ),
        name="grid_products",
    )(
        row_points, gauss_weight, arrived.reshape(send_shape), even_row, basis,
    )
    *moved, returned, wave_last = lax.optimization_barrier((*moved, returned, slot_wave))

    back = lax.all_to_all(returned.reshape(flat), both, split_axis=0, concat_axis=0, tiled=True)

    out_shape = jax.ShapeDtypeStruct(tiled.shape, jnp.float32)
    zeroed = pl.pallas_call(
        functools.partial(zeros_kernel, sz),
        in_specs=[smem()],
        out_specs=anywhere,
        out_shape=out_shape,
        scratch_shapes=[
            pltpu.VMEM((fields, sz.tiles - 1, 2, SLAB), jnp.float32),
            pltpu.SemaphoreType.DMA((pairs,)),
        ],
        compiler_params=params(56),
        cost_estimate=pl.CostEstimate(
            flops=0, bytes_accessed=2 * slots * fields * degrees * 2, transcendentals=0,
        ),
        name="dead_zeros",
    )(wave_last)
    out = pl.pallas_call(
        functools.partial(forward_kernel, sz),
        in_specs=[smem(), smem()] + [vmem] * (1 + len(rounds)) + [anywhere] * 3,
        out_specs=anywhere,
        out_shape=out_shape,
        input_output_aliases={5 + len(rounds): 0},
        scratch_shapes=[
            wide_shape, spots_shape,
            pltpu.VMEM((sz.tiles, fields * sz.pitch, SLAB), jnp.float32),
            pltpu.VMEM((BEHIND, sz.block // 2, fields * sz.pitch, SLAB), jnp.float32),
            pltpu.SemaphoreType.DMA((BEHIND, sz.block // 2)),
            *stream_scratch,
        ],
        compiler_params=params(56),
        name="forward_legendre",
    )(slot_wave, mode_speed, back.reshape(send_shape), *moved, tiled, tables, zeroed)

    out = out.transpose(0, 1, 3, 2, 4)
    return out.reshape(slots, fields, 2, degrees).transpose(0, 2, 1, 3)


def solution(mesh):
    return jax.shard_map(
        shards,
        mesh=mesh,
        in_specs=(
            P("band", None, "lev", None),
            P("band", None, None),
            P(),
            P(),
            P(),
            P(),
            P("lev"),
        ),
        out_specs=P("band", None, "lev", None),
        check_vma=False,
    )
```

```python
import functools
import math

import jax
import jax.numpy as jnp
from jax import lax
from jax.experimental import pallas as pl
from jax.experimental.layout import Layout, with_layout_constraint
from jax.experimental.pallas import tpu as pltpu
from jax.sharding import PartitionSpec as P

FIELDS = 5
LEVELS = 24
TEMPER = 2
ENERGY = 4
LVL_ROWS = 8
SLAB = 128
MIB = 1024 * 1024

time_step = 1.0

COS_POLY = (
    0.9999999890590235, -19.739204499453994, 64.93911745989843, -85.45013953092186,
    60.167630951185615, -25.967599249120923, 6.528658161956132,
)
SIN_POLY = (
    6.283185302511506, -41.3417004053176, 81.60513138579954, -76.70301535389986,
    42.02592698629647, -14.89984666973851, 3.2381375126489513,
)


def up_to(value, unit):
    return -(-value // unit) * unit


class Sizes:
    def __init__(self, bands, groups, slots, fields, degrees, rows):
        self.bands, self.groups = bands, groups
        self.slots, self.fields, self.degrees, self.rows = slots, fields, degrees, rows
        self.tiles = degrees // SLAB
        self.packed = self.tiles + 1
        self.pitch = up_to(2 * self.packed, 8)
        self.stride = self.pitch + 1
        self.pitch_bf16 = up_to(2 * self.packed, 16)
        self.slot_rows = fields * self.tiles * 2
        self.field_pad = up_to(fields, 8)
        self.share = -(-fields // groups)
        self.lanes = 4 * self.share
        self.quarters = 2
        if 4 * self.lanes <= SLAB and slots % 4 == 0:
            self.quarters = 4
        self.halves = self.quarters // 2
        self.chunk_live = slots // self.quarters
        self.chunk = up_to(self.chunk_live, 8)
        self.spots = self.quarters * self.chunk
        self.block = slots
        for size in (8, 4):
            if slots % size == 0 and (size * self.slot_rows) % 16 == 0:
                self.block = size
                break
        self.steps = slots // self.block
        self.pairs = self.halves * bands * self.chunk
        self.trunc = degrees - 1
        self.sorted = degrees // 2
        self.orbits = up_to((4 * self.trunc + 40) // 4 + 2, SLAB)
        self.levels = LEVELS // groups


def owners(sizes, field):
    first, last = field * LEVELS, (field + 1) * LEVELS
    return [
        g for g in range(sizes.groups)
        if g * sizes.fields < last and (g + 1) * sizes.fields > first
    ]


def geo_rounds(sizes):
    sources, targets = owners(sizes, TEMPER), owners(sizes, ENERGY)
    wide = max(len(sources), len(targets))
    rounds = []
    for turn in range(wide):
        pairs = []
        for k in range(wide):
            s, t = k, (k + turn) % wide
            if s < len(sources) and t < len(targets):
                pairs.append((sources[s], targets[t]))
        if pairs:
            rounds.append(pairs)
    return rounds


def iota(shape, dim):
    return lax.broadcasted_iota(jnp.int32, shape, dim)


def one_hot(cond):
    return jnp.where(cond, 1.0, 0.0).astype(jnp.bfloat16)


def dot(a, b, dims=((1,), (0,))):
    return lax.dot_general(a, b, (dims, ((), ())), preferred_element_type=jnp.float32)


def halving(value):
    return value.bit_length() - 1 if value & (value - 1) == 0 else None


def quotient(x, by):
    bits = halving(by)
    return x >> bits if bits is not None else lax.div(x, jnp.int32(by))


def remainder(x, by):
    return x & (by - 1) if halving(by) is not None else lax.rem(x, jnp.int32(by))


def spread_matrix(sizes, lev):
    sz = sizes
    tall = sz.quarters * 4 * sz.field_pad
    wide = sz.groups * SLAB
    dst = iota((1, wide), 1)
    group = quotient(dst, SLAB)
    lane = remainder(dst, SLAB)
    quarter = quotient(lane, sz.lanes)
    rest = remainder(lane, sz.lanes)
    row = quotient(rest, 2 * sz.share)
    rest = remainder(rest, 2 * sz.share)
    comp = quotient(rest, sz.share)
    item = remainder(rest, sz.share)
    start = remainder(lev * sz.fields, sz.groups)
    field = remainder(group - start + sz.groups, sz.groups) + sz.groups * item
    want = ((quarter * 2 + row) * 2 + comp) * sz.field_pad + field
    want = jnp.where((field < sz.fields) & (quarter < sz.quarters), want, -1)
    return one_hot(iota((tall, wide), 0) == want)


def spot_of(sizes, place, odd):
    half = place // sizes.chunk_live
    return (odd * sizes.halves + half) * sizes.chunk + (place - half * sizes.chunk_live)


class Pair:
    def __init__(self, sizes, wave, band, place):
        self.sizes, self.place = sizes, place
        slot = band * sizes.slots + 2 * place
        self.numbers = wave[slot], wave[slot + 1]
        odd = self.numbers[0] & 1
        self.odds = odd, 1 - odd
        self.start = quotient(jnp.maximum(self.numbers[0], 0), SLAB)
        self.split = sizes.tiles - self.start

    def spot(self, side):
        sz = self.sizes
        half = self.place // sz.chunk_live
        first = (self.odds[side] * sz.halves + half) * sz.chunk
        return first + (self.place - half * sz.chunk_live)

    def rows(self, side):
        return pl.ds(pl.multiple_of(self.spot(side) * self.sizes.rows, self.sizes.rows), self.sizes.rows)

    def tile(self, k):
        return jnp.where(k < self.split, self.start + k, k - 1)

    def columns(self):
        place = iota((1, self.sizes.packed * SLAB), 1)
        first = place < self.split * SLAB
        degree = jnp.where(first, place + self.start * SLAB, place - SLAB)
        floors = [jnp.where(n < 0, self.sizes.degrees, n) for n in self.numbers]
        return first, degree >= jnp.where(first, floors[0], floors[1])

    def parts(self):
        tiles = self.sizes.tiles
        first = 2 * self.place
        return (
            (first, self.start, self.split, 0),
            (first + 1, self.split - 1, tiles + 1 - self.split, self.split),
        )

    def tables(self, leg):
        first, live = self.columns()
        leg = leg.astype(jnp.float32)
        own = jnp.where(first & live, leg, 0.0)
        other = jnp.where(first, 0.0, jnp.where(live, leg, 0.0))
        return jnp.concatenate([own, other], axis=0).astype(jnp.bfloat16)


AHEAD = 4
BEHIND = 4


def span(first, count, unit):
    return pl.ds(pl.multiple_of(first * unit, unit), pl.multiple_of(count * unit, unit))


def await_tiles(hbm, sem):
    for some in (hbm.at[0], hbm.at[0, :, pl.ds(0, 1)]):
        pltpu.make_async_copy(some, some, sem).wait()


class Stream:
    def __init__(self, sizes, pair_at, x_hbm, leg_hbm, x_all, leg_all, x_sems, leg_sems):
        self.sizes, self.pair_at = sizes, pair_at
        self.x_hbm, self.leg_hbm, self.x_all, self.leg_all = x_hbm, leg_hbm, x_all, leg_all
        self.x_sems, self.leg_sems = x_sems, leg_sems

    def start(self, place):
        sz = self.sizes
        x_rows = self.x_hbm.reshape(sz.slots, sz.fields, 2 * sz.tiles, SLAB)
        for slot, first, count, here in self.pair_at(place).parts():
            pltpu.make_async_copy(
                x_rows.at[slot, :, span(first, count, 2)],
                self.x_all.at[place, :, span(here, count, 2)],
                self.x_sems.at[place],
            ).start()
            pltpu.make_async_copy(
                self.leg_hbm.at[slot, :, span(first, count, SLAB)],
                self.leg_all.at[place, :, span(here, count, SLAB)],
                self.leg_sems.at[place],
            ).start()

    def begin(self):
        def one(place, carry):
            self.start(place)
            return carry

        lax.fori_loop(0, min(AHEAD * self.sizes.block // 2, self.sizes.slots // 2), one, 0)

    def take(self, step):
        each = self.sizes.block // 2

        @pl.when(step + AHEAD < self.sizes.steps)
        def _():
            for k in range(each):
                self.start((step + AHEAD) * each + k)

        for k in range(each):
            place = step * each + k
            await_tiles(self.x_hbm, self.x_sems.at[place])
            here = self.leg_all.at[place]
            pltpu.make_async_copy(here, here, self.leg_sems.at[place]).wait()


def inverse_kernel(sizes, rounds, wave, points, gauss, layer_depth, x_hbm, leg_hbm, send_ref, *refs):
    sz = sizes
    geo_refs = refs[:len(rounds)]
    wide, spots, numbers, x_all, leg_all, *sems = refs[len(rounds):]
    band = lax.axis_index("band")
    lev = lax.axis_index("lev")
    pair_at = functools.partial(Pair, sz, wave, band)
    stream = Stream(sz, pair_at, x_hbm, leg_hbm, x_all, leg_all, *sems)
    stream.begin()
    pad = 2 * sz.field_pad
    spots[...] = jnp.zeros_like(spots)
    numbers[...] = jnp.full_like(numbers, -1)
    wide[...] = jnp.zeros_like(wide)

    def block(step, carry):
        stream.take(step)
        found = []
        for k in range(sz.block // 2):
            place = step * (sz.block // 2) + k
            for f in range(sz.fields):
                rows = x_all[place, f].astype(jnp.float32)
                wide[k, pl.ds(f * sz.stride, sz.pitch), :] = rows[0:sz.pitch]
        pairs, tables, values = [], [], []
        for k in range(sz.block // 2):
            place = step * (sz.block // 2) + k
            pairs.append(pair_at(place))
            tables.append(pairs[k].tables(leg_all[place]))
            values.append(jnp.concatenate([
                jnp.concatenate([
                    wide[k, pl.ds(2 * t + c, sz.field_pad, stride=sz.stride), :] for c in range(2)
                ], axis=0).astype(jnp.bfloat16)
                for t in range(sz.packed)
            ], axis=1))
        totals = dot(jnp.concatenate(tables, axis=0), jnp.concatenate(values, axis=0), ((1,), (1,)))
        for k, pair in enumerate(pairs):
            for side in range(2):
                first = (2 * k + side) * sz.rows
                found.append((pair, side, totals[first:first + sz.rows, k * pad:(k + 1) * pad]))
        for pair, side, total in found:
            spots[pair.rows(side), 0:pad] = total
            number = jnp.full((1, SLAB), pair.numbers[side], jnp.int32)
            numbers[pl.ds(pair.spot(side), 1), :] = number
        return carry

    lax.fori_loop(0, sz.steps, block, 0)
    spread = spread_matrix(sz, lev)
    shape = (2 * pad, SLAB)
    src, dst = iota(shape, 0), iota(shape, 1)
    bits = sz.field_pad.bit_length() - 1
    from_field, from_side = src & (sz.field_pad - 1), src >> bits
    to_field, to_side = dst & (sz.field_pad - 1), dst >> bits
    weights = []
    for pairs in rounds:
        first = jnp.int32(2 * LEVELS + sz.fields)
        for source, target in pairs:
            first = jnp.where(lev == source, target * sz.fields - ENERGY * LEVELS, first)
        under = lev * sz.fields + from_field - TEMPER * LEVELS
        above = first + to_field
        hit = (
            (from_side == to_side)
            & (from_field < sz.fields) & (to_field < sz.fields)
            & (above >= 0) & (above <= under)
        )
        weight = jnp.zeros(shape, jnp.float32)
        for level in range(LEVELS):
            weight = jnp.where(hit & (under == level), layer_depth[level], weight)
        high = weight.astype(jnp.bfloat16)
        low = (weight - high.astype(jnp.float32)).astype(jnp.bfloat16)
        weights.append(jnp.concatenate([high, low], axis=0))
    number = numbers[...]
    lane = iota((sz.spots, SLAB), 1)
    known = (number >= 0) & ~((number == 0) & (lane & sz.field_pad != 0))
    exacts, cuts, scales = [], [], []
    for rp in range(sz.rows // 2):
        exact = jnp.concatenate([
            spots[pl.ds(2 * rp + r, sz.spots, stride=sz.rows), :][:, 0:pad] for r in range(2)
        ], axis=1)
        cuts.append(jnp.concatenate([
            exact[q * sz.chunk:(q + 1) * sz.chunk] for q in range(sz.quarters)
        ], axis=1))
        exacts.append(exact)
        count = jnp.where(lane < pad, points[2 * rp], points[2 * rp + 1])
        scale = jnp.where(lane < pad, gauss[2 * rp], gauss[2 * rp + 1])
        scales.append(jnp.where(known & (2 * number <= count - 1), scale, 0.0))
    chunks = dot(jnp.concatenate(cuts, axis=0).astype(jnp.bfloat16), spread)
    exact = jnp.concatenate(exacts, axis=0).astype(jnp.bfloat16)
    double = jnp.concatenate([exact, exact], axis=1)
    for turn in range(len(rounds)):
        sums = dot(double, weights[turn])
        for rp in range(sz.rows // 2):
            own = sums[rp * sz.spots:(rp + 1) * sz.spots] * scales[rp]
            geo_refs[turn][rp] = own.astype(jnp.bfloat16)
    for rp in range(sz.rows // 2):
        for g in range(sz.groups):
            chunk = chunks[rp * sz.chunk:(rp + 1) * sz.chunk, g * SLAB:(g + 1) * SLAB]
            send_ref[rp, g] = chunk.astype(jnp.bfloat16)


def cos_sin(z):
    y = z * z
    c = jnp.full_like(y, COS_POLY[-1])
    for a in COS_POLY[-2::-1]:
        c = c * y + a
    s = jnp.full_like(y, SIN_POLY[-1])
    for a in SIN_POLY[-2::-1]:
        s = s * y + a
    return c, s * z


def basis_kernel(sizes, points, out_ref, cosines, sines):
    sz = sizes
    step = pl.program_id(0)
    turns = sz.sorted // 16
    bands_row = 16 + up_to(turns, 8)

    @pl.when(step == 0)
    def _():
        first = lax.axis_index("band") * 2
        length_a, length_b = points[first], points[first + 1]
        count_a = length_a // 4 + 1
        high = cosines.shape[0]
        row = iota((high, SLAB), 0)
        number = jnp.where(row < 16, 2 * row, jnp.where(row < bands_row, 32 * (row - 16), sz.trunc))
        number = number.astype(jnp.float32)
        for at in range(0, sz.orbits, SLAB):
            place = iota((1, SLAB), 1) + at
            second = place >= count_a
            column = (place - jnp.where(second, count_a, 0)).astype(jnp.float32)
            length = jnp.where(second, length_b, length_a).astype(jnp.float32)
            inverse = 1.0 / length
            scale = jnp.where(row < 16, 1.0 / jnp.sqrt(length), 1.0)
            product = number * column
            whole = jnp.floor(product * inverse + 0.5)
            c, s = cos_sin((product - whole * length) * inverse)
            cosines[:, pl.ds(at, SLAB)] = c * scale
            sines[:, pl.ds(at, SLAB)] = s * scale

    groups = out_ref.shape[1] // 16
    for at in range(0, sz.orbits, SLAB):
        cols = pl.ds(at, SLAB)
        base_c, base_n = cosines[0:16, cols], -sines[0:16, cols]
        top_c, top_n = cosines[pl.ds(bands_row, 1), cols], -sines[pl.ds(bands_row, 1), cols]
        turn_rows = pl.ds(pl.multiple_of(16 + step * groups, 8), groups)
        all_c, all_s = cosines[turn_rows, cols], sines[turn_rows, cols]
        for k in range(groups):
            turn_c, turn_s = all_c[k:k + 1], all_s[k:k + 1]
            c = turn_c * base_c + turn_s * base_n
            n = turn_c * base_n - turn_s * base_c
            rows = pl.ds(16 * k, 16)
            out_ref[0, rows, cols] = c.astype(jnp.bfloat16)
            out_ref[1, rows, cols] = n.astype(jnp.bfloat16)
            out_ref[2, rows, cols] = (top_c * c + top_n * n).astype(jnp.bfloat16)
            out_ref[3, rows, cols] = (top_n * c - top_c * n).astype(jnp.bfloat16)


def take_matrix(sizes, lev):
    sz = sizes
    tall = sz.groups * SLAB
    wide = sz.quarters * 2 * SLAB
    dst = iota((1, wide), 1)
    piece = quotient(dst, SLAB)
    lane = remainder(dst, SLAB)
    row = quotient(lane, SLAB // 2)
    field = quotient(remainder(lane, SLAB // 2), LVL_ROWS)
    level = remainder(lane, LVL_ROWS)
    whole = field * LEVELS + level * sz.groups + lev
    owner = quotient(whole, sz.fields)
    start = owner * sz.fields
    first = remainder(lev - remainder(start, sz.groups) + sz.groups, sz.groups)
    item = quotient(whole - start - first, sz.groups)
    want = owner * SLAB + (piece >> 1) * sz.lanes + (row * 2 + (piece & 1)) * sz.share + item
    want = jnp.where((field < FIELDS) & (level < sz.levels), want, -1)
    return one_hot(iota((tall, wide), 0) == want)


def grid_kernel(
    sizes, points, gauss, recv_ref, even_row, basis_hbm, send_ref, basis, terms, arrivals,
):
    sz = sizes
    step = 2 * SLAB
    parts = -(-sz.orbits // step)
    copies = []
    for part in range(parts):
        cols = pl.ds(part * step, min(step, sz.orbits - part * step))
        copies.append(pltpu.make_async_copy(basis_hbm.at[:, :, cols], basis.at[:, :, cols], arrivals.at[part]))
        copies[-1].start()
    lev = lax.axis_index("lev")
    first_row = lax.axis_index("band") * 2
    length_a, length_b = points[first_row], points[first_row + 1]
    count_a, count_b = length_a // 4 + 1, length_b // 4 + 1
    high = FIELDS * LVL_ROWS
    half_slab = SLAB // 2
    width = sz.bands * sz.chunk
    take = take_matrix(sz, lev)
    order = one_hot(iota((sz.sorted, sz.pairs), 0) * 2 == even_row[...])
    joined = jnp.concatenate([
        recv_ref[:, g].astype(jnp.float32).reshape(width, SLAB) for g in range(sz.groups)
    ], axis=1).astype(jnp.bfloat16)
    taken = dot(joined, take)
    coeffs = []
    number = iota((2 * SLAB, sz.sorted), 1) * 2
    bound = jnp.where(iota((2 * SLAB, sz.sorted), 0) & half_slab == 0, length_a, length_b) - 1
    kept = (0, half_slab, SLAB, SLAB + half_slab)
    sources = []
    for parity in range(2):
        rows = []
        for half in range(sz.halves):
            piece = (parity * sz.halves + half) * 2
            rows.append(taken[:, piece * SLAB:(piece + 2) * SLAB])
        sources.append(jnp.concatenate(rows, axis=0).T)
    ordered = dot(jnp.concatenate(sources, axis=0).astype(jnp.bfloat16), order, ((1,), (1,)))
    for parity in range(2):
        placed = ordered[parity * 2 * SLAB:(parity + 1) * 2 * SLAB]
        mine = number if parity == 0 else sz.trunc - number
        mult = jnp.where(mine == 0, 1.0, 2.0)
        placed = jnp.where(2 * mine <= bound, placed * mult, 0.0)
        placed = jnp.concatenate([placed[k:k + high] for k in kept], axis=0).astype(jnp.bfloat16)
        coeffs += [placed[:2 * high], placed[2 * high:]]
    for part in range(parts):
        copies[part].wait()
        at = part * step
        many = min(step, sz.orbits - at)
        cols = pl.ds(at, many)
        place = iota((1, many), 1) + at
        second = place >= count_a
        grids = []
        for k in range(4):
            both = dot(coeffs[k], basis[k, :, cols])
            grids.append(jnp.where(second, both[high:], both[:high]))
        ce, se, co, so = grids
        plus, minus = ce + co, ce - co
        splus, sminus = se + so, se - so
        values = (plus + splus, minus - sminus, minus + sminus, plus - splus)
        outs = []
        for v in values:
            u, w, tem, hum, ozo = (v[i * LVL_ROWS:(i + 1) * LVL_ROWS] for i in range(FIELDS))
            outs.append(jnp.concatenate(
                [u * tem, w * tem, u * hum, w * ozo, 0.5 * (u * u + w * w)], axis=0
            ))
        offset = place - jnp.where(second, count_a, 0)
        count = jnp.where(second, count_b, count_a)
        weight = jnp.where((offset == 0) | (offset == count - 1), 0.5, 1.0)
        weight = jnp.where(offset < count, weight, 0.0)
        t0, t1, t2, t3 = (o * weight for o in outs)
        a, b, c, d = t0 + t3, t1 + t2, t0 - t3, t2 - t1
        folds = (a + b, c + d, a - b, c - d)
        empty = jnp.zeros((half_slab - high, many), jnp.float32)
        for k in range(4):
            first = jnp.where(second, 0.0, folds[k])
            last = jnp.where(second, folds[k], 0.0)
            terms[k, :, cols] = jnp.concatenate([first, empty, last, empty], axis=0).astype(jnp.bfloat16)
    lane = iota((1, SLAB), 1)
    scale = jnp.where(lane < half_slab, gauss[first_row], gauss[first_row + 1])
    bound = jnp.where(lane < half_slab, length_a, length_b) - 1
    number = iota((sz.sorted, SLAB), 0) * 2
    even_col = jnp.broadcast_to(even_row[...].astype(jnp.float32), (8, sz.pairs)).T[:, 0:1]
    back_order = one_hot(iota((sz.pairs, sz.sorted), 1) * 2 == even_col.astype(jnp.int32))
    sums = []
    for parity in range(2):
        mine = number if parity == 0 else sz.trunc - number
        for k in (2 * parity, 2 * parity + 1):
            total = dot(basis[k], terms[k], ((1,), (1,))) * scale
            sums.append(jnp.where(2 * mine <= bound, total, 0.0).astype(jnp.bfloat16))
    slots = dot(back_order, jnp.concatenate(sums, axis=1)).astype(jnp.bfloat16)
    pieces = [
        slots[half * width:(half + 1) * width, 2 * parity * SLAB:2 * (parity + 1) * SLAB]
        for parity in range(2) for half in range(sz.halves)
    ]
    sent = dot(jnp.concatenate(pieces, axis=1), take, ((1,), (1,)))
    for g in range(sz.groups):
        part = sent[:, g * SLAB:(g + 1) * SLAB].reshape(sz.bands, sz.chunk, SLAB)
        send_ref[:, g] = part.astype(jnp.bfloat16)


def zeros_kernel(sizes, wave, out_hbm, zeros, sems):
    sz = sizes
    band = lax.axis_index("band")
    zeros[...] = jnp.zeros_like(zeros)

    def one(place, carry):
        pair = Pair(sz, wave, band, place)
        for side, count in ((0, pair.start), (1, pair.split - 1)):

            @pl.when(count > 0)
            def _():
                pltpu.make_async_copy(
                    zeros.at[:, pl.ds(0, count)],
                    out_hbm.at[2 * place + side, :, pl.ds(0, count)],
                    sems.at[place],
                ).start()

        return carry

    def done(place, carry):
        pltpu.make_async_copy(zeros, zeros, sems.at[place]).wait()
        return carry

    lax.fori_loop(0, sz.slots // 2, one, 0)
    lax.fori_loop(0, sz.slots // 2, done, 0)


def forward_kernel(sizes, wave, speed, back_ref, *refs):
    sz = sizes
    geo_refs = refs[:-13]
    x_hbm, leg_hbm, _, out_hbm, wide, spots, inverse, out_all, out_sems, x_all, leg_all, *sems = refs[-13:]
    band = lax.axis_index("band")
    pair_at = functools.partial(Pair, sz, wave, band)
    stream = Stream(sz, pair_at, x_hbm, leg_hbm, x_all, leg_all, *sems)
    stream.begin()
    pad = 2 * sz.field_pad
    each = sz.block // 2

    gather = spread_matrix(sz, lax.axis_index("lev"))
    cuts = [
        jnp.concatenate([back_ref[rp, g].astype(jnp.float32) for g in range(sz.groups)], axis=1)
        for rp in range(sz.rows // 2)
    ]
    wholes = dot(jnp.concatenate(cuts, axis=0).astype(jnp.bfloat16), gather, ((1,), (1,)))
    for rp in range(sz.rows // 2):
        whole = wholes[rp * sz.chunk:(rp + 1) * sz.chunk]
        rows = jnp.concatenate([
            whole[:, q * 2 * pad:(q + 1) * 2 * pad] for q in range(sz.quarters)
        ], axis=0)
        for geo_ref in geo_refs:
            rows = rows + geo_ref[rp].astype(jnp.float32)[:, 0:2 * pad]
        for r in range(2):
            part = rows[:, r * pad:(r + 1) * pad]
            part = jnp.concatenate([part, jnp.zeros((sz.spots, SLAB - pad), jnp.float32)], axis=1)
            spots[pl.ds(2 * rp + r, sz.spots, stride=sz.rows), :] = part
    row = quotient(iota((sz.pitch, SLAB), 0), 2)
    lane = iota((sz.pitch, SLAB), 1)
    for start in range(sz.tiles):
        degree = jnp.where(row < sz.tiles - start, row + start, row - 1) * SLAB + lane
        helm = (degree * (degree + 1)).astype(jnp.float32) / float(sz.trunc * (sz.trunc + 1))
        for f in range(sz.fields):
            denominator = 1.0 + time_step * time_step * helm * speed[f]
            inverse[start, pl.ds(f * sz.pitch, sz.pitch), :] = 1.0 / denominator
    out_tiles = out_all.reshape(BEHIND, each, sz.fields, sz.pitch // 2, 2, SLAB)

    def leave(place, k):
        at = lax.rem(place // each, BEHIND)

        for slot, first, count, here in pair_at(place).parts():
            pltpu.make_async_copy(
                out_tiles.at[at, k, :, pl.ds(here, count)],
                out_hbm.at[slot, :, pl.ds(first, count)],
                out_sems.at[at, k],
            ).start()

    def left(step):
        at = lax.rem(step, BEHIND)
        for k in range(each):
            await_tiles(out_hbm, out_sems.at[at, k])

    def block(step, carry):
        stream.take(step)
        work = []
        for k in range(each):
            place = step * each + k
            pair = pair_at(place)
            values = jnp.concatenate([spots[pair.rows(side), :] for side in range(2)], axis=0)
            values = values.T.astype(jnp.bfloat16)[0:pad]
            work.append((place, pair, values, pair.tables(leg_all[place])))

        for k in range(each):
            _, _, values, tables = work[k]
            for first in range(0, sz.packed, 2):
                count = min(2, sz.packed - first)
                tends = dot(values, tables[:, first * SLAB:(first + count) * SLAB])
                for t in range(first, first + count):
                    for c in range(2):
                        rows = pl.ds(2 * t + c, sz.field_pad, stride=sz.stride)
                        wide[k, rows, :] = tends[
                            c * sz.field_pad:(c + 1) * sz.field_pad, (t - first) * SLAB:(t - first + 1) * SLAB
                        ]

        @pl.when(step >= BEHIND)
        def _():
            left(step)

        at = lax.rem(step, BEHIND)
        for k in range(each):
            place, pair, _, _ = work[k]
            mine = row < pair.split
            degree = jnp.where(mine, row + pair.start, row - 1) * SLAB + lane
            floors = [jnp.where(n < 0, sz.degrees, n) for n in pair.numbers]
            live = degree >= jnp.where(mine, floors[0], floors[1])
            for f in range(sz.fields):
                rows = pl.ds(f * sz.pitch, sz.pitch)
                old = x_all[place, f].astype(jnp.float32)[0:sz.pitch]
                tend = wide[k, pl.ds(f * sz.stride, sz.pitch), :]
                new = (old + time_step * tend) * inverse[pair.start, rows, :]
                out_all[at, k, rows, :] = jnp.where(live, new, 0.0)
        for k in range(each):
            leave(step * each + k, k)
        return carry

    lax.fori_loop(0, sz.steps, block, 0)
    for step in range(max(0, sz.steps - BEHIND), sz.steps):
        left(jnp.int32(step))


def params(mib):
    return pltpu.CompilerParams(vmem_limit_bytes=mib * MIB)


def smem():
    return pl.BlockSpec(memory_space=pltpu.SMEM)


def shards(spectra, legendre, slot_wave, row_points, gauss_weight, layer_depth, mode_speed):
    slots, _, fields, degrees = spectra.shape
    rows = legendre.shape[2]
    sz = Sizes(lax.axis_size("band"), lax.axis_size("lev"), slots, fields, degrees, rows)

    tiled = spectra.reshape(slots, 2, fields, sz.tiles, SLAB)
    tiled = with_layout_constraint(tiled, Layout((0, 2, 3, 1, 4)))
    tiled = tiled.transpose(0, 2, 3, 1, 4)
    tables = legendre.transpose(0, 2, 1)

    rounds = geo_rounds(sz)
    senders = [source for pairs in rounds for source, _ in pairs]
    sums = [sum(rounds, [])] if len(set(senders)) == len(senders) else rounds
    spots_shape = pltpu.VMEM((sz.spots * sz.rows, SLAB), jnp.float32)
    pairs = slots // 2
    stream_scratch = [
        pltpu.VMEM((pairs, fields, sz.pitch_bf16, SLAB), jnp.bfloat16),
        pltpu.VMEM((pairs, rows, sz.packed * SLAB), jnp.bfloat16),
        pltpu.SemaphoreType.DMA((pairs,)),
        pltpu.SemaphoreType.DMA((pairs,)),
    ]
    wide_shape = pltpu.VMEM((sz.block // 2, up_to(sz.field_pad * sz.stride, 8), SLAB), jnp.float32)
    anywhere = pl.BlockSpec(memory_space=pl.ANY)
    vmem = pl.BlockSpec(memory_space=pltpu.VMEM)
    send_shape = (sz.bands, sz.groups, sz.chunk, SLAB)
    geo_shape = (sz.rows // 2, sz.spots, SLAB)

    sent, *geo = pl.pallas_call(
        functools.partial(inverse_kernel, sz, sums),
        in_specs=[smem(), smem(), smem(), smem(), anywhere, anywhere],
        out_specs=[vmem] * (1 + len(sums)),
        out_shape=[jax.ShapeDtypeStruct(send_shape, jnp.bfloat16)]
        + [jax.ShapeDtypeStruct(geo_shape, jnp.bfloat16)] * len(sums),
        scratch_shapes=[wide_shape, spots_shape, pltpu.VMEM((sz.spots, SLAB), jnp.int32), *stream_scratch],
        compiler_params=params(56),
        name="inverse_legendre",
    )(slot_wave, row_points, gauss_weight, layer_depth, tiled, tables)

    sent, points_later, wave_later = lax.optimization_barrier((sent, row_points, slot_wave))
    both = ("band", "lev")
    total = sz.bands * sz.groups
    flat = (total * sz.chunk, SLAB)
    arrived = lax.all_to_all(sent.reshape(flat), both, split_axis=0, concat_axis=0, tiled=True)

    pair_wave = wave_later.reshape(-1, 2)
    even_wave = jnp.where(pair_wave[:, 0] % 2 == 0, pair_wave[:, 0], pair_wave[:, 1])
    even_wave = even_wave.reshape(sz.bands, sz.halves, sz.chunk_live)
    even_wave = jnp.pad(even_wave, ((0, 0), (0, 0), (0, sz.chunk - sz.chunk_live)), constant_values=-1)
    even_wave = even_wave.transpose(1, 0, 2).reshape(sz.pairs)

    high = SLAB if sz.sorted % SLAB == 0 else sz.sorted
    table_rows = 16 + up_to(sz.sorted // 16, 8) + 8
    basis = pl.pallas_call(
        functools.partial(basis_kernel, sz),
        grid=(sz.sorted // high,),
        in_specs=[smem()],
        out_specs=pl.BlockSpec((4, high, sz.orbits), lambda i: (0, i, 0)),
        out_shape=jax.ShapeDtypeStruct((4, sz.sorted, sz.orbits), jnp.bfloat16),
        scratch_shapes=[pltpu.VMEM((table_rows, sz.orbits), jnp.float32)] * 2,
        compiler_params=params(56),
        cost_estimate=pl.CostEstimate(
            flops=20 * sz.sorted * sz.orbits, bytes_accessed=8 * sz.sorted * sz.orbits, transcendentals=0,
        ),
        name="basis",
    )(points_later)

    even_row = even_wave.reshape(1, sz.pairs)
    *geo, arrived, basis, even_row = lax.optimization_barrier((*geo, arrived, basis, even_row))
    moved = [lax.ppermute(geo[turn % len(sums)], "lev", pairs) for turn, pairs in enumerate(rounds)]
    returned = pl.pallas_call(
        functools.partial(grid_kernel, sz),
        in_specs=[smem(), smem(), vmem, vmem, anywhere],
        out_specs=vmem,
        out_shape=jax.ShapeDtypeStruct(send_shape, jnp.bfloat16),
        scratch_shapes=[
            pltpu.VMEM((4, sz.sorted, sz.orbits), jnp.bfloat16),
            pltpu.VMEM((4, SLAB, sz.orbits), jnp.bfloat16),
            pltpu.SemaphoreType.DMA((-(-sz.orbits // (2 * SLAB)),)),
        ],
        compiler_params=params(56),
        cost_estimate=pl.CostEstimate(
            flops=4 * 4 * SLAB * sz.sorted * sz.orbits, bytes_accessed=8 * sz.sorted * sz.orbits, transcendentals=0,
        ),
        name="grid_products",
    )(
        row_points, gauss_weight, arrived.reshape(send_shape), even_row, basis,
    )
    *moved, returned, wave_last = lax.optimization_barrier((*moved, returned, slot_wave))

    back = lax.all_to_all(returned.reshape(flat), both, split_axis=0, concat_axis=0, tiled=True)

    out_shape = jax.ShapeDtypeStruct(tiled.shape, jnp.float32)
    zeroed = pl.pallas_call(
        functools.partial(zeros_kernel, sz),
        in_specs=[smem()],
        out_specs=anywhere,
        out_shape=out_shape,
        scratch_shapes=[
            pltpu.VMEM((fields, sz.tiles - 1, 2, SLAB), jnp.float32),
            pltpu.SemaphoreType.DMA((pairs,)),
        ],
        compiler_params=params(56),
        cost_estimate=pl.CostEstimate(
            flops=0, bytes_accessed=2 * slots * fields * degrees * 2, transcendentals=0,
        ),
        name="dead_zeros",
    )(wave_last)
    out = pl.pallas_call(
        functools.partial(forward_kernel, sz),
        in_specs=[smem(), smem()] + [vmem] * (1 + len(rounds)) + [anywhere] * 3,
        out_specs=anywhere,
        out_shape=out_shape,
        input_output_aliases={5 + len(rounds): 0},
        scratch_shapes=[
            wide_shape, spots_shape,
            pltpu.VMEM((sz.tiles, fields * sz.pitch, SLAB), jnp.float32),
            pltpu.VMEM((BEHIND, sz.block // 2, fields * sz.pitch, SLAB), jnp.float32),
            pltpu.SemaphoreType.DMA((BEHIND, sz.block // 2)),
            *stream_scratch,
        ],
        compiler_params=params(56),
        name="forward_legendre",
    )(slot_wave, mode_speed, back.reshape(send_shape), *moved, tiled, tables, zeroed)

    out = out.transpose(0, 1, 3, 2, 4)
    return out.reshape(slots, fields, 2, degrees).transpose(0, 2, 1, 3)


def solution(mesh):
    return jax.shard_map(
        shards,
        mesh=mesh,
        in_specs=(
            P("band", None, "lev", None),
            P("band", None, None),
            P(),
            P(),
            P(),
            P(),
            P("lev"),
        ),
        out_specs=P("band", None, "lev", None),
        check_vma=False,
    )
```

```python
import functools
import math

import jax
import jax.numpy as jnp
from jax import lax
from jax.experimental import pallas as pl
from jax.experimental.layout import Layout, with_layout_constraint
from jax.experimental.pallas import tpu as pltpu
from jax.sharding import PartitionSpec as P

FIELDS = 5
LEVELS = 24
TEMPER = 2
ENERGY = 4
LVL_ROWS = 8
SLAB = 128
MIB = 1024 * 1024

time_step = 1.0

COS_POLY = (
    0.9999999890590235, -19.739204499453994, 64.93911745989843, -85.45013953092186,
    60.167630951185615, -25.967599249120923, 6.528658161956132,
)
SIN_POLY = (
    6.283185302511506, -41.3417004053176, 81.60513138579954, -76.70301535389986,
    42.02592698629647, -14.89984666973851, 3.2381375126489513,
)


def up_to(value, unit):
    return -(-value // unit) * unit


class Sizes:
    def __init__(self, bands, groups, slots, fields, degrees, rows):
        self.bands, self.groups = bands, groups
        self.slots, self.fields, self.degrees, self.rows = slots, fields, degrees, rows
        self.tiles = degrees // SLAB
        self.packed = self.tiles + 1
        self.pitch = up_to(2 * self.packed, 8)
        self.stride = self.pitch + 1
        self.pitch_bf16 = up_to(2 * self.packed, 16)
        self.slot_rows = fields * self.tiles * 2
        self.field_pad = up_to(fields, 8)
        self.share = -(-fields // groups)
        self.lanes = 4 * self.share
        self.quarters = 2
        if 4 * self.lanes <= SLAB and slots % 4 == 0:
            self.quarters = 4
        self.halves = self.quarters // 2
        self.chunk_live = slots // self.quarters
        self.chunk = up_to(self.chunk_live, 8)
        self.spots = self.quarters * self.chunk
        self.plane = self.spots | 1
        self.block = slots
        for size in (8, 4):
            if slots % size == 0 and (size * self.slot_rows) % 16 == 0:
                self.block = size
                break
        self.steps = slots // self.block
        self.pairs = self.halves * bands * self.chunk
        self.trunc = degrees - 1
        self.sorted = degrees // 2
        self.orbits = up_to((4 * self.trunc + 40) // 4 + 2, SLAB)
        self.levels = LEVELS // groups


def owners(sizes, field):
    first, last = field * LEVELS, (field + 1) * LEVELS
    return [
        g for g in range(sizes.groups)
        if g * sizes.fields < last and (g + 1) * sizes.fields > first
    ]


def geo_rounds(sizes):
    sources, targets = owners(sizes, TEMPER), owners(sizes, ENERGY)
    wide = max(len(sources), len(targets))
    rounds = []
    for turn in range(wide):
        pairs = []
        for k in range(wide):
            s, t = k, (k + turn) % wide
            if s < len(sources) and t < len(targets):
                pairs.append((sources[s], targets[t]))
        if pairs:
            rounds.append(pairs)
    return rounds


def iota(shape, dim):
    return lax.broadcasted_iota(jnp.int32, shape, dim)


def one_hot(cond):
    return jnp.where(cond, 1.0, 0.0).astype(jnp.bfloat16)


def dot(a, b, dims=((1,), (0,))):
    return lax.dot_general(a, b, (dims, ((), ())), preferred_element_type=jnp.float32)


def halving(value):
    return value.bit_length() - 1 if value & (value - 1) == 0 else None


def quotient(x, by):
    bits = halving(by)
    return x >> bits if bits is not None else lax.div(x, jnp.int32(by))


def remainder(x, by):
    return x & (by - 1) if halving(by) is not None else lax.rem(x, jnp.int32(by))


def spread_matrix(sizes, lev):
    sz = sizes
    tall = sz.quarters * 4 * sz.field_pad
    wide = sz.groups * SLAB
    dst = iota((1, wide), 1)
    group = quotient(dst, SLAB)
    lane = remainder(dst, SLAB)
    quarter = quotient(lane, sz.lanes)
    rest = remainder(lane, sz.lanes)
    row = quotient(rest, 2 * sz.share)
    rest = remainder(rest, 2 * sz.share)
    comp = quotient(rest, sz.share)
    item = remainder(rest, sz.share)
    start = remainder(lev * sz.fields, sz.groups)
    field = remainder(group - start + sz.groups, sz.groups) + sz.groups * item
    want = ((quarter * 2 + row) * 2 + comp) * sz.field_pad + field
    want = jnp.where((field < sz.fields) & (quarter < sz.quarters), want, -1)
    return one_hot(iota((tall, wide), 0) == want)


def spot_of(sizes, place, odd):
    half = place // sizes.chunk_live
    return (odd * sizes.halves + half) * sizes.chunk + (place - half * sizes.chunk_live)


class Pair:
    def __init__(self, sizes, wave, band, place):
        self.sizes, self.place = sizes, place
        slot = band * sizes.slots + 2 * place
        self.numbers = wave[slot], wave[slot + 1]
        odd = self.numbers[0] & 1
        self.odds = odd, 1 - odd
        self.start = quotient(jnp.maximum(self.numbers[0], 0), SLAB)
        self.split = sizes.tiles - self.start

    def spot(self, side):
        sz = self.sizes
        half = self.place // sz.chunk_live
        first = (self.odds[side] * sz.halves + half) * sz.chunk
        return first + (self.place - half * sz.chunk_live)

    def rows(self, side):
        return pl.ds(self.spot(side), self.sizes.rows, stride=self.sizes.plane)

    def tile(self, k):
        return jnp.where(k < self.split, self.start + k, k - 1)

    def columns(self):
        place = iota((1, self.sizes.packed * SLAB), 1)
        first = place < self.split * SLAB
        degree = jnp.where(first, place + self.start * SLAB, place - SLAB)
        floors = [jnp.where(n < 0, self.sizes.degrees, n) for n in self.numbers]
        return first, degree >= jnp.where(first, floors[0], floors[1])

    def parts(self):
        tiles = self.sizes.tiles
        first = 2 * self.place
        return (
            (first, self.start, self.split, 0),
            (first + 1, self.split - 1, tiles + 1 - self.split, self.split),
        )

    def tables(self, leg):
        first, live = self.columns()
        leg = leg.astype(jnp.float32)
        own = jnp.where(first & live, leg, 0.0)
        other = jnp.where(first, 0.0, jnp.where(live, leg, 0.0))
        return jnp.concatenate([own, other], axis=0).astype(jnp.bfloat16)


AHEAD = 4
BEHIND = 4


def span(first, count, unit):
    return pl.ds(pl.multiple_of(first * unit, unit), pl.multiple_of(count * unit, unit))


def await_tiles(hbm, sem):
    for some in (hbm.at[0], hbm.at[0, :, pl.ds(0, 1)]):
        pltpu.make_async_copy(some, some, sem).wait()


class Stream:
    def __init__(self, sizes, pair_at, x_hbm, leg_hbm, x_all, leg_all, x_sems, leg_sems):
        self.sizes, self.pair_at = sizes, pair_at
        self.x_hbm, self.leg_hbm, self.x_all, self.leg_all = x_hbm, leg_hbm, x_all, leg_all
        self.x_sems, self.leg_sems = x_sems, leg_sems

    def start(self, place):
        sz = self.sizes
        x_rows = self.x_hbm.reshape(sz.slots, sz.fields, 2 * sz.tiles, SLAB)
        for slot, first, count, here in self.pair_at(place).parts():
            pltpu.make_async_copy(
                x_rows.at[slot, :, span(first, count, 2)],
                self.x_all.at[place, :, span(here, count, 2)],
                self.x_sems.at[place],
            ).start()
            pltpu.make_async_copy(
                self.leg_hbm.at[slot, :, span(first, count, SLAB)],
                self.leg_all.at[place, :, span(here, count, SLAB)],
                self.leg_sems.at[place],
            ).start()

    def begin(self, turn=0):
        each = self.sizes.block // 2
        first, last = (min((turn + k) * AHEAD, self.sizes.steps) * each for k in range(2))

        def one(place, carry):
            self.start(place)
            return carry

        lax.fori_loop(first, last, one, 0)
        self.ahead = (turn + 1) * AHEAD

    def take(self, step):
        each = self.sizes.block // 2

        @pl.when(step + self.ahead < self.sizes.steps)
        def _():
            for k in range(each):
                self.start((step + self.ahead) * each + k)

        for k in range(each):
            place = step * each + k
            await_tiles(self.x_hbm, self.x_sems.at[place])
            here = self.leg_all.at[place]
            pltpu.make_async_copy(here, here, self.leg_sems.at[place]).wait()


def inverse_kernel(sizes, rounds, wave, points, gauss, layer_depth, x_hbm, leg_hbm, send_ref, *refs):
    sz = sizes
    geo_refs = refs[:len(rounds)]
    wide, spots, numbers, x_all, leg_all, *sems = refs[len(rounds):]
    band = lax.axis_index("band")
    lev = lax.axis_index("lev")
    pair_at = functools.partial(Pair, sz, wave, band)
    stream = Stream(sz, pair_at, x_hbm, leg_hbm, x_all, leg_all, *sems)
    stream.begin()
    pad = 2 * sz.field_pad
    spots[...] = jnp.zeros_like(spots)
    numbers[...] = jnp.full_like(numbers, -1)
    wide[...] = jnp.zeros_like(wide)

    def block(step, carry):
        stream.take(step)
        found = []
        for k in range(sz.block // 2):
            place = step * (sz.block // 2) + k
            for f in range(sz.fields):
                rows = x_all[place, f].astype(jnp.float32)
                wide[k, pl.ds(f * sz.stride, sz.pitch), :] = rows[0:sz.pitch]
        empty = jnp.zeros((sz.rows, SLAB - pad), jnp.float32)
        for k in range(sz.block // 2):
            place = step * (sz.block // 2) + k
            pair = pair_at(place)
            values = jnp.concatenate([
                jnp.concatenate([
                    wide[k, pl.ds(2 * t + c, sz.field_pad, stride=sz.stride), :] for c in range(2)
                ], axis=0).astype(jnp.bfloat16)
                for t in range(sz.packed)
            ], axis=1)
            total = dot(pair.tables(leg_all[place]), values, ((1,), (1,)))
            for side in range(2):
                own = total[side * sz.rows:(side + 1) * sz.rows]
                found.append((pair, side, jnp.concatenate([own, empty], axis=1)))
        for pair, side, total in found:
            spots[pair.rows(side), :] = total
            number = jnp.full((1, SLAB), pair.numbers[side], jnp.int32)
            numbers[pl.ds(pair.spot(side), 1), :] = number
        return carry

    lax.fori_loop(0, sz.steps, block, 0)
    spread = spread_matrix(sz, lev)
    shape = (2 * pad, SLAB)
    src, dst = iota(shape, 0), iota(shape, 1)
    bits = sz.field_pad.bit_length() - 1
    from_field, from_side = src & (sz.field_pad - 1), src >> bits
    to_field, to_side = dst & (sz.field_pad - 1), dst >> bits
    weights = []
    for pairs in rounds:
        first = jnp.int32(2 * LEVELS + sz.fields)
        for source, target in pairs:
            first = jnp.where(lev == source, target * sz.fields - ENERGY * LEVELS, first)
        under = lev * sz.fields + from_field - TEMPER * LEVELS
        above = first + to_field
        hit = (
            (from_side == to_side)
            & (from_field < sz.fields) & (to_field < sz.fields)
            & (above >= 0) & (above <= under)
        )
        weight = jnp.zeros(shape, jnp.float32)
        for level in range(LEVELS):
            weight = jnp.where(hit & (under == level), layer_depth[level], weight)
        high = weight.astype(jnp.bfloat16)
        low = (weight - high.astype(jnp.float32)).astype(jnp.bfloat16)
        weights.append(jnp.concatenate([high, low], axis=0))
    number = numbers[...]
    lane = iota((sz.spots, SLAB), 1)
    known = (number >= 0) & ~((number == 0) & (lane & sz.field_pad != 0))
    exacts, cuts, scales = [], [], []
    for rp in range(sz.rows // 2):
        exact = jnp.concatenate([
            spots[pl.ds((2 * rp + r) * sz.plane, sz.spots), :][:, 0:pad] for r in range(2)
        ], axis=1)
        cuts.append(jnp.concatenate([
            exact[q * sz.chunk:(q + 1) * sz.chunk] for q in range(sz.quarters)
        ], axis=1))
        exacts.append(exact)
        count = jnp.where(lane < pad, points[2 * rp], points[2 * rp + 1])
        scale = jnp.where(lane < pad, gauss[2 * rp], gauss[2 * rp + 1])
        scales.append(jnp.where(known & (2 * number <= count - 1), scale, 0.0))
    chunks = dot(jnp.concatenate(cuts, axis=0).astype(jnp.bfloat16), spread)
    exact = jnp.concatenate(exacts, axis=0).astype(jnp.bfloat16)
    double = jnp.concatenate([exact, exact], axis=1)
    for turn in range(len(rounds)):
        sums = dot(double, weights[turn])
        for rp in range(sz.rows // 2):
            own = sums[rp * sz.spots:(rp + 1) * sz.spots] * scales[rp]
            geo_refs[turn][rp] = own.astype(jnp.bfloat16)
    for rp in range(sz.rows // 2):
        for g in range(sz.groups):
            chunk = chunks[rp * sz.chunk:(rp + 1) * sz.chunk, g * SLAB:(g + 1) * SLAB]
            send_ref[rp, g] = chunk.astype(jnp.bfloat16)


def cos_sin(z):
    y = z * z
    c = jnp.full_like(y, COS_POLY[-1])
    for a in COS_POLY[-2::-1]:
        c = c * y + a
    s = jnp.full_like(y, SIN_POLY[-1])
    for a in SIN_POLY[-2::-1]:
        s = s * y + a
    return c, s * z


def basis_kernel(sizes, points, out_hbm, out_all, cosines, sines, sems):
    sz = sizes
    turns = sz.sorted // 16
    bands_row = 16 + up_to(turns, 8)

    first = lax.axis_index("band") * 2
    length_a, length_b = points[first], points[first + 1]
    count_a = length_a // 4 + 1
    high = cosines.shape[0]
    row = iota((high, SLAB), 0)
    number = jnp.where(row < 16, 2 * row, jnp.where(row < bands_row, 32 * (row - 16), sz.trunc))
    number = number.astype(jnp.float32)
    for at in range(0, sz.orbits, SLAB):
        place = iota((1, SLAB), 1) + at
        second = place >= count_a
        column = (place - jnp.where(second, count_a, 0)).astype(jnp.float32)
        length = jnp.where(second, length_b, length_a).astype(jnp.float32)
        inverse = 1.0 / length
        scale = jnp.where(row < 16, 1.0 / jnp.sqrt(length), 1.0)
        product = number * column
        whole = jnp.floor(product * inverse + 0.5)
        c, s = cos_sin((product - whole * length) * inverse)
        cosines[:, pl.ds(at, SLAB)] = c * scale
        sines[:, pl.ds(at, SLAB)] = s * scale

    steps, _, tall, _ = out_all.shape
    groups = tall // 16

    def leave(step):
        rows = pl.ds(pl.multiple_of(step * tall, tall), tall)
        return pltpu.make_async_copy(out_all.at[step], out_hbm.at[:, rows], sems.at[step])

    def part(step, carry):
        out_ref = out_all.at[step]
        for at in range(0, sz.orbits, SLAB):
            cols = pl.ds(at, SLAB)
            base_c, base_n = cosines[0:16, cols], -sines[0:16, cols]
            top_c, top_n = cosines[pl.ds(bands_row, 1), cols], -sines[pl.ds(bands_row, 1), cols]
            turn_rows = pl.ds(pl.multiple_of(16 + step * groups, 8), groups)
            all_c, all_s = cosines[turn_rows, cols], sines[turn_rows, cols]
            for k in range(groups):
                turn_c, turn_s = all_c[k:k + 1], all_s[k:k + 1]
                c = turn_c * base_c + turn_s * base_n
                n = turn_c * base_n - turn_s * base_c
                rows = pl.ds(16 * k, 16)
                out_ref[0, rows, cols] = c.astype(jnp.bfloat16)
                out_ref[1, rows, cols] = n.astype(jnp.bfloat16)
                out_ref[2, rows, cols] = (top_c * c + top_n * n).astype(jnp.bfloat16)
                out_ref[3, rows, cols] = (top_n * c - top_c * n).astype(jnp.bfloat16)
        leave(step).start()
        return carry

    lax.fori_loop(0, steps, part, 0)
    for step in range(steps):
        leave(jnp.int32(step)).wait()


def take_matrix(sizes, lev):
    sz = sizes
    tall = sz.groups * SLAB
    wide = sz.quarters * 2 * SLAB
    dst = iota((1, wide), 1)
    piece = quotient(dst, SLAB)
    lane = remainder(dst, SLAB)
    row = quotient(lane, SLAB // 2)
    field = quotient(remainder(lane, SLAB // 2), LVL_ROWS)
    level = remainder(lane, LVL_ROWS)
    whole = field * LEVELS + level * sz.groups + lev
    owner = quotient(whole, sz.fields)
    start = owner * sz.fields
    first = remainder(lev - remainder(start, sz.groups) + sz.groups, sz.groups)
    item = quotient(whole - start - first, sz.groups)
    want = owner * SLAB + (piece >> 1) * sz.lanes + (row * 2 + (piece & 1)) * sz.share + item
    want = jnp.where((field < FIELDS) & (level < sz.levels), want, -1)
    return one_hot(iota((tall, wide), 0) == want)


def grid_kernel(
    sizes, points, gauss, recv_ref, even_row, basis_hbm, send_ref, basis, terms, arrivals,
):
    sz = sizes
    step = 2 * SLAB
    parts = -(-sz.orbits // step)
    copies = []
    for part in range(parts):
        cols = pl.ds(part * step, min(step, sz.orbits - part * step))
        copies.append(pltpu.make_async_copy(basis_hbm.at[:, :, cols], basis.at[:, :, cols], arrivals.at[part]))
        copies[-1].start()
    lev = lax.axis_index("lev")
    first_row = lax.axis_index("band") * 2
    length_a, length_b = points[first_row], points[first_row + 1]
    count_a, count_b = length_a // 4 + 1, length_b // 4 + 1
    high = FIELDS * LVL_ROWS
    half_slab = SLAB // 2
    width = sz.bands * sz.chunk
    take = take_matrix(sz, lev)
    order = one_hot(iota((sz.sorted, sz.pairs), 0) * 2 == even_row[...])
    joined = jnp.concatenate([
        recv_ref[:, g].astype(jnp.float32).reshape(width, SLAB) for g in range(sz.groups)
    ], axis=1).astype(jnp.bfloat16)
    taken = dot(joined, take)
    coeffs = []
    number = iota((2 * SLAB, sz.sorted), 1) * 2
    bound = jnp.where(iota((2 * SLAB, sz.sorted), 0) & half_slab == 0, length_a, length_b) - 1
    kept = (0, half_slab, SLAB, SLAB + half_slab)
    sources = []
    for parity in range(2):
        rows = []
        for half in range(sz.halves):
            piece = (parity * sz.halves + half) * 2
            rows.append(taken[:, piece * SLAB:(piece + 2) * SLAB])
        sources.append(jnp.concatenate(rows, axis=0).T)
    ordered = dot(jnp.concatenate(sources, axis=0).astype(jnp.bfloat16), order, ((1,), (1,)))
    for parity in range(2):
        placed = ordered[parity * 2 * SLAB:(parity + 1) * 2 * SLAB]
        mine = number if parity == 0 else sz.trunc - number
        mult = jnp.where(mine == 0, 1.0, 2.0)
        placed = jnp.where(2 * mine <= bound, placed * mult, 0.0)
        placed = jnp.concatenate([placed[k:k + high] for k in kept], axis=0).astype(jnp.bfloat16)
        coeffs += [placed[:2 * high], placed[2 * high:]]
    for part in range(parts):
        copies[part].wait()
        at = part * step
        many = min(step, sz.orbits - at)
        cols = pl.ds(at, many)
        place = iota((1, many), 1) + at
        second = place >= count_a
        grids = []
        for k in range(4):
            both = dot(coeffs[k], basis[k, :, cols])
            grids.append(jnp.where(second, both[high:], both[:high]))
        ce, se, co, so = grids
        plus, minus = ce + co, ce - co
        splus, sminus = se + so, se - so
        values = (plus + splus, minus - sminus, minus + sminus, plus - splus)
        outs = []
        for v in values:
            u, w, tem, hum, ozo = (v[i * LVL_ROWS:(i + 1) * LVL_ROWS] for i in range(FIELDS))
            outs.append(jnp.concatenate(
                [u * tem, w * tem, u * hum, w * ozo, 0.5 * (u * u + w * w)], axis=0
            ))
        offset = place - jnp.where(second, count_a, 0)
        count = jnp.where(second, count_b, count_a)
        weight = jnp.where((offset == 0) | (offset == count - 1), 0.5, 1.0)
        weight = jnp.where(offset < count, weight, 0.0)
        t0, t1, t2, t3 = (o * weight for o in outs)
        a, b, c, d = t0 + t3, t1 + t2, t0 - t3, t2 - t1
        folds = (a + b, c + d, a - b, c - d)
        empty = jnp.zeros((half_slab - high, many), jnp.float32)
        for k in range(4):
            first = jnp.where(second, 0.0, folds[k])
            last = jnp.where(second, folds[k], 0.0)
            terms[k, :, cols] = jnp.concatenate([first, empty, last, empty], axis=0).astype(jnp.bfloat16)
    lane = iota((1, SLAB), 1)
    scale = jnp.where(lane < half_slab, gauss[first_row], gauss[first_row + 1])
    bound = jnp.where(lane < half_slab, length_a, length_b) - 1
    number = iota((sz.sorted, SLAB), 0) * 2
    even_col = jnp.broadcast_to(even_row[...].astype(jnp.float32), (8, sz.pairs)).T[:, 0:1]
    back_order = one_hot(iota((sz.pairs, sz.sorted), 1) * 2 == even_col.astype(jnp.int32))
    sums = []
    for parity in range(2):
        mine = number if parity == 0 else sz.trunc - number
        for k in (2 * parity, 2 * parity + 1):
            total = dot(basis[k], terms[k], ((1,), (1,))) * scale
            sums.append(jnp.where(2 * mine <= bound, total, 0.0).astype(jnp.bfloat16))
    slots = dot(back_order, jnp.concatenate(sums, axis=1)).astype(jnp.bfloat16)
    pieces = [
        slots[half * width:(half + 1) * width, 2 * parity * SLAB:2 * (parity + 1) * SLAB]
        for parity in range(2) for half in range(sz.halves)
    ]
    sent = dot(jnp.concatenate(pieces, axis=1), take, ((1,), (1,)))
    for g in range(sz.groups):
        part = sent[:, g * SLAB:(g + 1) * SLAB].reshape(sz.bands, sz.chunk, SLAB)
        send_ref[:, g] = part.astype(jnp.bfloat16)


def zeros_kernel(sizes, wave, out_hbm, zeros, sems):
    sz = sizes
    band = lax.axis_index("band")
    zeros[...] = jnp.zeros_like(zeros)

    def one(place, carry):
        pair = Pair(sz, wave, band, place)
        for side, count in ((0, pair.start), (1, pair.split - 1)):

            @pl.when(count > 0)
            def _():
                pltpu.make_async_copy(
                    zeros.at[:, pl.ds(0, count)],
                    out_hbm.at[2 * place + side, :, pl.ds(0, count)],
                    sems.at[place],
                ).start()

        return carry

    def done(place, carry):
        pltpu.make_async_copy(zeros, zeros, sems.at[place]).wait()
        return carry

    lax.fori_loop(0, sz.slots // 2, one, 0)
    lax.fori_loop(0, sz.slots // 2, done, 0)


def forward_kernel(sizes, wave, speed, back_ref, *refs):
    sz = sizes
    geo_refs = refs[:-13]
    x_hbm, leg_hbm, _, out_hbm, wide, spots, inverse, out_all, out_sems, x_all, leg_all, *sems = refs[-13:]
    band = lax.axis_index("band")
    pair_at = functools.partial(Pair, sz, wave, band)
    stream = Stream(sz, pair_at, x_hbm, leg_hbm, x_all, leg_all, *sems)
    stream.begin()
    pad = 2 * sz.field_pad
    each = sz.block // 2

    gather = spread_matrix(sz, lax.axis_index("lev"))
    cuts = [
        jnp.concatenate([back_ref[rp, g].astype(jnp.float32) for g in range(sz.groups)], axis=1)
        for rp in range(sz.rows // 2)
    ]
    wholes = dot(jnp.concatenate(cuts, axis=0).astype(jnp.bfloat16), gather, ((1,), (1,)))
    for rp in range(sz.rows // 2):
        whole = wholes[rp * sz.chunk:(rp + 1) * sz.chunk]
        rows = jnp.concatenate([
            whole[:, q * 2 * pad:(q + 1) * 2 * pad] for q in range(sz.quarters)
        ], axis=0)
        for geo_ref in geo_refs:
            rows = rows + geo_ref[rp].astype(jnp.float32)[:, 0:2 * pad]
        for r in range(2):
            part = rows[:, r * pad:(r + 1) * pad]
            part = jnp.concatenate([part, jnp.zeros((sz.spots, SLAB - pad), jnp.float32)], axis=1)
            spots[pl.ds((2 * rp + r) * sz.plane, sz.spots), :] = part
    stream.begin(1)
    row = quotient(iota((sz.pitch, SLAB), 0), 2)
    lane = iota((sz.pitch, SLAB), 1)
    for start in range(sz.tiles):
        degree = jnp.where(row < sz.tiles - start, row + start, row - 1) * SLAB + lane
        helm = (degree * (degree + 1)).astype(jnp.float32) / float(sz.trunc * (sz.trunc + 1))
        for f in range(sz.fields):
            denominator = 1.0 + time_step * time_step * helm * speed[f]
            inverse[start, pl.ds(f * sz.pitch, sz.pitch), :] = 1.0 / denominator
    stream.begin(2)
    out_tiles = out_all.reshape(BEHIND, each, sz.fields, sz.pitch // 2, 2, SLAB)

    def leave(place, k):
        at = lax.rem(place // each, BEHIND)

        for slot, first, count, here in pair_at(place).parts():
            pltpu.make_async_copy(
                out_tiles.at[at, k, :, pl.ds(here, count)],
                out_hbm.at[slot, :, pl.ds(first, count)],
                out_sems.at[at, k],
            ).start()

    def left(step):
        at = lax.rem(step, BEHIND)
        for k in range(each):
            await_tiles(out_hbm, out_sems.at[at, k])

    def block(step, carry):
        stream.take(step)
        work = []
        for k in range(each):
            place = step * each + k
            pair = pair_at(place)
            values = jnp.concatenate([spots[pair.rows(side), :] for side in range(2)], axis=0)
            values = values.T.astype(jnp.bfloat16)[0:pad]
            work.append((place, pair, values, pair.tables(leg_all[place])))

        for k in range(each):
            _, _, values, tables = work[k]
            for first in range(0, sz.packed, 2):
                count = min(2, sz.packed - first)
                tends = dot(values, tables[:, first * SLAB:(first + count) * SLAB])
                for t in range(first, first + count):
                    for c in range(2):
                        rows = pl.ds(2 * t + c, sz.field_pad, stride=sz.stride)
                        wide[k, rows, :] = tends[
                            c * sz.field_pad:(c + 1) * sz.field_pad, (t - first) * SLAB:(t - first + 1) * SLAB
                        ]

        @pl.when(step >= BEHIND)
        def _():
            left(step)

        at = lax.rem(step, BEHIND)
        for k in range(each):
            place, pair, _, _ = work[k]
            mine = row < pair.split
            degree = jnp.where(mine, row + pair.start, row - 1) * SLAB + lane
            floors = [jnp.where(n < 0, sz.degrees, n) for n in pair.numbers]
            live = degree >= jnp.where(mine, floors[0], floors[1])
            for f in range(sz.fields):
                rows = pl.ds(f * sz.pitch, sz.pitch)
                old = x_all[place, f].astype(jnp.float32)[0:sz.pitch]
                tend = wide[k, pl.ds(f * sz.stride, sz.pitch), :]
                new = (old + time_step * tend) * inverse[pair.start, rows, :]
                out_all[at, k, rows, :] = jnp.where(live, new, 0.0)
        for k in range(each):
            leave(step * each + k, k)
        return carry

    lax.fori_loop(0, sz.steps, block, 0)
    for step in range(max(0, sz.steps - BEHIND), sz.steps):
        left(jnp.int32(step))


def params(mib):
    return pltpu.CompilerParams(vmem_limit_bytes=mib * MIB)


def smem():
    return pl.BlockSpec(memory_space=pltpu.SMEM)


def shards(spectra, legendre, slot_wave, row_points, gauss_weight, layer_depth, mode_speed):
    slots, _, fields, degrees = spectra.shape
    rows = legendre.shape[2]
    sz = Sizes(lax.axis_size("band"), lax.axis_size("lev"), slots, fields, degrees, rows)

    tiled = spectra.reshape(slots, 2, fields, sz.tiles, SLAB)
    tiled = with_layout_constraint(tiled, Layout((0, 2, 3, 1, 4)))
    tiled = tiled.transpose(0, 2, 3, 1, 4)
    tables = legendre.transpose(0, 2, 1)

    rounds = geo_rounds(sz)
    senders = [source for pairs in rounds for source, _ in pairs]
    sums = [sum(rounds, [])] if len(set(senders)) == len(senders) else rounds
    spots_shape = pltpu.VMEM((up_to(sz.plane * sz.rows, 8), SLAB), jnp.float32)
    pairs = slots // 2
    stream_scratch = [
        pltpu.VMEM((pairs, fields, sz.pitch_bf16, SLAB), jnp.bfloat16),
        pltpu.VMEM((pairs, rows, sz.packed * SLAB), jnp.bfloat16),
        pltpu.SemaphoreType.DMA((pairs,)),
        pltpu.SemaphoreType.DMA((pairs,)),
    ]
    wide_shape = pltpu.VMEM((sz.block // 2, up_to(sz.field_pad * sz.stride, 8), SLAB), jnp.float32)
    anywhere = pl.BlockSpec(memory_space=pl.ANY)
    vmem = pl.BlockSpec(memory_space=pltpu.VMEM)
    send_shape = (sz.bands, sz.groups, sz.chunk, SLAB)
    geo_shape = (sz.rows // 2, sz.spots, SLAB)

    sent, *geo = pl.pallas_call(
        functools.partial(inverse_kernel, sz, sums),
        in_specs=[smem(), smem(), smem(), smem(), anywhere, anywhere],
        out_specs=[vmem] * (1 + len(sums)),
        out_shape=[jax.ShapeDtypeStruct(send_shape, jnp.bfloat16)]
        + [jax.ShapeDtypeStruct(geo_shape, jnp.bfloat16)] * len(sums),
        scratch_shapes=[wide_shape, spots_shape, pltpu.VMEM((sz.spots, SLAB), jnp.int32), *stream_scratch],
        compiler_params=params(56),
        name="inverse_legendre",
    )(slot_wave, row_points, gauss_weight, layer_depth, tiled, tables)

    sent, points_later, wave_later = lax.optimization_barrier((sent, row_points, slot_wave))
    both = ("band", "lev")
    total = sz.bands * sz.groups
    flat = (total * sz.chunk, SLAB)
    arrived = lax.all_to_all(sent.reshape(flat), both, split_axis=0, concat_axis=0, tiled=True)

    pair_wave = wave_later.reshape(-1, 2)
    even_wave = jnp.where(pair_wave[:, 0] % 2 == 0, pair_wave[:, 0], pair_wave[:, 1])
    even_wave = even_wave.reshape(sz.bands, sz.halves, sz.chunk_live)
    even_wave = jnp.pad(even_wave, ((0, 0), (0, 0), (0, sz.chunk - sz.chunk_live)), constant_values=-1)
    even_wave = even_wave.transpose(1, 0, 2).reshape(sz.pairs)

    high = SLAB if sz.sorted % SLAB == 0 else sz.sorted
    table_rows = 16 + up_to(sz.sorted // 16, 8) + 8
    basis = pl.pallas_call(
        functools.partial(basis_kernel, sz),
        in_specs=[smem()],
        out_specs=anywhere,
        out_shape=jax.ShapeDtypeStruct((4, sz.sorted, sz.orbits), jnp.bfloat16),
        scratch_shapes=[
            pltpu.VMEM((sz.sorted // high, 4, high, sz.orbits), jnp.bfloat16),
            pltpu.VMEM((table_rows, sz.orbits), jnp.float32),
            pltpu.VMEM((table_rows, sz.orbits), jnp.float32),
            pltpu.SemaphoreType.DMA((sz.sorted // high,)),
        ],
        compiler_params=params(56),
        cost_estimate=pl.CostEstimate(
            flops=20 * sz.sorted * sz.orbits, bytes_accessed=8 * sz.sorted * sz.orbits, transcendentals=0,
        ),
        name="basis",
    )(points_later)

    even_row = even_wave.reshape(1, sz.pairs)
    moved = [lax.ppermute(geo[turn % len(sums)], "lev", pairs) for turn, pairs in enumerate(rounds)]
    *moved, arrived, basis, even_row = lax.optimization_barrier((*moved, arrived, basis, even_row))
    returned = pl.pallas_call(
        functools.partial(grid_kernel, sz),
        in_specs=[smem(), smem(), vmem, vmem, anywhere],
        out_specs=vmem,
        out_shape=jax.ShapeDtypeStruct(send_shape, jnp.bfloat16),
        scratch_shapes=[
            pltpu.VMEM((4, sz.sorted, sz.orbits), jnp.bfloat16),
            pltpu.VMEM((4, SLAB, sz.orbits), jnp.bfloat16),
            pltpu.SemaphoreType.DMA((-(-sz.orbits // (2 * SLAB)),)),
        ],
        compiler_params=params(56),
        cost_estimate=pl.CostEstimate(
            flops=4 * 4 * SLAB * sz.sorted * sz.orbits, bytes_accessed=8 * sz.sorted * sz.orbits, transcendentals=0,
        ),
        name="grid_products",
    )(
        row_points, gauss_weight, arrived.reshape(send_shape), even_row, basis,
    )
    returned, wave_last = lax.optimization_barrier((returned, slot_wave))

    back = lax.all_to_all(returned.reshape(flat), both, split_axis=0, concat_axis=0, tiled=True)

    out_shape = jax.ShapeDtypeStruct(tiled.shape, jnp.float32)
    zeroed = pl.pallas_call(
        functools.partial(zeros_kernel, sz),
        in_specs=[smem()],
        out_specs=anywhere,
        out_shape=out_shape,
        scratch_shapes=[
            pltpu.VMEM((fields, sz.tiles - 1, 2, SLAB), jnp.float32),
            pltpu.SemaphoreType.DMA((pairs,)),
        ],
        compiler_params=params(56),
        cost_estimate=pl.CostEstimate(
            flops=0, bytes_accessed=2 * slots * fields * degrees * 2, transcendentals=0,
        ),
        name="dead_zeros",
    )(wave_last)
    out = pl.pallas_call(
        functools.partial(forward_kernel, sz),
        in_specs=[smem(), smem()] + [vmem] * (1 + len(rounds)) + [anywhere] * 3,
        out_specs=anywhere,
        out_shape=out_shape,
        input_output_aliases={5 + len(rounds): 0},
        scratch_shapes=[
            wide_shape, spots_shape,
            pltpu.VMEM((sz.tiles, fields * sz.pitch, SLAB), jnp.float32),
            pltpu.VMEM((BEHIND, sz.block // 2, fields * sz.pitch, SLAB), jnp.float32),
            pltpu.SemaphoreType.DMA((BEHIND, sz.block // 2)),
            *stream_scratch,
        ],
        compiler_params=params(56),
        name="forward_legendre",
    )(slot_wave, mode_speed, back.reshape(send_shape), *moved, tiled, tables, zeroed)

    out = out.transpose(0, 1, 3, 2, 4)
    return out.reshape(slots, fields, 2, degrees).transpose(0, 2, 1, 3)


def solution(mesh):
    return jax.shard_map(
        shards,
        mesh=mesh,
        in_specs=(
            P("band", None, "lev", None),
            P("band", None, None),
            P(),
            P(),
            P(),
            P(),
            P("lev"),
        ),
        out_specs=P("band", None, "lev", None),
        check_vma=False,
    )
```

```python
import functools
import math

import jax
import jax.numpy as jnp
from jax import lax
from jax.experimental import pallas as pl
from jax.experimental.layout import Layout, with_layout_constraint
from jax.experimental.pallas import tpu as pltpu
from jax.sharding import PartitionSpec as P

FIELDS = 5
LEVELS = 24
TEMPER = 2
ENERGY = 4
LVL_ROWS = 8
SLAB = 128
MIB = 1024 * 1024

time_step = 1.0

COS_POLY = (
    0.9999999890590235, -19.739204499453994, 64.93911745989843, -85.45013953092186,
    60.167630951185615, -25.967599249120923, 6.528658161956132,
)
SIN_POLY = (
    6.283185302511506, -41.3417004053176, 81.60513138579954, -76.70301535389986,
    42.02592698629647, -14.89984666973851, 3.2381375126489513,
)


def up_to(value, unit):
    return -(-value // unit) * unit


class Sizes:
    def __init__(self, bands, groups, slots, fields, degrees, rows):
        self.bands, self.groups = bands, groups
        self.slots, self.fields, self.degrees, self.rows = slots, fields, degrees, rows
        self.tiles = degrees // SLAB
        self.packed = self.tiles + 1
        self.pitch = up_to(2 * self.packed, 8)
        self.stride = self.pitch + 1
        self.pitch_bf16 = up_to(2 * self.packed, 16)
        self.slot_rows = fields * self.tiles * 2
        self.field_pad = up_to(fields, 8)
        self.share = -(-fields // groups)
        self.lanes = 4 * self.share
        self.quarters = 2
        if 4 * self.lanes <= SLAB and slots % 4 == 0:
            self.quarters = 4
        self.halves = self.quarters // 2
        self.chunk_live = slots // self.quarters
        self.chunk = up_to(self.chunk_live, 8)
        self.spots = self.quarters * self.chunk
        self.plane = self.spots | 1
        self.block = slots
        for size in (8, 4):
            if slots % size == 0 and (size * self.slot_rows) % 16 == 0:
                self.block = size
                break
        self.steps = slots // self.block
        self.pairs = self.halves * bands * self.chunk
        self.trunc = degrees - 1
        self.sorted = degrees // 2
        self.orbits = up_to((4 * self.trunc + 40) // 4 + 2, SLAB)
        self.levels = LEVELS // groups


def owners(sizes, field):
    first, last = field * LEVELS, (field + 1) * LEVELS
    return [
        g for g in range(sizes.groups)
        if g * sizes.fields < last and (g + 1) * sizes.fields > first
    ]


def geo_rounds(sizes):
    sources, targets = owners(sizes, TEMPER), owners(sizes, ENERGY)
    wide = max(len(sources), len(targets))
    rounds = []
    for turn in range(wide):
        pairs = []
        for k in range(wide):
            s, t = k, (k + turn) % wide
            if s < len(sources) and t < len(targets):
                pairs.append((sources[s], targets[t]))
        if pairs:
            rounds.append(pairs)
    return rounds


def iota(shape, dim):
    return lax.broadcasted_iota(jnp.int32, shape, dim)


def one_hot(cond):
    return jnp.where(cond, 1.0, 0.0).astype(jnp.bfloat16)


def dot(a, b, dims=((1,), (0,))):
    return lax.dot_general(a, b, (dims, ((), ())), preferred_element_type=jnp.float32)


def halving(value):
    return value.bit_length() - 1 if value & (value - 1) == 0 else None


def quotient(x, by):
    bits = halving(by)
    return x >> bits if bits is not None else lax.div(x, jnp.int32(by))


def remainder(x, by):
    return x & (by - 1) if halving(by) is not None else lax.rem(x, jnp.int32(by))


def spread_matrix(sizes, lev):
    sz = sizes
    tall = sz.quarters * 4 * sz.field_pad
    wide = sz.groups * SLAB
    dst = iota((1, wide), 1)
    group = quotient(dst, SLAB)
    lane = remainder(dst, SLAB)
    quarter = quotient(lane, sz.lanes)
    rest = remainder(lane, sz.lanes)
    row = quotient(rest, 2 * sz.share)
    rest = remainder(rest, 2 * sz.share)
    comp = quotient(rest, sz.share)
    item = remainder(rest, sz.share)
    start = remainder(lev * sz.fields, sz.groups)
    field = remainder(group - start + sz.groups, sz.groups) + sz.groups * item
    want = ((quarter * 2 + row) * 2 + comp) * sz.field_pad + field
    want = jnp.where((field < sz.fields) & (quarter < sz.quarters), want, -1)
    return one_hot(iota((tall, wide), 0) == want)


def spot_of(sizes, place, odd):
    half = place // sizes.chunk_live
    return (odd * sizes.halves + half) * sizes.chunk + (place - half * sizes.chunk_live)


class Pair:
    def __init__(self, sizes, wave, band, place):
        self.sizes, self.place = sizes, place
        slot = band * sizes.slots + 2 * place
        self.numbers = wave[slot], wave[slot + 1]
        odd = self.numbers[0] & 1
        self.odds = odd, 1 - odd
        self.start = quotient(jnp.maximum(self.numbers[0], 0), SLAB)
        self.split = sizes.tiles - self.start

    def spot(self, side):
        sz = self.sizes
        half = self.place // sz.chunk_live
        first = (self.odds[side] * sz.halves + half) * sz.chunk
        return first + (self.place - half * sz.chunk_live)

    def rows(self, side):
        return pl.ds(self.spot(side), self.sizes.rows, stride=self.sizes.plane)

    def tile(self, k):
        return jnp.where(k < self.split, self.start + k, k - 1)

    def columns(self):
        place = iota((1, self.sizes.packed * SLAB), 1)
        first = place < self.split * SLAB
        degree = jnp.where(first, place + self.start * SLAB, place - SLAB)
        floors = [jnp.where(n < 0, self.sizes.degrees, n) for n in self.numbers]
        return first, degree >= jnp.where(first, floors[0], floors[1])

    def parts(self):
        tiles = self.sizes.tiles
        first = 2 * self.place
        return (
            (first, self.start, self.split, 0),
            (first + 1, self.split - 1, tiles + 1 - self.split, self.split),
        )

    def tables(self, leg):
        first, live = self.columns()
        leg = leg.astype(jnp.float32)
        own = jnp.where(first & live, leg, 0.0)
        other = jnp.where(first, 0.0, jnp.where(live, leg, 0.0))
        return jnp.concatenate([own, other], axis=0).astype(jnp.bfloat16)


AHEAD = 4
BEHIND = 4


def span(first, count, unit):
    return pl.ds(pl.multiple_of(first * unit, unit), pl.multiple_of(count * unit, unit))


def await_tiles(hbm, sem):
    for some in (hbm.at[0], hbm.at[0, :, pl.ds(0, 1)]):
        pltpu.make_async_copy(some, some, sem).wait()


class Stream:
    def __init__(self, sizes, pair_at, x_hbm, leg_hbm, x_all, leg_all, x_sems, leg_sems):
        self.sizes, self.pair_at = sizes, pair_at
        self.x_hbm, self.leg_hbm, self.x_all, self.leg_all = x_hbm, leg_hbm, x_all, leg_all
        self.x_sems, self.leg_sems = x_sems, leg_sems

    def start(self, place):
        sz = self.sizes
        x_rows = self.x_hbm.reshape(sz.slots, sz.fields, 2 * sz.tiles, SLAB)
        for slot, first, count, here in self.pair_at(place).parts():
            pltpu.make_async_copy(
                x_rows.at[slot, :, span(first, count, 2)],
                self.x_all.at[place, :, span(here, count, 2)],
                self.x_sems.at[place],
            ).start()
            pltpu.make_async_copy(
                self.leg_hbm.at[slot, :, span(first, count, SLAB)],
                self.leg_all.at[place, :, span(here, count, SLAB)],
                self.leg_sems.at[place],
            ).start()

    def begin(self, turn=0):
        each = self.sizes.block // 2
        first, last = (min((turn + k) * AHEAD, self.sizes.steps) * each for k in range(2))

        def one(place, carry):
            self.start(place)
            return carry

        lax.fori_loop(first, last, one, 0)
        self.ahead = (turn + 1) * AHEAD

    def take(self, step):
        each = self.sizes.block // 2

        @pl.when(step + self.ahead < self.sizes.steps)
        def _():
            for k in range(each):
                self.start((step + self.ahead) * each + k)

        for k in range(each):
            place = step * each + k
            await_tiles(self.x_hbm, self.x_sems.at[place])
            here = self.leg_all.at[place]
            pltpu.make_async_copy(here, here, self.leg_sems.at[place]).wait()


def inverse_kernel(sizes, rounds, wave, points, gauss, layer_depth, x_hbm, leg_hbm, send_ref, *refs):
    sz = sizes
    geo_refs = refs[:len(rounds)]
    wide, spots, numbers, x_all, leg_all, *sems = refs[len(rounds):]
    band = lax.axis_index("band")
    lev = lax.axis_index("lev")
    pair_at = functools.partial(Pair, sz, wave, band)
    stream = Stream(sz, pair_at, x_hbm, leg_hbm, x_all, leg_all, *sems)
    stream.begin()
    pad = 2 * sz.field_pad
    spots[...] = jnp.zeros_like(spots)
    numbers[...] = jnp.full_like(numbers, -1)
    wide[...] = jnp.zeros_like(wide)

    def block(step, carry):
        stream.take(step)
        found = []
        each = sz.block // 2
        empty = jnp.zeros((sz.rows, SLAB - pad), jnp.float32)

        def unpack(k):
            for f in range(sz.fields):
                rows = x_all[step * each + k, f].astype(jnp.float32)
                wide[k, pl.ds(f * sz.stride, sz.pitch), :] = rows[0:sz.pitch]

        def multiply(k):
            place = step * each + k
            pair = pair_at(place)
            values = jnp.concatenate([
                jnp.concatenate([
                    wide[k, pl.ds(2 * t + c, sz.field_pad, stride=sz.stride), :] for c in range(2)
                ], axis=0).astype(jnp.bfloat16)
                for t in range(sz.packed)
            ], axis=1)
            total = dot(pair.tables(leg_all[place]), values, ((1,), (1,)))
            for side in range(2):
                own = total[side * sz.rows:(side + 1) * sz.rows]
                found.append((pair, side, jnp.concatenate([own, empty], axis=1)))

        unpack(0)
        for k in range(each):
            if k + 1 < each:
                unpack(k + 1)
            multiply(k)
        for pair, side, total in found:
            spots[pair.rows(side), :] = total
            number = jnp.full((1, SLAB), pair.numbers[side], jnp.int32)
            numbers[pl.ds(pair.spot(side), 1), :] = number
        return carry

    lax.fori_loop(0, sz.steps, block, 0)
    spread = spread_matrix(sz, lev)
    shape = (2 * pad, SLAB)
    src, dst = iota(shape, 0), iota(shape, 1)
    bits = sz.field_pad.bit_length() - 1
    from_field, from_side = src & (sz.field_pad - 1), src >> bits
    to_field, to_side = dst & (sz.field_pad - 1), dst >> bits
    weights = []
    for pairs in rounds:
        first = jnp.int32(2 * LEVELS + sz.fields)
        for source, target in pairs:
            first = jnp.where(lev == source, target * sz.fields - ENERGY * LEVELS, first)
        under = lev * sz.fields + from_field - TEMPER * LEVELS
        above = first + to_field
        hit = (
            (from_side == to_side)
            & (from_field < sz.fields) & (to_field < sz.fields)
            & (above >= 0) & (above <= under)
        )
        weight = jnp.zeros(shape, jnp.float32)
        for level in range(LEVELS):
            weight = jnp.where(hit & (under == level), layer_depth[level], weight)
        high = weight.astype(jnp.bfloat16)
        low = (weight - high.astype(jnp.float32)).astype(jnp.bfloat16)
        weights.append(jnp.concatenate([high, low], axis=0))
    number = numbers[...]
    lane = iota((sz.spots, SLAB), 1)
    known = (number >= 0) & ~((number == 0) & (lane & sz.field_pad != 0))
    exacts, cuts, scales = [], [], []
    for rp in range(sz.rows // 2):
        exact = jnp.concatenate([
            spots[pl.ds((2 * rp + r) * sz.plane, sz.spots), :][:, 0:pad] for r in range(2)
        ], axis=1)
        cuts.append(jnp.concatenate([
            exact[q * sz.chunk:(q + 1) * sz.chunk] for q in range(sz.quarters)
        ], axis=1))
        exacts.append(exact)
        count = jnp.where(lane < pad, points[2 * rp], points[2 * rp + 1])
        scale = jnp.where(lane < pad, gauss[2 * rp], gauss[2 * rp + 1])
        scales.append(jnp.where(known & (2 * number <= count - 1), scale, 0.0))
    chunks = dot(jnp.concatenate(cuts, axis=0).astype(jnp.bfloat16), spread)
    exact = jnp.concatenate(exacts, axis=0).astype(jnp.bfloat16)
    double = jnp.concatenate([exact, exact], axis=1)
    for turn in range(len(rounds)):
        sums = dot(double, weights[turn])
        for rp in range(sz.rows // 2):
            own = sums[rp * sz.spots:(rp + 1) * sz.spots] * scales[rp]
            geo_refs[turn][rp] = own.astype(jnp.bfloat16)
    for rp in range(sz.rows // 2):
        for g in range(sz.groups):
            chunk = chunks[rp * sz.chunk:(rp + 1) * sz.chunk, g * SLAB:(g + 1) * SLAB]
            send_ref[rp, g] = chunk.astype(jnp.bfloat16)


def cos_sin(z):
    y = z * z
    c = jnp.full_like(y, COS_POLY[-1])
    for a in COS_POLY[-2::-1]:
        c = c * y + a
    s = jnp.full_like(y, SIN_POLY[-1])
    for a in SIN_POLY[-2::-1]:
        s = s * y + a
    return c, s * z


def basis_kernel(sizes, points, out_hbm, out_all, cosines, sines, sems):
    sz = sizes
    turns = sz.sorted // 16
    bands_row = 16 + up_to(turns, 8)

    first = lax.axis_index("band") * 2
    length_a, length_b = points[first], points[first + 1]
    count_a = length_a // 4 + 1
    high = cosines.shape[0]
    row = iota((high, SLAB), 0)
    number = jnp.where(row < 16, 2 * row, jnp.where(row < bands_row, 32 * (row - 16), sz.trunc))
    number = number.astype(jnp.float32)
    for at in range(0, sz.orbits, SLAB):
        place = iota((1, SLAB), 1) + at
        second = place >= count_a
        column = (place - jnp.where(second, count_a, 0)).astype(jnp.float32)
        length = jnp.where(second, length_b, length_a).astype(jnp.float32)
        inverse = 1.0 / length
        scale = jnp.where(row < 16, 1.0 / jnp.sqrt(length), 1.0)
        product = number * column
        whole = jnp.floor(product * inverse + 0.5)
        c, s = cos_sin((product - whole * length) * inverse)
        cosines[:, pl.ds(at, SLAB)] = c * scale
        sines[:, pl.ds(at, SLAB)] = s * scale

    steps, _, tall, _ = out_all.shape
    groups = tall // 16

    def leave(step):
        rows = pl.ds(pl.multiple_of(step * tall, tall), tall)
        return pltpu.make_async_copy(out_all.at[step], out_hbm.at[:, rows], sems.at[step])

    def part(step, carry):
        out_ref = out_all.at[step]
        for at in range(0, sz.orbits, SLAB):
            cols = pl.ds(at, SLAB)
            base_c, base_n = cosines[0:16, cols], -sines[0:16, cols]
            top_c, top_n = cosines[pl.ds(bands_row, 1), cols], -sines[pl.ds(bands_row, 1), cols]
            turn_rows = pl.ds(pl.multiple_of(16 + step * groups, 8), groups)
            all_c, all_s = cosines[turn_rows, cols], sines[turn_rows, cols]
            for k in range(groups):
                turn_c, turn_s = all_c[k:k + 1], all_s[k:k + 1]
                c = turn_c * base_c + turn_s * base_n
                n = turn_c * base_n - turn_s * base_c
                rows = pl.ds(16 * k, 16)
                out_ref[0, rows, cols] = c.astype(jnp.bfloat16)
                out_ref[1, rows, cols] = n.astype(jnp.bfloat16)
                out_ref[2, rows, cols] = (top_c * c + top_n * n).astype(jnp.bfloat16)
                out_ref[3, rows, cols] = (top_n * c - top_c * n).astype(jnp.bfloat16)
        leave(step).start()
        return carry

    lax.fori_loop(0, steps, part, 0)
    for step in range(steps):
        leave(jnp.int32(step)).wait()


def take_matrix(sizes, lev):
    sz = sizes
    tall = sz.groups * SLAB
    wide = sz.quarters * 2 * SLAB
    dst = iota((1, wide), 1)
    piece = quotient(dst, SLAB)
    lane = remainder(dst, SLAB)
    row = quotient(lane, SLAB // 2)
    field = quotient(remainder(lane, SLAB // 2), LVL_ROWS)
    level = remainder(lane, LVL_ROWS)
    whole = field * LEVELS + level * sz.groups + lev
    owner = quotient(whole, sz.fields)
    start = owner * sz.fields
    first = remainder(lev - remainder(start, sz.groups) + sz.groups, sz.groups)
    item = quotient(whole - start - first, sz.groups)
    want = owner * SLAB + (piece >> 1) * sz.lanes + (row * 2 + (piece & 1)) * sz.share + item
    want = jnp.where((field < FIELDS) & (level < sz.levels), want, -1)
    return one_hot(iota((tall, wide), 0) == want)


def grid_kernel(
    sizes, points, gauss, recv_ref, even_row, basis_hbm, send_ref, basis, terms, arrivals,
):
    sz = sizes
    step = 2 * SLAB
    parts = -(-sz.orbits // step)
    copies = []
    for part in range(parts):
        cols = pl.ds(part * step, min(step, sz.orbits - part * step))
        copies.append(pltpu.make_async_copy(basis_hbm.at[:, :, cols], basis.at[:, :, cols], arrivals.at[part]))
        copies[-1].start()
    lev = lax.axis_index("lev")
    first_row = lax.axis_index("band") * 2
    length_a, length_b = points[first_row], points[first_row + 1]
    count_a, count_b = length_a // 4 + 1, length_b // 4 + 1
    high = FIELDS * LVL_ROWS
    half_slab = SLAB // 2
    width = sz.bands * sz.chunk
    take = take_matrix(sz, lev)
    order = one_hot(iota((sz.sorted, sz.pairs), 0) * 2 == even_row[...])
    joined = jnp.concatenate([
        recv_ref[:, g].astype(jnp.float32).reshape(width, SLAB) for g in range(sz.groups)
    ], axis=1).astype(jnp.bfloat16)
    taken = dot(joined, take)
    coeffs = []
    number = iota((2 * SLAB, sz.sorted), 1) * 2
    bound = jnp.where(iota((2 * SLAB, sz.sorted), 0) & half_slab == 0, length_a, length_b) - 1
    kept = (0, half_slab, SLAB, SLAB + half_slab)
    sources = []
    for parity in range(2):
        rows = []
        for half in range(sz.halves):
            piece = (parity * sz.halves + half) * 2
            rows.append(taken[:, piece * SLAB:(piece + 2) * SLAB])
        sources.append(jnp.concatenate(rows, axis=0).T)
    ordered = dot(jnp.concatenate(sources, axis=0).astype(jnp.bfloat16), order, ((1,), (1,)))
    for parity in range(2):
        placed = ordered[parity * 2 * SLAB:(parity + 1) * 2 * SLAB]
        mine = number if parity == 0 else sz.trunc - number
        mult = jnp.where(mine == 0, 1.0, 2.0)
        placed = jnp.where(2 * mine <= bound, placed * mult, 0.0)
        placed = jnp.concatenate([placed[k:k + high] for k in kept], axis=0).astype(jnp.bfloat16)
        coeffs += [placed[:2 * high], placed[2 * high:]]
    for part in range(parts):
        copies[part].wait()
        at = part * step
        many = min(step, sz.orbits - at)
        cols = pl.ds(at, many)
        place = iota((1, many), 1) + at
        second = place >= count_a
        grids = []
        for k in range(4):
            both = dot(coeffs[k], basis[k, :, cols])
            grids.append(jnp.where(second, both[high:], both[:high]))
        ce, se, co, so = grids
        plus, minus = ce + co, ce - co
        splus, sminus = se + so, se - so
        values = (plus + splus, minus - sminus, minus + sminus, plus - splus)
        outs = []
        for v in values:
            u, w, tem, hum, ozo = (v[i * LVL_ROWS:(i + 1) * LVL_ROWS] for i in range(FIELDS))
            outs.append(jnp.concatenate(
                [u * tem, w * tem, u * hum, w * ozo, 0.5 * (u * u + w * w)], axis=0
            ))
        offset = place - jnp.where(second, count_a, 0)
        count = jnp.where(second, count_b, count_a)
        weight = jnp.where((offset == 0) | (offset == count - 1), 0.5, 1.0)
        weight = jnp.where(offset < count, weight, 0.0)
        t0, t1, t2, t3 = (o * weight for o in outs)
        a, b, c, d = t0 + t3, t1 + t2, t0 - t3, t2 - t1
        folds = (a + b, c + d, a - b, c - d)
        empty = jnp.zeros((half_slab - high, many), jnp.float32)
        for k in range(4):
            first = jnp.where(second, 0.0, folds[k])
            last = jnp.where(second, folds[k], 0.0)
            terms[k, :, cols] = jnp.concatenate([first, empty, last, empty], axis=0).astype(jnp.bfloat16)
    lane = iota((1, SLAB), 1)
    scale = jnp.where(lane < half_slab, gauss[first_row], gauss[first_row + 1])
    bound = jnp.where(lane < half_slab, length_a, length_b) - 1
    number = iota((sz.sorted, SLAB), 0) * 2
    even_col = jnp.broadcast_to(even_row[...].astype(jnp.float32), (8, sz.pairs)).T[:, 0:1]
    back_order = one_hot(iota((sz.pairs, sz.sorted), 1) * 2 == even_col.astype(jnp.int32))
    sums = []
    for parity in range(2):
        mine = number if parity == 0 else sz.trunc - number
        for k in (2 * parity, 2 * parity + 1):
            total = dot(basis[k], terms[k], ((1,), (1,))) * scale
            sums.append(jnp.where(2 * mine <= bound, total, 0.0).astype(jnp.bfloat16))
    slots = dot(back_order, jnp.concatenate(sums, axis=1)).astype(jnp.bfloat16)
    pieces = [
        slots[half * width:(half + 1) * width, 2 * parity * SLAB:2 * (parity + 1) * SLAB]
        for parity in range(2) for half in range(sz.halves)
    ]
    sent = dot(jnp.concatenate(pieces, axis=1), take, ((1,), (1,)))
    for g in range(sz.groups):
        part = sent[:, g * SLAB:(g + 1) * SLAB].reshape(sz.bands, sz.chunk, SLAB)
        send_ref[:, g] = part.astype(jnp.bfloat16)


def zeros_kernel(sizes, wave, out_hbm, zeros, sems):
    sz = sizes
    band = lax.axis_index("band")
    zeros[...] = jnp.zeros_like(zeros)

    def one(place, carry):
        pair = Pair(sz, wave, band, place)
        for side, count in ((0, pair.start), (1, pair.split - 1)):

            @pl.when(count > 0)
            def _():
                pltpu.make_async_copy(
                    zeros.at[:, pl.ds(0, count)],
                    out_hbm.at[2 * place + side, :, pl.ds(0, count)],
                    sems.at[place],
                ).start()

        return carry

    def done(place, carry):
        pltpu.make_async_copy(zeros, zeros, sems.at[place]).wait()
        return carry

    lax.fori_loop(0, sz.slots // 2, one, 0)
    lax.fori_loop(0, sz.slots // 2, done, 0)


def forward_kernel(sizes, wave, speed, back_ref, *refs):
    sz = sizes
    geo_refs = refs[:-13]
    x_hbm, leg_hbm, _, out_hbm, wide, spots, inverse, out_all, out_sems, x_all, leg_all, *sems = refs[-13:]
    band = lax.axis_index("band")
    pair_at = functools.partial(Pair, sz, wave, band)
    stream = Stream(sz, pair_at, x_hbm, leg_hbm, x_all, leg_all, *sems)
    stream.begin()
    pad = 2 * sz.field_pad
    each = sz.block // 2

    gather = spread_matrix(sz, lax.axis_index("lev"))
    cuts = [
        jnp.concatenate([back_ref[rp, g].astype(jnp.float32) for g in range(sz.groups)], axis=1)
        for rp in range(sz.rows // 2)
    ]
    wholes = dot(jnp.concatenate(cuts, axis=0).astype(jnp.bfloat16), gather, ((1,), (1,)))
    for rp in range(sz.rows // 2):
        whole = wholes[rp * sz.chunk:(rp + 1) * sz.chunk]
        rows = jnp.concatenate([
            whole[:, q * 2 * pad:(q + 1) * 2 * pad] for q in range(sz.quarters)
        ], axis=0)
        for geo_ref in geo_refs:
            rows = rows + geo_ref[rp].astype(jnp.float32)[:, 0:2 * pad]
        for r in range(2):
            part = rows[:, r * pad:(r + 1) * pad]
            part = jnp.concatenate([part, jnp.zeros((sz.spots, SLAB - pad), jnp.float32)], axis=1)
            spots[pl.ds((2 * rp + r) * sz.plane, sz.spots), :] = part
    stream.begin(1)
    row = quotient(iota((sz.pitch, SLAB), 0), 2)
    lane = iota((sz.pitch, SLAB), 1)
    for start in range(sz.tiles):
        degree = jnp.where(row < sz.tiles - start, row + start, row - 1) * SLAB + lane
        helm = (degree * (degree + 1)).astype(jnp.float32) / float(sz.trunc * (sz.trunc + 1))
        for f in range(sz.fields):
            denominator = 1.0 + time_step * time_step * helm * speed[f]
            inverse[start, pl.ds(f * sz.pitch, sz.pitch), :] = 1.0 / denominator
    stream.begin(2)
    out_tiles = out_all.reshape(BEHIND, each, sz.fields, sz.pitch // 2, 2, SLAB)

    def leave(place, k):
        at = lax.rem(place // each, BEHIND)

        for slot, first, count, here in pair_at(place).parts():
            pltpu.make_async_copy(
                out_tiles.at[at, k, :, pl.ds(here, count)],
                out_hbm.at[slot, :, pl.ds(first, count)],
                out_sems.at[at, k],
            ).start()

    def left(step):
        at = lax.rem(step, BEHIND)
        for k in range(each):
            await_tiles(out_hbm, out_sems.at[at, k])

    def block(step, carry):
        stream.take(step)

        @pl.when(step >= BEHIND)
        def _():
            left(step)

        at = lax.rem(step, BEHIND)

        def products(k):
            pair = pair_at(step * each + k)
            values = jnp.concatenate([spots[pair.rows(side), :] for side in range(2)], axis=0)
            values = values.T.astype(jnp.bfloat16)[0:pad]
            tables = pair.tables(leg_all[step * each + k])
            for first in range(0, sz.packed, 2):
                count = min(2, sz.packed - first)
                tends = dot(values, tables[:, first * SLAB:(first + count) * SLAB])
                for t in range(first, first + count):
                    for c in range(2):
                        rows = pl.ds(2 * t + c, sz.field_pad, stride=sz.stride)
                        wide[k, rows, :] = tends[
                            c * sz.field_pad:(c + 1) * sz.field_pad, (t - first) * SLAB:(t - first + 1) * SLAB
                        ]

        def finish(k):
            place = step * each + k
            pair = pair_at(place)
            mine = row < pair.split
            degree = jnp.where(mine, row + pair.start, row - 1) * SLAB + lane
            floors = [jnp.where(n < 0, sz.degrees, n) for n in pair.numbers]
            live = degree >= jnp.where(mine, floors[0], floors[1])
            for f in range(sz.fields):
                rows = pl.ds(f * sz.pitch, sz.pitch)
                old = x_all[place, f].astype(jnp.float32)[0:sz.pitch]
                tend = wide[k, pl.ds(f * sz.stride, sz.pitch), :]
                new = (old + time_step * tend) * inverse[pair.start, rows, :]
                out_all[at, k, rows, :] = jnp.where(live, new, 0.0)

        products(0)
        for k in range(each):
            if k + 1 < each:
                products(k + 1)
            finish(k)
            leave(step * each + k, k)
        return carry

    lax.fori_loop(0, sz.steps, block, 0)
    for step in range(max(0, sz.steps - BEHIND), sz.steps):
        left(jnp.int32(step))


def params(mib):
    return pltpu.CompilerParams(vmem_limit_bytes=mib * MIB)


def smem():
    return pl.BlockSpec(memory_space=pltpu.SMEM)


def shards(spectra, legendre, slot_wave, row_points, gauss_weight, layer_depth, mode_speed):
    slots, _, fields, degrees = spectra.shape
    rows = legendre.shape[2]
    sz = Sizes(lax.axis_size("band"), lax.axis_size("lev"), slots, fields, degrees, rows)

    tiled = spectra.reshape(slots, 2, fields, sz.tiles, SLAB)
    tiled = with_layout_constraint(tiled, Layout((0, 2, 3, 1, 4)))
    tiled = tiled.transpose(0, 2, 3, 1, 4)
    tables = legendre.transpose(0, 2, 1)

    rounds = geo_rounds(sz)
    senders = [source for pairs in rounds for source, _ in pairs]
    sums = [sum(rounds, [])] if len(set(senders)) == len(senders) else rounds
    spots_shape = pltpu.VMEM((up_to(sz.plane * sz.rows, 8), SLAB), jnp.float32)
    pairs = slots // 2
    stream_scratch = [
        pltpu.VMEM((pairs, fields, sz.pitch_bf16, SLAB), jnp.bfloat16),
        pltpu.VMEM((pairs, rows, sz.packed * SLAB), jnp.bfloat16),
        pltpu.SemaphoreType.DMA((pairs,)),
        pltpu.SemaphoreType.DMA((pairs,)),
    ]
    wide_shape = pltpu.VMEM((sz.block // 2, up_to(sz.field_pad * sz.stride, 8), SLAB), jnp.float32)
    anywhere = pl.BlockSpec(memory_space=pl.ANY)
    vmem = pl.BlockSpec(memory_space=pltpu.VMEM)
    send_shape = (sz.bands, sz.groups, sz.chunk, SLAB)
    geo_shape = (sz.rows // 2, sz.spots, SLAB)

    sent, *geo = pl.pallas_call(
        functools.partial(inverse_kernel, sz, sums),
        in_specs=[smem(), smem(), smem(), smem(), anywhere, anywhere],
        out_specs=[vmem] * (1 + len(sums)),
        out_shape=[jax.ShapeDtypeStruct(send_shape, jnp.bfloat16)]
        + [jax.ShapeDtypeStruct(geo_shape, jnp.bfloat16)] * len(sums),
        scratch_shapes=[wide_shape, spots_shape, pltpu.VMEM((sz.spots, SLAB), jnp.int32), *stream_scratch],
        compiler_params=params(56),
        name="inverse_legendre",
    )(slot_wave, row_points, gauss_weight, layer_depth, tiled, tables)

    sent, points_later, wave_later = lax.optimization_barrier((sent, row_points, slot_wave))
    both = ("band", "lev")
    total = sz.bands * sz.groups
    flat = (total * sz.chunk, SLAB)
    arrived = lax.all_to_all(sent.reshape(flat), both, split_axis=0, concat_axis=0, tiled=True)

    pair_wave = wave_later.reshape(-1, 2)
    even_wave = jnp.where(pair_wave[:, 0] % 2 == 0, pair_wave[:, 0], pair_wave[:, 1])
    even_wave = even_wave.reshape(sz.bands, sz.halves, sz.chunk_live)
    even_wave = jnp.pad(even_wave, ((0, 0), (0, 0), (0, sz.chunk - sz.chunk_live)), constant_values=-1)
    even_wave = even_wave.transpose(1, 0, 2).reshape(sz.pairs)

    high = SLAB if sz.sorted % SLAB == 0 else sz.sorted
    table_rows = 16 + up_to(sz.sorted // 16, 8) + 8
    basis = pl.pallas_call(
        functools.partial(basis_kernel, sz),
        in_specs=[smem()],
        out_specs=anywhere,
        out_shape=jax.ShapeDtypeStruct((4, sz.sorted, sz.orbits), jnp.bfloat16),
        scratch_shapes=[
            pltpu.VMEM((sz.sorted // high, 4, high, sz.orbits), jnp.bfloat16),
            pltpu.VMEM((table_rows, sz.orbits), jnp.float32),
            pltpu.VMEM((table_rows, sz.orbits), jnp.float32),
            pltpu.SemaphoreType.DMA((sz.sorted // high,)),
        ],
        compiler_params=params(56),
        cost_estimate=pl.CostEstimate(
            flops=20 * sz.sorted * sz.orbits, bytes_accessed=8 * sz.sorted * sz.orbits, transcendentals=0,
        ),
        name="basis",
    )(points_later)

    even_row = even_wave.reshape(1, sz.pairs)
    moved = [lax.ppermute(geo[turn % len(sums)], "lev", pairs) for turn, pairs in enumerate(rounds)]
    *moved, arrived, basis, even_row = lax.optimization_barrier((*moved, arrived, basis, even_row))
    returned = pl.pallas_call(
        functools.partial(grid_kernel, sz),
        in_specs=[smem(), smem(), vmem, vmem, anywhere],
        out_specs=vmem,
        out_shape=jax.ShapeDtypeStruct(send_shape, jnp.bfloat16),
        scratch_shapes=[
            pltpu.VMEM((4, sz.sorted, sz.orbits), jnp.bfloat16),
            pltpu.VMEM((4, SLAB, sz.orbits), jnp.bfloat16),
            pltpu.SemaphoreType.DMA((-(-sz.orbits // (2 * SLAB)),)),
        ],
        compiler_params=params(56),
        cost_estimate=pl.CostEstimate(
            flops=4 * 4 * SLAB * sz.sorted * sz.orbits, bytes_accessed=8 * sz.sorted * sz.orbits, transcendentals=0,
        ),
        name="grid_products",
    )(
        row_points, gauss_weight, arrived.reshape(send_shape), even_row, basis,
    )
    returned, wave_last = lax.optimization_barrier((returned, slot_wave))

    back = lax.all_to_all(returned.reshape(flat), both, split_axis=0, concat_axis=0, tiled=True)

    out_shape = jax.ShapeDtypeStruct(tiled.shape, jnp.float32)
    zeroed = pl.pallas_call(
        functools.partial(zeros_kernel, sz),
        in_specs=[smem()],
        out_specs=anywhere,
        out_shape=out_shape,
        scratch_shapes=[
            pltpu.VMEM((fields, sz.tiles - 1, 2, SLAB), jnp.float32),
            pltpu.SemaphoreType.DMA((pairs,)),
        ],
        compiler_params=params(56),
        cost_estimate=pl.CostEstimate(
            flops=0, bytes_accessed=2 * slots * fields * degrees * 2, transcendentals=0,
        ),
        name="dead_zeros",
    )(wave_last)
    out = pl.pallas_call(
        functools.partial(forward_kernel, sz),
        in_specs=[smem(), smem()] + [vmem] * (1 + len(rounds)) + [anywhere] * 3,
        out_specs=anywhere,
        out_shape=out_shape,
        input_output_aliases={5 + len(rounds): 0},
        scratch_shapes=[
            wide_shape, spots_shape,
            pltpu.VMEM((sz.tiles, fields * sz.pitch, SLAB), jnp.float32),
            pltpu.VMEM((BEHIND, sz.block // 2, fields * sz.pitch, SLAB), jnp.float32),
            pltpu.SemaphoreType.DMA((BEHIND, sz.block // 2)),
            *stream_scratch,
        ],
        compiler_params=params(56),
        name="forward_legendre",
    )(slot_wave, mode_speed, back.reshape(send_shape), *moved, tiled, tables, zeroed)

    out = out.transpose(0, 1, 3, 2, 4)
    return out.reshape(slots, fields, 2, degrees).transpose(0, 2, 1, 3)


def solution(mesh):
    return jax.shard_map(
        shards,
        mesh=mesh,
        in_specs=(
            P("band", None, "lev", None),
            P("band", None, None),
            P(),
            P(),
            P(),
            P(),
            P("lev"),
        ),
        out_specs=P("band", None, "lev", None),
        check_vma=False,
    )
```

```python
import functools
import math

import jax
import jax.numpy as jnp
from jax import lax
from jax.experimental import pallas as pl
from jax.experimental.layout import Layout, with_layout_constraint
from jax.experimental.pallas import tpu as pltpu
from jax.sharding import PartitionSpec as P

FIELDS = 5
LEVELS = 24
TEMPER = 2
ENERGY = 4
LVL_ROWS = 8
SLAB = 128
MIB = 1024 * 1024

time_step = 1.0

COS_POLY = (
    0.9999999890590235, -19.739204499453994, 64.93911745989843, -85.45013953092186,
    60.167630951185615, -25.967599249120923, 6.528658161956132,
)
SIN_POLY = (
    6.283185302511506, -41.3417004053176, 81.60513138579954, -76.70301535389986,
    42.02592698629647, -14.89984666973851, 3.2381375126489513,
)


def up_to(value, unit):
    return -(-value // unit) * unit


class Sizes:
    def __init__(self, bands, groups, slots, fields, degrees, rows):
        self.bands, self.groups = bands, groups
        self.slots, self.fields, self.degrees, self.rows = slots, fields, degrees, rows
        self.tiles = degrees // SLAB
        self.packed = self.tiles + 1
        self.pitch = up_to(2 * self.packed, 8)
        self.stride = self.pitch + 1
        self.pitch_bf16 = up_to(2 * self.packed, 16)
        self.slot_rows = fields * self.tiles * 2
        self.field_pad = up_to(fields, 8)
        self.share = -(-fields // groups)
        self.lanes = 4 * self.share
        self.quarters = 2
        if 4 * self.lanes <= SLAB and slots % 4 == 0:
            self.quarters = 4
        self.halves = self.quarters // 2
        self.chunk_live = slots // self.quarters
        self.chunk = up_to(self.chunk_live, 8)
        self.spots = self.quarters * self.chunk
        self.plane = self.spots | 1
        self.block = slots
        for size in (8, 4):
            if slots % size == 0 and (size * self.slot_rows) % 16 == 0:
                self.block = size
                break
        self.steps = slots // self.block
        self.pairs = self.halves * bands * self.chunk
        self.trunc = degrees - 1
        self.sorted = degrees // 2
        self.orbits = up_to((4 * self.trunc + 40) // 4 + 2, SLAB)
        self.levels = LEVELS // groups


def owners(sizes, field):
    first, last = field * LEVELS, (field + 1) * LEVELS
    return [
        g for g in range(sizes.groups)
        if g * sizes.fields < last and (g + 1) * sizes.fields > first
    ]


def geo_rounds(sizes):
    sources, targets = owners(sizes, TEMPER), owners(sizes, ENERGY)
    wide = max(len(sources), len(targets))
    rounds = []
    for turn in range(wide):
        pairs = []
        for k in range(wide):
            s, t = k, (k + turn) % wide
            if s < len(sources) and t < len(targets):
                pairs.append((sources[s], targets[t]))
        if pairs:
            rounds.append(pairs)
    return rounds


def iota(shape, dim):
    return lax.broadcasted_iota(jnp.int32, shape, dim)


def one_hot(cond):
    return jnp.where(cond, 1.0, 0.0).astype(jnp.bfloat16)


def dot(a, b, dims=((1,), (0,))):
    return lax.dot_general(a, b, (dims, ((), ())), preferred_element_type=jnp.float32)


def halving(value):
    return value.bit_length() - 1 if value & (value - 1) == 0 else None


def quotient(x, by):
    bits = halving(by)
    return x >> bits if bits is not None else lax.div(x, jnp.int32(by))


def remainder(x, by):
    return x & (by - 1) if halving(by) is not None else lax.rem(x, jnp.int32(by))


def spread_matrix(sizes, lev):
    sz = sizes
    tall = sz.quarters * 4 * sz.field_pad
    wide = sz.groups * SLAB
    dst = iota((1, wide), 1)
    group = quotient(dst, SLAB)
    lane = remainder(dst, SLAB)
    quarter = quotient(lane, sz.lanes)
    rest = remainder(lane, sz.lanes)
    row = quotient(rest, 2 * sz.share)
    rest = remainder(rest, 2 * sz.share)
    comp = quotient(rest, sz.share)
    item = remainder(rest, sz.share)
    start = remainder(lev * sz.fields, sz.groups)
    field = remainder(group - start + sz.groups, sz.groups) + sz.groups * item
    want = ((quarter * 2 + row) * 2 + comp) * sz.field_pad + field
    want = jnp.where((field < sz.fields) & (quarter < sz.quarters), want, -1)
    return one_hot(iota((tall, wide), 0) == want)


def spot_of(sizes, place, odd):
    half = place // sizes.chunk_live
    return (odd * sizes.halves + half) * sizes.chunk + (place - half * sizes.chunk_live)


class Pair:
    def __init__(self, sizes, wave, band, place):
        self.sizes, self.place = sizes, place
        slot = band * sizes.slots + 2 * place
        self.numbers = wave[slot], wave[slot + 1]
        odd = self.numbers[0] & 1
        self.odds = odd, 1 - odd
        self.start = quotient(jnp.maximum(self.numbers[0], 0), SLAB)
        self.split = sizes.tiles - self.start

    def spot(self, side):
        sz = self.sizes
        half = self.place // sz.chunk_live
        first = (self.odds[side] * sz.halves + half) * sz.chunk
        return first + (self.place - half * sz.chunk_live)

    def rows(self, side):
        return pl.ds(self.spot(side), self.sizes.rows, stride=self.sizes.plane)

    def tile(self, k):
        return jnp.where(k < self.split, self.start + k, k - 1)

    def columns(self):
        place = iota((1, self.sizes.packed * SLAB), 1)
        first = place < self.split * SLAB
        degree = jnp.where(first, place + self.start * SLAB, place - SLAB)
        floors = [jnp.where(n < 0, self.sizes.degrees, n) for n in self.numbers]
        return first, degree >= jnp.where(first, floors[0], floors[1])

    def parts(self):
        tiles = self.sizes.tiles
        first = 2 * self.place
        return (
            (first, self.start, self.split, 0),
            (first + 1, self.split - 1, tiles + 1 - self.split, self.split),
        )

    def tables(self, leg):
        first, live = self.columns()
        leg = leg.astype(jnp.float32)
        own = jnp.where(first & live, leg, 0.0)
        other = jnp.where(first, 0.0, jnp.where(live, leg, 0.0))
        return jnp.concatenate([own, other], axis=0).astype(jnp.bfloat16)


AHEAD = 4
BEHIND = 4


def span(first, count, unit):
    return pl.ds(pl.multiple_of(first * unit, unit), pl.multiple_of(count * unit, unit))


def await_tiles(hbm, sem):
    for some in (hbm.at[0], hbm.at[0, :, pl.ds(0, 1)]):
        pltpu.make_async_copy(some, some, sem).wait()


class Stream:
    def __init__(self, sizes, pair_at, x_hbm, leg_hbm, x_all, leg_all, x_sems, leg_sems):
        self.sizes, self.pair_at = sizes, pair_at
        self.x_hbm, self.leg_hbm, self.x_all, self.leg_all = x_hbm, leg_hbm, x_all, leg_all
        self.x_sems, self.leg_sems = x_sems, leg_sems

    def start(self, place):
        sz = self.sizes
        x_rows = self.x_hbm.reshape(sz.slots, sz.fields, 2 * sz.tiles, SLAB)
        for slot, first, count, here in self.pair_at(place).parts():
            pltpu.make_async_copy(
                x_rows.at[slot, :, span(first, count, 2)],
                self.x_all.at[place, :, span(here, count, 2)],
                self.x_sems.at[place],
            ).start()
            pltpu.make_async_copy(
                self.leg_hbm.at[slot, :, span(first, count, SLAB)],
                self.leg_all.at[place, :, span(here, count, SLAB)],
                self.leg_sems.at[place],
            ).start()

    def begin(self, turn=0):
        each = self.sizes.block // 2
        first, last = (min((turn + k) * AHEAD, self.sizes.steps) * each for k in range(2))

        def one(place, carry):
            self.start(place)
            return carry

        lax.fori_loop(first, last, one, 0)
        self.ahead = (turn + 1) * AHEAD

    def arrive(self, place):
        await_tiles(self.x_hbm, self.x_sems.at[place])
        here = self.leg_all.at[place]
        pltpu.make_async_copy(here, here, self.leg_sems.at[place]).wait()

    def run(self, body):
        each = self.sizes.block // 2
        steps = self.sizes.steps
        middle = max(steps - self.ahead, 0)

        def feeding(step, carry):
            body(step, lambda k: self.start((step + self.ahead) * each + k))
            return carry

        def last(step, carry):
            body(step, lambda k: None)
            return carry

        lax.fori_loop(0, middle, feeding, 0)
        lax.fori_loop(middle, steps, last, 0)


def inverse_kernel(sizes, rounds, wave, points, gauss, layer_depth, x_hbm, leg_hbm, send_ref, *refs):
    sz = sizes
    geo_refs = refs[:len(rounds)]
    wide, spots, numbers, x_all, leg_all, *sems = refs[len(rounds):]
    band = lax.axis_index("band")
    lev = lax.axis_index("lev")
    pair_at = functools.partial(Pair, sz, wave, band)
    stream = Stream(sz, pair_at, x_hbm, leg_hbm, x_all, leg_all, *sems)
    stream.begin()
    pad = 2 * sz.field_pad
    spots[...] = jnp.zeros_like(spots)
    numbers[...] = jnp.full_like(numbers, -1)
    wide[...] = jnp.zeros_like(wide)

    def block(step, feed):
        found = []
        each = sz.block // 2
        empty = jnp.zeros((sz.rows, SLAB - pad), jnp.float32)

        def unpack(k):
            stream.arrive(step * each + k)
            feed(k)
            for f in range(sz.fields):
                rows = x_all[step * each + k, f].astype(jnp.float32)
                wide[k, pl.ds(f * sz.stride, sz.pitch), :] = rows[0:sz.pitch]

        def multiply(k):
            place = step * each + k
            pair = pair_at(place)
            values = jnp.concatenate([
                jnp.concatenate([
                    wide[k, pl.ds(2 * t + c, sz.field_pad, stride=sz.stride), :] for c in range(2)
                ], axis=0).astype(jnp.bfloat16)
                for t in range(sz.packed)
            ], axis=1)
            total = dot(pair.tables(leg_all[place]), values, ((1,), (1,)))
            for side in range(2):
                own = total[side * sz.rows:(side + 1) * sz.rows]
                found.append((pair, side, jnp.concatenate([own, empty], axis=1)))

        unpack(0)
        for k in range(each):
            if k + 1 < each:
                unpack(k + 1)
            multiply(k)
        for pair, side, total in found:
            spots[pair.rows(side), :] = total
            number = jnp.full((1, SLAB), pair.numbers[side], jnp.int32)
            numbers[pl.ds(pair.spot(side), 1), :] = number

    stream.run(block)
    spread = spread_matrix(sz, lev)
    shape = (2 * pad, SLAB)
    src, dst = iota(shape, 0), iota(shape, 1)
    bits = sz.field_pad.bit_length() - 1
    from_field, from_side = src & (sz.field_pad - 1), src >> bits
    to_field, to_side = dst & (sz.field_pad - 1), dst >> bits
    weights = []
    for pairs in rounds:
        first = jnp.int32(2 * LEVELS + sz.fields)
        for source, target in pairs:
            first = jnp.where(lev == source, target * sz.fields - ENERGY * LEVELS, first)
        under = lev * sz.fields + from_field - TEMPER * LEVELS
        above = first + to_field
        hit = (
            (from_side == to_side)
            & (from_field < sz.fields) & (to_field < sz.fields)
            & (above >= 0) & (above <= under)
        )
        weight = jnp.zeros(shape, jnp.float32)
        for level in range(LEVELS):
            weight = jnp.where(hit & (under == level), layer_depth[level], weight)
        high = weight.astype(jnp.bfloat16)
        low = (weight - high.astype(jnp.float32)).astype(jnp.bfloat16)
        weights.append(jnp.concatenate([high, low], axis=0))
    number = numbers[...]
    lane = iota((sz.spots, SLAB), 1)
    known = (number >= 0) & ~((number == 0) & (lane & sz.field_pad != 0))
    exacts, cuts, scales = [], [], []
    for rp in range(sz.rows // 2):
        exact = jnp.concatenate([
            spots[pl.ds((2 * rp + r) * sz.plane, sz.spots), :][:, 0:pad] for r in range(2)
        ], axis=1)
        cuts.append(jnp.concatenate([
            exact[q * sz.chunk:(q + 1) * sz.chunk] for q in range(sz.quarters)
        ], axis=1))
        exacts.append(exact)
        count = jnp.where(lane < pad, points[2 * rp], points[2 * rp + 1])
        scale = jnp.where(lane < pad, gauss[2 * rp], gauss[2 * rp + 1])
        scales.append(jnp.where(known & (2 * number <= count - 1), scale, 0.0))
    chunks = dot(jnp.concatenate(cuts, axis=0).astype(jnp.bfloat16), spread)
    exact = jnp.concatenate(exacts, axis=0).astype(jnp.bfloat16)
    double = jnp.concatenate([exact, exact], axis=1)
    for turn in range(len(rounds)):
        sums = dot(double, weights[turn])
        for rp in range(sz.rows // 2):
            own = sums[rp * sz.spots:(rp + 1) * sz.spots] * scales[rp]
            geo_refs[turn][rp] = own.astype(jnp.bfloat16)
    for rp in range(sz.rows // 2):
        for g in range(sz.groups):
            chunk = chunks[rp * sz.chunk:(rp + 1) * sz.chunk, g * SLAB:(g + 1) * SLAB]
            send_ref[rp, g] = chunk.astype(jnp.bfloat16)


def cos_sin(z):
    y = z * z
    c = jnp.full_like(y, COS_POLY[-1])
    for a in COS_POLY[-2::-1]:
        c = c * y + a
    s = jnp.full_like(y, SIN_POLY[-1])
    for a in SIN_POLY[-2::-1]:
        s = s * y + a
    return c, s * z


def basis_kernel(sizes, points, out_hbm, out_all, cosines, sines, sems):
    sz = sizes
    turns = sz.sorted // 16
    bands_row = 16 + up_to(turns, 8)

    first = lax.axis_index("band") * 2
    length_a, length_b = points[first], points[first + 1]
    count_a = length_a // 4 + 1
    high = cosines.shape[0]
    row = iota((high, SLAB), 0)
    number = jnp.where(row < 16, 2 * row, jnp.where(row < bands_row, 32 * (row - 16), sz.trunc))
    number = number.astype(jnp.float32)
    for at in range(0, sz.orbits, SLAB):
        place = iota((1, SLAB), 1) + at
        second = place >= count_a
        column = (place - jnp.where(second, count_a, 0)).astype(jnp.float32)
        length = jnp.where(second, length_b, length_a).astype(jnp.float32)
        inverse = 1.0 / length
        scale = jnp.where(row < 16, 1.0 / jnp.sqrt(length), 1.0)
        product = number * column
        whole = jnp.floor(product * inverse + 0.5)
        c, s = cos_sin((product - whole * length) * inverse)
        cosines[:, pl.ds(at, SLAB)] = c * scale
        sines[:, pl.ds(at, SLAB)] = s * scale

    steps, _, tall, _ = out_all.shape
    groups = tall // 16

    def leave(step):
        rows = pl.ds(pl.multiple_of(step * tall, tall), tall)
        return pltpu.make_async_copy(out_all.at[step], out_hbm.at[:, rows], sems.at[step])

    def part(step, carry):
        out_ref = out_all.at[step]
        for at in range(0, sz.orbits, SLAB):
            cols = pl.ds(at, SLAB)
            base_c, base_n = cosines[0:16, cols], -sines[0:16, cols]
            top_c, top_n = cosines[pl.ds(bands_row, 1), cols], -sines[pl.ds(bands_row, 1), cols]
            turn_rows = pl.ds(pl.multiple_of(16 + step * groups, 8), groups)
            all_c, all_s = cosines[turn_rows, cols], sines[turn_rows, cols]
            for k in range(groups):
                turn_c, turn_s = all_c[k:k + 1], all_s[k:k + 1]
                c = turn_c * base_c + turn_s * base_n
                n = turn_c * base_n - turn_s * base_c
                rows = pl.ds(16 * k, 16)
                out_ref[0, rows, cols] = c.astype(jnp.bfloat16)
                out_ref[1, rows, cols] = n.astype(jnp.bfloat16)
                out_ref[2, rows, cols] = (top_c * c + top_n * n).astype(jnp.bfloat16)
                out_ref[3, rows, cols] = (top_n * c - top_c * n).astype(jnp.bfloat16)
        leave(step).start()
        return carry

    lax.fori_loop(0, steps, part, 0)
    for step in range(steps):
        leave(jnp.int32(step)).wait()


def take_matrix(sizes, lev):
    sz = sizes
    tall = sz.groups * SLAB
    wide = sz.quarters * 2 * SLAB
    dst = iota((1, wide), 1)
    piece = quotient(dst, SLAB)
    lane = remainder(dst, SLAB)
    row = quotient(lane, SLAB // 2)
    field = quotient(remainder(lane, SLAB // 2), LVL_ROWS)
    level = remainder(lane, LVL_ROWS)
    whole = field * LEVELS + level * sz.groups + lev
    owner = quotient(whole, sz.fields)
    start = owner * sz.fields
    first = remainder(lev - remainder(start, sz.groups) + sz.groups, sz.groups)
    item = quotient(whole - start - first, sz.groups)
    want = owner * SLAB + (piece >> 1) * sz.lanes + (row * 2 + (piece & 1)) * sz.share + item
    want = jnp.where((field < FIELDS) & (level < sz.levels), want, -1)
    return one_hot(iota((tall, wide), 0) == want)


def grid_kernel(
    sizes, points, gauss, recv_ref, even_row, basis_hbm, send_ref, basis, terms, arrivals,
):
    sz = sizes
    step = 2 * SLAB
    parts = -(-sz.orbits // step)
    copies = []
    for part in range(parts):
        cols = pl.ds(part * step, min(step, sz.orbits - part * step))
        copies.append(pltpu.make_async_copy(basis_hbm.at[:, :, cols], basis.at[:, :, cols], arrivals.at[part]))
        copies[-1].start()
    lev = lax.axis_index("lev")
    first_row = lax.axis_index("band") * 2
    length_a, length_b = points[first_row], points[first_row + 1]
    count_a, count_b = length_a // 4 + 1, length_b // 4 + 1
    high = FIELDS * LVL_ROWS
    half_slab = SLAB // 2
    width = sz.bands * sz.chunk
    take = take_matrix(sz, lev)
    order = one_hot(iota((sz.sorted, sz.pairs), 0) * 2 == even_row[...])
    joined = jnp.concatenate([
        recv_ref[:, g].astype(jnp.float32).reshape(width, SLAB) for g in range(sz.groups)
    ], axis=1).astype(jnp.bfloat16)
    taken = dot(joined, take)
    coeffs = []
    number = iota((2 * SLAB, sz.sorted), 1) * 2
    bound = jnp.where(iota((2 * SLAB, sz.sorted), 0) & half_slab == 0, length_a, length_b) - 1
    kept = (0, half_slab, SLAB, SLAB + half_slab)
    sources = []
    for parity in range(2):
        rows = []
        for half in range(sz.halves):
            piece = (parity * sz.halves + half) * 2
            rows.append(taken[:, piece * SLAB:(piece + 2) * SLAB])
        sources.append(jnp.concatenate(rows, axis=0).T)
    ordered = dot(jnp.concatenate(sources, axis=0).astype(jnp.bfloat16), order, ((1,), (1,)))
    for parity in range(2):
        placed = ordered[parity * 2 * SLAB:(parity + 1) * 2 * SLAB]
        mine = number if parity == 0 else sz.trunc - number
        mult = jnp.where(mine == 0, 1.0, 2.0)
        placed = jnp.where(2 * mine <= bound, placed * mult, 0.0)
        placed = jnp.concatenate([placed[k:k + high] for k in kept], axis=0).astype(jnp.bfloat16)
        coeffs += [placed[:2 * high], placed[2 * high:]]
    for part in range(parts):
        copies[part].wait()
        at = part * step
        many = min(step, sz.orbits - at)
        cols = pl.ds(at, many)
        place = iota((1, many), 1) + at
        second = place >= count_a
        grids = []
        for k in range(4):
            both = dot(coeffs[k], basis[k, :, cols])
            grids.append(jnp.where(second, both[high:], both[:high]))
        ce, se, co, so = grids
        plus, minus = ce + co, ce - co
        splus, sminus = se + so, se - so
        values = (plus + splus, minus - sminus, minus + sminus, plus - splus)
        outs = []
        for v in values:
            u, w, tem, hum, ozo = (v[i * LVL_ROWS:(i + 1) * LVL_ROWS] for i in range(FIELDS))
            outs.append(jnp.concatenate(
                [u * tem, w * tem, u * hum, w * ozo, 0.5 * (u * u + w * w)], axis=0
            ))
        offset = place - jnp.where(second, count_a, 0)
        count = jnp.where(second, count_b, count_a)
        weight = jnp.where((offset == 0) | (offset == count - 1), 0.5, 1.0)
        weight = jnp.where(offset < count, weight, 0.0)
        t0, t1, t2, t3 = (o * weight for o in outs)
        a, b, c, d = t0 + t3, t1 + t2, t0 - t3, t2 - t1
        folds = (a + b, c + d, a - b, c - d)
        empty = jnp.zeros((half_slab - high, many), jnp.float32)
        for k in range(4):
            first = jnp.where(second, 0.0, folds[k])
            last = jnp.where(second, folds[k], 0.0)
            terms[k, :, cols] = jnp.concatenate([first, empty, last, empty], axis=0).astype(jnp.bfloat16)
    lane = iota((1, SLAB), 1)
    scale = jnp.where(lane < half_slab, gauss[first_row], gauss[first_row + 1])
    bound = jnp.where(lane < half_slab, length_a, length_b) - 1
    number = iota((sz.sorted, SLAB), 0) * 2
    even_col = jnp.broadcast_to(even_row[...].astype(jnp.float32), (8, sz.pairs)).T[:, 0:1]
    back_order = one_hot(iota((sz.pairs, sz.sorted), 1) * 2 == even_col.astype(jnp.int32))
    sums = []
    for parity in range(2):
        mine = number if parity == 0 else sz.trunc - number
        for k in (2 * parity, 2 * parity + 1):
            total = dot(basis[k], terms[k], ((1,), (1,))) * scale
            sums.append(jnp.where(2 * mine <= bound, total, 0.0).astype(jnp.bfloat16))
    slots = dot(back_order, jnp.concatenate(sums, axis=1)).astype(jnp.bfloat16)
    pieces = [
        slots[half * width:(half + 1) * width, 2 * parity * SLAB:2 * (parity + 1) * SLAB]
        for parity in range(2) for half in range(sz.halves)
    ]
    sent = dot(jnp.concatenate(pieces, axis=1), take, ((1,), (1,)))
    for g in range(sz.groups):
        part = sent[:, g * SLAB:(g + 1) * SLAB].reshape(sz.bands, sz.chunk, SLAB)
        send_ref[:, g] = part.astype(jnp.bfloat16)


def zeros_kernel(sizes, wave, out_hbm, zeros, sems):
    sz = sizes
    band = lax.axis_index("band")
    zeros[...] = jnp.zeros_like(zeros)

    def one(place, carry):
        pair = Pair(sz, wave, band, place)
        for side, count in ((0, pair.start), (1, pair.split - 1)):

            @pl.when(count > 0)
            def _():
                pltpu.make_async_copy(
                    zeros.at[:, pl.ds(0, count)],
                    out_hbm.at[2 * place + side, :, pl.ds(0, count)],
                    sems.at[place],
                ).start()

        return carry

    def done(place, carry):
        pltpu.make_async_copy(zeros, zeros, sems.at[place]).wait()
        return carry

    lax.fori_loop(0, sz.slots // 2, one, 0)
    lax.fori_loop(0, sz.slots // 2, done, 0)


def forward_kernel(sizes, wave, speed, back_ref, *refs):
    sz = sizes
    geo_refs = refs[:-13]
    x_hbm, leg_hbm, _, out_hbm, wide, spots, inverse, out_all, out_sems, x_all, leg_all, *sems = refs[-13:]
    band = lax.axis_index("band")
    pair_at = functools.partial(Pair, sz, wave, band)
    stream = Stream(sz, pair_at, x_hbm, leg_hbm, x_all, leg_all, *sems)
    stream.begin()
    pad = 2 * sz.field_pad
    each = sz.block // 2

    gather = spread_matrix(sz, lax.axis_index("lev"))
    cuts = [
        jnp.concatenate([back_ref[rp, g].astype(jnp.float32) for g in range(sz.groups)], axis=1)
        for rp in range(sz.rows // 2)
    ]
    wholes = dot(jnp.concatenate(cuts, axis=0).astype(jnp.bfloat16), gather, ((1,), (1,)))
    for rp in range(sz.rows // 2):
        whole = wholes[rp * sz.chunk:(rp + 1) * sz.chunk]
        rows = jnp.concatenate([
            whole[:, q * 2 * pad:(q + 1) * 2 * pad] for q in range(sz.quarters)
        ], axis=0)
        for geo_ref in geo_refs:
            rows = rows + geo_ref[rp].astype(jnp.float32)[:, 0:2 * pad]
        for r in range(2):
            part = rows[:, r * pad:(r + 1) * pad]
            part = jnp.concatenate([part, jnp.zeros((sz.spots, SLAB - pad), jnp.float32)], axis=1)
            spots[pl.ds((2 * rp + r) * sz.plane, sz.spots), :] = part
    stream.begin(1)
    row = quotient(iota((sz.pitch, SLAB), 0), 2)
    lane = iota((sz.pitch, SLAB), 1)
    for start in range(sz.tiles):
        degree = jnp.where(row < sz.tiles - start, row + start, row - 1) * SLAB + lane
        helm = (degree * (degree + 1)).astype(jnp.float32) / float(sz.trunc * (sz.trunc + 1))
        for f in range(sz.fields):
            denominator = 1.0 + time_step * time_step * helm * speed[f]
            inverse[start, pl.ds(f * sz.pitch, sz.pitch), :] = 1.0 / denominator
    stream.begin(2)
    out_tiles = out_all.reshape(BEHIND, each, sz.fields, sz.pitch // 2, 2, SLAB)

    def leave(place, k):
        at = lax.rem(place // each, BEHIND)

        for slot, first, count, here in pair_at(place).parts():
            pltpu.make_async_copy(
                out_tiles.at[at, k, :, pl.ds(here, count)],
                out_hbm.at[slot, :, pl.ds(first, count)],
                out_sems.at[at, k],
            ).start()

    def left(step):
        at = lax.rem(step, BEHIND)
        for k in range(each):
            await_tiles(out_hbm, out_sems.at[at, k])

    def block(step, feed):
        @pl.when(step >= BEHIND)
        def _():
            left(step)

        at = lax.rem(step, BEHIND)

        def products(k):
            stream.arrive(step * each + k)
            feed(k)
            pair = pair_at(step * each + k)
            values = jnp.concatenate([spots[pair.rows(side), :] for side in range(2)], axis=0)
            values = values.T.astype(jnp.bfloat16)[0:pad]
            tables = pair.tables(leg_all[step * each + k])
            for first in range(0, sz.packed, 2):
                count = min(2, sz.packed - first)
                tends = dot(values, tables[:, first * SLAB:(first + count) * SLAB])
                for t in range(first, first + count):
                    for c in range(2):
                        rows = pl.ds(2 * t + c, sz.field_pad, stride=sz.stride)
                        wide[k, rows, :] = tends[
                            c * sz.field_pad:(c + 1) * sz.field_pad, (t - first) * SLAB:(t - first + 1) * SLAB
                        ]

        def finish(k):
            place = step * each + k
            pair = pair_at(place)
            mine = row < pair.split
            degree = jnp.where(mine, row + pair.start, row - 1) * SLAB + lane
            floors = [jnp.where(n < 0, sz.degrees, n) for n in pair.numbers]
            live = degree >= jnp.where(mine, floors[0], floors[1])
            for f in range(sz.fields):
                rows = pl.ds(f * sz.pitch, sz.pitch)
                old = x_all[place, f].astype(jnp.float32)[0:sz.pitch]
                tend = wide[k, pl.ds(f * sz.stride, sz.pitch), :]
                new = (old + time_step * tend) * inverse[pair.start, rows, :]
                out_all[at, k, rows, :] = jnp.where(live, new, 0.0)

        products(0)
        for k in range(each):
            if k + 1 < each:
                products(k + 1)
            finish(k)
            leave(step * each + k, k)

    stream.run(block)
    for step in range(max(0, sz.steps - BEHIND), sz.steps):
        left(jnp.int32(step))


def params(mib):
    return pltpu.CompilerParams(vmem_limit_bytes=mib * MIB)


def smem():
    return pl.BlockSpec(memory_space=pltpu.SMEM)


def shards(spectra, legendre, slot_wave, row_points, gauss_weight, layer_depth, mode_speed):
    slots, _, fields, degrees = spectra.shape
    rows = legendre.shape[2]
    sz = Sizes(lax.axis_size("band"), lax.axis_size("lev"), slots, fields, degrees, rows)

    tiled = spectra.reshape(slots, 2, fields, sz.tiles, SLAB)
    tiled = with_layout_constraint(tiled, Layout((0, 2, 3, 1, 4)))
    tiled = tiled.transpose(0, 2, 3, 1, 4)
    tables = legendre.transpose(0, 2, 1)

    rounds = geo_rounds(sz)
    senders = [source for pairs in rounds for source, _ in pairs]
    sums = [sum(rounds, [])] if len(set(senders)) == len(senders) else rounds
    spots_shape = pltpu.VMEM((up_to(sz.plane * sz.rows, 8), SLAB), jnp.float32)
    pairs = slots // 2
    stream_scratch = [
        pltpu.VMEM((pairs, fields, sz.pitch_bf16, SLAB), jnp.bfloat16),
        pltpu.VMEM((pairs, rows, sz.packed * SLAB), jnp.bfloat16),
        pltpu.SemaphoreType.DMA((pairs,)),
        pltpu.SemaphoreType.DMA((pairs,)),
    ]
    wide_shape = pltpu.VMEM((sz.block // 2, up_to(sz.field_pad * sz.stride, 8), SLAB), jnp.float32)
    anywhere = pl.BlockSpec(memory_space=pl.ANY)
    vmem = pl.BlockSpec(memory_space=pltpu.VMEM)
    send_shape = (sz.bands, sz.groups, sz.chunk, SLAB)
    geo_shape = (sz.rows // 2, sz.spots, SLAB)

    sent, *geo = pl.pallas_call(
        functools.partial(inverse_kernel, sz, sums),
        in_specs=[smem(), smem(), smem(), smem(), anywhere, anywhere],
        out_specs=[vmem] * (1 + len(sums)),
        out_shape=[jax.ShapeDtypeStruct(send_shape, jnp.bfloat16)]
        + [jax.ShapeDtypeStruct(geo_shape, jnp.bfloat16)] * len(sums),
        scratch_shapes=[wide_shape, spots_shape, pltpu.VMEM((sz.spots, SLAB), jnp.int32), *stream_scratch],
        compiler_params=params(56),
        name="inverse_legendre",
    )(slot_wave, row_points, gauss_weight, layer_depth, tiled, tables)

    sent, points_later, wave_later = lax.optimization_barrier((sent, row_points, slot_wave))
    both = ("band", "lev")
    total = sz.bands * sz.groups
    flat = (total * sz.chunk, SLAB)
    arrived = lax.all_to_all(sent.reshape(flat), both, split_axis=0, concat_axis=0, tiled=True)

    pair_wave = wave_later.reshape(-1, 2)
    even_wave = jnp.where(pair_wave[:, 0] % 2 == 0, pair_wave[:, 0], pair_wave[:, 1])
    even_wave = even_wave.reshape(sz.bands, sz.halves, sz.chunk_live)
    even_wave = jnp.pad(even_wave, ((0, 0), (0, 0), (0, sz.chunk - sz.chunk_live)), constant_values=-1)
    even_wave = even_wave.transpose(1, 0, 2).reshape(sz.pairs)

    high = SLAB if sz.sorted % SLAB == 0 else sz.sorted
    table_rows = 16 + up_to(sz.sorted // 16, 8) + 8
    basis = pl.pallas_call(
        functools.partial(basis_kernel, sz),
        in_specs=[smem()],
        out_specs=anywhere,
        out_shape=jax.ShapeDtypeStruct((4, sz.sorted, sz.orbits), jnp.bfloat16),
        scratch_shapes=[
            pltpu.VMEM((sz.sorted // high, 4, high, sz.orbits), jnp.bfloat16),
            pltpu.VMEM((table_rows, sz.orbits), jnp.float32),
            pltpu.VMEM((table_rows, sz.orbits), jnp.float32),
            pltpu.SemaphoreType.DMA((sz.sorted // high,)),
        ],
        compiler_params=params(56),
        cost_estimate=pl.CostEstimate(
            flops=20 * sz.sorted * sz.orbits, bytes_accessed=8 * sz.sorted * sz.orbits, transcendentals=0,
        ),
        name="basis",
    )(points_later)

    even_row = even_wave.reshape(1, sz.pairs)
    moved = [lax.ppermute(geo[turn % len(sums)], "lev", pairs) for turn, pairs in enumerate(rounds)]
    *moved, arrived, basis, even_row = lax.optimization_barrier((*moved, arrived, basis, even_row))
    returned = pl.pallas_call(
        functools.partial(grid_kernel, sz),
        in_specs=[smem(), smem(), vmem, vmem, anywhere],
        out_specs=vmem,
        out_shape=jax.ShapeDtypeStruct(send_shape, jnp.bfloat16),
        scratch_shapes=[
            pltpu.VMEM((4, sz.sorted, sz.orbits), jnp.bfloat16),
            pltpu.VMEM((4, SLAB, sz.orbits), jnp.bfloat16),
            pltpu.SemaphoreType.DMA((-(-sz.orbits // (2 * SLAB)),)),
        ],
        compiler_params=params(56),
        cost_estimate=pl.CostEstimate(
            flops=4 * 4 * SLAB * sz.sorted * sz.orbits, bytes_accessed=8 * sz.sorted * sz.orbits, transcendentals=0,
        ),
        name="grid_products",
    )(
        row_points, gauss_weight, arrived.reshape(send_shape), even_row, basis,
    )
    returned, wave_last = lax.optimization_barrier((returned, slot_wave))

    back = lax.all_to_all(returned.reshape(flat), both, split_axis=0, concat_axis=0, tiled=True)

    out_shape = jax.ShapeDtypeStruct(tiled.shape, jnp.float32)
    zeroed = pl.pallas_call(
        functools.partial(zeros_kernel, sz),
        in_specs=[smem()],
        out_specs=anywhere,
        out_shape=out_shape,
        scratch_shapes=[
            pltpu.VMEM((fields, sz.tiles - 1, 2, SLAB), jnp.float32),
            pltpu.SemaphoreType.DMA((pairs,)),
        ],
        compiler_params=params(56),
        cost_estimate=pl.CostEstimate(
            flops=0, bytes_accessed=2 * slots * fields * degrees * 2, transcendentals=0,
        ),
        name="dead_zeros",
    )(wave_last)
    out = pl.pallas_call(
        functools.partial(forward_kernel, sz),
        in_specs=[smem(), smem()] + [vmem] * (1 + len(rounds)) + [anywhere] * 3,
        out_specs=anywhere,
        out_shape=out_shape,
        input_output_aliases={5 + len(rounds): 0},
        scratch_shapes=[
            wide_shape, spots_shape,
            pltpu.VMEM((sz.tiles, fields * sz.pitch, SLAB), jnp.float32),
            pltpu.VMEM((BEHIND, sz.block // 2, fields * sz.pitch, SLAB), jnp.float32),
            pltpu.SemaphoreType.DMA((BEHIND, sz.block // 2)),
            *stream_scratch,
        ],
        compiler_params=params(56),
        name="forward_legendre",
    )(slot_wave, mode_speed, back.reshape(send_shape), *moved, tiled, tables, zeroed)

    out = out.transpose(0, 1, 3, 2, 4)
    return out.reshape(slots, fields, 2, degrees).transpose(0, 2, 1, 3)


def solution(mesh):
    return jax.shard_map(
        shards,
        mesh=mesh,
        in_specs=(
            P("band", None, "lev", None),
            P("band", None, None),
            P(),
            P(),
            P(),
            P(),
            P("lev"),
        ),
        out_specs=P("band", None, "lev", None),
        check_vma=False,
    )
```
